128 devices in a mesh: dp: 16 (over z, y), tensor: 8 (over x, core).
Axes of the slice: x: 4, y: 4, z: 4, core: 2. Of those that a mesh axis runs over, the one named last changes fastest.
Arguments:
- query: bfloat16 [32, 128, 8192], P('dp', None, 'tensor'), may hold values from -6 to 6
- image: bfloat16 [32, 512, 8192], P('dp', None, 'tensor'), may hold values from -6 to 6
- tiles: int32 [32], replicated, may hold values from 0 to 4, as said below
- image_slot: int32 [32], replicated, may hold values from 0 to 31, as said below
- key_weight_matrix: bfloat16 [8192, 1024], P('dp', 'tensor'), may hold values from -0.0625 to 0.0625
- value_weight_matrix: bfloat16 [8192, 1024], P('dp', 'tensor'), may hold values from -0.0625 to 0.0625
- query_gain: float32 [128], replicated, may hold values from 0.5 to 2
- key_gain: float32 [128], replicated, may hold values from 0.5 to 2
- gate: float32 [1], replicated, may hold values from 0.3 to 1.5
- cotangent: bfloat16 [32, 128, 8192], P('dp', None, 'tensor'), may hold values from -6 to 6
Outputs:
- context: bfloat16 [32, 128, 8192], P('dp', None, 'tensor')
- d_query: bfloat16 [32, 128, 8192], P('dp', None, 'tensor')
- d_w_key: float32 [8192, 1024], P('dp', 'tensor')
- d_w_value: float32 [8192, 1024], P('dp', 'tensor')
The draws below stay inside these ranges and needn't reach their ends.
Inputs may be any that keep to these rules, and one draw needn't show every extreme that they name: Some sample has 4 tiles and some has none. image_slot is a permutation of the samples. Sample s sits at dp index s // 2; the image rows image_slot[s] sit at the same dp index or at the one that differs from it by half the dp axis, and of the two samples at one dp index at most one has its image at the other index.
All inputs are finite; a program needn't handle non-finite values.
Results may differ from the reference program's by a relative error of at most 0.02.
Values may be sent and summed in bfloat16 or wider, within the bound.
No kernel may reach another device: no remote copies, remote signals or barrier semaphores. Data moves between devices by JAX's collectives and lax.ppermute only.
A program may use at most 128 MiB of HBM per device.

```python
import math
import jax
import jax.numpy as jnp
from jax import lax

MODEL_WIDTH = 8192
HQ = 64
KEY_VALUE_HEADS = 8
HEAD_SIZE = 128
TXT = 128
TILE = 128
MAX_TILES = 4
IMG = 512
SAMPLES = 32
N_DP = 16


def tile_counts(key):
    counts = jax.random.randint(jax.random.fold_in(key, 11), (SAMPLES,), 0, MAX_TILES + 1)
    order = jax.random.permutation(jax.random.fold_in(key, 12), SAMPLES)
    counts = counts.at[order[0]].set(MAX_TILES)
    counts = counts.at[order[1]].set(0)
    return counts.astype(jnp.int32)


def draw_tiles(key, part):
    return tile_counts(key)


def draw_image_slot(key, part):
    counts = tile_counts(key)
    half = N_DP // 2
    shard = jnp.arange(half, dtype=jnp.int32)
    first = 2 * shard
    second = first + 1
    third = 2 * (shard + half)
    fourth = third + 1
    load_a = counts[first]
    load_b = counts[second]
    load_c = counts[third]
    load_d = counts[fourth]
    loads = jnp.stack([jnp.maximum(load_a + load_c, load_b + load_d), jnp.maximum(load_a + load_d, load_b + load_c), jnp.maximum(load_a + load_b, load_c + load_d)])
    best = jnp.argmin(loads, axis=0).astype(jnp.int32)
    slot_b = jnp.where(best == 2, second, third)
    slot_c = jnp.where(best == 0, second, jnp.where(best == 1, fourth, third))
    slot_d = jnp.where(best == 1, second, fourth)
    slots = jnp.zeros((SAMPLES,), jnp.int32)
    slots = slots.at[first].set(first).at[second].set(slot_b)
    slots = slots.at[third].set(slot_c).at[fourth].set(slot_d)
    return slots.astype(jnp.int32)


def strengthened(values, own_key, source, target, blocks, factor):
    def block_of(dim):
        return (jnp.arange(values.shape[dim]) // (values.shape[dim] // blocks)).reshape((-1,) + (1,) * (values.ndim - 1 - dim))

    first = jax.random.permutation(own_key, blocks)[block_of(target)]
    second = (block_of(target) + blocks // 2) % blocks
    return jnp.where((block_of(source) == first) | (block_of(source) == second), factor * values, values)


def levels(key, extent, cuts, low, high):
    factor_of = 1.0
    for position, parts in cuts:
        steps = jax.random.uniform(jax.random.fold_in(jax.random.fold_in(key, 6), position), (parts,), jnp.float32, low / len(cuts), high / len(cuts))
        factor_of = factor_of * jnp.repeat(jnp.exp(steps), extent[position] // parts).reshape((-1,) + (1,) * (len(extent) - 1 - position))
    return factor_of


def noise(stream_key, shape, spread, bound, pieces=(), held_as=jnp.bfloat16):
    entries = spread * jax.random.normal(stream_key, shape, jnp.float32)
    if pieces:
        entries = entries * levels(stream_key, shape, pieces, -0.22, 0.18)
    return jnp.clip(entries, -bound, bound).astype(held_as)


def heavy_noise(own_key, shape, spread, limit, cuts, heavy, kind=jnp.bfloat16):
    drawn = spread * jax.random.normal(own_key, shape, jnp.float32)
    if cuts:
        drawn = drawn * levels(own_key, shape, cuts, -0.22, 0.18)
    return jnp.clip(strengthened(drawn, jax.random.fold_in(own_key, 3), *heavy), -limit, limit).astype(kind)


def setup_inputs(seed: int = 0) -> dict:
    key_list = jax.random.split(jax.random.key(seed), 11)
    return {
        "query": noise(key_list[0], (SAMPLES, TXT, HQ * HEAD_SIZE), 1.0, 6.0, ((0, 16), (2, 8))),
        "image": heavy_noise(key_list[1], (SAMPLES, IMG, MODEL_WIDTH), 1.0, 6.0, ((0, 16), (2, 8)), (0, 2, 16, 2.0)),
        "tiles": draw_tiles(jax.random.fold_in(key_list[10], 71), 0),
        "image_slot": draw_image_slot(jax.random.fold_in(key_list[10], 71), 0),
        "key_weight_matrix": noise(key_list[4], (MODEL_WIDTH, KEY_VALUE_HEADS * HEAD_SIZE), MODEL_WIDTH ** -0.5, 0.0625, ((0, 16), (1, 8))),
        "value_weight_matrix": noise(key_list[5], (MODEL_WIDTH, KEY_VALUE_HEADS * HEAD_SIZE), MODEL_WIDTH ** -0.5, 0.0625, ((0, 16), (1, 8))),
        "query_gain": jnp.clip(jnp.exp(jax.random.uniform(key_list[6], (HEAD_SIZE,), jnp.float32, math.log(0.5), math.log(2.0))), 0.5, 2.0),
        "key_gain": jnp.clip(jnp.exp(jax.random.uniform(key_list[7], (HEAD_SIZE,), jnp.float32, math.log(0.5), math.log(2.0))), 0.5, 2.0),
        "gate": jnp.clip(jax.random.uniform(key_list[8], (1,), jnp.float32, 0.3, 1.5), 0.3, 1.5),
        "cotangent": noise(key_list[9], (SAMPLES, TXT, HQ * HEAD_SIZE), 1.0, 6.0, ((0, 16), (2, 8))),
    }


EPS = 1e-06

def rms_factor(values):
    return lax.rsqrt(lax.optimization_barrier(jnp.mean(values * values, axis=-1, keepdims=True)) + EPS)

def norm_back(values, norm_multiplier, gain, grad):
    weighted = grad * gain
    inner = lax.optimization_barrier(jnp.sum(weighted * values, axis=-1, keepdims=True))
    return norm_multiplier * weighted - values * (norm_multiplier * norm_multiplier * norm_multiplier) * inner / values.shape[-1]

def reference(query, image, tiles, image_slot, key_weight_matrix, value_weight_matrix, query_gain, key_gain, gate, cotangent):
    head_dim = query_gain.shape[0]
    kv_cols = key_weight_matrix.shape[1]
    kv_heads = kv_cols // head_dim
    group = query.shape[2] // kv_cols
    text_rows = query.shape[1]
    img_rows = image.shape[1]
    ratio = jnp.tanh(gate[0])
    scale = head_dim ** (-0.5)
    key_pos = jnp.arange(img_rows, dtype=jnp.int32)

    def one_sample(carry, inputs):
        q_in, cot_in, count, slot = inputs
        feats = lax.dynamic_index_in_dim(image, slot.astype(jnp.int32), 0, keepdims=False)
        kraw = jnp.dot(feats, key_weight_matrix, preferred_element_type=jnp.float32).reshape(img_rows, kv_heads, head_dim)
        vals = jnp.dot(feats, value_weight_matrix, preferred_element_type=jnp.float32).astype(jnp.bfloat16)
        vals = vals.reshape(img_rows, kv_heads, head_dim)
        key_factor = rms_factor(kraw)
        keys = (kraw * key_factor * key_gain).astype(jnp.bfloat16)
        q_raw = q_in.astype(jnp.float32).reshape(text_rows, kv_heads, group, head_dim)
        q_factor = rms_factor(q_raw)
        q_norm = (q_raw * q_factor * query_gain).astype(jnp.bfloat16)
        scores = jnp.einsum('tkgd,skd->kgts', q_norm.astype(jnp.float32), keys.astype(jnp.float32)) * scale
        valid = key_pos < count * TILE
        expo = jnp.where(valid, jnp.exp(scores), 0.0)
        total = lax.optimization_barrier(jnp.sum(expo, axis=-1, keepdims=True)) + (count == 0).astype(jnp.float32)
        total_rows = jnp.transpose(total[..., 0], (2, 0, 1))[..., None]
        weights_b = expo.astype(jnp.bfloat16)
        attended = jnp.einsum('kgts,skd->tkgd', weights_b.astype(jnp.float32), vals.astype(jnp.float32)) / total_rows
        context = (ratio * attended).astype(jnp.bfloat16).reshape(text_rows, -1)
        d_att = ratio * cot_in.astype(jnp.float32).reshape(text_rows, kv_heads, group, head_dim)
        d_att_b = d_att.astype(jnp.bfloat16)
        scaled_b = (d_att / total_rows).astype(jnp.bfloat16)
        delta = jnp.transpose(lax.optimization_barrier(jnp.sum(d_att * attended, axis=-1)), (1, 2, 0))[..., None]
        d_prob = jnp.einsum('tkgd,skd->kgts', d_att_b.astype(jnp.float32), vals.astype(jnp.float32))
        d_score = (expo / total * (d_prob - delta)).astype(jnp.bfloat16).astype(jnp.float32)
        d_qn = scale * jnp.einsum('kgts,skd->tkgd', d_score, keys.astype(jnp.float32))
        d_query = norm_back(q_raw, q_factor, query_gain, d_qn).astype(jnp.bfloat16).reshape(text_rows, -1)
        d_keys = scale * jnp.einsum('kgts,tkgd->skd', d_score, q_norm.astype(jnp.float32))
        d_vals = jnp.einsum('kgts,tkgd->skd', weights_b.astype(jnp.float32), scaled_b.astype(jnp.float32))
        grad_key_unnormed = norm_back(kraw, key_factor, key_gain, d_keys).astype(jnp.bfloat16).reshape(img_rows, -1)
        d_vals_b = d_vals.astype(jnp.bfloat16).reshape(img_rows, -1)
        dims = (((0,), (0,)), ((), ()))
        grad_key = lax.dot_general(feats, grad_key_unnormed, dims, preferred_element_type=jnp.float32)
        grad_value = lax.dot_general(feats, d_vals_b, dims, preferred_element_type=jnp.float32)
        return ((carry[0] + grad_key, carry[1] + grad_value), (context, d_query))
    start = (jnp.zeros(key_weight_matrix.shape, jnp.float32), jnp.zeros(value_weight_matrix.shape, jnp.float32))
    grads, outputs = lax.scan(one_sample, start, (query, cotangent, tiles, image_slot))
    return (outputs[0], outputs[1], grads[0], grads[1])
```

```python
import functools

import jax
import jax.numpy as jnp
from jax import lax
from jax.experimental import pallas as pl
from jax.experimental.pallas import tpu as pltpu
from jax.sharding import PartitionSpec as P

TILE = 128
RING = 4
EPS = 1e-06


def along_z(x, step):
    pairs = [(z * RING + y, (z + step) % RING * RING + y) for z in range(RING) for y in range(RING)]
    return lax.ppermute(x, "dp", pairs)


def along_y(x, step):
    pairs = [(z * RING + y, z * RING + (y + step) % RING) for z in range(RING) for y in range(RING)]
    return lax.ppermute(x, "dp", pairs)


def along_x(x, step):
    pairs = [(i * 2 + c, (i + step) % RING * 2 + c) for i in range(RING) for c in range(2)]
    return lax.ppermute(x, "tensor", pairs)


def other_core(x):
    return lax.ppermute(x, "tensor", [(i, i ^ 1) for i in range(2 * RING)])


def exchange_xz(x):
    pairs = []
    for z in range(RING):
        for y in range(RING):
            for i in range(RING):
                for c in range(2):
                    source = (z * RING + y) * 2 * RING + i * 2 + c
                    target = (i * RING + y) * 2 * RING + z * 2 + c
                    pairs.append((source, target))
    return lax.ppermute(x, ("dp", "tensor"), pairs)


def gathered(x, move):
    return [x] + [move(x, step) for step in range(1, RING)]


def scattered(blocks, move):
    arrived = [move(blocks[step], step) for step in range(1, RING)]
    total = blocks[0].astype(jnp.float32)
    for block in arrived:
        total = total + block.astype(jnp.float32)
    return total


def rms_factor(values):
    return lax.rsqrt(jnp.mean(values * values, axis=-1, keepdims=True) + EPS)


def norm_back(values, norm_multiplier, gain, grad):
    weighted = grad * gain
    inner = jnp.sum(weighted * values, axis=-1, keepdims=True)
    return (
        norm_multiplier * weighted
        - values * (norm_multiplier * norm_multiplier * norm_multiplier) * inner / values.shape[-1]
    )


def matmul(a, b, contract):
    return lax.dot_general(a, b, (contract, ((), ())), preferred_element_type=jnp.float32)


def attend_kernel(heads, index, ratio_ref, q_ref, cot_ref, kv_ref, gain_ref, *refs):
    context_ref, d_query_ref, d_kv_ref, d_key_sum, d_value_sum = refs[-5:]
    step = pl.program_id(0)
    head_dim = gain_ref.shape[1]
    scale = head_dim ** (-0.5)
    count = index[1]
    ratio = ratio_ref[0]
    gain = gain_ref[...]
    keys = kv_ref[:, :head_dim]
    vals = kv_ref[:, head_dim:]

    def stacked(ref):
        parts = [ref[0, :, h * head_dim : (h + 1) * head_dim] for h in range(heads)]
        return jnp.concatenate(parts, axis=0).astype(jnp.float32)

    def unstacked(ref, rows):
        text = rows.shape[0] // heads
        for h in range(heads):
            part = rows[h * text : (h + 1) * text]
            ref[0, :, h * head_dim : (h + 1) * head_dim] = part.astype(ref.dtype)

    @pl.when(step == 0)
    def _():
        d_key_sum[...] = jnp.zeros_like(d_key_sum)
        d_value_sum[...] = jnp.zeros_like(d_value_sum)

    q_raw = stacked(q_ref)
    q_factor = rms_factor(q_raw)
    q_norm = (q_raw * q_factor * gain).astype(jnp.bfloat16)
    raw = matmul(q_norm, keys, ((1,), (1,))) * scale
    place = lax.broadcasted_iota(jnp.int32, raw.shape, 1)
    expo = jnp.where(place < count * TILE, jnp.exp(raw), 0.0)
    total = jnp.sum(expo, axis=1, keepdims=True) + (count == 0).astype(jnp.float32)
    inverse = 1.0 / total
    weights_b = expo.astype(jnp.bfloat16)
    attended = matmul(weights_b, vals, ((1,), (0,))) * inverse
    unstacked(context_ref, ratio * attended)
    d_att = ratio * stacked(cot_ref)
    d_att_b = d_att.astype(jnp.bfloat16)
    scaled_b = (d_att * inverse).astype(jnp.bfloat16)
    delta = jnp.sum(d_att * attended, axis=1, keepdims=True)
    d_prob = matmul(d_att_b, vals, ((1,), (1,)))
    d_score = (expo * inverse * (d_prob - delta)).astype(jnp.bfloat16)
    d_qn = scale * matmul(d_score, keys, ((1,), (0,)))
    unstacked(d_query_ref, norm_back(q_raw, q_factor, gain, d_qn))
    d_key_sum[...] += matmul(d_score, q_norm, ((0,), (0,)))
    d_value_sum[...] += matmul(weights_b, scaled_b, ((0,), (0,)))

    @pl.when(step == pl.num_programs(0) - 1)
    def _():
        d_kv_ref[:, :head_dim] = (scale * d_key_sum[...]).astype(d_kv_ref.dtype)
        d_kv_ref[:, head_dim:] = d_value_sum[...].astype(d_kv_ref.dtype)


def attend(own, count, ratio, query, cot, key_value, gain, earlier, heads=2):
    rows, both = key_value.shape
    head_dim = both // 2
    text = query.shape[1]
    width = heads * head_dim
    block = pl.BlockSpec((1, text, width), lambda h, index: (index[0], 0, h))
    whole = lambda shape: pl.BlockSpec(shape, lambda h, index: (0, 0))
    in_specs = [
        pl.BlockSpec(memory_space=pltpu.SMEM),
        block,
        block,
        whole((rows, both)),
        whole((1, head_dim)),
    ]
    aliases = {}
    if earlier:
        in_specs += [pl.BlockSpec(memory_space=pl.ANY)] * 2
        aliases = {6: 0, 7: 1}
    steps = query.shape[2] // width
    return pl.pallas_call(
        functools.partial(attend_kernel, heads),
        grid_spec=pltpu.PrefetchScalarGridSpec(
            num_scalar_prefetch=1,
            grid=(steps,),
            in_specs=in_specs,
            out_specs=[block, block, whole((rows, both))],
            scratch_shapes=[pltpu.VMEM((rows, head_dim), jnp.float32)] * 2,
        ),
        out_shape=[
            jax.ShapeDtypeStruct(query.shape, jnp.bfloat16),
            jax.ShapeDtypeStruct(query.shape, jnp.bfloat16),
            jax.ShapeDtypeStruct((rows, both), jnp.bfloat16),
        ],
        input_output_aliases=aliases,
        compiler_params=pltpu.CompilerParams(
            dimension_semantics=("arbitrary",), vmem_limit_bytes=24 * 1024 * 1024
        ),
        cost_estimate=pl.CostEstimate(
            flops=14 * steps * heads * text * rows * head_dim,
            bytes_accessed=8 * text * steps * width + 6 * rows * head_dim,
            transcendentals=steps * heads * text * rows,
        ),
    )(
        jnp.stack([own, count]).astype(jnp.int32),
        ratio,
        query,
        cot,
        key_value,
        gain[None, :],
        *earlier,
    )


def per_device(
    query,
    image,
    tiles,
    image_slot,
    key_weight_matrix,
    value_weight_matrix,
    query_gain,
    key_gain,
    gate,
    cotangent,
):
    head_dim = query_gain.shape[0]
    samp_local, img_rows, depth = image.shape
    ratio = jnp.tanh(gate)
    rank = lax.axis_index("dp")
    place = lax.axis_index("tensor")
    z, y = rank // RING, rank % RING
    x, core = place // 2, place % 2

    shard = jnp.concatenate([key_weight_matrix, value_weight_matrix], axis=1)
    shard = exchange_xz(shard)
    half = shard.shape[0] // 2
    both = shard.shape[1]
    upper = jnp.concatenate(gathered(shard[:half], along_z), axis=1)
    lower = jnp.concatenate(gathered(shard[half:], along_y), axis=0)
    upper = jnp.concatenate(gathered(upper, along_y), axis=0)
    lower = jnp.concatenate(gathered(lower, along_z), axis=1)

    first = rank * samp_local
    every = jnp.arange(tiles.shape[0], dtype=jnp.int32)
    local_ids = first + jnp.arange(samp_local, dtype=jnp.int32)
    match = image_slot[None, :] == local_ids[:, None]
    slot_sample = jnp.sum(jnp.where(match, every[None, :], 0), axis=1)
    slot_away = slot_sample // samp_local != rank
    swaps = jnp.any(slot_away)
    far_slot = jnp.where(slot_away[1], 1, 0)
    home_slot = lax.dynamic_slice_in_dim(image_slot, first, samp_local)
    own_away = home_slot // samp_local != rank
    own_of_slot = (home_slot[1] == first + far_slot).astype(jnp.int32)
    far_own = jnp.where(swaps, jnp.where(own_away[1], 1, 0), own_of_slot)
    home_tiles = lax.dynamic_slice_in_dim(tiles, first, samp_local)

    columns = jnp.concatenate([image, other_core(image)], axis=2)
    feats = []
    for slot in (far_slot, 1 - far_slot):
        parts = []
        for h in range(2):
            for o in range(RING):
                block = ((y - o) % RING) ^ (2 * core)
                start = (slot, 0, block * 2 * half + h * half)
                parts.append(lax.dynamic_slice(columns, start, (1, img_rows, half))[0])
        feats.append(jnp.concatenate(parts, axis=1))

    raw_rows, key_values = [], []
    for rows in feats:
        blocks = []
        for d in range(RING):
            group = (z - x - d) % RING * both
            weights = jnp.concatenate(
                [
                    lax.dynamic_slice_in_dim(upper, group, both, 1),
                    lax.dynamic_slice_in_dim(lower, group, both, 1),
                ],
                axis=0,
            )
            block = matmul(rows, weights, ((1,), (0,)))
            blocks.append(block if d == 0 else block.astype(jnp.bfloat16))
        projected = scattered(blocks, along_x)
        raw = projected[:, :head_dim]
        keys = (raw * rms_factor(raw) * key_gain).astype(jnp.bfloat16)
        raw_rows.append(raw)
        key_values.append(
            jnp.concatenate([keys, projected[:, head_dim:].astype(jnp.bfloat16)], axis=1)
        )

    away = along_z(key_values[0], RING // 2)
    away = jnp.where(swaps, away, key_values[0])
    near_own = 1 - far_own
    earlier = ()
    grads = [None, None]
    order = ((0, far_own, away), (1, near_own, key_values[1]))
    for slot, own, key_value in order:
        result = attend(
            own, home_tiles[own], ratio, query, cotangent, key_value, query_gain, earlier
        )
        earlier = result[:2]
        grads[slot] = result[2]
    context, d_query = earlier
    back = along_z(grads[0], RING // 2)
    grads[0] = jnp.where(swaps, back, grads[0])

    d_rows = [[], []]
    for slot in (1, 0):
        raw = raw_rows[slot]
        grad = grads[slot].astype(jnp.float32)
        d_raw = norm_back(raw, rms_factor(raw), key_gain, grad[:, :head_dim])
        own = jnp.concatenate([d_raw.astype(jnp.bfloat16), grads[slot][:, head_dim:]], axis=1)
        d_rows[slot] = gathered(own, along_x)
    by_source = jnp.stack([jnp.concatenate([d_rows[0][o], d_rows[1][o]], axis=0) for o in range(RING)])
    groups = [
        lax.dynamic_index_in_dim(by_source, (x - z - d) % RING, 0, keepdims=False)
        for d in range(RING)
    ]
    all_groups = jnp.concatenate(groups, axis=1)
    all_feats = jnp.concatenate(feats, axis=0)

    def sent(block, d):
        return block if d == 0 else block.astype(jnp.bfloat16)

    upper_blocks, lower_blocks = [], []
    wide = RING * half
    for d in range(RING):
        o = -d % RING
        rows = all_feats[:, o * half : (o + 1) * half]
        upper_blocks.append(sent(matmul(rows, all_groups, ((0,), (0,))), d))
        lower_blocks.append(sent(matmul(all_feats[:, wide:], groups[d], ((0,), (0,))), d))
    upper_sum = scattered(upper_blocks, along_y)
    lower_sum = scattered(lower_blocks, along_z)
    upper_parts = [sent(upper_sum[:, d * both : (d + 1) * both], d) for d in range(RING)]
    lower_parts = [
        sent(lower_sum[-d % RING * half : (-d % RING + 1) * half], d) for d in range(RING)
    ]
    upper_sum = scattered(upper_parts, along_z)
    lower_sum = scattered(lower_parts, along_y)
    share = jnp.concatenate([upper_sum, lower_sum], axis=0).astype(jnp.bfloat16)
    share = exchange_xz(share).astype(jnp.float32)
    return (context, d_query, share[:, :head_dim], share[:, head_dim:])


def solution(mesh):
    placed = (
        P("dp", None, "tensor"),
        P("dp", None, "tensor"),
        P(),
        P(),
        P("dp", "tensor"),
        P("dp", "tensor"),
        P(),
        P(),
        P(),
        P("dp", None, "tensor"),
    )
    return jax.shard_map(
        per_device,
        mesh=mesh,
        in_specs=placed,
        out_specs=(
            P("dp", None, "tensor"),
            P("dp", None, "tensor"),
            P("dp", "tensor"),
            P("dp", "tensor"),
        ),
        check_vma=False,
    )
```

```python
import functools

import jax
import jax.numpy as jnp
from jax import lax
from jax.experimental import pallas as pl
from jax.experimental.pallas import tpu as pltpu
from jax.sharding import PartitionSpec as P

TILE = 128
RING = 4
EPS = 1e-06


def along_z(x, step):
    pairs = [(z * RING + y, (z + step) % RING * RING + y) for z in range(RING) for y in range(RING)]
    return lax.ppermute(x, "dp", pairs)


def along_y(x, step):
    pairs = [(z * RING + y, z * RING + (y + step) % RING) for z in range(RING) for y in range(RING)]
    return lax.ppermute(x, "dp", pairs)


def along_x(x, step):
    pairs = [(i * 2 + c, (i + step) % RING * 2 + c) for i in range(RING) for c in range(2)]
    return lax.ppermute(x, "tensor", pairs)


def other_core(x):
    return lax.ppermute(x, "tensor", [(i, i ^ 1) for i in range(2 * RING)])


def exchange_xz(x):
    pairs = []
    for z in range(RING):
        for y in range(RING):
            for i in range(RING):
                for c in range(2):
                    source = (z * RING + y) * 2 * RING + i * 2 + c
                    target = (i * RING + y) * 2 * RING + z * 2 + c
                    pairs.append((source, target))
    return lax.ppermute(x, ("dp", "tensor"), pairs)


def gathered(x, move):
    return [x] + [move(x, step) for step in (1, 3, 2)]


def ring_gather(blocks, moves):
    blocks = lax.optimization_barrier(tuple(blocks))
    near = []
    for block, move in zip(blocks, moves):
        near += [move(block, 1), move(block, 3)]
    near = lax.optimization_barrier(tuple(near))
    halves = []
    for i, move in enumerate(moves):
        half = near[2 * i].shape[0] // 2
        halves += [(near[2 * i][:half], 1, move), (near[2 * i + 1][half:], 3, move)]
    far = [move(block, step) for block, step, move in halves]
    return [
        (blocks[i], near[2 * i], near[2 * i + 1], far[2 * i], far[2 * i + 1])
        for i in range(len(moves))
    ]


def ring_sum(parts, moves):
    outgoing = []
    for part in parts:
        outgoing += [part[3], part[4]]
    outgoing = lax.optimization_barrier(tuple(outgoing))
    passing = []
    for i, move in enumerate(moves):
        passing += [move(outgoing[2 * i], 1), move(outgoing[2 * i + 1], 3)]
    passing = lax.optimization_barrier(tuple(passing))
    sent = []
    for i, part in enumerate(parts):
        half = part[3].shape[0]
        after, before = part[1], part[2]
        upper = after[:half] + passing[2 * i].astype(jnp.float32)
        lower = before[half:] + passing[2 * i + 1].astype(jnp.float32)
        sent += [
            jnp.concatenate([upper, after[half:]], axis=0).astype(jnp.bfloat16),
            jnp.concatenate([before[:half], lower], axis=0).astype(jnp.bfloat16),
        ]
    sent = lax.optimization_barrier(tuple(sent))
    arrived = []
    for i, move in enumerate(moves):
        arrived += [move(sent[2 * i], 1), move(sent[2 * i + 1], 3)]
    arrived = lax.optimization_barrier(tuple(arrived))
    return [
        part[0] + arrived[2 * i].astype(jnp.float32) + arrived[2 * i + 1].astype(jnp.float32)
        for i, part in enumerate(parts)
    ]


def scattered(parts, moves):
    sent = [[part[step].astype(jnp.bfloat16) for step in (1, 3, 2)] for part in parts]
    sent = lax.optimization_barrier(tuple(block for blocks in sent for block in blocks))
    order = [(i, k) for k in range(3) for i in range(len(parts))]
    totals = [part[0] for part in parts]
    for i, k in order:
        totals[i] = totals[i] + moves[i](sent[3 * i + k], (1, 3, 2)[k]).astype(jnp.float32)
    return totals


def rms_factor(values):
    return lax.rsqrt(jnp.mean(values * values, axis=-1, keepdims=True) + EPS)


def norm_back(values, norm_multiplier, gain, grad):
    weighted = grad * gain
    inner = jnp.sum(weighted * values, axis=-1, keepdims=True)
    return (
        norm_multiplier * weighted
        - values * (norm_multiplier * norm_multiplier * norm_multiplier) * inner / values.shape[-1]
    )


def matmul(a, b, contract):
    return lax.dot_general(a, b, (contract, ((), ())), preferred_element_type=jnp.float32)


def project_kernel(index, rows_ref, *refs):
    uppers, lowers, outs = refs[:5], refs[5:10], refs[10:]
    own_ref, after_ref, before_ref, far_key_ref, far_value_ref = outs
    both = own_ref.shape[1]
    head_dim = both // 2
    half = uppers[0].shape[0]
    lower_at = RING * half
    order = ((uppers[0], 0), (uppers[1], half), (uppers[3], 2 * half))
    order += ((uppers[4], 2 * half + half // 2), (uppers[2], 3 * half))

    def product(o):
        total = None
        for block, at in order:
            part = matmul(
                rows_ref[:, at : at + block.shape[0]],
                block[:, o * both : (o + 1) * both],
                ((1,), (0,)),
            )
            total = part if total is None else total + part
        if o == 2:
            middle = lower_at + lowers[3].shape[0]
            total = total + matmul(rows_ref[:, lower_at:middle], lowers[3][...], ((1,), (0,)))
            return total + matmul(rows_ref[:, middle:], lowers[4][...], ((1,), (0,)))
        return total + matmul(rows_ref[:, lower_at:], lowers[min(o, 2)][...], ((1,), (0,)))

    for o in range(RING):
        total = product(o)
        target = (index[0] - o + RING) % RING

        @pl.when(target == 0)
        def _():
            own_ref[...] = total

        @pl.when(target == 1)
        def _():
            after_ref[...] = total.astype(after_ref.dtype)

        @pl.when(target == 3)
        def _():
            before_ref[...] = total.astype(before_ref.dtype)

        @pl.when(target == 2)
        def _():
            far_key_ref[...] = total[:, :head_dim].astype(far_key_ref.dtype)
            far_value_ref[...] = total[:, head_dim:].astype(far_value_ref.dtype)


VMEM = pl.BlockSpec(memory_space=pltpu.VMEM)
SMEM = pl.BlockSpec(memory_space=pltpu.SMEM)


def project(shift, rows, upper, lower):
    count, depth = rows.shape
    both = lower[0].shape[1]
    wide = jax.ShapeDtypeStruct((count, both), jnp.bfloat16)
    narrow = jax.ShapeDtypeStruct((count, both // 2), jnp.bfloat16)
    return pl.pallas_call(
        project_kernel,
        in_specs=[SMEM] + [VMEM] * 11,
        out_specs=[VMEM] * 5,
        out_shape=[jax.ShapeDtypeStruct((count, both), jnp.float32), wide, wide, narrow, narrow],
        compiler_params=pltpu.CompilerParams(vmem_limit_bytes=24 * 1024 * 1024),
        cost_estimate=pl.CostEstimate(
            flops=2 * RING * count * depth * both, bytes_accessed=8 * 1024 * 1024, transcendentals=0
        ),
    )(shift, rows, *upper, *lower)


def passed_kernel(after_ref, before_ref, key_ref, value_ref, to_after_ref, to_before_ref):
    head_dim = key_ref.shape[1]

    def added(block, piece):
        return (block.astype(jnp.float32) + piece.astype(jnp.float32)).astype(jnp.bfloat16)

    to_after_ref[:, :head_dim] = added(after_ref[:, :head_dim], key_ref[...])
    to_after_ref[:, head_dim:] = after_ref[:, head_dim:]
    to_before_ref[:, :head_dim] = before_ref[:, :head_dim]
    to_before_ref[:, head_dim:] = added(before_ref[:, head_dim:], value_ref[...])


def passed(after, before, key_piece, value_piece):
    return pl.pallas_call(
        passed_kernel,
        in_specs=[VMEM] * 4,
        out_specs=[VMEM] * 2,
        out_shape=[jax.ShapeDtypeStruct(after.shape, after.dtype)] * 2,
        cost_estimate=pl.CostEstimate(
            flops=after.size, bytes_accessed=10 * after.size, transcendentals=0
        ),
    )(after, before, key_piece, value_piece)


def finish_kernel(own_ref, left_ref, right_ref, gain_ref, raw_ref, key_value_ref):
    head_dim = raw_ref.shape[1]
    total = own_ref[...] + left_ref[...].astype(jnp.float32) + right_ref[...].astype(jnp.float32)
    raw = total[:, :head_dim]
    raw_ref[...] = raw
    key_value_ref[:, :head_dim] = (raw * rms_factor(raw) * gain_ref[...]).astype(jnp.bfloat16)
    key_value_ref[:, head_dim:] = total[:, head_dim:].astype(jnp.bfloat16)


def finish(own, left, right, gain):
    rows, both = own.shape
    return pl.pallas_call(
        finish_kernel,
        in_specs=[VMEM] * 4,
        out_specs=[VMEM] * 2,
        out_shape=[
            jax.ShapeDtypeStruct((rows, both // 2), jnp.float32),
            jax.ShapeDtypeStruct((rows, both), jnp.bfloat16),
        ],
        cost_estimate=pl.CostEstimate(
            flops=6 * own.size, bytes_accessed=12 * own.size, transcendentals=rows
        ),
    )(own, left, right, gain[None, :])


def turn_kernel(flag, raw_ref, grad_ref, other_ref, gain_ref, out_ref):
    head_dim = raw_ref.shape[1]
    grad = jnp.where(flag[0] != 0, other_ref[...], grad_ref[...])
    raw = raw_ref[...]
    d_raw = norm_back(raw, rms_factor(raw), gain_ref[...], grad[:, :head_dim].astype(jnp.float32))
    out_ref[:, :head_dim] = d_raw.astype(jnp.bfloat16)
    out_ref[:, head_dim:] = grad[:, head_dim:]


def turn(flag, raw, grad, other, gain):
    return pl.pallas_call(
        turn_kernel,
        in_specs=[SMEM] + [VMEM] * 4,
        out_specs=VMEM,
        out_shape=jax.ShapeDtypeStruct(grad.shape, jnp.bfloat16),
        cost_estimate=pl.CostEstimate(
            flops=6 * grad.size, bytes_accessed=8 * grad.size, transcendentals=raw.shape[0]
        ),
    )(flag, raw, grad, other, gain[None, :])


def attend_kernel(heads, index, ratio_ref, q_ref, cot_ref, kv_ref, away_ref, gain_ref, *refs):
    context_ref, d_query_ref, d_kv_ref, d_key_sum, d_value_sum = refs[-5:]
    step = pl.program_id(0)
    head_dim = gain_ref.shape[1]
    scale = head_dim ** (-0.5)
    count = index[1]
    ratio = ratio_ref[0]
    gain = gain_ref[...]
    key_value = jnp.where(index[2] != 0, away_ref[...], kv_ref[...])
    keys = key_value[:, :head_dim]
    vals = key_value[:, head_dim:]

    def stacked(ref):
        parts = [ref[0, :, h * head_dim : (h + 1) * head_dim] for h in range(heads)]
        return jnp.concatenate(parts, axis=0).astype(jnp.float32)

    def unstacked(ref, rows):
        text = rows.shape[0] // heads
        for h in range(heads):
            part = rows[h * text : (h + 1) * text]
            ref[0, :, h * head_dim : (h + 1) * head_dim] = part.astype(ref.dtype)

    @pl.when(step == 0)
    def _():
        d_key_sum[...] = jnp.zeros_like(d_key_sum)
        d_value_sum[...] = jnp.zeros_like(d_value_sum)

    q_raw = stacked(q_ref)
    q_factor = rms_factor(q_raw)
    q_norm = (q_raw * q_factor * gain).astype(jnp.bfloat16)
    raw = matmul(q_norm, keys, ((1,), (1,))) * scale
    place = lax.broadcasted_iota(jnp.int32, raw.shape, 1)
    expo = jnp.where(place < count * TILE, jnp.exp(raw), 0.0)
    total = jnp.sum(expo, axis=1, keepdims=True) + (count == 0).astype(jnp.float32)
    inverse = 1.0 / total
    weights_b = expo.astype(jnp.bfloat16)
    attended = matmul(weights_b, vals, ((1,), (0,))) * inverse
    unstacked(context_ref, ratio * attended)
    d_att = ratio * stacked(cot_ref)
    d_att_b = d_att.astype(jnp.bfloat16)
    scaled_b = (d_att * inverse).astype(jnp.bfloat16)
    delta = jnp.sum(d_att * attended, axis=1, keepdims=True)
    d_prob = matmul(d_att_b, vals, ((1,), (1,)))
    d_score = (expo * inverse * (d_prob - delta)).astype(jnp.bfloat16)
    d_qn = scale * matmul(d_score, keys, ((1,), (0,)))
    unstacked(d_query_ref, norm_back(q_raw, q_factor, gain, d_qn))
    d_key_sum[...] += matmul(d_score, q_norm, ((0,), (0,)))
    d_value_sum[...] += matmul(weights_b, scaled_b, ((0,), (0,)))

    @pl.when(step == pl.num_programs(0) - 1)
    def _():
        d_kv_ref[:, :head_dim] = (scale * d_key_sum[...]).astype(d_kv_ref.dtype)
        d_kv_ref[:, head_dim:] = d_value_sum[...].astype(d_kv_ref.dtype)


def attend(own, count, flag, ratio, query, cot, key_value, away, gain, earlier, heads=2):
    rows, both = key_value.shape
    head_dim = both // 2
    text = query.shape[1]
    width = heads * head_dim
    block = pl.BlockSpec((1, text, width), lambda h, index: (index[0], 0, h))
    whole = lambda shape: pl.BlockSpec(shape, lambda h, index: (0, 0))
    in_specs = [
        pl.BlockSpec(memory_space=pltpu.SMEM),
        block,
        block,
        whole((rows, both)),
        whole((rows, both)),
        whole((1, head_dim)),
    ]
    aliases = {}
    if earlier:
        in_specs += [pl.BlockSpec(memory_space=pl.ANY)] * 2
        aliases = {7: 0, 8: 1}
    steps = query.shape[2] // width
    return pl.pallas_call(
        functools.partial(attend_kernel, heads),
        grid_spec=pltpu.PrefetchScalarGridSpec(
            num_scalar_prefetch=1,
            grid=(steps,),
            in_specs=in_specs,
            out_specs=[block, block, whole((rows, both))],
            scratch_shapes=[pltpu.VMEM((rows, head_dim), jnp.float32)] * 2,
        ),
        out_shape=[
            jax.ShapeDtypeStruct(query.shape, jnp.bfloat16),
            jax.ShapeDtypeStruct(query.shape, jnp.bfloat16),
            jax.ShapeDtypeStruct((rows, both), jnp.bfloat16),
        ],
        input_output_aliases=aliases,
        compiler_params=pltpu.CompilerParams(
            dimension_semantics=("arbitrary",), vmem_limit_bytes=24 * 1024 * 1024
        ),
        cost_estimate=pl.CostEstimate(
            flops=14 * steps * heads * text * rows * head_dim,
            bytes_accessed=8 * text * steps * width + 6 * rows * head_dim,
            transcendentals=steps * heads * text * rows,
        ),
    )(
        jnp.stack([own, count, flag]).astype(jnp.int32),
        ratio,
        query,
        cot,
        key_value,
        away,
        gain[None, :],
        *earlier,
    )


def per_device(
    query,
    image,
    tiles,
    image_slot,
    key_weight_matrix,
    value_weight_matrix,
    query_gain,
    key_gain,
    gate,
    cotangent,
):
    head_dim = query_gain.shape[0]
    samp_local, img_rows, depth = image.shape
    ratio = jnp.tanh(gate)
    rank = lax.axis_index("dp")
    place = lax.axis_index("tensor")
    z, y = rank // RING, rank % RING
    x, core = place // 2, place % 2

    first = rank * samp_local
    every = jnp.arange(tiles.shape[0], dtype=jnp.int32)
    local_ids = first + jnp.arange(samp_local, dtype=jnp.int32)
    match = image_slot[None, :] == local_ids[:, None]
    slot_sample = jnp.sum(jnp.where(match, every[None, :], 0), axis=1)
    slot_away = slot_sample // samp_local != rank
    swaps = jnp.any(slot_away)
    far_slot = jnp.where(slot_away[1], 1, 0)
    home_slot = lax.dynamic_slice_in_dim(image_slot, first, samp_local)
    own_away = home_slot // samp_local != rank
    own_of_slot = (home_slot[1] == first + far_slot).astype(jnp.int32)
    far_own = jnp.where(swaps, jnp.where(own_away[1], 1, 0), own_of_slot)
    home_tiles = lax.dynamic_slice_in_dim(tiles, first, samp_local)

    shard = jnp.concatenate([key_weight_matrix, value_weight_matrix], axis=1)
    half = shard.shape[0] // 2
    both = shard.shape[1]
    shard = exchange_xz(shard)

    columns = jnp.concatenate([image, other_core(image)], axis=2)
    feats = []
    for slot in (far_slot, 1 - far_slot):
        parts = []
        for h in range(2):
            for o in range(RING):
                block = ((y - o) % RING) ^ (2 * core)
                start = (slot, 0, block * 2 * half + h * half)
                parts.append(lax.dynamic_slice(columns, start, (1, img_rows, half))[0])
        feats.append(jnp.concatenate(parts, axis=1))
    shard, *feats = lax.optimization_barrier((shard, *feats))
    upper, lower = shard[:half], shard[half:]
    moved = [[upper], [lower]]
    for step in (1, 3, 2):
        moved[0].append(along_z(upper, step))
        moved[1].append(along_y(lower, step))
    moved = lax.optimization_barrier(tuple(moved[0]) + tuple(moved[1]))
    upper = jnp.concatenate([moved[i] for i in (0, 1, 3, 2)], axis=1)
    lower = jnp.concatenate([moved[i] for i in (4, 5, 7, 6)], axis=0)
    upper, lower = ring_gather([upper, lower], [along_y, along_z])

    shift = ((z - x) % RING).astype(jnp.int32)[None]
    made = [project(shift, rows, upper, lower) for rows in feats]
    arrived = []
    for own, after, before, far_key, far_value in made:
        arrived.append((along_x(far_key, 1), along_x(far_value, 3)))
    raw_rows, key_values = [], []
    for (own, after, before, _, _), (key_piece, value_piece) in zip(made, arrived):
        to_after, to_before = passed(after, before, key_piece, value_piece)
        left, right = along_x(to_after, 1), along_x(to_before, 3)
        raw, key_value = finish(own, left, right, key_gain)
        raw_rows.append(raw)
        key_values.append(key_value)

    flag = swaps.astype(jnp.int32)
    away = along_z(key_values[0], RING // 2)
    near_own = 1 - far_own
    shared = (ratio, query, cotangent)
    *earlier, far_grad = attend(
        far_own, home_tiles[far_own], flag, *shared, key_values[0], away, query_gain, ()
    )
    back = along_z(far_grad, RING // 2)
    context, d_query, near_grad = attend(
        near_own, home_tiles[near_own], 0, *shared, key_values[1], key_values[1], query_gain, earlier
    )

    near_rows = turn(jnp.zeros_like(flag)[None], raw_rows[1], near_grad, near_grad, key_gain)
    far_rows = turn(flag[None], raw_rows[0], far_grad, back, key_gain)
    d_rows = []
    for rows in (far_rows, near_rows):
        d_rows.append([rows, along_x(rows, 1), along_x(rows, 3)])
    for entry in d_rows:
        left = along_x(entry[1][:, :head_dim], 1)
        right = along_x(entry[2][:, head_dim:], 3)
        entry.insert(2, jnp.concatenate([left, right], axis=1))
    by_source = jnp.stack([jnp.concatenate([d_rows[0][o], d_rows[1][o]], axis=0) for o in range(RING)])
    groups = [
        lax.dynamic_index_in_dim(by_source, (x - z - d) % RING, 0, keepdims=False)
        for d in range(RING)
    ]
    all_groups = jnp.concatenate(groups, axis=1)
    all_feats = jnp.concatenate(feats, axis=0)

    wide = RING * half

    def upper_product(start, count):
        return matmul(all_feats[:, start : start + count], all_groups, ((0,), (0,)))

    def lower_product(start, count, d):
        return matmul(all_feats[:, wide + start : wide + start + count], groups[d], ((0,), (0,)))

    def sent(block):
        return block.astype(jnp.bfloat16)

    upper_parts = (
        upper_product(0, half),
        upper_product(3 * half, half),
        upper_product(half, half),
        sent(upper_product(2 * half, half // 2)),
        sent(upper_product(2 * half + half // 2, half // 2)),
    )
    lower_parts = (
        lower_product(0, wide, 0),
        lower_product(0, wide, 1),
        lower_product(0, wide, 3),
        sent(lower_product(0, wide // 2, 2)),
        sent(lower_product(wide // 2, wide // 2, 2)),
    )
    upper_sum, lower_sum = ring_sum([upper_parts, lower_parts], [along_y, along_z])
    upper_parts = [upper_sum[:, d * both : (d + 1) * both] for d in range(RING)]
    lower_parts = [lower_sum[-d % RING * half : (-d % RING + 1) * half] for d in range(RING)]
    upper_sum, lower_sum = scattered([upper_parts, lower_parts], [along_z, along_y])
    share = jnp.concatenate([upper_sum, lower_sum], axis=0).astype(jnp.bfloat16)
    share = exchange_xz(share).astype(jnp.float32)
    return (context, d_query, share[:, :head_dim], share[:, head_dim:])


def solution(mesh):
    placed = (
        P("dp", None, "tensor"),
        P("dp", None, "tensor"),
        P(),
        P(),
        P("dp", "tensor"),
        P("dp", "tensor"),
        P(),
        P(),
        P(),
        P("dp", None, "tensor"),
    )
    return jax.shard_map(
        per_device,
        mesh=mesh,
        in_specs=placed,
        out_specs=(
            P("dp", None, "tensor"),
            P("dp", None, "tensor"),
            P("dp", "tensor"),
            P("dp", "tensor"),
        ),
        check_vma=False,
    )
```

```python
import functools

import jax
import jax.numpy as jnp
from jax import lax
from jax.experimental import pallas as pl
from jax.experimental.pallas import tpu as pltpu
from jax.sharding import PartitionSpec as P

TILE = 128
RING = 4
EPS = 1e-06


def along_z(x, step):
    pairs = [(z * RING + y, (z + step) % RING * RING + y) for z in range(RING) for y in range(RING)]
    return lax.ppermute(x, "dp", pairs)


def along_y(x, step):
    pairs = [(z * RING + y, z * RING + (y + step) % RING) for z in range(RING) for y in range(RING)]
    return lax.ppermute(x, "dp", pairs)


def along_x(x, step):
    pairs = [(i * 2 + c, (i + step) % RING * 2 + c) for i in range(RING) for c in range(2)]
    return lax.ppermute(x, "tensor", pairs)


def other_core(x):
    return lax.ppermute(x, "tensor", [(i, i ^ 1) for i in range(2 * RING)])


def exchange_xz(x):
    pairs = []
    for z in range(RING):
        for y in range(RING):
            for i in range(RING):
                for c in range(2):
                    source = (z * RING + y) * 2 * RING + i * 2 + c
                    target = (i * RING + y) * 2 * RING + z * 2 + c
                    pairs.append((source, target))
    return lax.ppermute(x, ("dp", "tensor"), pairs)


def gathered(x, move):
    far, after, before = (move(x, step) for step in (2, 1, 3))
    return [x, after, far, before]


def scattered(parts, moves):
    totals = [[part[0]] for part in parts]
    for step in (2, 1, 3):
        for i, move in enumerate(moves):
            totals[i].append(move(parts[i][step].astype(jnp.bfloat16), step))
    return totals


def summed(blocks):
    total = blocks[0].astype(jnp.float32)
    for block in blocks[1:]:
        total = total + block.astype(jnp.float32)
    return total


def rms_factor(values):
    return lax.rsqrt(jnp.mean(values * values, axis=-1, keepdims=True) + EPS)


def norm_back(values, norm_multiplier, gain, grad):
    weighted = grad * gain
    inner = jnp.sum(weighted * values, axis=-1, keepdims=True)
    return (
        norm_multiplier * weighted
        - values * (norm_multiplier * norm_multiplier * norm_multiplier) * inner / values.shape[-1]
    )


def matmul(a, b, contract):
    return lax.dot_general(a, b, (contract, ((), ())), preferred_element_type=jnp.float32)


VMEM = pl.BlockSpec(memory_space=pltpu.VMEM)
SMEM = pl.BlockSpec(memory_space=pltpu.SMEM)
HBM = pl.BlockSpec(memory_space=pltpu.HBM)
PARAMS = pltpu.CompilerParams(vmem_limit_bytes=60 * 1024 * 1024)


def arrange_kernel(half, index, own_ref, other_ref, out_ref, sems):
    slots, rows, depth = own_ref.shape
    waits = []
    for s in range(slots):
        for h in range(2):
            for o in range(RING):
                block = ((index[0] - o + RING) % RING) ^ (2 * index[1])
                start = pl.multiple_of(block % 2 * 2 * half + h * half, half)
                target = out_ref.at[pl.ds(s * rows, rows), pl.ds((h * RING + o) * half, half)]
                sem = sems.at[len(waits)]
                columns = pl.ds(start, half)
                own = pltpu.make_async_copy(own_ref.at[s ^ index[2], :, columns], target, sem)
                other = pltpu.make_async_copy(other_ref.at[s ^ index[2], :, columns], target, sem)
                pl.when(block < 2)(own.start)
                pl.when(block >= 2)(other.start)
                waits.append(own)
    for copy in waits:
        copy.wait()


def arrange(index, own, other, half):
    slots, rows, depth = own.shape
    return pl.pallas_call(
        functools.partial(arrange_kernel, half),
        in_specs=[SMEM, HBM, HBM],
        out_specs=HBM,
        out_shape=jax.ShapeDtypeStruct((slots * rows, 2 * depth), own.dtype),
        scratch_shapes=[pltpu.SemaphoreType.DMA((slots * 2 * RING,))],
        compiler_params=PARAMS,
        cost_estimate=pl.CostEstimate(flops=0, bytes_accessed=8 * own.size, transcendentals=0),
    )(index, own, other)


def project_kernel(index, rows_ref, *refs):
    uppers, lowers, outs = refs[:RING], refs[RING : 2 * RING], refs[2 * RING : 3 * RING]
    rows, weights, stage, row_sems, sems, out_sems = refs[3 * RING :]
    half = uppers[0].shape[0]
    both = lowers[0].shape[1]
    slots = row_sems.shape[0]
    count = rows.shape[0] // slots
    row_copies, copies = [], []
    for s in range(slots):
        part = pl.ds(s * count, count)
        row_copies.append(pltpu.make_async_copy(rows_ref.at[part], rows.at[part], row_sems.at[s]))
    row_copies[0].start()
    for o in range(RING):
        for k in range(RING):
            source = uppers[k].at[:, pl.ds(o * both, both)]
            target = weights.at[o, pl.ds(k * half, half)]
            copies.append(pltpu.make_async_copy(source, target, sems.at[o, k]))
        target = weights.at[o, pl.ds(RING * half, RING * half)]
        copies.append(pltpu.make_async_copy(lowers[o], target, sems.at[o, RING]))
    for copy in copies:
        copy.start()
    for copy in row_copies[1:]:
        copy.start()
    row_copies[0].wait()
    for copy in copies:
        copy.wait()
    stores = []
    for s in range(slots):
        if s:
            row_copies[s].wait()
        for d in (2, 1, 3, 0):
            o = (index[0] - d + RING) % RING
            part = pl.ds(s * count, count)
            stage[d, part] = matmul(rows[part], weights[o], ((1,), (0,))).astype(stage.dtype)
            store = pltpu.make_async_copy(stage.at[d, part], outs[d].at[part], out_sems.at[d, s])
            store.start()
            stores.append(store)
    for store in stores:
        store.wait()


def project(shift, rows, uppers, lowers):
    count, depth = rows.shape
    both = lowers[0].shape[1]
    slots = 2
    return pl.pallas_call(
        project_kernel,
        in_specs=[SMEM] + [HBM] * (1 + 2 * RING),
        out_specs=[HBM] * RING,
        out_shape=[jax.ShapeDtypeStruct((count, both), jnp.bfloat16)] * RING,
        scratch_shapes=[
            pltpu.VMEM((count, depth), jnp.bfloat16),
            pltpu.VMEM((RING, depth, both), jnp.bfloat16),
            pltpu.VMEM((RING, count, both), jnp.bfloat16),
            pltpu.SemaphoreType.DMA((slots,)),
            pltpu.SemaphoreType.DMA((RING, RING + 1)),
            pltpu.SemaphoreType.DMA((RING, slots)),
        ],
        compiler_params=PARAMS,
        cost_estimate=pl.CostEstimate(
            flops=2 * RING * count * depth * both,
            bytes_accessed=2 * count * depth + 2 * RING * both * (depth + count),
            transcendentals=0,
        ),
    )(shift, rows, *uppers, *lowers)


def finish_kernel(own_ref, far_ref, left_ref, right_ref, gain_ref, raw_ref, first_ref, second_ref):
    step = pl.program_id(0)
    head_dim = raw_ref.shape[1]
    total = summed([own_ref[...], far_ref[...], left_ref[...], right_ref[...]])
    raw = total[:, :head_dim]
    raw_ref[...] = raw
    keys = (raw * rms_factor(raw) * gain_ref[...]).astype(jnp.bfloat16)
    vals = total[:, head_dim:].astype(jnp.bfloat16)
    parts = pl.num_programs(0) // 2

    @pl.when(step < parts)
    def _():
        first_ref[:, :head_dim] = keys
        first_ref[:, head_dim:] = vals

    @pl.when(step >= parts)
    def _():
        second_ref[:, :head_dim] = keys
        second_ref[:, head_dim:] = vals


def finish(blocks, gain, parts=2):
    rows, both = blocks[0].shape
    count = rows // (2 * parts)
    block = pl.BlockSpec((count, both), lambda i: (i, 0))
    return pl.pallas_call(
        finish_kernel,
        grid=(2 * parts,),
        in_specs=[block] * RING + [pl.BlockSpec((1, both // 2), lambda i: (0, 0))],
        out_specs=[
            pl.BlockSpec((count, both // 2), lambda i: (i, 0)),
            pl.BlockSpec((count, both), lambda i: (jnp.minimum(i, parts - 1), 0)),
            pl.BlockSpec((count, both), lambda i: (jnp.maximum(i - parts, 0), 0)),
        ],
        out_shape=[
            jax.ShapeDtypeStruct((rows, both // 2), jnp.float32),
            jax.ShapeDtypeStruct((rows // 2, both), jnp.bfloat16),
            jax.ShapeDtypeStruct((rows // 2, both), jnp.bfloat16),
        ],
        compiler_params=PARAMS,
        cost_estimate=pl.CostEstimate(
            flops=6 * rows * both, bytes_accessed=12 * rows * both, transcendentals=rows
        ),
    )(*blocks, gain[None, :])


def turn_kernel(flag, raw_ref, grad_ref, other_ref, gain_ref, out_ref):
    head_dim = raw_ref.shape[1]
    grad = jnp.where(flag[0] != 0, other_ref[...], grad_ref[...])
    raw = raw_ref[...]
    d_raw = norm_back(raw, rms_factor(raw), gain_ref[...], grad[:, :head_dim].astype(jnp.float32))
    out_ref[:, :head_dim] = d_raw.astype(jnp.bfloat16)
    out_ref[:, head_dim:] = grad[:, head_dim:]


def turn(flag, slot, raw, grad, other, gain, parts=2):
    rows, both = grad.shape
    count = rows // parts
    block = pl.BlockSpec((count, both), lambda i: (i, 0))
    return pl.pallas_call(
        turn_kernel,
        grid=(parts,),
        in_specs=[
            SMEM,
            pl.BlockSpec((count, both // 2), lambda i: (slot * parts + i, 0)),
            block,
            block,
            pl.BlockSpec((1, both // 2), lambda i: (0, 0)),
        ],
        out_specs=block,
        out_shape=jax.ShapeDtypeStruct(grad.shape, jnp.bfloat16),
        compiler_params=PARAMS,
        cost_estimate=pl.CostEstimate(
            flops=6 * grad.size, bytes_accessed=8 * grad.size, transcendentals=rows
        ),
    )(flag, raw, grad, other, gain[None, :])


def collect_kernel(index, *refs):
    sources, out_ref, sems = refs[:-2], refs[-2], refs[-1]
    rows, both = sources[0].shape
    copies = []
    for i, source in enumerate(sources):
        slot, o = i // RING, i % RING
        start = pl.multiple_of((index[0] - o + RING) % RING * both, both)
        target = out_ref.at[pl.ds(slot * rows, rows), pl.ds(start, both)]
        copies.append(pltpu.make_async_copy(source, target, sems.at[i]))
    for copy in copies:
        copy.start()
    for copy in copies:
        copy.wait()


def collect(shift, first, second):
    rows, both = first[0].shape
    return pl.pallas_call(
        collect_kernel,
        in_specs=[SMEM] + [HBM] * (2 * RING),
        out_specs=HBM,
        out_shape=jax.ShapeDtypeStruct((2 * rows, RING * both), first[0].dtype),
        scratch_shapes=[pltpu.SemaphoreType.DMA((2 * RING,))],
        compiler_params=PARAMS,
        cost_estimate=pl.CostEstimate(
            flops=0, bytes_accessed=8 * RING * rows * both, transcendentals=0
        ),
    )(shift, *first, *second)


def attend_kernel(heads, index, ratio_ref, q_ref, cot_ref, kv_ref, away_ref, gain_ref, *refs):
    context_ref, d_query_ref, d_kv_ref, d_key_sum, d_value_sum = refs[-5:]
    step = pl.program_id(0)
    head_dim = gain_ref.shape[1]
    scale = head_dim ** (-0.5)
    count = index[1]
    ratio = ratio_ref[0]
    gain = gain_ref[...]
    key_value = jnp.where(index[2] != 0, away_ref[...], kv_ref[...])
    keys = key_value[:, :head_dim]
    vals = key_value[:, head_dim:]

    def stacked(ref):
        parts = [ref[0, :, h * head_dim : (h + 1) * head_dim] for h in range(heads)]
        return jnp.concatenate(parts, axis=0).astype(jnp.float32)

    def unstacked(ref, rows):
        text = rows.shape[0] // heads
        for h in range(heads):
            part = rows[h * text : (h + 1) * text]
            ref[0, :, h * head_dim : (h + 1) * head_dim] = part.astype(ref.dtype)

    @pl.when(step == 0)
    def _():
        d_key_sum[...] = jnp.zeros_like(d_key_sum)
        d_value_sum[...] = jnp.zeros_like(d_value_sum)

    q_raw = stacked(q_ref)
    q_factor = rms_factor(q_raw)
    q_norm = (q_raw * q_factor * gain).astype(jnp.bfloat16)
    raw = matmul(q_norm, keys, ((1,), (1,))) * scale
    place = lax.broadcasted_iota(jnp.int32, raw.shape, 1)
    expo = jnp.where(place < count * TILE, jnp.exp(raw), 0.0)
    total = jnp.sum(expo, axis=1, keepdims=True) + (count == 0).astype(jnp.float32)
    inverse = 1.0 / total
    weights_b = expo.astype(jnp.bfloat16)
    attended = matmul(weights_b, vals, ((1,), (0,))) * inverse
    unstacked(context_ref, ratio * attended)
    d_att = ratio * stacked(cot_ref)
    d_att_b = d_att.astype(jnp.bfloat16)
    scaled_b = (d_att * inverse).astype(jnp.bfloat16)
    delta = jnp.sum(d_att * attended, axis=1, keepdims=True)
    d_prob = matmul(d_att_b, vals, ((1,), (1,)))
    d_score = (expo * inverse * (d_prob - delta)).astype(jnp.bfloat16)
    d_qn = scale * matmul(d_score, keys, ((1,), (0,)))
    unstacked(d_query_ref, norm_back(q_raw, q_factor, gain, d_qn))
    d_key_sum[...] += matmul(d_score, q_norm, ((0,), (0,)))
    d_value_sum[...] += matmul(weights_b, scaled_b, ((0,), (0,)))

    @pl.when(step == pl.num_programs(0) - 1)
    def _():
        d_kv_ref[:, :head_dim] = (scale * d_key_sum[...]).astype(d_kv_ref.dtype)
        d_kv_ref[:, head_dim:] = d_value_sum[...].astype(d_kv_ref.dtype)


def attend(own, count, flag, ratio, query, cot, key_value, away, gain, earlier, heads=2):
    rows, both = key_value.shape
    head_dim = both // 2
    text = query.shape[1]
    width = heads * head_dim
    block = pl.BlockSpec((1, text, width), lambda h, index: (index[0], 0, h))
    whole = lambda shape: pl.BlockSpec(shape, lambda h, index: (0, 0))
    in_specs = [
        pl.BlockSpec(memory_space=pltpu.SMEM),
        block,
        block,
        whole((rows, both)),
        whole((rows, both)),
        whole((1, head_dim)),
    ]
    aliases = {}
    if earlier:
        in_specs += [pl.BlockSpec(memory_space=pl.ANY)] * 2
        aliases = {7: 0, 8: 1}
    steps = query.shape[2] // width
    return pl.pallas_call(
        functools.partial(attend_kernel, heads),
        grid_spec=pltpu.PrefetchScalarGridSpec(
            num_scalar_prefetch=1,
            grid=(steps,),
            in_specs=in_specs,
            out_specs=[block, block, whole((rows, both))],
            scratch_shapes=[pltpu.VMEM((rows, head_dim), jnp.float32)] * 2,
        ),
        out_shape=[
            jax.ShapeDtypeStruct(query.shape, jnp.bfloat16),
            jax.ShapeDtypeStruct(query.shape, jnp.bfloat16),
            jax.ShapeDtypeStruct((rows, both), jnp.bfloat16),
        ],
        input_output_aliases=aliases,
        compiler_params=pltpu.CompilerParams(
            vmem_limit_bytes=60 * 1024 * 1024
        ),
        cost_estimate=pl.CostEstimate(
            flops=14 * steps * heads * text * rows * head_dim,
            bytes_accessed=8 * text * steps * width + 6 * rows * head_dim,
            transcendentals=steps * heads * text * rows,
        ),
    )(
        jnp.stack([own, count, flag]).astype(jnp.int32),
        ratio,
        query,
        cot,
        key_value,
        away,
        gain[None, :],
        *earlier,
    )


def per_device(
    query,
    image,
    tiles,
    image_slot,
    key_weight_matrix,
    value_weight_matrix,
    query_gain,
    key_gain,
    gate,
    cotangent,
):
    head_dim = query_gain.shape[0]
    samp_local, img_rows, depth = image.shape
    ratio = jnp.tanh(gate)
    rank = lax.axis_index("dp")
    place = lax.axis_index("tensor")
    z, y = rank // RING, rank % RING
    x, core = place // 2, place % 2

    half = key_weight_matrix.shape[0] // 2
    both = 2 * head_dim
    halves = []
    for start in (0, half):
        key_rows = key_weight_matrix[start : start + half]
        value_rows = value_weight_matrix[start : start + half]
        halves.append(jnp.concatenate([key_rows, value_rows], axis=1))
    *halves, image = lax.optimization_barrier((*halves, image))
    upper, lower = (exchange_xz(rows) for rows in halves)
    upper = jnp.concatenate(gathered(upper, along_z), axis=1)
    lower = jnp.concatenate(gathered(lower, along_y), axis=0)
    uppers, lowers = gathered(upper, along_y), gathered(lower, along_z)

    first = rank * samp_local
    every = jnp.arange(tiles.shape[0], dtype=jnp.int32)
    local_ids = first + jnp.arange(samp_local, dtype=jnp.int32)
    match = image_slot[None, :] == local_ids[:, None]
    slot_sample = jnp.sum(jnp.where(match, every[None, :], 0), axis=1)
    slot_away = slot_sample // samp_local != rank
    swaps = jnp.any(slot_away)
    far_slot = jnp.where(slot_away[1], 1, 0)
    home_slot = lax.dynamic_slice_in_dim(image_slot, first, samp_local)
    own_away = home_slot // samp_local != rank
    own_of_slot = (home_slot[1] == first + far_slot).astype(jnp.int32)
    far_own = jnp.where(swaps, jnp.where(own_away[1], 1, 0), own_of_slot)
    home_tiles = lax.dynamic_slice_in_dim(tiles, first, samp_local)

    feats = arrange(jnp.stack([y, core, far_slot]).astype(jnp.int32), image, other_core(image), half)

    made = project(((z - x) % RING).astype(jnp.int32)[None], feats, uppers, lowers)
    (blocks,) = scattered([made], [along_x])
    raw, far_key_value, near_key_value = finish(blocks, key_gain)

    flag = swaps.astype(jnp.int32)
    away = along_z(far_key_value, RING // 2)
    near_own = 1 - far_own
    shared = (ratio, query, cotangent)
    *earlier, near_grad = attend(
        near_own, home_tiles[near_own], 0, *shared, near_key_value, near_key_value, query_gain, ()
    )
    near_rows = turn(jnp.zeros_like(flag)[None], 1, raw, near_grad, near_grad, key_gain)
    context, d_query, far_grad = attend(
        far_own, home_tiles[far_own], flag, *shared, far_key_value, away, query_gain, earlier
    )
    back = along_z(far_grad, RING // 2)
    far_rows = turn(flag[None], 0, raw, far_grad, back, key_gain)

    near_all = gathered(near_rows, along_x)
    far_all = gathered(far_rows, along_x)
    grads = collect(((x - z) % RING).astype(jnp.int32)[None], far_all, near_all)

    wide = RING * half
    upper_parts, lower_parts = [None] * RING, [None] * RING
    for d in (2, 1, 3, 0):
        o = -d % RING
        rows = feats[:, o * half : (o + 1) * half]
        upper_parts[d] = matmul(rows, grads, ((0,), (0,)))
        columns = grads[:, d * both : (d + 1) * both]
        lower_parts[d] = matmul(feats[:, wide:], columns, ((0,), (0,)))
    upper_sum, lower_sum = scattered([upper_parts, lower_parts], [along_y, along_z])
    upper_sum, lower_sum = summed(upper_sum), summed(lower_sum)
    upper_parts = [upper_sum[:, d * both : (d + 1) * both] for d in range(RING)]
    lower_parts = [lower_sum[-d % RING * half : (-d % RING + 1) * half] for d in range(RING)]
    upper_sum, lower_sum = scattered([upper_parts, lower_parts], [along_z, along_y])
    share = jnp.concatenate([summed(upper_sum), summed(lower_sum)], axis=0).astype(jnp.bfloat16)
    share = exchange_xz(share).astype(jnp.float32)
    return (context, d_query, share[:, :head_dim], share[:, head_dim:])


def solution(mesh):
    placed = (
        P("dp", None, "tensor"),
        P("dp", None, "tensor"),
        P(),
        P(),
        P("dp", "tensor"),
        P("dp", "tensor"),
        P(),
        P(),
        P(),
        P("dp", None, "tensor"),
    )
    return jax.shard_map(
        per_device,
        mesh=mesh,
        in_specs=placed,
        out_specs=(
            P("dp", None, "tensor"),
            P("dp", None, "tensor"),
            P("dp", "tensor"),
            P("dp", "tensor"),
        ),
        check_vma=False,
    )
```

```python
import functools

import jax
import jax.numpy as jnp
from jax import lax
from jax.experimental import pallas as pl
from jax.experimental.pallas import tpu as pltpu
from jax.sharding import PartitionSpec as P

TILE = 128
RING = 4
EPS = 1e-06


def along_z(x, step):
    pairs = [(z * RING + y, (z + step) % RING * RING + y) for z in range(RING) for y in range(RING)]
    return lax.ppermute(x, "dp", pairs)


def along_y(x, step):
    pairs = [(z * RING + y, z * RING + (y + step) % RING) for z in range(RING) for y in range(RING)]
    return lax.ppermute(x, "dp", pairs)


def along_x(x, step):
    pairs = [(i * 2 + c, (i + step) % RING * 2 + c) for i in range(RING) for c in range(2)]
    return lax.ppermute(x, "tensor", pairs)


def other_core(x):
    return lax.ppermute(x, "tensor", [(i, i ^ 1) for i in range(2 * RING)])


def exchange_xz(x):
    pairs = []
    for z in range(RING):
        for y in range(RING):
            for i in range(RING):
                for c in range(2):
                    source = (z * RING + y) * 2 * RING + i * 2 + c
                    target = (i * RING + y) * 2 * RING + z * 2 + c
                    pairs.append((source, target))
    return lax.ppermute(x, ("dp", "tensor"), pairs)


def gathered(blocks, moves):
    found = [[x, None, None, None] for x in blocks]
    for step in (2, 1, 3):
        for i, move in enumerate(moves):
            found[i][step] = move(blocks[i], step)
    return found


def scattered(parts, moves):
    arrived = [[] for _ in parts]
    for step in (2, 1, 3):
        for i, move in enumerate(moves):
            arrived[i].append(move(parts[i][step].astype(jnp.bfloat16), step))
    return arrived


def summed(blocks):
    total = blocks[0].astype(jnp.float32)
    for block in blocks[1:]:
        total = total + block.astype(jnp.float32)
    return total


def rms_factor(values):
    return lax.rsqrt(jnp.mean(values * values, axis=-1, keepdims=True) + EPS)


def norm_back(values, norm_multiplier, gain, grad):
    weighted = grad * gain
    inner = jnp.sum(weighted * values, axis=-1, keepdims=True)
    return (
        norm_multiplier * weighted
        - values * (norm_multiplier * norm_multiplier * norm_multiplier) * inner / values.shape[-1]
    )


def matmul(a, b, contract):
    return lax.dot_general(a, b, (contract, ((), ())), preferred_element_type=jnp.float32)


VMEM = pl.BlockSpec(memory_space=pltpu.VMEM)
SMEM = pl.BlockSpec(memory_space=pltpu.SMEM)
HBM = pl.BlockSpec(memory_space=pltpu.HBM)
PARAMS = pltpu.CompilerParams(vmem_limit_bytes=60 * 1024 * 1024)


def arrange_kernel(half, index, own_ref, other_ref, out_ref, held, sems):
    slots, rows, depth = own_ref.shape
    waits = []
    for s in range(slots):
        for h in range(2):
            for o in range(RING):
                block = ((index[0] - o + RING) % RING) ^ (2 * index[1])
                start = pl.multiple_of(block % 2 * 2 * half + h * half, half)
                target = held.at[pl.ds(s * rows, rows), pl.ds((h * RING + o) * half, half)]
                sem = sems.at[len(waits)]
                columns = pl.ds(start, half)
                own = pltpu.make_async_copy(own_ref.at[s ^ index[2], :, columns], target, sem)
                other = pltpu.make_async_copy(other_ref.at[s ^ index[2], :, columns], target, sem)
                pl.when(block < 2)(own.start)
                pl.when(block >= 2)(other.start)
                waits.append(own)
    stores = []
    for s in range(slots):
        for copy in waits[s * 2 * RING : (s + 1) * 2 * RING]:
            copy.wait()
        part = pl.ds(s * rows, rows)
        sem = sems.at[len(waits) + s]
        stores.append(pltpu.make_async_copy(held.at[part], out_ref.at[part], sem))
        stores[s].start()
    for store in stores:
        store.wait()


def arrange(index, own, other, half):
    slots, rows, depth = own.shape
    return pl.pallas_call(
        functools.partial(arrange_kernel, half),
        in_specs=[SMEM, HBM, HBM],
        out_specs=HBM,
        out_shape=jax.ShapeDtypeStruct((slots * rows, 2 * depth), own.dtype),
        scratch_shapes=[
            pltpu.VMEM((slots * rows, 2 * depth), own.dtype),
            pltpu.SemaphoreType.DMA((slots * (2 * RING + 1),)),
        ],
        compiler_params=PARAMS,
        cost_estimate=pl.CostEstimate(flops=0, bytes_accessed=8 * own.size, transcendentals=0),
    )(index, own, other)


def project_kernel(index, rows_ref, *refs):
    uppers, lowers, outs = refs[:RING], refs[RING : 2 * RING], refs[2 * RING : 3 * RING]
    rows, weights, stage, row_sems, sems, out_sems = refs[3 * RING :]
    half = uppers[0].shape[0]
    both = lowers[0].shape[1]
    slots = row_sems.shape[0]
    count = rows.shape[0] // slots
    row_copies = []
    for s in range(slots):
        part = pl.ds(s * count, count)
        row_copies.append(pltpu.make_async_copy(rows_ref.at[part], rows.at[part], row_sems.at[s]))
    row_copies[0].start()
    order = (2, 1, 3, 0)
    copies = {}
    for d in order:
        o = (index[0] - d + RING) % RING
        copies[d] = []
        for k in range(RING):
            source = uppers[k].at[:, pl.ds(pl.multiple_of(o * both, both), both)]
            target = weights.at[d, pl.ds(k * half, half)]
            copies[d].append(pltpu.make_async_copy(source, target, sems.at[d, k]))
            copies[d][k].start()
        target = weights.at[d, pl.ds(RING * half, RING * half)]
        for k in range(RING):
            copy = pltpu.make_async_copy(lowers[k], target, sems.at[d, RING])
            pl.when(o == k)(copy.start)
        copies[d].append(copy)
    for copy in row_copies[1:]:
        copy.start()
    stores = []
    for s in range(slots):
        row_copies[s].wait()
        for d in order:
            if s == 0:
                for copy in copies[d]:
                    copy.wait()
            part = pl.ds(s * count, count)
            stage[d, part] = matmul(rows[part], weights[d], ((1,), (0,))).astype(stage.dtype)
            store = pltpu.make_async_copy(stage.at[d, part], outs[d].at[part], out_sems.at[d, s])
            store.start()
            stores.append(store)
    for store in stores:
        store.wait()


def project(shift, rows, uppers, lowers):
    count, depth = rows.shape
    both = lowers[0].shape[1]
    slots = 2
    return pl.pallas_call(
        project_kernel,
        in_specs=[SMEM] + [HBM] * (1 + 2 * RING),
        out_specs=[HBM] * RING,
        out_shape=[jax.ShapeDtypeStruct((count, both), jnp.bfloat16)] * RING,
        scratch_shapes=[
            pltpu.VMEM((count, depth), jnp.bfloat16),
            pltpu.VMEM((RING, depth, both), jnp.bfloat16),
            pltpu.VMEM((RING, count, both), jnp.bfloat16),
            pltpu.SemaphoreType.DMA((slots,)),
            pltpu.SemaphoreType.DMA((RING, RING + 1)),
            pltpu.SemaphoreType.DMA((RING, slots)),
        ],
        compiler_params=PARAMS,
        cost_estimate=pl.CostEstimate(
            flops=2 * RING * count * depth * both,
            bytes_accessed=2 * count * depth + 2 * RING * both * (depth + count),
            transcendentals=0,
        ),
    )(shift, rows, *uppers, *lowers)


def finish_kernel(own_ref, far_ref, left_ref, right_ref, gain_ref, raw_ref, first_ref, second_ref):
    step = pl.program_id(0)
    head_dim = raw_ref.shape[1]
    total = summed([own_ref[...], far_ref[...], left_ref[...], right_ref[...]])
    raw = total[:, :head_dim]
    raw_ref[...] = raw
    keys = (raw * rms_factor(raw) * gain_ref[...]).astype(jnp.bfloat16)
    vals = total[:, head_dim:].astype(jnp.bfloat16)
    parts = pl.num_programs(0) // 2

    @pl.when(step < parts)
    def _():
        first_ref[:, :head_dim] = keys
        first_ref[:, head_dim:] = vals

    @pl.when(step >= parts)
    def _():
        second_ref[:, :head_dim] = keys
        second_ref[:, head_dim:] = vals


def finish(blocks, gain, parts=2):
    rows, both = blocks[0].shape
    count = rows // (2 * parts)
    block = pl.BlockSpec((count, both), lambda i: (i, 0))
    return pl.pallas_call(
        finish_kernel,
        grid=(2 * parts,),
        in_specs=[block] * RING + [pl.BlockSpec((1, both // 2), lambda i: (0, 0))],
        out_specs=[
            pl.BlockSpec((count, both // 2), lambda i: (i, 0)),
            pl.BlockSpec((count, both), lambda i: (jnp.minimum(i, parts - 1), 0)),
            pl.BlockSpec((count, both), lambda i: (jnp.maximum(i - parts, 0), 0)),
        ],
        out_shape=[
            jax.ShapeDtypeStruct((rows, both // 2), jnp.float32),
            jax.ShapeDtypeStruct((rows // 2, both), jnp.bfloat16),
            jax.ShapeDtypeStruct((rows // 2, both), jnp.bfloat16),
        ],
        compiler_params=PARAMS,
        cost_estimate=pl.CostEstimate(
            flops=6 * rows * both, bytes_accessed=12 * rows * both, transcendentals=rows
        ),
    )(*blocks, gain[None, :])


def turn_kernel(flag, raw_ref, grad_ref, other_ref, gain_ref, out_ref):
    head_dim = raw_ref.shape[1]
    grad = jnp.where(flag[0] != 0, other_ref[...], grad_ref[...])
    raw = raw_ref[...]
    d_raw = norm_back(raw, rms_factor(raw), gain_ref[...], grad[:, :head_dim].astype(jnp.float32))
    out_ref[:, :head_dim] = d_raw.astype(jnp.bfloat16)
    out_ref[:, head_dim:] = grad[:, head_dim:]


def turn(flag, slot, raw, grad, other, gain, parts=2):
    rows, both = grad.shape
    count = rows // parts
    block = pl.BlockSpec((count, both), lambda i: (i, 0))
    return pl.pallas_call(
        turn_kernel,
        grid=(parts,),
        in_specs=[
            SMEM,
            pl.BlockSpec((count, both // 2), lambda i: (slot * parts + i, 0)),
            block,
            block,
            pl.BlockSpec((1, both // 2), lambda i: (0, 0)),
        ],
        out_specs=block,
        out_shape=jax.ShapeDtypeStruct(grad.shape, jnp.bfloat16),
        compiler_params=PARAMS,
        cost_estimate=pl.CostEstimate(
            flops=6 * grad.size, bytes_accessed=8 * grad.size, transcendentals=rows
        ),
    )(flag, raw, grad, other, gain[None, :])


def collect_kernel(index, *refs):
    sources, (out_ref, held, sems) = refs[:-3], refs[-3:]
    rows, both = sources[0].shape
    copies = []
    for i, source in enumerate(sources):
        slot, o = i // RING, i % RING
        start = pl.multiple_of((index[0] - o + RING) % RING * both, both)
        target = held.at[pl.ds(slot * rows, rows), pl.ds(start, both)]
        copies.append(pltpu.make_async_copy(source, target, sems.at[i]))
    for copy in copies:
        copy.start()
    for copy in copies:
        copy.wait()
    store = pltpu.make_async_copy(held, out_ref, sems.at[len(sources)])
    store.start()
    store.wait()


def collect(shift, first, second):
    rows, both = first[0].shape
    return pl.pallas_call(
        collect_kernel,
        in_specs=[SMEM] + [HBM] * (2 * RING),
        out_specs=HBM,
        out_shape=jax.ShapeDtypeStruct((2 * rows, RING * both), first[0].dtype),
        scratch_shapes=[
            pltpu.VMEM((2 * rows, RING * both), first[0].dtype),
            pltpu.SemaphoreType.DMA((2 * RING + 1,)),
        ],
        compiler_params=PARAMS,
        cost_estimate=pl.CostEstimate(
            flops=0, bytes_accessed=8 * RING * rows * both, transcendentals=0
        ),
    )(shift, *first, *second)


def attend_kernel(heads, index, ratio_ref, q_ref, cot_ref, kv_ref, away_ref, gain_ref, *refs):
    context_ref, d_query_ref, d_kv_ref, d_key_sum, d_value_sum = refs[-5:]
    step = pl.program_id(0)
    head_dim = gain_ref.shape[1]
    scale = head_dim ** (-0.5)
    count = index[1]
    ratio = ratio_ref[0]
    gain = gain_ref[...]
    key_value = jnp.where(index[2] != 0, away_ref[...], kv_ref[...])
    keys = key_value[:, :head_dim]
    vals = key_value[:, head_dim:]

    def stacked(ref):
        parts = [ref[0, :, h * head_dim : (h + 1) * head_dim] for h in range(heads)]
        return jnp.concatenate(parts, axis=0).astype(jnp.float32)

    def unstacked(ref, rows):
        text = rows.shape[0] // heads
        for h in range(heads):
            part = rows[h * text : (h + 1) * text]
            ref[0, :, h * head_dim : (h + 1) * head_dim] = part.astype(ref.dtype)

    @pl.when(step == 0)
    def _():
        d_key_sum[...] = jnp.zeros_like(d_key_sum)
        d_value_sum[...] = jnp.zeros_like(d_value_sum)

    q_raw = stacked(q_ref)
    q_factor = rms_factor(q_raw)
    q_norm = (q_raw * q_factor * gain).astype(jnp.bfloat16)
    raw = matmul(q_norm, keys, ((1,), (1,))) * scale
    place = lax.broadcasted_iota(jnp.int32, raw.shape, 1)
    expo = jnp.where(place < count * TILE, jnp.exp(raw), 0.0)
    total = jnp.sum(expo, axis=1, keepdims=True) + (count == 0).astype(jnp.float32)
    inverse = 1.0 / total
    weights_b = expo.astype(jnp.bfloat16)
    attended = matmul(weights_b, vals, ((1,), (0,))) * inverse
    unstacked(context_ref, ratio * attended)
    d_att = ratio * stacked(cot_ref)
    d_att_b = d_att.astype(jnp.bfloat16)
    scaled_b = (d_att * inverse).astype(jnp.bfloat16)
    delta = jnp.sum(d_att * attended, axis=1, keepdims=True)
    d_prob = matmul(d_att_b, vals, ((1,), (1,)))
    d_score = (expo * inverse * (d_prob - delta)).astype(jnp.bfloat16)
    d_qn = scale * matmul(d_score, keys, ((1,), (0,)))
    unstacked(d_query_ref, norm_back(q_raw, q_factor, gain, d_qn))
    d_key_sum[...] += matmul(d_score, q_norm, ((0,), (0,)))
    d_value_sum[...] += matmul(weights_b, scaled_b, ((0,), (0,)))

    @pl.when(step == pl.num_programs(0) - 1)
    def _():
        d_kv_ref[:, :head_dim] = (scale * d_key_sum[...]).astype(d_kv_ref.dtype)
        d_kv_ref[:, head_dim:] = d_value_sum[...].astype(d_kv_ref.dtype)


def attend(own, count, flag, ratio, query, cot, key_value, away, gain, earlier, heads=2):
    rows, both = key_value.shape
    head_dim = both // 2
    text = query.shape[1]
    width = heads * head_dim
    block = pl.BlockSpec((1, text, width), lambda h, index: (index[0], 0, h))
    whole = lambda shape: pl.BlockSpec(shape, lambda h, index: (0, 0))
    in_specs = [
        pl.BlockSpec(memory_space=pltpu.SMEM),
        block,
        block,
        whole((rows, both)),
        whole((rows, both)),
        whole((1, head_dim)),
    ]
    aliases = {}
    if earlier:
        in_specs += [pl.BlockSpec(memory_space=pl.ANY)] * 2
        aliases = {7: 0, 8: 1}
    steps = query.shape[2] // width
    return pl.pallas_call(
        functools.partial(attend_kernel, heads),
        grid_spec=pltpu.PrefetchScalarGridSpec(
            num_scalar_prefetch=1,
            grid=(steps,),
            in_specs=in_specs,
            out_specs=[block, block, whole((rows, both))],
            scratch_shapes=[pltpu.VMEM((rows, head_dim), jnp.float32)] * 2,
        ),
        out_shape=[
            jax.ShapeDtypeStruct(query.shape, jnp.bfloat16),
            jax.ShapeDtypeStruct(query.shape, jnp.bfloat16),
            jax.ShapeDtypeStruct((rows, both), jnp.bfloat16),
        ],
        input_output_aliases=aliases,
        compiler_params=pltpu.CompilerParams(
            vmem_limit_bytes=60 * 1024 * 1024
        ),
        cost_estimate=pl.CostEstimate(
            flops=14 * steps * heads * text * rows * head_dim,
            bytes_accessed=8 * text * steps * width + 6 * rows * head_dim,
            transcendentals=steps * heads * text * rows,
        ),
    )(
        jnp.stack([own, count, flag]).astype(jnp.int32),
        ratio,
        query,
        cot,
        key_value,
        away,
        gain[None, :],
        *earlier,
    )


def per_device(
    query,
    image,
    tiles,
    image_slot,
    key_weight_matrix,
    value_weight_matrix,
    query_gain,
    key_gain,
    gate,
    cotangent,
):
    head_dim = query_gain.shape[0]
    samp_local, img_rows, depth = image.shape
    ratio = jnp.tanh(gate)
    rank = lax.axis_index("dp")
    place = lax.axis_index("tensor")
    z, y = rank // RING, rank % RING
    x, core = place // 2, place % 2

    half = key_weight_matrix.shape[0] // 2
    both = 2 * head_dim
    halves = []
    for start in (0, half):
        key_rows = key_weight_matrix[start : start + half]
        value_rows = value_weight_matrix[start : start + half]
        halves.append(jnp.concatenate([key_rows, value_rows], axis=1))
    *halves, image = lax.optimization_barrier((*halves, image))
    upper, lower = (exchange_xz(rows) for rows in halves)
    upper, lower, other = lax.optimization_barrier((upper, lower, other_core(image)))
    uppers, lowers = gathered([upper, lower], [along_z, along_y])
    *uppers, y1, y2, y3, y4 = lax.optimization_barrier((*uppers, *lowers))
    upper = jnp.concatenate(uppers, axis=1)
    lower = jnp.concatenate([y1, y2, y3, y4], axis=0)
    uppers, lowers = gathered([upper, lower], [along_y, along_z])

    first = rank * samp_local
    every = jnp.arange(tiles.shape[0], dtype=jnp.int32)
    local_ids = first + jnp.arange(samp_local, dtype=jnp.int32)
    match = image_slot[None, :] == local_ids[:, None]
    slot_sample = jnp.sum(jnp.where(match, every[None, :], 0), axis=1)
    slot_away = slot_sample // samp_local != rank
    swaps = jnp.any(slot_away)
    far_slot = jnp.where(slot_away[1], 1, 0)
    home_slot = lax.dynamic_slice_in_dim(image_slot, first, samp_local)
    own_away = home_slot // samp_local != rank
    own_of_slot = (home_slot[1] == first + far_slot).astype(jnp.int32)
    far_own = jnp.where(swaps, jnp.where(own_away[1], 1, 0), own_of_slot)
    home_tiles = lax.dynamic_slice_in_dim(tiles, first, samp_local)

    feats = arrange(jnp.stack([y, core, far_slot]).astype(jnp.int32), image, other, half)

    made = project(((z - x) % RING).astype(jnp.int32)[None], feats, uppers, lowers)
    (arrived,) = scattered([made], [along_x])
    raw, far_key_value, near_key_value = finish([made[0], *arrived], key_gain)

    flag = swaps.astype(jnp.int32)
    away = along_z(far_key_value, RING // 2)
    near_own = 1 - far_own
    shared = (ratio, query, cotangent)
    *earlier, near_grad = attend(
        near_own, home_tiles[near_own], 0, *shared, near_key_value, near_key_value, query_gain, ()
    )
    near_rows = turn(jnp.zeros_like(flag)[None], 1, raw, near_grad, near_grad, key_gain)
    context, d_query, far_grad = attend(
        far_own, home_tiles[far_own], flag, *shared, far_key_value, away, query_gain, earlier
    )
    back = along_z(far_grad, RING // 2)
    far_rows = turn(flag[None], 0, raw, far_grad, back, key_gain)

    (near_all,) = gathered([near_rows], [along_x])
    (far_all,) = gathered([far_rows], [along_x])
    grads = collect(((x - z) % RING).astype(jnp.int32)[None], far_all, near_all)

    wide = RING * half

    def products(feats, grads, d):
        o = -d % RING
        rows = feats[:, o * half : (o + 1) * half]
        columns = grads[:, d * both : (d + 1) * both]
        return (
            matmul(rows, grads, ((0,), (0,))),
            matmul(feats[:, wide:], columns, ((0,), (0,))),
        )

    sent = [None] + [products(feats, grads, d) for d in range(1, RING)]
    sent = [None] + [[part.astype(jnp.bfloat16) for part in parts] for parts in sent[1:]]
    upper, lower = scattered([[parts and parts[i] for parts in sent] for i in range(2)], [along_y, along_z])
    feats, grads, upper[0], lower[0] = lax.optimization_barrier((feats, grads, upper[0], lower[0]))
    own = products(feats, grads, 0)
    upper_sum, lower_sum = summed([own[0], *upper]), summed([own[1], *lower])
    upper_parts = [upper_sum[:, d * both : (d + 1) * both] for d in range(RING)]
    lower_parts = [lower_sum[-d % RING * half : (-d % RING + 1) * half] for d in range(RING)]
    upper, lower = scattered([upper_parts, lower_parts], [along_z, along_y])
    share = jnp.concatenate(
        [summed([upper_parts[0], *upper]), summed([lower_parts[0], *lower])], axis=0
    ).astype(jnp.bfloat16)
    share = exchange_xz(share).astype(jnp.float32)
    return (context, d_query, share[:, :head_dim], share[:, head_dim:])


def solution(mesh):
    placed = (
        P("dp", None, "tensor"),
        P("dp", None, "tensor"),
        P(),
        P(),
        P("dp", "tensor"),
        P("dp", "tensor"),
        P(),
        P(),
        P(),
        P("dp", None, "tensor"),
    )
    return jax.shard_map(
        per_device,
        mesh=mesh,
        in_specs=placed,
        out_specs=(
            P("dp", None, "tensor"),
            P("dp", None, "tensor"),
            P("dp", "tensor"),
            P("dp", "tensor"),
        ),
        check_vma=False,
    )
```

```python
import functools

import jax
import jax.numpy as jnp
from jax import lax
from jax.experimental import pallas as pl
from jax.experimental.pallas import tpu as pltpu
from jax.sharding import PartitionSpec as P

TILE = 128
RING = 4
EPS = 1e-06


def along_z(x, step):
    pairs = [(z * RING + y, (z + step) % RING * RING + y) for z in range(RING) for y in range(RING)]
    return lax.ppermute(x, "dp", pairs)


def by_core(x, step, z_core):
    pairs = []
    for z in range(RING):
        for y in range(RING):
            for i in range(RING):
                for c in range(2):
                    to_z, to_y = (z + step, y) if c == z_core else (z, y + step)
                    source = (z * RING + y) * 2 * RING + i * 2 + c
                    target = (to_z % RING * RING + to_y % RING) * 2 * RING + i * 2 + c
                    pairs.append((source, target))
    return lax.ppermute(x, ("dp", "tensor"), pairs)


def inner(x, step):
    return by_core(x, step, 0)


def outer(x, step):
    return by_core(x, step, 1)


def along_x(x, step):
    pairs = [(i * 2 + c, (i + step) % RING * 2 + c) for i in range(RING) for c in range(2)]
    return lax.ppermute(x, "tensor", pairs)


def other_core(x):
    return lax.ppermute(x, "tensor", [(i, i ^ 1) for i in range(2 * RING)])


def exchange_xz(x):
    pairs = []
    for z in range(RING):
        for y in range(RING):
            for i in range(RING):
                for c in range(2):
                    source = (z * RING + y) * 2 * RING + i * 2 + c
                    target = (i * RING + y) * 2 * RING + z * 2 + c
                    pairs.append((source, target))
    return lax.ppermute(x, ("dp", "tensor"), pairs)


def gathered(block, move):
    far, after, before = (move(block, step) for step in (2, 1, 3))
    return [block, after, far, before]


def scattered(parts, move):
    return [move(parts[step], step) for step in (2, 1, 3)]


def summed(blocks):
    total = blocks[0].astype(jnp.float32)
    for block in blocks[1:]:
        total = total + block.astype(jnp.float32)
    return total


def rms_factor(values):
    return lax.rsqrt(jnp.mean(values * values, axis=-1, keepdims=True) + EPS)


def norm_back(values, norm_multiplier, gain, grad):
    weighted = grad * gain
    inner = jnp.sum(weighted * values, axis=-1, keepdims=True)
    return (
        norm_multiplier * weighted
        - values * (norm_multiplier * norm_multiplier * norm_multiplier) * inner / values.shape[-1]
    )


def matmul(a, b, contract):
    return lax.dot_general(a, b, (contract, ((), ())), preferred_element_type=jnp.float32)


VMEM = pl.BlockSpec(memory_space=pltpu.VMEM)
SMEM = pl.BlockSpec(memory_space=pltpu.SMEM)
ANY = pl.BlockSpec(memory_space=pl.ANY)
PARAMS = pltpu.CompilerParams(vmem_limit_bytes=16 * 1024 * 1024)


def arrange_kernel(index, own_ref, other_ref, out_ref, sems):
    slots, rows, depth = own_ref.shape
    width = 2 * depth // RING
    y, core, far_slot = index[0], index[1], index[2]
    waits = []
    for s in range(slots):
        for o in range(RING):
            block = ((y - o + RING) % RING) ^ (2 * core)
            columns = pl.ds(pl.multiple_of(block % 2 * width, width), width)
            target = out_ref.at[pl.ds(s * rows, rows), pl.ds(o * width, width)]
            sem = sems.at[len(waits)]
            own = pltpu.make_async_copy(own_ref.at[s ^ far_slot, :, columns], target, sem)
            other = pltpu.make_async_copy(other_ref.at[s ^ far_slot, :, columns], target, sem)
            pl.when(block < 2)(own.start)
            pl.when(block >= 2)(other.start)
            waits.append(own)
    for copy in waits:
        copy.wait()


def arrange(index, own, other):
    slots, rows, depth = own.shape
    return pl.pallas_call(
        arrange_kernel,
        in_specs=[SMEM, ANY, ANY],
        out_specs=VMEM,
        out_shape=jax.ShapeDtypeStruct((slots * rows, 2 * depth), own.dtype),
        scratch_shapes=[pltpu.SemaphoreType.DMA((slots * RING,))],
        compiler_params=PARAMS,
        cost_estimate=pl.CostEstimate(flops=0, bytes_accessed=8 * own.size, transcendentals=0),
    )(index, own, other)


def assemble_kernel(index, *refs):
    pieces, out_ref, sems = refs[:RING], refs[RING], refs[RING + 1]
    rows, both = pieces[0].shape
    count = rows // RING
    shift, core = index[0], index[1]
    copies = []
    for b in range(RING):
        for a in range(RING):
            along_z_by = jnp.where(core == 0, a, b)
            along_y_by = jnp.where(core == 0, b, a)
            start = pl.multiple_of(along_y_by * count, count)
            column = pl.multiple_of((shift - along_z_by + RING) % RING * both, both)
            target = out_ref.at[pl.ds(start, count), pl.ds(column, both)]
            source = pieces[b].at[pl.ds(a * count, count)]
            copies.append(pltpu.make_async_copy(source, target, sems.at[b, a]))
    for copy in copies:
        copy.start()
    for copy in copies:
        copy.wait()


def assemble(index, pieces):
    rows, both = pieces[0].shape
    return pl.pallas_call(
        assemble_kernel,
        in_specs=[SMEM] + [ANY] * RING,
        out_specs=VMEM,
        out_shape=jax.ShapeDtypeStruct((rows, RING * both), pieces[0].dtype),
        scratch_shapes=[pltpu.SemaphoreType.DMA((RING, RING))],
        compiler_params=PARAMS,
        cost_estimate=pl.CostEstimate(
            flops=0, bytes_accessed=4 * RING * rows * both, transcendentals=0
        ),
    )(index, *pieces)


def finish_kernel(own_ref, far_ref, left_ref, right_ref, gain_ref, raw_ref, first_ref, second_ref):
    rows, head_dim = raw_ref.shape
    total = summed([own_ref[...], far_ref[...], left_ref[...], right_ref[...]])
    raw = total[:, :head_dim]
    raw_ref[...] = raw
    keys = (raw * rms_factor(raw) * gain_ref[...]).astype(jnp.bfloat16)
    vals = total[:, head_dim:].astype(jnp.bfloat16)
    for i, out_ref in enumerate((first_ref, second_ref)):
        part = slice(i * rows // 2, (i + 1) * rows // 2)
        out_ref[:, :head_dim] = keys[part]
        out_ref[:, head_dim:] = vals[part]


def finish(blocks, gain):
    rows, both = blocks[0].shape
    return pl.pallas_call(
        finish_kernel,
        in_specs=[VMEM] * (RING + 1),
        out_specs=[VMEM] * 3,
        out_shape=[
            jax.ShapeDtypeStruct((rows, both // 2), jnp.float32),
            jax.ShapeDtypeStruct((rows // 2, both), jnp.bfloat16),
            jax.ShapeDtypeStruct((rows // 2, both), jnp.bfloat16),
        ],
        compiler_params=PARAMS,
        cost_estimate=pl.CostEstimate(
            flops=6 * rows * both, bytes_accessed=12 * rows * both, transcendentals=rows
        ),
    )(*blocks, gain[None, :])


def turn_kernel(slot, flag, raw_ref, grad_ref, other_ref, gain_ref, out_ref):
    rows, head_dim = grad_ref.shape[0], raw_ref.shape[1]
    grad = jnp.where(flag[2] != 0, other_ref[...], grad_ref[...])
    raw = raw_ref[slot * rows : (slot + 1) * rows]
    d_raw = norm_back(raw, rms_factor(raw), gain_ref[...], grad[:, :head_dim].astype(jnp.float32))
    out_ref[:, :head_dim] = d_raw.astype(jnp.bfloat16)
    out_ref[:, head_dim:] = grad[:, head_dim:]


def turn(flag, slot, raw, grad, other, gain):
    return pl.pallas_call(
        functools.partial(turn_kernel, slot),
        in_specs=[SMEM] + [VMEM] * 4,
        out_specs=VMEM,
        out_shape=jax.ShapeDtypeStruct(grad.shape, jnp.bfloat16),
        compiler_params=PARAMS,
        cost_estimate=pl.CostEstimate(
            flops=6 * grad.size, bytes_accessed=8 * grad.size, transcendentals=grad.shape[0]
        ),
    )(flag, raw, grad, other, gain[None, :])


def collect_kernel(index, *refs):
    sources, (out_ref, sems) = refs[:-2], refs[-2:]
    rows, both = sources[0].shape
    copies = []
    for i, source in enumerate(sources):
        slot, o = i // RING, i % RING
        start = pl.multiple_of((RING - index[0] - o + RING) % RING * both, both)
        target = out_ref.at[pl.ds(slot * rows, rows), pl.ds(start, both)]
        copies.append(pltpu.make_async_copy(source, target, sems.at[i]))
    for copy in copies:
        copy.start()
    for copy in copies:
        copy.wait()


def collect(index, first, second):
    rows, both = first[0].shape
    return pl.pallas_call(
        collect_kernel,
        in_specs=[SMEM] + [ANY] * (2 * RING),
        out_specs=VMEM,
        out_shape=jax.ShapeDtypeStruct((2 * rows, RING * both), first[0].dtype),
        scratch_shapes=[pltpu.SemaphoreType.DMA((2 * RING,))],
        compiler_params=PARAMS,
        cost_estimate=pl.CostEstimate(
            flops=0, bytes_accessed=8 * RING * rows * both, transcendentals=0
        ),
    )(index, *first, *second)


def product_kernel(step, index, feats_ref, grads_ref, out_ref):
    both = out_ref.shape[1]
    count = out_ref.shape[0] // RING
    core = index[1]
    for s in range(RING):
        row = jnp.where(core == 0, -step % RING, -s % RING)
        column = jnp.where(core == 0, s, step)
        block = matmul(
            feats_ref[:, pl.ds(pl.multiple_of(row * count, count), count)],
            grads_ref[:, pl.ds(pl.multiple_of(column * both, both), both)],
            ((0,), (0,)),
        )
        out_ref[s * count : (s + 1) * count] = block.astype(out_ref.dtype)


def product(step, index, feats, grads):
    shape = (feats.shape[1], grads.shape[1] // RING)
    return pl.pallas_call(
        functools.partial(product_kernel, step),
        in_specs=[SMEM, VMEM, VMEM],
        out_specs=VMEM,
        out_shape=jax.ShapeDtypeStruct(shape, jnp.bfloat16),
        compiler_params=PARAMS,
        cost_estimate=pl.CostEstimate(
            flops=2 * feats.shape[0] * shape[0] * shape[1],
            bytes_accessed=2 * feats.size + 2 * grads.size + 2 * shape[0] * shape[1],
            transcendentals=0,
        ),
    )(index, feats, grads)


def attend_kernel(heads, index, ratio_ref, q_ref, cot_ref, kv_ref, away_ref, gain_ref, *refs):
    context_ref, d_query_ref, d_kv_ref, d_key_sum, d_value_sum = refs[-5:]
    step = pl.program_id(0)
    head_dim = gain_ref.shape[1]
    scale = head_dim ** (-0.5)
    count = index[1]
    ratio = ratio_ref[0]
    gain = gain_ref[...]
    key_value = jnp.where(index[2] != 0, away_ref[...], kv_ref[...])
    keys = key_value[:, :head_dim]
    vals = key_value[:, head_dim:]

    def stacked(ref):
        parts = [ref[0, :, h * head_dim : (h + 1) * head_dim] for h in range(heads)]
        return jnp.concatenate(parts, axis=0).astype(jnp.float32)

    def unstacked(ref, rows):
        text = rows.shape[0] // heads
        for h in range(heads):
            part = rows[h * text : (h + 1) * text]
            ref[0, :, h * head_dim : (h + 1) * head_dim] = part.astype(ref.dtype)

    @pl.when(step == 0)
    def _():
        d_key_sum[...] = jnp.zeros_like(d_key_sum)
        d_value_sum[...] = jnp.zeros_like(d_value_sum)

    q_raw = stacked(q_ref)
    q_factor = rms_factor(q_raw)
    q_norm = (q_raw * q_factor * gain).astype(jnp.bfloat16)
    raw = matmul(q_norm, keys, ((1,), (1,))) * scale
    place = lax.broadcasted_iota(jnp.int32, raw.shape, 1)
    expo = jnp.where(place < count * TILE, jnp.exp(raw), 0.0)
    total = jnp.sum(expo, axis=1, keepdims=True) + (count == 0).astype(jnp.float32)
    inverse = 1.0 / total
    weights_b = expo.astype(jnp.bfloat16)
    attended = matmul(weights_b, vals, ((1,), (0,))) * inverse
    unstacked(context_ref, ratio * attended)
    d_att = ratio * stacked(cot_ref)
    d_att_b = d_att.astype(jnp.bfloat16)
    scaled_b = (d_att * inverse).astype(jnp.bfloat16)
    delta = jnp.sum(d_att * attended, axis=1, keepdims=True)
    d_prob = matmul(d_att_b, vals, ((1,), (1,)))
    d_score = (expo * inverse * (d_prob - delta)).astype(jnp.bfloat16)
    d_qn = scale * matmul(d_score, keys, ((1,), (0,)))
    unstacked(d_query_ref, norm_back(q_raw, q_factor, gain, d_qn))
    d_key_sum[...] += matmul(d_score, q_norm, ((0,), (0,)))
    d_value_sum[...] += matmul(weights_b, scaled_b, ((0,), (0,)))

    @pl.when(step == pl.num_programs(0) - 1)
    def _():
        d_kv_ref[:, :head_dim] = (scale * d_key_sum[...]).astype(d_kv_ref.dtype)
        d_kv_ref[:, head_dim:] = d_value_sum[...].astype(d_kv_ref.dtype)


def attend(index, ratio, query, cot, key_value, away, gain, earlier, heads=2):
    rows, both = key_value.shape
    head_dim = both // 2
    text = query.shape[1]
    width = heads * head_dim
    block = pl.BlockSpec((1, text, width), lambda h, index: (index[0], 0, h))
    whole = lambda shape: pl.BlockSpec(shape, lambda h, index: (0, 0))
    in_specs = [
        pl.BlockSpec(memory_space=pltpu.SMEM),
        block,
        block,
        whole((rows, both)),
        whole((rows, both)),
        whole((1, head_dim)),
    ]
    aliases = {}
    if earlier:
        in_specs += [pl.BlockSpec(memory_space=pl.ANY)] * 2
        aliases = {7: 0, 8: 1}
    steps = query.shape[2] // width
    return pl.pallas_call(
        functools.partial(attend_kernel, heads),
        grid_spec=pltpu.PrefetchScalarGridSpec(
            num_scalar_prefetch=1,
            grid=(steps,),
            in_specs=in_specs,
            out_specs=[block, block, whole((rows, both))],
            scratch_shapes=[pltpu.VMEM((rows, head_dim), jnp.float32)] * 2,
        ),
        out_shape=[
            jax.ShapeDtypeStruct(query.shape, jnp.bfloat16),
            jax.ShapeDtypeStruct(query.shape, jnp.bfloat16),
            jax.ShapeDtypeStruct((rows, both), jnp.bfloat16),
        ],
        input_output_aliases=aliases,
        compiler_params=pltpu.CompilerParams(
            vmem_limit_bytes=24 * 1024 * 1024
        ),
        cost_estimate=pl.CostEstimate(
            flops=14 * steps * heads * text * rows * head_dim,
            bytes_accessed=8 * text * steps * width + 6 * rows * head_dim,
            transcendentals=steps * heads * text * rows,
        ),
    )(
        index,
        ratio,
        query,
        cot,
        key_value,
        away,
        gain[None, :],
        *earlier,
    )


def per_device(
    query,
    image,
    tiles,
    image_slot,
    key_weight_matrix,
    value_weight_matrix,
    query_gain,
    key_gain,
    gate,
    cotangent,
):
    head_dim = query_gain.shape[0]
    samp_local, img_rows, depth = image.shape
    ratio = jnp.tanh(gate)
    rank = lax.axis_index("dp")
    place = lax.axis_index("tensor")
    z, y = rank // RING, rank % RING
    x, core = place // 2, place % 2

    first = rank * samp_local
    every = jnp.arange(tiles.shape[0], dtype=jnp.int32)
    local_ids = first + jnp.arange(samp_local, dtype=jnp.int32)
    match = image_slot[None, :] == local_ids[:, None]
    slot_sample = jnp.sum(jnp.where(match, every[None, :], 0), axis=1)
    slot_away = slot_sample // samp_local != rank
    swaps = jnp.any(slot_away)
    far_slot = jnp.where(slot_away[1], 1, 0)
    home_slot = lax.dynamic_slice_in_dim(image_slot, first, samp_local)
    own_away = home_slot // samp_local != rank
    own_of_slot = (home_slot[1] == first + far_slot).astype(jnp.int32)
    far_own = jnp.where(swaps, jnp.where(own_away[1], 1, 0), own_of_slot)
    home_tiles = lax.dynamic_slice_in_dim(tiles, first, samp_local)

    near_own = 1 - far_own
    zero = jnp.zeros((), jnp.int32)
    swapped = swaps.astype(jnp.int32)
    near_index = jnp.stack([near_own, home_tiles[near_own], zero]).astype(jnp.int32)
    far_index = jnp.stack([far_own, home_tiles[far_own], swapped]).astype(jnp.int32)
    feat_index = jnp.stack([y, core, far_slot]).astype(jnp.int32)
    ring_index = jnp.stack([(z - x + RING) % RING, core]).astype(jnp.int32)

    shard = jnp.concatenate([key_weight_matrix, value_weight_matrix], axis=1)
    shard, image = lax.optimization_barrier((shard, image))
    shard = exchange_xz(shard)
    other = other_core(image)
    shard, other, near_index, far_index, feat_index, ring_index, ratio = lax.optimization_barrier(
        (shard, other, near_index, far_index, feat_index, ring_index, ratio)
    )
    pieces = gathered(jnp.concatenate(gathered(shard, inner), axis=0), outer)
    weights = assemble(ring_index, pieces)

    feats = arrange(feat_index, image, other)

    both = 2 * head_dim
    blocks = [None] * RING
    for d in (2, 1, 3, 0):
        columns = weights[:, d * both : (d + 1) * both]
        blocks[d] = matmul(feats, columns, ((1,), (0,))).astype(jnp.bfloat16)
    arrived = scattered(blocks, along_x)
    raw, far_key_value, near_key_value = finish([blocks[0], *arrived], key_gain)

    away = along_z(far_key_value, RING // 2)
    shared = (ratio, query, cotangent)
    *earlier, near_grad = attend(
        near_index, *shared, near_key_value, near_key_value, query_gain, ()
    )
    near_rows = turn(near_index, 1, raw, near_grad, near_grad, key_gain)
    near_rows, away = lax.optimization_barrier((near_rows, away))
    near_all = gathered(near_rows, along_x)
    context, d_query, far_grad = attend(
        far_index, *shared, far_key_value, away, query_gain, earlier
    )
    back = along_z(far_grad, RING // 2)
    far_rows = turn(far_index, 0, raw, far_grad, back, key_gain)

    far_all = gathered(far_rows, along_x)
    grads = collect(ring_index, far_all, near_all)

    sent = [None] + [product(d, ring_index, feats, grads) for d in range(1, RING)]
    arrived = scattered(sent, outer)
    feats, grads, arrived[0] = lax.optimization_barrier((feats, grads, arrived[0]))
    total = summed([product(0, ring_index, feats, grads), *arrived])
    count = total.shape[0] // RING
    parts = [total[d * count : (d + 1) * count] for d in range(RING)]
    sent = [None] + [part.astype(jnp.bfloat16) for part in parts[1:]]
    arrived = scattered(sent, inner)
    share = summed([parts[0], *arrived]).astype(jnp.bfloat16)
    share = exchange_xz(share).astype(jnp.float32)
    return (context, d_query, share[:, :head_dim], share[:, head_dim:])


def solution(mesh):
    placed = (
        P("dp", None, "tensor"),
        P("dp", None, "tensor"),
        P(),
        P(),
        P("dp", "tensor"),
        P("dp", "tensor"),
        P(),
        P(),
        P(),
        P("dp", None, "tensor"),
    )
    return jax.shard_map(
        per_device,
        mesh=mesh,
        in_specs=placed,
        out_specs=(
            P("dp", None, "tensor"),
            P("dp", None, "tensor"),
            P("dp", "tensor"),
            P("dp", "tensor"),
        ),
        check_vma=False,
    )
```

```python
import functools

import jax
import jax.numpy as jnp
from jax import lax
from jax.experimental import pallas as pl
from jax.experimental.pallas import tpu as pltpu
from jax.sharding import PartitionSpec as P

TILE = 128
RING = 4
EPS = 1e-06


def along_z(x, step):
    pairs = [(z * RING + y, (z + step) % RING * RING + y) for z in range(RING) for y in range(RING)]
    return lax.ppermute(x, "dp", pairs)


def by_core(x, step, z_core):
    pairs = []
    for z in range(RING):
        for y in range(RING):
            for i in range(RING):
                for c in range(2):
                    to_z, to_y = (z + step, y) if c == z_core else (z, y + step)
                    source = (z * RING + y) * 2 * RING + i * 2 + c
                    target = (to_z % RING * RING + to_y % RING) * 2 * RING + i * 2 + c
                    pairs.append((source, target))
    return lax.ppermute(x, ("dp", "tensor"), pairs)


def inner(x, step):
    return by_core(x, step, 0)


def outer(x, step):
    return by_core(x, step, 1)


def along_x(x, step):
    pairs = [(i * 2 + c, (i + step) % RING * 2 + c) for i in range(RING) for c in range(2)]
    return lax.ppermute(x, "tensor", pairs)


def other_core(x):
    return lax.ppermute(x, "tensor", [(i, i ^ 1) for i in range(2 * RING)])


def gathered(block, move):
    far, after, before = (move(block, step) for step in (2, 1, 3))
    return [block, after, far, before]


def scattered(parts, move):
    return [move(parts[step], step) for step in (2, 1, 3)]


def summed(blocks):
    total = blocks[0].astype(jnp.float32)
    for block in blocks[1:]:
        total = total + block.astype(jnp.float32)
    return total


def rms_factor(values):
    return lax.rsqrt(jnp.mean(values * values, axis=-1, keepdims=True) + EPS)


def norm_back(values, norm_multiplier, gain, grad):
    weighted = grad * gain
    inner = jnp.sum(weighted * values, axis=-1, keepdims=True)
    return (
        norm_multiplier * weighted
        - values * (norm_multiplier * norm_multiplier * norm_multiplier) * inner / values.shape[-1]
    )


def matmul(a, b, contract):
    return lax.dot_general(a, b, (contract, ((), ())), preferred_element_type=jnp.float32)


VMEM = pl.BlockSpec(memory_space=pltpu.VMEM)
SMEM = pl.BlockSpec(memory_space=pltpu.SMEM)
ANY = pl.BlockSpec(memory_space=pl.ANY)
PARAMS = pltpu.CompilerParams(vmem_limit_bytes=16 * 1024 * 1024)


def route_kernel(tiles, slots, image_ref, near, far, chip, far_ref, near_ref, sems):
    rank, place = lax.axis_index("dp"), lax.axis_index("tensor")
    first = 2 * rank

    def sample_of(slot):
        found = lambda i, at: jnp.where(slots[i] == slot, i, at)
        return lax.fori_loop(0, slots.shape[0], found, 0)

    away = [sample_of(first + i) >> 1 != rank for i in range(2)]
    swaps = jnp.logical_or(away[0], away[1])
    far_slot = jnp.where(away[1], 1, 0)
    copies = []
    for i, (slot, target) in enumerate(((far_slot, far_ref), (1 - far_slot, near_ref))):
        copies.append(pltpu.make_async_copy(image_ref.at[slot], target, sems.at[i]))
        copies[i].start()
    second_home = slots[first + 1]
    of_slot = jnp.where(second_home == first + far_slot, 1, 0)
    far_own = jnp.where(swaps, jnp.where(second_home >> 1 != rank, 1, 0), of_slot)
    near[0] = 1 - far_own
    near[1] = tiles[first + 1 - far_own]
    near[2] = 0
    far[0] = far_own
    far[1] = tiles[first + far_own]
    far[2] = jnp.where(swaps, 1, 0)
    chip[0] = rank // RING
    chip[1] = rank % RING
    chip[2] = place // 2
    chip[3] = place % 2
    for copy in copies:
        copy.wait()


def route(tiles, image_slot, image):
    rows = jax.ShapeDtypeStruct(image.shape[1:], image.dtype)
    numbers = lambda n: jax.ShapeDtypeStruct((n,), jnp.int32)
    return pl.pallas_call(
        route_kernel,
        in_specs=[SMEM, SMEM, ANY],
        out_specs=[SMEM, SMEM, SMEM, VMEM, VMEM],
        out_shape=[numbers(3), numbers(3), numbers(4), rows, rows],
        scratch_shapes=[pltpu.SemaphoreType.DMA((2,))],
        compiler_params=PARAMS,
        cost_estimate=pl.CostEstimate(flops=0, bytes_accessed=4 * image.size, transcendentals=0),
    )(tiles, image_slot, image)


def assemble_kernel(chip, *refs):
    pieces, out_ref, sems = refs[:RING], refs[RING], refs[RING + 1]
    rows, both = pieces[0].shape
    count = rows // RING
    z, y, x, core = chip[0], chip[1], chip[2], chip[3]
    copies = []
    for b in range(RING):
        for a in range(RING):
            from_z = (z - jnp.where(core == 0, a, b) + RING) % RING
            from_y = (y - jnp.where(core == 0, b, a) + RING) % RING
            o = (x - from_z + RING) % RING
            start = ((o * 2 + ((from_y >> 1) ^ core)) * 2 + from_y % 2) * count
            target = out_ref.at[pl.ds(pl.multiple_of(start, count), count)]
            source = pieces[b].at[pl.ds(a * count, count)]
            copies.append(pltpu.make_async_copy(source, target, sems.at[b, a]))
    for copy in copies:
        copy.start()
    for copy in copies:
        copy.wait()


def assemble(chip, pieces):
    rows, both = pieces[0].shape
    return pl.pallas_call(
        assemble_kernel,
        in_specs=[SMEM] + [ANY] * RING,
        out_specs=VMEM,
        out_shape=jax.ShapeDtypeStruct((RING * rows, both), pieces[0].dtype),
        scratch_shapes=[pltpu.SemaphoreType.DMA((RING, RING))],
        compiler_params=PARAMS,
        cost_estimate=pl.CostEstimate(
            flops=0, bytes_accessed=4 * RING * rows * both, transcendentals=0
        ),
    )(chip, *pieces)


def finish_kernel(total_ref, gain_ref, key_value_ref):
    head_dim = gain_ref.shape[1]
    raw = total_ref[:, :head_dim]
    keys = (raw * rms_factor(raw) * gain_ref[...]).astype(jnp.bfloat16)
    key_value_ref[:, :head_dim] = keys
    key_value_ref[:, head_dim:] = total_ref[:, head_dim:].astype(jnp.bfloat16)


def finish(total, gain):
    return pl.pallas_call(
        finish_kernel,
        in_specs=[VMEM] * 2,
        out_specs=VMEM,
        out_shape=jax.ShapeDtypeStruct(total.shape, jnp.bfloat16),
        compiler_params=PARAMS,
        cost_estimate=pl.CostEstimate(
            flops=3 * total.size, bytes_accessed=6 * total.size, transcendentals=total.shape[0]
        ),
    )(total, gain[None, :])


def turn_kernel(flag, total_ref, grad_ref, other_ref, gain_ref, out_ref):
    head_dim = gain_ref.shape[1]
    grad = jnp.where(flag[2] != 0, other_ref[...], grad_ref[...])
    raw = total_ref[:, :head_dim]
    d_raw = norm_back(raw, rms_factor(raw), gain_ref[...], grad[:, :head_dim].astype(jnp.float32))
    out_ref[:, :head_dim] = d_raw.astype(jnp.bfloat16)
    out_ref[:, head_dim:] = grad[:, head_dim:]


def turn(flag, total, grad, other, gain):
    return pl.pallas_call(
        turn_kernel,
        in_specs=[SMEM] + [VMEM] * 4,
        out_specs=VMEM,
        out_shape=jax.ShapeDtypeStruct(grad.shape, jnp.bfloat16),
        compiler_params=PARAMS,
        cost_estimate=pl.CostEstimate(
            flops=6 * grad.size, bytes_accessed=8 * grad.size, transcendentals=grad.shape[0]
        ),
    )(flag, total, grad, other, gain[None, :])


def product_kernel(step, chip, *refs):
    sources, (far_ref, near_ref, out_ref, held, sems) = refs[:-5], refs[-5:]
    blocks = 2 * RING
    rows = far_ref.shape[0]
    count = out_ref.shape[0] // RING
    z, y, x, core = chip[0], chip[1], chip[2], chip[3]
    waits = []
    for s in range(RING):
        to_z = (z + jnp.where(core == 0, s, step)) % RING
        to_y = (y + jnp.where(core == 0, step, s)) % RING
        block = (x - to_z + RING) % RING * 2 + ((to_y >> 1) ^ core)
        columns = pl.ds(pl.multiple_of(to_y % 2 * count, count), count)
        for i in range(2):
            target = held.at[s, pl.ds(i * rows, rows)]
            for k in range(blocks):
                source = sources[i * blocks + k].at[:, columns]
                copy = pltpu.make_async_copy(source, target, sems.at[s, i])
                pl.when(block == k)(copy.start)
            waits.append(copy)
    grads = jnp.concatenate([far_ref[...], near_ref[...]], axis=0)
    for s in range(RING):
        for copy in waits[2 * s : 2 * s + 2]:
            copy.wait()
        total = matmul(held[s], grads, ((0,), (0,)))
        out_ref[s * count : (s + 1) * count] = total.astype(out_ref.dtype)


def product(step, chip, far_feats, near_feats, far_rows, near_rows):
    rows, depth = far_feats[0].shape
    both = far_rows.shape[1]
    count = depth // 2
    return pl.pallas_call(
        functools.partial(product_kernel, step),
        in_specs=[SMEM] + [ANY] * (4 * RING) + [VMEM, VMEM],
        out_specs=VMEM,
        out_shape=jax.ShapeDtypeStruct((RING * count, both), jnp.bfloat16),
        scratch_shapes=[
            pltpu.VMEM((RING, 2 * rows, count), jnp.bfloat16),
            pltpu.SemaphoreType.DMA((RING, 2)),
        ],
        compiler_params=PARAMS,
        cost_estimate=pl.CostEstimate(
            flops=4 * RING * rows * count * both,
            bytes_accessed=4 * RING * rows * count,
            transcendentals=0,
        ),
    )(chip, *far_feats, *near_feats, far_rows, near_rows)


def attend_kernel(heads, index, ratio_ref, q_ref, cot_ref, kv_ref, away_ref, gain_ref, *refs):
    context_ref, d_query_ref, d_kv_ref, d_key_sum, d_value_sum = refs[-5:]
    step = pl.program_id(0)
    head_dim = gain_ref.shape[1]
    scale = head_dim ** (-0.5)
    count = index[1]
    ratio = ratio_ref[0]
    gain = gain_ref[...]
    key_value = jnp.where(index[2] != 0, away_ref[...], kv_ref[...])
    keys = key_value[:, :head_dim]
    vals = key_value[:, head_dim:]

    def stacked(ref):
        parts = [ref[0, :, h * head_dim : (h + 1) * head_dim] for h in range(heads)]
        return jnp.concatenate(parts, axis=0).astype(jnp.float32)

    def unstacked(ref, rows):
        text = rows.shape[0] // heads
        for h in range(heads):
            part = rows[h * text : (h + 1) * text]
            ref[0, :, h * head_dim : (h + 1) * head_dim] = part.astype(ref.dtype)

    @pl.when(step == 0)
    def _():
        d_key_sum[...] = jnp.zeros_like(d_key_sum)
        d_value_sum[...] = jnp.zeros_like(d_value_sum)

    q_raw = stacked(q_ref)
    q_factor = rms_factor(q_raw)
    q_norm = (q_raw * q_factor * gain).astype(jnp.bfloat16)
    raw = matmul(q_norm, keys, ((1,), (1,))) * scale
    place = lax.broadcasted_iota(jnp.int32, raw.shape, 1)
    expo = jnp.where(place < count * TILE, jnp.exp(raw), 0.0)
    total = jnp.sum(expo, axis=1, keepdims=True) + (count == 0).astype(jnp.float32)
    inverse = 1.0 / total
    weights_b = expo.astype(jnp.bfloat16)
    attended = matmul(weights_b, vals, ((1,), (0,))) * inverse
    unstacked(context_ref, ratio * attended)
    d_att = ratio * stacked(cot_ref)
    d_att_b = d_att.astype(jnp.bfloat16)
    scaled_b = (d_att * inverse).astype(jnp.bfloat16)
    delta = jnp.sum(d_att * attended, axis=1, keepdims=True)
    d_prob = matmul(d_att_b, vals, ((1,), (1,)))
    d_score = (expo * inverse * (d_prob - delta)).astype(jnp.bfloat16)
    d_qn = scale * matmul(d_score, keys, ((1,), (0,)))
    unstacked(d_query_ref, norm_back(q_raw, q_factor, gain, d_qn))
    d_key_sum[...] += matmul(d_score, q_norm, ((0,), (0,)))
    d_value_sum[...] += matmul(weights_b, scaled_b, ((0,), (0,)))

    @pl.when(step == pl.num_programs(0) - 1)
    def _():
        d_kv_ref[:, :head_dim] = (scale * d_key_sum[...]).astype(d_kv_ref.dtype)
        d_kv_ref[:, head_dim:] = d_value_sum[...].astype(d_kv_ref.dtype)


def attend(index, ratio, query, cot, key_value, away, gain, earlier, heads=2):
    rows, both = key_value.shape
    head_dim = both // 2
    text = query.shape[1]
    width = heads * head_dim
    block = pl.BlockSpec((1, text, width), lambda h, index: (index[0], 0, h))
    whole = lambda shape: pl.BlockSpec(shape, lambda h, index: (0, 0))
    in_specs = [
        pl.BlockSpec(memory_space=pltpu.SMEM),
        block,
        block,
        whole((rows, both)),
        whole((rows, both)),
        whole((1, head_dim)),
    ]
    aliases = {}
    if earlier:
        in_specs += [pl.BlockSpec(memory_space=pl.ANY)] * 2
        aliases = {7: 0, 8: 1}
    steps = query.shape[2] // width
    return pl.pallas_call(
        functools.partial(attend_kernel, heads),
        grid_spec=pltpu.PrefetchScalarGridSpec(
            num_scalar_prefetch=1,
            grid=(steps,),
            in_specs=in_specs,
            out_specs=[block, block, whole((rows, both))],
            scratch_shapes=[pltpu.VMEM((rows, head_dim), jnp.float32)] * 2,
        ),
        out_shape=[
            jax.ShapeDtypeStruct(query.shape, jnp.bfloat16),
            jax.ShapeDtypeStruct(query.shape, jnp.bfloat16),
            jax.ShapeDtypeStruct((rows, both), jnp.bfloat16),
        ],
        input_output_aliases=aliases,
        compiler_params=pltpu.CompilerParams(
            vmem_limit_bytes=24 * 1024 * 1024
        ),
        cost_estimate=pl.CostEstimate(
            flops=14 * steps * heads * text * rows * head_dim,
            bytes_accessed=8 * text * steps * width + 6 * rows * head_dim,
            transcendentals=steps * heads * text * rows,
        ),
    )(
        index,
        ratio,
        query,
        cot,
        key_value,
        away,
        gain[None, :],
        *earlier,
    )


def per_device(
    query,
    image,
    tiles,
    image_slot,
    key_weight_matrix,
    value_weight_matrix,
    query_gain,
    key_gain,
    gate,
    cotangent,
):
    ratio = jnp.tanh(gate)
    near_index, far_index, chip, far_own, near_own = route(tiles, image_slot, image)

    shard = jnp.concatenate([key_weight_matrix, value_weight_matrix], axis=1)
    far_x = gathered(far_own, along_x)
    pieces = gathered(jnp.concatenate(gathered(shard, inner), axis=0), outer)
    weights = assemble(chip, pieces)
    near_own, *arrived = lax.optimization_barrier((near_own, *far_x[1:]))
    far_x[1:] = arrived
    near_x = gathered(near_own, along_x)

    def both_cores(blocks):
        return [block for own in blocks for block in (own, other_core(own))]

    def project(feats):
        depth = feats[0].shape[1]
        total = None
        for o in (0, 2, 1, 3):
            for k in (2 * o, 2 * o + 1):
                part = matmul(feats[k], weights[k * depth : (k + 1) * depth], ((1,), (0,)))
                total = part if total is None else total + part
        return total

    shared = (ratio, query, cotangent)
    far_feats = both_cores(far_x)
    far_total = project(far_feats)
    far_key_value = finish(far_total, key_gain)
    away = along_z(far_key_value, RING // 2)
    *earlier, far_grad = attend(far_index, *shared, far_key_value, away, query_gain, ())
    back = along_z(far_grad, RING // 2)
    far_rows = turn(far_index, far_total, far_grad, back, key_gain)

    near_feats = both_cores(near_x)
    near_total = project(near_feats)
    near_key_value = finish(near_total, key_gain)
    context, d_query, near_grad = attend(
        near_index, *shared, near_key_value, near_key_value, query_gain, earlier
    )
    near_rows = turn(near_index, near_total, near_grad, near_grad, key_gain)

    operands = (chip, far_feats, near_feats, far_rows, near_rows)
    sent = [None] + [product(d, *operands) for d in range(1, RING)]
    arrived = scattered(sent, outer)
    near_rows, arrived[0] = lax.optimization_barrier((near_rows, arrived[0]))
    total = summed([product(0, *operands[:-1], near_rows), *arrived])
    count = total.shape[0] // RING
    parts = [total[d * count : (d + 1) * count] for d in range(RING)]
    sent = [None] + [part.astype(jnp.bfloat16) for part in parts[1:]]
    share = summed([parts[0], *scattered(sent, inner)])
    head_dim = query_gain.shape[0]
    return (context, d_query, share[:, :head_dim], share[:, head_dim:])


def solution(mesh):
    placed = (
        P("dp", None, "tensor"),
        P("dp", None, "tensor"),
        P(),
        P(),
        P("dp", "tensor"),
        P("dp", "tensor"),
        P(),
        P(),
        P(),
        P("dp", None, "tensor"),
    )
    return jax.shard_map(
        per_device,
        mesh=mesh,
        in_specs=placed,
        out_specs=(
            P("dp", None, "tensor"),
            P("dp", None, "tensor"),
            P("dp", "tensor"),
            P("dp", "tensor"),
        ),
        check_vma=False,
    )
```

```python
import functools

import jax
import jax.numpy as jnp
from jax import lax
from jax.experimental import pallas as pl
from jax.experimental.pallas import tpu as pltpu
from jax.sharding import PartitionSpec as P

TILE = 128
RING = 4
EPS = 1e-06


def along_z(x, step):
    pairs = [(z * RING + y, (z + step) % RING * RING + y) for z in range(RING) for y in range(RING)]
    return lax.ppermute(x, "dp", pairs)


def by_core(x, step, z_core):
    pairs = []
    for z in range(RING):
        for y in range(RING):
            for i in range(RING):
                for c in range(2):
                    to_z, to_y = (z + step, y) if c == z_core else (z, y + step)
                    source = (z * RING + y) * 2 * RING + i * 2 + c
                    target = (to_z % RING * RING + to_y % RING) * 2 * RING + i * 2 + c
                    pairs.append((source, target))
    return lax.ppermute(x, ("dp", "tensor"), pairs)


def inner(x, step):
    return by_core(x, step, 0)


def outer(x, step):
    return by_core(x, step, 1)


def along_x(x, step):
    pairs = [(i * 2 + c, (i + step) % RING * 2 + c) for i in range(RING) for c in range(2)]
    return lax.ppermute(x, "tensor", pairs)


def other_core(x):
    return lax.ppermute(x, "tensor", [(i, i ^ 1) for i in range(2 * RING)])


def gathered(block, move):
    far, after, before = (move(block, step) for step in (2, 1, 3))
    return [block, after, far, before]


def scattered(parts, move):
    return [move(parts[step], step) for step in (2, 1, 3)]


def summed(blocks):
    total = blocks[0].astype(jnp.float32)
    for block in blocks[1:]:
        total = total + block.astype(jnp.float32)
    return total


def rms_factor(values):
    return lax.rsqrt(jnp.mean(values * values, axis=-1, keepdims=True) + EPS)


def norm_back(values, norm_multiplier, gain, grad):
    weighted = grad * gain
    inner = jnp.sum(weighted * values, axis=-1, keepdims=True)
    return (
        norm_multiplier * weighted
        - values * (norm_multiplier * norm_multiplier * norm_multiplier) * inner / values.shape[-1]
    )


def matmul(a, b, contract):
    return lax.dot_general(a, b, (contract, ((), ())), preferred_element_type=jnp.float32)


VMEM = pl.BlockSpec(memory_space=pltpu.VMEM)
SMEM = pl.BlockSpec(memory_space=pltpu.SMEM)
ANY = pl.BlockSpec(memory_space=pl.ANY)
HBM = pl.BlockSpec(memory_space=pltpu.HBM)
PARAMS = pltpu.CompilerParams(vmem_limit_bytes=16 * 1024 * 1024)


def route_kernel(tiles, slots, image_ref, key_ref, value_ref, near, far, chip, far_ref, near_ref, shard_ref, sems):
    rank, place = lax.axis_index("dp"), lax.axis_index("tensor")
    first = 2 * rank

    def sample_of(slot):
        found = lambda i, at: jnp.where(slots[i] == slot, i, at)
        return lax.fori_loop(0, slots.shape[0], found, 0)

    away = [sample_of(first + i) >> 1 != rank for i in range(2)]
    swaps = jnp.logical_or(away[0], away[1])
    far_slot = jnp.where(away[1], 1, 0)
    copies = []
    for i, (slot, target) in enumerate(((far_slot, far_ref), (1 - far_slot, near_ref))):
        copies.append(pltpu.make_async_copy(image_ref.at[slot], target, sems.at[i]))
        copies[i].start()
    head_dim = key_ref.shape[1]
    for i, source in enumerate((key_ref, value_ref)):
        target = shard_ref.at[:, pl.ds(i * head_dim, head_dim)]
        copies.append(pltpu.make_async_copy(source, target, sems.at[2 + i]))
        copies[2 + i].start()
    second_home = slots[first + 1]
    of_slot = jnp.where(second_home == first + far_slot, 1, 0)
    far_own = jnp.where(swaps, jnp.where(second_home >> 1 != rank, 1, 0), of_slot)
    near[0] = 1 - far_own
    near[1] = tiles[first + 1 - far_own]
    near[2] = 0
    far[0] = far_own
    far[1] = tiles[first + far_own]
    far[2] = jnp.where(swaps, 1, 0)
    chip[0] = rank // RING
    chip[1] = rank % RING
    chip[2] = place // 2
    chip[3] = place % 2
    for copy in copies:
        copy.wait()


def route(tiles, image_slot, image, key_weights, value_weights):
    rows = jax.ShapeDtypeStruct(image.shape[1:], image.dtype)
    count, head_dim = key_weights.shape
    weights = jax.ShapeDtypeStruct((count, 2 * head_dim), key_weights.dtype)
    numbers = lambda n: jax.ShapeDtypeStruct((n,), jnp.int32)
    return pl.pallas_call(
        route_kernel,
        in_specs=[SMEM, SMEM, HBM, HBM, HBM],
        out_specs=[SMEM, SMEM, SMEM, VMEM, VMEM, VMEM],
        out_shape=[numbers(3), numbers(3), numbers(4), rows, rows, weights],
        scratch_shapes=[pltpu.SemaphoreType.DMA((4,))],
        compiler_params=PARAMS,
        cost_estimate=pl.CostEstimate(flops=0, bytes_accessed=4 * image.size, transcendentals=0),
    )(tiles, image_slot, image, key_weights, value_weights)


def assemble_kernel(chip, *refs):
    pieces, out_ref, sems = refs[:RING], refs[RING], refs[RING + 1]
    rows, both = pieces[0].shape
    count = rows // RING
    z, y, x, core = chip[0], chip[1], chip[2], chip[3]
    copies = []
    for b in range(RING):
        for a in range(RING):
            from_z = (z - jnp.where(core == 0, a, b) + RING) % RING
            from_y = (y - jnp.where(core == 0, b, a) + RING) % RING
            o = (x - from_z + RING) % RING
            start = ((o * 2 + ((from_y >> 1) ^ core)) * 2 + from_y % 2) * count
            target = out_ref.at[pl.ds(pl.multiple_of(start, count), count)]
            source = pieces[b].at[pl.ds(a * count, count)]
            copies.append(pltpu.make_async_copy(source, target, sems.at[b, a]))
    for copy in copies:
        copy.start()
    for copy in copies:
        copy.wait()


def assemble(chip, pieces):
    rows, both = pieces[0].shape
    return pl.pallas_call(
        assemble_kernel,
        in_specs=[SMEM] + [ANY] * RING,
        out_specs=VMEM,
        out_shape=jax.ShapeDtypeStruct((RING * rows, both), pieces[0].dtype),
        scratch_shapes=[pltpu.SemaphoreType.DMA((RING, RING))],
        compiler_params=PARAMS,
        cost_estimate=pl.CostEstimate(
            flops=0, bytes_accessed=4 * RING * rows * both, transcendentals=0
        ),
    )(chip, *pieces)


def finish_kernel(total_ref, gain_ref, key_value_ref):
    head_dim = gain_ref.shape[1]
    raw = total_ref[:, :head_dim]
    keys = (raw * rms_factor(raw) * gain_ref[...]).astype(jnp.bfloat16)
    key_value_ref[:, :head_dim] = keys
    key_value_ref[:, head_dim:] = total_ref[:, head_dim:].astype(jnp.bfloat16)


def finish(total, gain):
    return pl.pallas_call(
        finish_kernel,
        in_specs=[VMEM] * 2,
        out_specs=VMEM,
        out_shape=jax.ShapeDtypeStruct(total.shape, jnp.bfloat16),
        compiler_params=PARAMS,
        cost_estimate=pl.CostEstimate(
            flops=3 * total.size, bytes_accessed=6 * total.size, transcendentals=total.shape[0]
        ),
    )(total, gain[None, :])


def turn_kernel(flag, total_ref, grad_ref, other_ref, gain_ref, out_ref):
    head_dim = gain_ref.shape[1]
    grad = jnp.where(flag[2] != 0, other_ref[...], grad_ref[...])
    raw = total_ref[:, :head_dim]
    d_raw = norm_back(raw, rms_factor(raw), gain_ref[...], grad[:, :head_dim].astype(jnp.float32))
    out_ref[:, :head_dim] = d_raw.astype(jnp.bfloat16)
    out_ref[:, head_dim:] = grad[:, head_dim:]


def turn(flag, total, grad, other, gain):
    return pl.pallas_call(
        turn_kernel,
        in_specs=[SMEM] + [VMEM] * 4,
        out_specs=VMEM,
        out_shape=jax.ShapeDtypeStruct(grad.shape, jnp.bfloat16),
        compiler_params=PARAMS,
        cost_estimate=pl.CostEstimate(
            flops=6 * grad.size, bytes_accessed=8 * grad.size, transcendentals=grad.shape[0]
        ),
    )(flag, total, grad, other, gain[None, :])


def first_part_kernel(*refs):
    sources, (grads_ref, out_ref) = refs[:-2], refs[-2:]
    depth = sources[0].shape[1]
    for k, source in enumerate(sources):
        out_ref[k * depth : (k + 1) * depth] = matmul(source[...], grads_ref[...], ((0,), (0,)))


def first_part(feats, grads):
    rows, depth = feats[0].shape
    both = grads.shape[1]
    return pl.pallas_call(
        first_part_kernel,
        in_specs=[VMEM] * (len(feats) + 1),
        out_specs=VMEM,
        out_shape=jax.ShapeDtypeStruct((len(feats) * depth, both), jnp.float32),
        compiler_params=PARAMS,
        cost_estimate=pl.CostEstimate(
            flops=2 * len(feats) * rows * depth * both,
            bytes_accessed=2 * len(feats) * rows * depth,
            transcendentals=0,
        ),
    )(*feats, grads)


def product_kernel(chip, *refs):
    sources, (grads_ref, part_ref), refs = refs[: 2 * RING], refs[2 * RING : 2 * RING + 2], refs[2 * RING + 2 :]
    outs, (held, sems) = refs[:RING], refs[RING:]
    depth = sources[0].shape[1]
    count = depth // 2
    z, y, x, core = chip[0], chip[1], chip[2], chip[3]
    for k, source in enumerate(sources):
        total = matmul(source[...], grads_ref[...], ((0,), (0,)))
        total = (total + part_ref[k * depth : (k + 1) * depth]).astype(held.dtype)
        by_z = (x - k // 2 - z + 2 * RING) % RING
        for h in range(2):
            by_y = (2 * (k % 2 ^ core) + h - y + RING) % RING
            outer_by = jnp.where(core == 0, by_y, by_z)
            inner_by = jnp.where(core == 0, by_z, by_y)
            start = pl.multiple_of(inner_by * count, count)
            held[outer_by, pl.ds(start, count)] = total[h * count : (h + 1) * count]
    copies = [pltpu.make_async_copy(held.at[k], outs[k], sems.at[k]) for k in range(RING)]
    for copy in copies:
        copy.start()
    for copy in copies:
        copy.wait()


def product(chip, feats, grads, part):
    rows, depth = feats[0].shape
    both = grads.shape[1]
    shape = (RING * depth // 2, both)
    return pl.pallas_call(
        product_kernel,
        in_specs=[SMEM] + [VMEM] * (len(feats) + 2),
        out_specs=[ANY] * RING,
        out_shape=[jax.ShapeDtypeStruct(shape, jnp.bfloat16)] * RING,
        scratch_shapes=[
            pltpu.VMEM((RING, *shape), jnp.bfloat16),
            pltpu.SemaphoreType.DMA((RING,)),
        ],
        compiler_params=PARAMS,
        cost_estimate=pl.CostEstimate(
            flops=2 * len(feats) * rows * depth * both,
            bytes_accessed=2 * len(feats) * rows * depth,
            transcendentals=0,
        ),
    )(chip, *feats, grads, part)


def attend_kernel(heads, index, ratio_ref, q_ref, cot_ref, kv_ref, away_ref, gain_ref, *refs):
    context_ref, d_query_ref, d_kv_ref, d_key_sum, d_value_sum = refs[-5:]
    step = pl.program_id(0)
    head_dim = gain_ref.shape[1]
    scale = head_dim ** (-0.5)
    count = index[1]
    ratio = ratio_ref[0]
    gain = gain_ref[...]
    key_value = jnp.where(index[2] != 0, away_ref[...], kv_ref[...])
    keys = key_value[:, :head_dim]
    vals = key_value[:, head_dim:]

    def stacked(ref):
        parts = [ref[0, :, h * head_dim : (h + 1) * head_dim] for h in range(heads)]
        return jnp.concatenate(parts, axis=0).astype(jnp.float32)

    def unstacked(ref, rows):
        text = rows.shape[0] // heads
        for h in range(heads):
            part = rows[h * text : (h + 1) * text]
            ref[0, :, h * head_dim : (h + 1) * head_dim] = part.astype(ref.dtype)

    @pl.when(step == 0)
    def _():
        d_key_sum[...] = jnp.zeros_like(d_key_sum)
        d_value_sum[...] = jnp.zeros_like(d_value_sum)

    q_raw = stacked(q_ref)
    q_factor = rms_factor(q_raw)
    q_norm = (q_raw * q_factor * gain).astype(jnp.bfloat16)
    raw = matmul(q_norm, keys, ((1,), (1,))) * scale
    place = lax.broadcasted_iota(jnp.int32, raw.shape, 1)
    expo = jnp.where(place < count * TILE, jnp.exp(raw), 0.0)
    total = jnp.sum(expo, axis=1, keepdims=True) + (count == 0).astype(jnp.float32)
    inverse = 1.0 / total
    weights_b = expo.astype(jnp.bfloat16)
    attended = matmul(weights_b, vals, ((1,), (0,))) * inverse
    unstacked(context_ref, ratio * attended)
    d_att = ratio * stacked(cot_ref)
    d_att_b = d_att.astype(jnp.bfloat16)
    scaled_b = (d_att * inverse).astype(jnp.bfloat16)
    delta = jnp.sum(d_att * attended, axis=1, keepdims=True)
    d_prob = matmul(d_att_b, vals, ((1,), (1,)))
    d_score = (expo * inverse * (d_prob - delta)).astype(jnp.bfloat16)
    d_qn = scale * matmul(d_score, keys, ((1,), (0,)))
    unstacked(d_query_ref, norm_back(q_raw, q_factor, gain, d_qn))
    d_key_sum[...] += matmul(d_score, q_norm, ((0,), (0,)))
    d_value_sum[...] += matmul(weights_b, scaled_b, ((0,), (0,)))

    @pl.when(step == pl.num_programs(0) - 1)
    def _():
        d_kv_ref[:, :head_dim] = (scale * d_key_sum[...]).astype(d_kv_ref.dtype)
        d_kv_ref[:, head_dim:] = d_value_sum[...].astype(d_kv_ref.dtype)


def attend(index, ratio, query, cot, key_value, away, gain, earlier, heads=2):
    rows, both = key_value.shape
    head_dim = both // 2
    text = query.shape[1]
    width = heads * head_dim
    block = pl.BlockSpec((1, text, width), lambda h, index: (index[0], 0, h))
    whole = lambda shape: pl.BlockSpec(shape, lambda h, index: (0, 0))
    in_specs = [
        pl.BlockSpec(memory_space=pltpu.SMEM),
        block,
        block,
        whole((rows, both)),
        whole((rows, both)),
        whole((1, head_dim)),
    ]
    aliases = {}
    if earlier:
        in_specs += [pl.BlockSpec(memory_space=pl.ANY)] * 2
        aliases = {7: 0, 8: 1}
    steps = query.shape[2] // width
    return pl.pallas_call(
        functools.partial(attend_kernel, heads),
        grid_spec=pltpu.PrefetchScalarGridSpec(
            num_scalar_prefetch=1,
            grid=(steps,),
            in_specs=in_specs,
            out_specs=[block, block, whole((rows, both))],
            scratch_shapes=[pltpu.VMEM((rows, head_dim), jnp.float32)] * 2,
        ),
        out_shape=[
            jax.ShapeDtypeStruct(query.shape, jnp.bfloat16),
            jax.ShapeDtypeStruct(query.shape, jnp.bfloat16),
            jax.ShapeDtypeStruct((rows, both), jnp.bfloat16),
        ],
        input_output_aliases=aliases,
        compiler_params=pltpu.CompilerParams(
            vmem_limit_bytes=24 * 1024 * 1024
        ),
        cost_estimate=pl.CostEstimate(
            flops=14 * steps * heads * text * rows * head_dim,
            bytes_accessed=8 * text * steps * width + 6 * rows * head_dim,
            transcendentals=steps * heads * text * rows,
        ),
    )(
        index,
        ratio,
        query,
        cot,
        key_value,
        away,
        gain[None, :],
        *earlier,
    )


def per_device(
    query,
    image,
    tiles,
    image_slot,
    key_weight_matrix,
    value_weight_matrix,
    query_gain,
    key_gain,
    gate,
    cotangent,
):
    ratio = jnp.tanh(gate)
    near_index, far_index, chip, far_own, near_own, shard = route(
        tiles, image_slot, image, key_weight_matrix, value_weight_matrix
    )

    def opposite(after, before):
        half = after.shape[0] // 2
        return along_x(after[:half], 1), along_x(before[half:], 3)

    far_x = [along_x(far_own, 1), along_x(far_own, 3)]
    pieces = gathered(jnp.concatenate(gathered(shard, inner), axis=0), outer)
    near_own, *far_x = lax.optimization_barrier((near_own, *far_x))
    far_halves = opposite(*far_x)
    near_x = [along_x(near_own, 1), along_x(near_own, 3)]
    weights = assemble(chip, pieces)
    near_halves = opposite(*near_x)

    def both_cores(own, after, before, halves):
        blocks = [own, after, jnp.concatenate(halves, axis=0), before]
        return [block for own in blocks for block in (own, other_core(own))]

    def project(feats):
        depth = feats[0].shape[1]
        total = None
        for o in (0, 1, 3, 2):
            for k in (2 * o, 2 * o + 1):
                part = matmul(feats[k], weights[k * depth : (k + 1) * depth], ((1,), (0,)))
                total = part if total is None else total + part
        return total

    shared = (ratio, query, cotangent)
    far_feats = both_cores(far_own, *far_x, far_halves)
    far_total = project(far_feats)
    far_key_value = finish(far_total, key_gain)
    away = along_z(far_key_value, RING // 2)
    *earlier, far_grad = attend(far_index, *shared, far_key_value, away, query_gain, ())
    back = along_z(far_grad, RING // 2)
    far_rows = turn(far_index, far_total, far_grad, back, key_gain)
    part = first_part(far_feats, far_rows)

    near_feats = both_cores(near_own, *near_x, near_halves)
    near_total = project(near_feats)
    near_key_value = finish(near_total, key_gain)
    context, d_query, near_grad = attend(
        near_index, *shared, near_key_value, near_key_value, query_gain, earlier
    )
    near_rows = turn(near_index, near_total, near_grad, near_grad, key_gain)

    blocks = product(chip, near_feats, near_rows, part)
    total = summed([blocks[0], *scattered(blocks, outer)])
    count = total.shape[0] // RING
    parts = [total[d * count : (d + 1) * count] for d in range(RING)]
    sent = [None] + [part.astype(jnp.bfloat16) for part in parts[1:]]
    share = summed([parts[0], *scattered(sent, inner)])
    head_dim = query_gain.shape[0]
    return (context, d_query, share[:, :head_dim], share[:, head_dim:])


def solution(mesh):
    placed = (
        P("dp", None, "tensor"),
        P("dp", None, "tensor"),
        P(),
        P(),
        P("dp", "tensor"),
        P("dp", "tensor"),
        P(),
        P(),
        P(),
        P("dp", None, "tensor"),
    )
    return jax.shard_map(
        per_device,
        mesh=mesh,
        in_specs=placed,
        out_specs=(
            P("dp", None, "tensor"),
            P("dp", None, "tensor"),
            P("dp", "tensor"),
            P("dp", "tensor"),
        ),
        check_vma=False,
    )
```

```python
import functools

import jax
import jax.numpy as jnp
from jax import lax
from jax.experimental import pallas as pl
from jax.experimental.pallas import tpu as pltpu
from jax.sharding import PartitionSpec as P

TILE = 128
RING = 4
EPS = 1e-06


def along_z(x, step):
    pairs = [(z * RING + y, (z + step) % RING * RING + y) for z in range(RING) for y in range(RING)]
    return lax.ppermute(x, "dp", pairs)


def by_core(x, step, z_core):
    pairs = []
    for z in range(RING):
        for y in range(RING):
            for i in range(RING):
                for c in range(2):
                    to_z, to_y = (z + step, y) if c == z_core else (z, y + step)
                    source = (z * RING + y) * 2 * RING + i * 2 + c
                    target = (to_z % RING * RING + to_y % RING) * 2 * RING + i * 2 + c
                    pairs.append((source, target))
    return lax.ppermute(x, ("dp", "tensor"), pairs)


def inner(x, step):
    return by_core(x, step, 0)


def outer(x, step):
    return by_core(x, step, 1)


def along_x(x, step):
    pairs = [(i * 2 + c, (i + step) % RING * 2 + c) for i in range(RING) for c in range(2)]
    return lax.ppermute(x, "tensor", pairs)


def other_core(x):
    return lax.ppermute(x, "tensor", [(i, i ^ 1) for i in range(2 * RING)])


def gathered(block, move):
    far, after, before = (move(block, step) for step in (2, 1, 3))
    return [block, after, far, before]


def scattered(parts, move):
    return [move(parts[step], step) for step in (2, 1, 3)]


def summed(blocks):
    total = blocks[0].astype(jnp.float32)
    for block in blocks[1:]:
        total = total + block.astype(jnp.float32)
    return total


def rms_factor(values):
    return lax.rsqrt(jnp.mean(values * values, axis=-1, keepdims=True) + EPS)


def norm_back(values, norm_multiplier, gain, grad):
    weighted = grad * gain
    inner = jnp.sum(weighted * values, axis=-1, keepdims=True)
    return (
        norm_multiplier * weighted
        - values * (norm_multiplier * norm_multiplier * norm_multiplier) * inner / values.shape[-1]
    )


def matmul(a, b, contract):
    return lax.dot_general(a, b, (contract, ((), ())), preferred_element_type=jnp.float32)


VMEM = pl.BlockSpec(memory_space=pltpu.VMEM)
SMEM = pl.BlockSpec(memory_space=pltpu.SMEM)
ANY = pl.BlockSpec(memory_space=pl.ANY)
HBM = pl.BlockSpec(memory_space=pltpu.HBM)
PARAMS = pltpu.CompilerParams(vmem_limit_bytes=16 * 1024 * 1024)


def route_kernel(tiles, slots, image_ref, key_ref, value_ref, near, far, chip, far_ref, near_ref, shard_ref, sems):
    rank, place = lax.axis_index("dp"), lax.axis_index("tensor")
    first = 2 * rank

    def sample_of(slot):
        found = lambda i, at: jnp.where(slots[i] == slot, i, at)
        return lax.fori_loop(0, slots.shape[0], found, 0)

    away = [sample_of(first + i) >> 1 != rank for i in range(2)]
    swaps = jnp.logical_or(away[0], away[1])
    far_slot = jnp.where(away[1], 1, 0)
    copies = []
    for i, (slot, target) in enumerate(((far_slot, far_ref), (1 - far_slot, near_ref))):
        copies.append(pltpu.make_async_copy(image_ref.at[slot], target, sems.at[i]))
        copies[i].start()
    head_dim = key_ref.shape[1]
    for i, source in enumerate((key_ref, value_ref)):
        target = shard_ref.at[:, pl.ds(i * head_dim, head_dim)]
        copies.append(pltpu.make_async_copy(source, target, sems.at[2 + i]))
        copies[2 + i].start()
    second_home = slots[first + 1]
    of_slot = jnp.where(second_home == first + far_slot, 1, 0)
    far_own = jnp.where(swaps, jnp.where(second_home >> 1 != rank, 1, 0), of_slot)
    near[0] = 1 - far_own
    near[1] = tiles[first + 1 - far_own]
    near[2] = 0
    far[0] = far_own
    far[1] = tiles[first + far_own]
    far[2] = jnp.where(swaps, 1, 0)
    chip[0] = rank // RING
    chip[1] = rank % RING
    chip[2] = place // 2
    chip[3] = place % 2
    for copy in copies:
        copy.wait()


def route(tiles, image_slot, image, key_weights, value_weights):
    rows = jax.ShapeDtypeStruct(image.shape[1:], image.dtype)
    count, head_dim = key_weights.shape
    weights = jax.ShapeDtypeStruct((count, 2 * head_dim), key_weights.dtype)
    numbers = lambda n: jax.ShapeDtypeStruct((n,), jnp.int32)
    return pl.pallas_call(
        route_kernel,
        in_specs=[SMEM, SMEM, HBM, HBM, HBM],
        out_specs=[SMEM, SMEM, SMEM, VMEM, VMEM, VMEM],
        out_shape=[numbers(3), numbers(3), numbers(4), rows, rows, weights],
        scratch_shapes=[pltpu.SemaphoreType.DMA((4,))],
        compiler_params=pltpu.CompilerParams(vmem_limit_bytes=60 * 1024 * 1024),
        cost_estimate=pl.CostEstimate(flops=0, bytes_accessed=4 * image.size, transcendentals=0),
    )(tiles, image_slot, image, key_weights, value_weights)


def assemble_kernel(chip, *refs):
    pieces, out_ref, sems = refs[:RING], refs[RING], refs[RING + 1]
    rows, both = pieces[0].shape
    count = rows // RING
    z, y, x, core = chip[0], chip[1], chip[2], chip[3]
    copies = []
    for b in range(RING):
        for a in range(RING):
            from_z = (z - jnp.where(core == 0, a, b) + RING) % RING
            from_y = (y - jnp.where(core == 0, b, a) + RING) % RING
            o = (x - from_z + RING) % RING
            start = ((o * 2 + ((from_y >> 1) ^ core)) * 2 + from_y % 2) * count
            target = out_ref.at[pl.ds(pl.multiple_of(start, count), count)]
            source = pieces[b].at[pl.ds(a * count, count)]
            copies.append(pltpu.make_async_copy(source, target, sems.at[b, a]))
    for copy in copies:
        copy.start()
    for copy in copies:
        copy.wait()


def assemble(chip, pieces):
    rows, both = pieces[0].shape
    return pl.pallas_call(
        assemble_kernel,
        in_specs=[SMEM] + [ANY] * RING,
        out_specs=VMEM,
        out_shape=jax.ShapeDtypeStruct((RING * rows, both), pieces[0].dtype),
        scratch_shapes=[pltpu.SemaphoreType.DMA((RING, RING))],
        compiler_params=PARAMS,
        cost_estimate=pl.CostEstimate(
            flops=0, bytes_accessed=4 * RING * rows * both, transcendentals=0
        ),
    )(chip, *pieces)


def finish_kernel(total_ref, gain_ref, key_value_ref):
    head_dim = gain_ref.shape[1]
    raw = total_ref[:, :head_dim]
    keys = (raw * rms_factor(raw) * gain_ref[...]).astype(jnp.bfloat16)
    key_value_ref[:, :head_dim] = keys
    key_value_ref[:, head_dim:] = total_ref[:, head_dim:].astype(jnp.bfloat16)


def finish(total, gain):
    return pl.pallas_call(
        finish_kernel,
        in_specs=[VMEM] * 2,
        out_specs=VMEM,
        out_shape=jax.ShapeDtypeStruct(total.shape, jnp.bfloat16),
        compiler_params=PARAMS,
        cost_estimate=pl.CostEstimate(
            flops=3 * total.size, bytes_accessed=6 * total.size, transcendentals=total.shape[0]
        ),
    )(total, gain[None, :])


def turn_kernel(flag, total_ref, grad_ref, other_ref, gain_ref, out_ref):
    head_dim = gain_ref.shape[1]
    grad = jnp.where(flag[2] != 0, other_ref[...], grad_ref[...])
    raw = total_ref[:, :head_dim]
    d_raw = norm_back(raw, rms_factor(raw), gain_ref[...], grad[:, :head_dim].astype(jnp.float32))
    out_ref[:, :head_dim] = d_raw.astype(jnp.bfloat16)
    out_ref[:, head_dim:] = grad[:, head_dim:]


def turn(flag, total, grad, other, gain):
    return pl.pallas_call(
        turn_kernel,
        in_specs=[SMEM] + [VMEM] * 4,
        out_specs=VMEM,
        out_shape=jax.ShapeDtypeStruct(grad.shape, jnp.bfloat16),
        compiler_params=PARAMS,
        cost_estimate=pl.CostEstimate(
            flops=6 * grad.size, bytes_accessed=8 * grad.size, transcendentals=grad.shape[0]
        ),
    )(flag, total, grad, other, gain[None, :])


def first_part_kernel(*refs):
    sources, (grads_ref, out_ref) = refs[:-2], refs[-2:]
    depth = sources[0].shape[1]
    for k, source in enumerate(sources):
        out_ref[k * depth : (k + 1) * depth] = matmul(source[...], grads_ref[...], ((0,), (0,)))


def first_part(feats, grads):
    rows, depth = feats[0].shape
    both = grads.shape[1]
    return pl.pallas_call(
        first_part_kernel,
        in_specs=[VMEM] * (len(feats) + 1),
        out_specs=VMEM,
        out_shape=jax.ShapeDtypeStruct((len(feats) * depth, both), jnp.float32),
        compiler_params=PARAMS,
        cost_estimate=pl.CostEstimate(
            flops=2 * len(feats) * rows * depth * both,
            bytes_accessed=2 * len(feats) * rows * depth,
            transcendentals=0,
        ),
    )(*feats, grads)


def product_kernel(chip, *refs):
    sources, (grads_ref, part_ref), refs = refs[: 2 * RING], refs[2 * RING : 2 * RING + 2], refs[2 * RING + 2 :]
    outs, (held, sems) = refs[: RING + 1], refs[RING + 1 :]
    sems_of = [sems.at[i] for i in range(len(outs))]
    depth = sources[0].shape[1]
    count = depth // 2
    z, y, x, core = chip[0], chip[1], chip[2], chip[3]
    for k, source in enumerate(sources):
        total = matmul(source[...], grads_ref[...], ((0,), (0,)))
        total = (total + part_ref[k * depth : (k + 1) * depth]).astype(held.dtype)
        by_z = (x - k // 2 - z + 2 * RING) % RING
        for h in range(2):
            by_y = (2 * (k % 2 ^ core) + h - y + RING) % RING
            outer_by = jnp.where(core == 0, by_y, by_z)
            inner_by = jnp.where(core == 0, by_z, by_y)
            start = pl.multiple_of(inner_by * count, count)
            held[outer_by, pl.ds(start, count)] = total[h * count : (h + 1) * count]
    half = held.shape[1] // 2
    parts = (held.at[0], held.at[1], held.at[2, pl.ds(0, half)], held.at[2, pl.ds(half, half)], held.at[3])
    copies = [pltpu.make_async_copy(part, out, sem) for part, out, sem in zip(parts, outs, sems_of)]
    for copy in copies:
        copy.start()
    for copy in copies:
        copy.wait()


def product(chip, feats, grads, part):
    rows, depth = feats[0].shape
    both = grads.shape[1]
    shape = (RING * depth // 2, both)
    whole = jax.ShapeDtypeStruct(shape, jnp.bfloat16)
    half = jax.ShapeDtypeStruct((shape[0] // 2, both), jnp.bfloat16)
    return pl.pallas_call(
        product_kernel,
        in_specs=[SMEM] + [VMEM] * (len(feats) + 2),
        out_specs=[ANY] * (RING + 1),
        out_shape=[whole, whole, half, half, whole],
        scratch_shapes=[
            pltpu.VMEM((RING, *shape), jnp.bfloat16),
            pltpu.SemaphoreType.DMA((RING + 1,)),
        ],
        compiler_params=PARAMS,
        cost_estimate=pl.CostEstimate(
            flops=2 * len(feats) * rows * depth * both,
            bytes_accessed=2 * len(feats) * rows * depth,
            transcendentals=0,
        ),
    )(chip, *feats, grads, part)


def passed_kernel(after_ref, before_ref, upper_ref, lower_ref, to_after_ref, to_before_ref):
    half = upper_ref.shape[0]

    def added(block, piece):
        return (block.astype(jnp.float32) + piece.astype(jnp.float32)).astype(jnp.bfloat16)

    to_after_ref[:half] = added(after_ref[:half], upper_ref[...])
    to_after_ref[half:] = after_ref[half:]
    to_before_ref[:half] = before_ref[:half]
    to_before_ref[half:] = added(before_ref[half:], lower_ref[...])


def passed(after, before, upper, lower):
    return pl.pallas_call(
        passed_kernel,
        in_specs=[VMEM] * 4,
        out_specs=[VMEM] * 2,
        out_shape=[jax.ShapeDtypeStruct(after.shape, after.dtype)] * 2,
        compiler_params=PARAMS,
        cost_estimate=pl.CostEstimate(
            flops=after.size, bytes_accessed=10 * after.size, transcendentals=0
        ),
    )(after, before, upper, lower)


def attend_kernel(heads, index, ratio_ref, q_ref, cot_ref, kv_ref, away_ref, gain_ref, *refs):
    context_ref, d_query_ref, d_kv_ref, d_key_sum, d_value_sum = refs[-5:]
    step = pl.program_id(0)
    head_dim = gain_ref.shape[1]
    scale = head_dim ** (-0.5)
    count = index[1]
    ratio = ratio_ref[0]
    gain = gain_ref[...]
    key_value = jnp.where(index[2] != 0, away_ref[...], kv_ref[...])
    keys = key_value[:, :head_dim]
    vals = key_value[:, head_dim:]

    def stacked(ref):
        parts = [ref[0, :, h * head_dim : (h + 1) * head_dim] for h in range(heads)]
        return jnp.concatenate(parts, axis=0).astype(jnp.float32)

    def unstacked(ref, rows):
        text = rows.shape[0] // heads
        for h in range(heads):
            part = rows[h * text : (h + 1) * text]
            ref[0, :, h * head_dim : (h + 1) * head_dim] = part.astype(ref.dtype)

    @pl.when(step == 0)
    def _():
        d_key_sum[...] = jnp.zeros_like(d_key_sum)
        d_value_sum[...] = jnp.zeros_like(d_value_sum)

    q_raw = stacked(q_ref)
    q_factor = rms_factor(q_raw)
    q_norm = (q_raw * q_factor * gain).astype(jnp.bfloat16)
    raw = matmul(q_norm, keys, ((1,), (1,))) * scale
    place = lax.broadcasted_iota(jnp.int32, raw.shape, 1)
    expo = jnp.where(place < count * TILE, jnp.exp(raw), 0.0)
    total = jnp.sum(expo, axis=1, keepdims=True) + (count == 0).astype(jnp.float32)
    inverse = 1.0 / total
    weights_b = expo.astype(jnp.bfloat16)
    attended = matmul(weights_b, vals, ((1,), (0,))) * inverse
    unstacked(context_ref, ratio * attended)
    d_att = ratio * stacked(cot_ref)
    d_att_b = d_att.astype(jnp.bfloat16)
    scaled_b = (d_att * inverse).astype(jnp.bfloat16)
    delta = jnp.sum(d_att * attended, axis=1, keepdims=True)
    d_prob = matmul(d_att_b, vals, ((1,), (1,)))
    d_score = (expo * inverse * (d_prob - delta)).astype(jnp.bfloat16)
    d_qn = scale * matmul(d_score, keys, ((1,), (0,)))
    unstacked(d_query_ref, norm_back(q_raw, q_factor, gain, d_qn))
    d_key_sum[...] += matmul(d_score, q_norm, ((0,), (0,)))
    d_value_sum[...] += matmul(weights_b, scaled_b, ((0,), (0,)))

    @pl.when(step == pl.num_programs(0) - 1)
    def _():
        d_kv_ref[:, :head_dim] = (scale * d_key_sum[...]).astype(d_kv_ref.dtype)
        d_kv_ref[:, head_dim:] = d_value_sum[...].astype(d_kv_ref.dtype)


def attend(index, ratio, query, cot, key_value, away, gain, earlier, heads=2):
    rows, both = key_value.shape
    head_dim = both // 2
    text = query.shape[1]
    width = heads * head_dim
    block = pl.BlockSpec((1, text, width), lambda h, index: (index[0], 0, h))
    whole = lambda shape: pl.BlockSpec(shape, lambda h, index: (0, 0))
    in_specs = [
        pl.BlockSpec(memory_space=pltpu.SMEM),
        block,
        block,
        whole((rows, both)),
        whole((rows, both)),
        whole((1, head_dim)),
    ]
    aliases = {}
    if earlier:
        in_specs += [pl.BlockSpec(memory_space=pl.ANY)] * 2
        aliases = {7: 0, 8: 1}
    steps = query.shape[2] // width
    return pl.pallas_call(
        functools.partial(attend_kernel, heads),
        grid_spec=pltpu.PrefetchScalarGridSpec(
            num_scalar_prefetch=1,
            grid=(steps,),
            in_specs=in_specs,
            out_specs=[block, block, whole((rows, both))],
            scratch_shapes=[pltpu.VMEM((rows, head_dim), jnp.float32)] * 2,
        ),
        out_shape=[
            jax.ShapeDtypeStruct(query.shape, jnp.bfloat16),
            jax.ShapeDtypeStruct(query.shape, jnp.bfloat16),
            jax.ShapeDtypeStruct((rows, both), jnp.bfloat16),
        ],
        input_output_aliases=aliases,
        compiler_params=pltpu.CompilerParams(
            vmem_limit_bytes=24 * 1024 * 1024
        ),
        cost_estimate=pl.CostEstimate(
            flops=14 * steps * heads * text * rows * head_dim,
            bytes_accessed=8 * text * steps * width + 6 * rows * head_dim,
            transcendentals=steps * heads * text * rows,
        ),
    )(
        index,
        ratio,
        query,
        cot,
        key_value,
        away,
        gain[None, :],
        *earlier,
    )


def per_device(
    query,
    image,
    tiles,
    image_slot,
    key_weight_matrix,
    value_weight_matrix,
    query_gain,
    key_gain,
    gate,
    cotangent,
):
    ratio = jnp.tanh(gate)
    near_index, far_index, chip, far_own, near_own, shard = route(
        tiles, image_slot, image, key_weight_matrix, value_weight_matrix
    )

    def opposite(after, before):
        half = after.shape[0] // 2
        return along_x(after[:half], 1), along_x(before[half:], 3)

    far_x = [along_x(far_own, 1), along_x(far_own, 3)]
    pieces = gathered(jnp.concatenate(gathered(shard, inner), axis=0), outer)
    far_halves = opposite(*far_x)
    near_own, *far_halves = lax.optimization_barrier((near_own, *far_halves))
    near_x = [along_x(near_own, 1), along_x(near_own, 3)]
    weights = assemble(chip, pieces)

    def both_cores(own, after, before, halves):
        blocks = [own, after, jnp.concatenate(halves, axis=0), before]
        return [block for own in blocks for block in (own, other_core(own))]

    def project(feats):
        depth = feats[0].shape[1]
        total = None
        for o in (0, 1, 3, 2):
            for k in (2 * o, 2 * o + 1):
                part = matmul(feats[k], weights[k * depth : (k + 1) * depth], ((1,), (0,)))
                total = part if total is None else total + part
        return total

    shared = (ratio, query, cotangent)
    far_feats = both_cores(far_own, *far_x, far_halves)
    far_total = project(far_feats)
    far_key_value = finish(far_total, key_gain)
    far_key_value, *near_x = lax.optimization_barrier((far_key_value, *near_x))
    near_halves = opposite(*near_x)
    away = along_z(far_key_value, RING // 2)
    *earlier, far_grad = attend(far_index, *shared, far_key_value, away, query_gain, ())
    back = along_z(far_grad, RING // 2)
    far_rows = turn(far_index, far_total, far_grad, back, key_gain)
    part = first_part(far_feats, far_rows)

    near_feats = both_cores(near_own, *near_x, near_halves)
    near_total = project(near_feats)
    near_key_value = finish(near_total, key_gain)
    context, d_query, near_grad = attend(
        near_index, *shared, near_key_value, near_key_value, query_gain, earlier
    )
    near_rows = turn(near_index, near_total, near_grad, near_grad, key_gain)

    blocks = product(chip, near_feats, near_rows, part)
    own, after, upper, lower, before = blocks
    after, before = passed(after, before, outer(upper, 1), outer(lower, 3))
    total = summed([own, outer(after, 1), outer(before, 3)])
    count = total.shape[0] // RING
    parts = [total[d * count : (d + 1) * count] for d in range(RING)]
    sent = [None] + [part.astype(jnp.bfloat16) for part in parts[1:]]
    share = summed([parts[0], *scattered(sent, inner)])
    head_dim = query_gain.shape[0]
    return (context, d_query, share[:, :head_dim], share[:, head_dim:])


def solution(mesh):
    placed = (
        P("dp", None, "tensor"),
        P("dp", None, "tensor"),
        P(),
        P(),
        P("dp", "tensor"),
        P("dp", "tensor"),
        P(),
        P(),
        P(),
        P("dp", None, "tensor"),
    )
    return jax.shard_map(
        per_device,
        mesh=mesh,
        in_specs=placed,
        out_specs=(
            P("dp", None, "tensor"),
            P("dp", None, "tensor"),
            P("dp", "tensor"),
            P("dp", "tensor"),
        ),
        check_vma=False,
    )
```

```python
import functools

import jax
import jax.numpy as jnp
from jax import lax
from jax.experimental import pallas as pl
from jax.experimental.pallas import tpu as pltpu
from jax.sharding import PartitionSpec as P

TILE = 128
RING = 4
EPS = 1e-06


def along_z(x, step):
    pairs = [(z * RING + y, (z + step) % RING * RING + y) for z in range(RING) for y in range(RING)]
    return lax.ppermute(x, "dp", pairs)


def by_core(x, step, z_core):
    pairs = []
    for z in range(RING):
        for y in range(RING):
            for i in range(RING):
                for c in range(2):
                    to_z, to_y = (z + step, y) if c == z_core else (z, y + step)
                    source = (z * RING + y) * 2 * RING + i * 2 + c
                    target = (to_z % RING * RING + to_y % RING) * 2 * RING + i * 2 + c
                    pairs.append((source, target))
    return lax.ppermute(x, ("dp", "tensor"), pairs)


def inner(x, step):
    return by_core(x, step, 0)


def outer(x, step):
    return by_core(x, step, 1)


def along_x(x, step):
    pairs = [(i * 2 + c, (i + step) % RING * 2 + c) for i in range(RING) for c in range(2)]
    return lax.ppermute(x, "tensor", pairs)


def other_core(x):
    return lax.ppermute(x, "tensor", [(i, i ^ 1) for i in range(2 * RING)])


def gathered(block, move):
    far, after, before = (move(block, step) for step in (2, 1, 3))
    return [block, after, far, before]


def scattered(parts, move):
    return [move(parts[step], step) for step in (2, 1, 3)]


def summed(blocks):
    total = blocks[0].astype(jnp.float32)
    for block in blocks[1:]:
        total = total + block.astype(jnp.float32)
    return total


def rms_factor(values):
    return lax.rsqrt(jnp.mean(values * values, axis=-1, keepdims=True) + EPS)


def norm_back(values, norm_multiplier, gain, grad):
    weighted = grad * gain
    inner = jnp.sum(weighted * values, axis=-1, keepdims=True)
    return (
        norm_multiplier * weighted
        - values * (norm_multiplier * norm_multiplier * norm_multiplier) * inner / values.shape[-1]
    )


def matmul(a, b, contract):
    return lax.dot_general(a, b, (contract, ((), ())), preferred_element_type=jnp.float32)


VMEM = pl.BlockSpec(memory_space=pltpu.VMEM)
SMEM = pl.BlockSpec(memory_space=pltpu.SMEM)
ANY = pl.BlockSpec(memory_space=pl.ANY)
HBM = pl.BlockSpec(memory_space=pltpu.HBM)
PARAMS = pltpu.CompilerParams(vmem_limit_bytes=16 * 1024 * 1024)


def route_kernel(tiles, slots, image_ref, key_ref, value_ref, near, far, chip, far_ref, near_ref, shard_ref, sems):
    rank, place = lax.axis_index("dp"), lax.axis_index("tensor")
    first = 2 * rank
    homes = (slots[first], slots[first + 1])
    away = [
        jnp.logical_and(homes[0] != first + i, homes[1] != first + i) for i in range(2)
    ]
    swaps = jnp.logical_or(away[0], away[1])
    far_slot = jnp.where(away[1], 1, 0)
    copies = []
    for i, (slot, target) in enumerate(((far_slot, far_ref), (1 - far_slot, near_ref))):
        copies.append(pltpu.make_async_copy(image_ref.at[slot], target, sems.at[i]))
        copies[i].start()
    head_dim = key_ref.shape[1]
    for i, source in enumerate((key_ref, value_ref)):
        target = shard_ref.at[:, pl.ds(i * head_dim, head_dim)]
        copies.append(pltpu.make_async_copy(source, target, sems.at[2 + i]))
        copies[2 + i].start()
    of_slot = jnp.where(homes[1] == first + far_slot, 1, 0)
    far_own = jnp.where(swaps, jnp.where(homes[1] >> 1 != rank, 1, 0), of_slot)
    near[0] = 1 - far_own
    near[1] = tiles[first + 1 - far_own]
    near[2] = 0
    far[0] = far_own
    far[1] = tiles[first + far_own]
    far[2] = jnp.where(swaps, 1, 0)
    chip[0] = rank // RING
    chip[1] = rank % RING
    chip[2] = place // 2
    chip[3] = place % 2
    for copy in copies:
        copy.wait()


def route(tiles, image_slot, image, key_weights, value_weights):
    rows = jax.ShapeDtypeStruct(image.shape[1:], image.dtype)
    count, head_dim = key_weights.shape
    weights = jax.ShapeDtypeStruct((count, 2 * head_dim), key_weights.dtype)
    numbers = lambda n: jax.ShapeDtypeStruct((n,), jnp.int32)
    return pl.pallas_call(
        route_kernel,
        in_specs=[SMEM, SMEM, HBM, HBM, HBM],
        out_specs=[SMEM, SMEM, SMEM, VMEM, VMEM, VMEM],
        out_shape=[numbers(3), numbers(3), numbers(4), rows, rows, weights],
        scratch_shapes=[pltpu.SemaphoreType.DMA((4,))],
        compiler_params=pltpu.CompilerParams(vmem_limit_bytes=60 * 1024 * 1024),
        cost_estimate=pl.CostEstimate(flops=0, bytes_accessed=4 * image.size, transcendentals=0),
    )(tiles, image_slot, image, key_weights, value_weights)


def assemble_kernel(chip, *refs):
    pieces, out_ref, sems = refs[:RING], refs[RING], refs[RING + 1]
    rows, both = pieces[0].shape
    count = rows // RING
    z, y, x, core = chip[0], chip[1], chip[2], chip[3]
    copies = []
    for b in range(RING):
        for a in range(RING):
            from_z = (z - jnp.where(core == 0, a, b) + RING) % RING
            from_y = (y - jnp.where(core == 0, b, a) + RING) % RING
            o = (x - from_z + RING) % RING
            start = ((o * 2 + ((from_y >> 1) ^ core)) * 2 + from_y % 2) * count
            target = out_ref.at[pl.ds(pl.multiple_of(start, count), count)]
            source = pieces[b].at[pl.ds(a * count, count)]
            copies.append(pltpu.make_async_copy(source, target, sems.at[b, a]))
    for copy in copies:
        copy.start()
    for copy in copies:
        copy.wait()


def assemble(chip, pieces):
    rows, both = pieces[0].shape
    return pl.pallas_call(
        assemble_kernel,
        in_specs=[SMEM] + [ANY] * RING,
        out_specs=VMEM,
        out_shape=jax.ShapeDtypeStruct((RING * rows, both), pieces[0].dtype),
        scratch_shapes=[pltpu.SemaphoreType.DMA((RING, RING))],
        compiler_params=PARAMS,
        cost_estimate=pl.CostEstimate(
            flops=0, bytes_accessed=4 * RING * rows * both, transcendentals=0
        ),
    )(chip, *pieces)


def finish_kernel(total_ref, gain_ref, key_value_ref):
    head_dim = gain_ref.shape[1]
    raw = total_ref[:, :head_dim]
    keys = (raw * rms_factor(raw) * gain_ref[...]).astype(jnp.bfloat16)
    key_value_ref[:, :head_dim] = keys
    key_value_ref[:, head_dim:] = total_ref[:, head_dim:].astype(jnp.bfloat16)


def finish(total, gain):
    return pl.pallas_call(
        finish_kernel,
        in_specs=[VMEM] * 2,
        out_specs=VMEM,
        out_shape=jax.ShapeDtypeStruct(total.shape, jnp.bfloat16),
        compiler_params=PARAMS,
        cost_estimate=pl.CostEstimate(
            flops=3 * total.size, bytes_accessed=6 * total.size, transcendentals=total.shape[0]
        ),
    )(total, gain[None, :])


def turn_kernel(flag, total_ref, grad_ref, other_ref, gain_ref, out_ref):
    head_dim = gain_ref.shape[1]
    grad = jnp.where(flag[2] != 0, other_ref[...], grad_ref[...])
    raw = total_ref[:, :head_dim]
    d_raw = norm_back(raw, rms_factor(raw), gain_ref[...], grad[:, :head_dim].astype(jnp.float32))
    out_ref[:, :head_dim] = d_raw.astype(jnp.bfloat16)
    out_ref[:, head_dim:] = grad[:, head_dim:]


def turn(flag, total, grad, other, gain):
    return pl.pallas_call(
        turn_kernel,
        in_specs=[SMEM] + [VMEM] * 4,
        out_specs=VMEM,
        out_shape=jax.ShapeDtypeStruct(grad.shape, jnp.bfloat16),
        compiler_params=PARAMS,
        cost_estimate=pl.CostEstimate(
            flops=6 * grad.size, bytes_accessed=8 * grad.size, transcendentals=grad.shape[0]
        ),
    )(flag, total, grad, other, gain[None, :])


def first_part_kernel(*refs):
    sources, (grads_ref, out_ref) = refs[:-2], refs[-2:]
    depth = sources[0].shape[1]
    for k, source in enumerate(sources):
        out_ref[k * depth : (k + 1) * depth] = matmul(source[...], grads_ref[...], ((0,), (0,)))


def first_part(feats, grads):
    rows, depth = feats[0].shape
    both = grads.shape[1]
    return pl.pallas_call(
        first_part_kernel,
        in_specs=[VMEM] * (len(feats) + 1),
        out_specs=VMEM,
        out_shape=jax.ShapeDtypeStruct((len(feats) * depth, both), jnp.float32),
        compiler_params=PARAMS,
        cost_estimate=pl.CostEstimate(
            flops=2 * len(feats) * rows * depth * both,
            bytes_accessed=2 * len(feats) * rows * depth,
            transcendentals=0,
        ),
    )(*feats, grads)


def product_kernel(chip, *refs):
    sources, (grads_ref, part_ref), refs = refs[: 2 * RING], refs[2 * RING : 2 * RING + 2], refs[2 * RING + 2 :]
    outs, (held, sems) = refs[: RING + 1], refs[RING + 1 :]
    sems_of = [sems.at[i] for i in range(len(outs))]
    depth = sources[0].shape[1]
    count = depth // 2
    z, y, x, core = chip[0], chip[1], chip[2], chip[3]
    for k, source in enumerate(sources):
        total = matmul(source[...], grads_ref[...], ((0,), (0,)))
        total = (total + part_ref[k * depth : (k + 1) * depth]).astype(held.dtype)
        by_z = (x - k // 2 - z + 2 * RING) % RING
        for h in range(2):
            by_y = (2 * (k % 2 ^ core) + h - y + RING) % RING
            outer_by = jnp.where(core == 0, by_y, by_z)
            inner_by = jnp.where(core == 0, by_z, by_y)
            start = pl.multiple_of(inner_by * count, count)
            held[outer_by, pl.ds(start, count)] = total[h * count : (h + 1) * count]
    half = held.shape[1] // 2
    parts = (held.at[0], held.at[1], held.at[2, pl.ds(0, half)], held.at[2, pl.ds(half, half)], held.at[3])
    copies = [pltpu.make_async_copy(part, out, sem) for part, out, sem in zip(parts, outs, sems_of)]
    for copy in copies:
        copy.start()
    for copy in copies:
        copy.wait()


def product(chip, feats, grads, part):
    rows, depth = feats[0].shape
    both = grads.shape[1]
    shape = (RING * depth // 2, both)
    whole = jax.ShapeDtypeStruct(shape, jnp.bfloat16)
    half = jax.ShapeDtypeStruct((shape[0] // 2, both), jnp.bfloat16)
    return pl.pallas_call(
        product_kernel,
        in_specs=[SMEM] + [VMEM] * (len(feats) + 2),
        out_specs=[ANY] * (RING + 1),
        out_shape=[whole, whole, half, half, whole],
        scratch_shapes=[
            pltpu.VMEM((RING, *shape), jnp.bfloat16),
            pltpu.SemaphoreType.DMA((RING + 1,)),
        ],
        compiler_params=PARAMS,
        cost_estimate=pl.CostEstimate(
            flops=2 * len(feats) * rows * depth * both,
            bytes_accessed=2 * len(feats) * rows * depth,
            transcendentals=0,
        ),
    )(chip, *feats, grads, part)


def passed_kernel(after_ref, before_ref, upper_ref, lower_ref, to_after_ref, to_before_ref):
    half = upper_ref.shape[0]

    def added(block, piece):
        return (block.astype(jnp.float32) + piece.astype(jnp.float32)).astype(jnp.bfloat16)

    to_after_ref[:half] = added(after_ref[:half], upper_ref[...])
    to_after_ref[half:] = after_ref[half:]
    to_before_ref[:half] = before_ref[:half]
    to_before_ref[half:] = added(before_ref[half:], lower_ref[...])


def passed(after, before, upper, lower):
    return pl.pallas_call(
        passed_kernel,
        in_specs=[VMEM] * 4,
        out_specs=[VMEM] * 2,
        out_shape=[jax.ShapeDtypeStruct(after.shape, after.dtype)] * 2,
        compiler_params=PARAMS,
        cost_estimate=pl.CostEstimate(
            flops=after.size, bytes_accessed=10 * after.size, transcendentals=0
        ),
    )(after, before, upper, lower)


def attend_kernel(heads, index, ratio_ref, q_ref, cot_ref, kv_ref, away_ref, gain_ref, *refs):
    context_ref, d_query_ref, d_kv_ref, d_key_sum, d_value_sum = refs[-5:]
    step = pl.program_id(0)
    head_dim = gain_ref.shape[1]
    scale = head_dim ** (-0.5)
    count = index[1]
    ratio = ratio_ref[0]
    gain = gain_ref[...]
    key_value = jnp.where(index[2] != 0, away_ref[...], kv_ref[...])
    keys = key_value[:, :head_dim]
    vals = key_value[:, head_dim:]

    def stacked(ref):
        parts = [ref[0, :, h * head_dim : (h + 1) * head_dim] for h in range(heads)]
        return jnp.concatenate(parts, axis=0).astype(jnp.float32)

    def unstacked(ref, rows):
        text = rows.shape[0] // heads
        for h in range(heads):
            part = rows[h * text : (h + 1) * text]
            ref[0, :, h * head_dim : (h + 1) * head_dim] = part.astype(ref.dtype)

    @pl.when(step == 0)
    def _():
        d_key_sum[...] = jnp.zeros_like(d_key_sum)
        d_value_sum[...] = jnp.zeros_like(d_value_sum)

    q_raw = stacked(q_ref)
    q_factor = rms_factor(q_raw)
    q_norm = (q_raw * q_factor * gain).astype(jnp.bfloat16)
    raw = matmul(q_norm, keys, ((1,), (1,))) * scale
    place = lax.broadcasted_iota(jnp.int32, raw.shape, 1)
    expo = jnp.where(place < count * TILE, jnp.exp(raw), 0.0)
    total = jnp.sum(expo, axis=1, keepdims=True) + (count == 0).astype(jnp.float32)
    inverse = 1.0 / total
    weights_b = expo.astype(jnp.bfloat16)
    attended = matmul(weights_b, vals, ((1,), (0,))) * inverse
    unstacked(context_ref, ratio * attended)
    d_att = ratio * stacked(cot_ref)
    d_att_b = d_att.astype(jnp.bfloat16)
    scaled_b = (d_att * inverse).astype(jnp.bfloat16)
    delta = jnp.sum(d_att * attended, axis=1, keepdims=True)
    d_prob = matmul(d_att_b, vals, ((1,), (1,)))
    d_score = (expo * inverse * (d_prob - delta)).astype(jnp.bfloat16)
    d_qn = scale * matmul(d_score, keys, ((1,), (0,)))
    unstacked(d_query_ref, norm_back(q_raw, q_factor, gain, d_qn))
    d_key_sum[...] += matmul(d_score, q_norm, ((0,), (0,)))
    d_value_sum[...] += matmul(weights_b, scaled_b, ((0,), (0,)))

    @pl.when(step == pl.num_programs(0) - 1)
    def _():
        d_kv_ref[:, :head_dim] = (scale * d_key_sum[...]).astype(d_kv_ref.dtype)
        d_kv_ref[:, head_dim:] = d_value_sum[...].astype(d_kv_ref.dtype)


def attend(index, ratio, query, cot, key_value, away, gain, earlier, heads=2):
    rows, both = key_value.shape
    head_dim = both // 2
    text = query.shape[1]
    width = heads * head_dim
    block = pl.BlockSpec((1, text, width), lambda h, index: (index[0], 0, h))
    whole = lambda shape: pl.BlockSpec(shape, lambda h, index: (0, 0))
    in_specs = [
        pl.BlockSpec(memory_space=pltpu.SMEM),
        block,
        block,
        whole((rows, both)),
        whole((rows, both)),
        whole((1, head_dim)),
    ]
    aliases = {}
    if earlier:
        in_specs += [pl.BlockSpec(memory_space=pl.ANY)] * 2
        aliases = {7: 0, 8: 1}
    steps = query.shape[2] // width
    return pl.pallas_call(
        functools.partial(attend_kernel, heads),
        grid_spec=pltpu.PrefetchScalarGridSpec(
            num_scalar_prefetch=1,
            grid=(steps,),
            in_specs=in_specs,
            out_specs=[block, block, whole((rows, both))],
            scratch_shapes=[pltpu.VMEM((rows, head_dim), jnp.float32)] * 2,
        ),
        out_shape=[
            jax.ShapeDtypeStruct(query.shape, jnp.bfloat16),
            jax.ShapeDtypeStruct(query.shape, jnp.bfloat16),
            jax.ShapeDtypeStruct((rows, both), jnp.bfloat16),
        ],
        input_output_aliases=aliases,
        compiler_params=pltpu.CompilerParams(
            vmem_limit_bytes=24 * 1024 * 1024
        ),
        cost_estimate=pl.CostEstimate(
            flops=14 * steps * heads * text * rows * head_dim,
            bytes_accessed=8 * text * steps * width + 6 * rows * head_dim,
            transcendentals=steps * heads * text * rows,
        ),
    )(
        index,
        ratio,
        query,
        cot,
        key_value,
        away,
        gain[None, :],
        *earlier,
    )


def per_device(
    query,
    image,
    tiles,
    image_slot,
    key_weight_matrix,
    value_weight_matrix,
    query_gain,
    key_gain,
    gate,
    cotangent,
):
    ratio = jnp.tanh(gate)
    near_index, far_index, chip, far_own, near_own, shard = route(
        tiles, image_slot, image, key_weight_matrix, value_weight_matrix
    )

    def opposite(after, before):
        half = after.shape[0] // 2
        return along_x(after[:half], 1), along_x(before[half:], 3)

    far_x = [along_x(far_own, 1), along_x(far_own, 3)]
    far_other = other_core(far_own)
    shard, far_other = lax.optimization_barrier((shard, far_other))
    pieces = gathered(jnp.concatenate(gathered(shard, inner), axis=0), outer)
    far_halves = opposite(*far_x)
    near_own, *far_halves = lax.optimization_barrier((near_own, *far_halves))
    near_x = [along_x(near_own, 1), along_x(near_own, 3)]
    weights = assemble(chip, pieces)
    weights, *far_blocks = lax.optimization_barrier((weights, *far_x, *far_halves))

    def both_cores(own, other, after, before, *halves):
        feats = [own, other]
        for block in (after, jnp.concatenate(halves, axis=0), before):
            feats += [block, other_core(block)]
        return feats

    def project(feats):
        depth = feats[0].shape[1]
        total = None
        for o in (0, 1, 3, 2):
            for k in (2 * o, 2 * o + 1):
                part = matmul(feats[k], weights[k * depth : (k + 1) * depth], ((1,), (0,)))
                total = part if total is None else total + part
        return total

    shared = (ratio, query, cotangent)
    far_feats = both_cores(far_own, far_other, *far_blocks)
    far_total = project(far_feats)
    far_key_value = finish(far_total, key_gain)
    _, *near_x = lax.optimization_barrier((far_key_value, *near_x))
    near_halves = opposite(*near_x)
    away = along_z(far_key_value, RING // 2)
    *earlier, far_grad = attend(far_index, *shared, far_key_value, away, query_gain, ())
    back = along_z(far_grad, RING // 2)
    far_rows = turn(far_index, far_total, far_grad, back, key_gain)
    part = first_part(far_feats, far_rows)

    near_feats = both_cores(near_own, other_core(near_own), *near_x, *near_halves)
    near_total = project(near_feats)
    near_key_value = finish(near_total, key_gain)
    context, d_query, near_grad = attend(
        near_index, *shared, near_key_value, near_key_value, query_gain, earlier
    )
    near_rows = turn(near_index, near_total, near_grad, near_grad, key_gain)

    blocks = product(chip, near_feats, near_rows, part)
    own, after, upper, lower, before = blocks
    after, before = passed(after, before, outer(upper, 1), outer(lower, 3))
    total = summed([own, outer(after, 1), outer(before, 3)])
    count = total.shape[0] // RING
    parts = [total[d * count : (d + 1) * count] for d in range(RING)]
    sent = [None] + [part.astype(jnp.bfloat16) for part in parts[1:]]
    share = summed([parts[0], *scattered(sent, inner)])
    head_dim = query_gain.shape[0]
    return (context, d_query, share[:, :head_dim], share[:, head_dim:])


def solution(mesh):
    placed = (
        P("dp", None, "tensor"),
        P("dp", None, "tensor"),
        P(),
        P(),
        P("dp", "tensor"),
        P("dp", "tensor"),
        P(),
        P(),
        P(),
        P("dp", None, "tensor"),
    )
    return jax.shard_map(
        per_device,
        mesh=mesh,
        in_specs=placed,
        out_specs=(
            P("dp", None, "tensor"),
            P("dp", None, "tensor"),
            P("dp", "tensor"),
            P("dp", "tensor"),
        ),
        check_vma=False,
    )
```

```python
import functools

import jax
import jax.numpy as jnp
from jax import lax
from jax.experimental import pallas as pl
from jax.experimental.pallas import tpu as pltpu
from jax.sharding import PartitionSpec as P

TILE = 128
RING = 4
EPS = 1e-06


def along_z(x, step):
    pairs = [(z * RING + y, (z + step) % RING * RING + y) for z in range(RING) for y in range(RING)]
    return lax.ppermute(x, "dp", pairs)


def by_core(x, step, z_core):
    pairs = []
    for z in range(RING):
        for y in range(RING):
            for i in range(RING):
                for c in range(2):
                    to_z, to_y = (z + step, y) if c == z_core else (z, y + step)
                    source = (z * RING + y) * 2 * RING + i * 2 + c
                    target = (to_z % RING * RING + to_y % RING) * 2 * RING + i * 2 + c
                    pairs.append((source, target))
    return lax.ppermute(x, ("dp", "tensor"), pairs)


def inner(x, step):
    return by_core(x, step, 0)


def outer(x, step):
    return by_core(x, step, 1)


def along_x(x, step):
    pairs = [(i * 2 + c, (i + step) % RING * 2 + c) for i in range(RING) for c in range(2)]
    return lax.ppermute(x, "tensor", pairs)


def other_core(x):
    return lax.ppermute(x, "tensor", [(i, i ^ 1) for i in range(2 * RING)])


def gathered(block, move):
    far, after, before = (move(block, step) for step in (2, 1, 3))
    return [block, after, far, before]


def scattered(parts, move):
    return [move(parts[step], step) for step in (2, 1, 3)]


def summed(blocks):
    total = blocks[0].astype(jnp.float32)
    for block in blocks[1:]:
        total = total + block.astype(jnp.float32)
    return total


def rms_factor(values):
    return lax.rsqrt(jnp.mean(values * values, axis=-1, keepdims=True) + EPS)


def norm_back(values, norm_multiplier, gain, grad):
    weighted = grad * gain
    inner = jnp.sum(weighted * values, axis=-1, keepdims=True)
    return (
        norm_multiplier * weighted
        - values * (norm_multiplier * norm_multiplier * norm_multiplier) * inner / values.shape[-1]
    )


def matmul(a, b, contract):
    return lax.dot_general(a, b, (contract, ((), ())), preferred_element_type=jnp.float32)


VMEM = pl.BlockSpec(memory_space=pltpu.VMEM)
SMEM = pl.BlockSpec(memory_space=pltpu.SMEM)
ANY = pl.BlockSpec(memory_space=pl.ANY)
HBM = pl.BlockSpec(memory_space=pltpu.HBM)
PARAMS = pltpu.CompilerParams(vmem_limit_bytes=16 * 1024 * 1024)


NEAR, FAR, CHIP = 0, 3, 6


def route_kernel(tiles, slots, image_ref, numbers, far_ref, near_ref, sems):
    rank, place = lax.axis_index("dp"), lax.axis_index("tensor")
    first = 2 * rank
    homes = (slots[first], slots[first + 1])
    away = [
        jnp.logical_and(homes[0] != first + i, homes[1] != first + i) for i in range(2)
    ]
    swaps = jnp.logical_or(away[0], away[1])
    far_slot = jnp.where(away[1], 1, 0)
    copies = []
    for i, (slot, target) in enumerate(((far_slot, far_ref), (1 - far_slot, near_ref))):
        copies.append(pltpu.make_async_copy(image_ref.at[slot], target, sems.at[i]))
        copies[i].start()
    of_slot = jnp.where(homes[1] == first + far_slot, 1, 0)
    far_own = jnp.where(swaps, jnp.where(homes[1] >> 1 != rank, 1, 0), of_slot)
    numbers[NEAR] = 1 - far_own
    numbers[NEAR + 1] = tiles[first + 1 - far_own]
    numbers[NEAR + 2] = 0
    numbers[FAR] = far_own
    numbers[FAR + 1] = tiles[first + far_own]
    numbers[FAR + 2] = jnp.where(swaps, 1, 0)
    numbers[CHIP] = rank // RING
    numbers[CHIP + 1] = rank % RING
    numbers[CHIP + 2] = place // 2
    numbers[CHIP + 3] = place % 2
    for copy in copies:
        copy.wait()


def route(tiles, image_slot, image):
    rows = jax.ShapeDtypeStruct(image.shape[1:], image.dtype)
    return pl.pallas_call(
        route_kernel,
        in_specs=[SMEM, SMEM, HBM],
        out_specs=[SMEM, VMEM, VMEM],
        out_shape=[jax.ShapeDtypeStruct((CHIP + 4,), jnp.int32), rows, rows],
        scratch_shapes=[pltpu.SemaphoreType.DMA((2,))],
        compiler_params=pltpu.CompilerParams(vmem_limit_bytes=60 * 1024 * 1024),
        cost_estimate=pl.CostEstimate(flops=0, bytes_accessed=4 * image.size, transcendentals=0),
    )(tiles, image_slot, image)


def lay_kernel(numbers, key_ref, value_ref, out_ref, sems):
    head_dim = key_ref.shape[1]
    copies = []
    for i, source in enumerate((key_ref, value_ref)):
        target = out_ref.at[:, pl.ds(i * head_dim, head_dim)]
        copies.append(pltpu.make_async_copy(source, target, sems.at[i]))
        copies[i].start()
    for copy in copies:
        copy.wait()


def lay(numbers, key_weights, value_weights):
    count, head_dim = key_weights.shape
    return pl.pallas_call(
        lay_kernel,
        in_specs=[SMEM, ANY, ANY],
        out_specs=VMEM,
        out_shape=jax.ShapeDtypeStruct((count, 2 * head_dim), key_weights.dtype),
        scratch_shapes=[pltpu.SemaphoreType.DMA((2,))],
        compiler_params=PARAMS,
        cost_estimate=pl.CostEstimate(
            flops=0, bytes_accessed=8 * count * head_dim, transcendentals=0
        ),
    )(numbers, key_weights, value_weights)


def assemble_kernel(chip, *refs):
    pieces, out_ref, sems = refs[:RING], refs[RING], refs[RING + 1]
    rows, both = pieces[0].shape
    count = rows // RING
    z, y, x, core = (chip[CHIP + i] for i in range(4))
    copies = []
    for b in range(RING):
        for a in range(RING):
            from_z = (z - jnp.where(core == 0, a, b) + RING) % RING
            from_y = (y - jnp.where(core == 0, b, a) + RING) % RING
            o = (x - from_z + RING) % RING
            start = ((o * 2 + ((from_y >> 1) ^ core)) * 2 + from_y % 2) * count
            target = out_ref.at[pl.ds(pl.multiple_of(start, count), count)]
            source = pieces[b].at[pl.ds(a * count, count)]
            copies.append(pltpu.make_async_copy(source, target, sems.at[b, a]))
    for copy in copies:
        copy.start()
    for copy in copies:
        copy.wait()


def assemble(chip, pieces):
    rows, both = pieces[0].shape
    return pl.pallas_call(
        assemble_kernel,
        in_specs=[SMEM] + [ANY] * RING,
        out_specs=VMEM,
        out_shape=jax.ShapeDtypeStruct((RING * rows, both), pieces[0].dtype),
        scratch_shapes=[pltpu.SemaphoreType.DMA((RING, RING))],
        compiler_params=PARAMS,
        cost_estimate=pl.CostEstimate(
            flops=0, bytes_accessed=4 * RING * rows * both, transcendentals=0
        ),
    )(chip, *pieces)


def finish_kernel(total_ref, gain_ref, key_value_ref):
    head_dim = gain_ref.shape[1]
    raw = total_ref[:, :head_dim]
    keys = (raw * rms_factor(raw) * gain_ref[...]).astype(jnp.bfloat16)
    key_value_ref[:, :head_dim] = keys
    key_value_ref[:, head_dim:] = total_ref[:, head_dim:].astype(jnp.bfloat16)


def finish(total, gain):
    return pl.pallas_call(
        finish_kernel,
        in_specs=[VMEM] * 2,
        out_specs=VMEM,
        out_shape=jax.ShapeDtypeStruct(total.shape, jnp.bfloat16),
        compiler_params=PARAMS,
        cost_estimate=pl.CostEstimate(
            flops=3 * total.size, bytes_accessed=6 * total.size, transcendentals=total.shape[0]
        ),
    )(total, gain[None, :])


def turn_kernel(base, numbers, total_ref, grad_ref, other_ref, gain_ref, out_ref):
    head_dim = gain_ref.shape[1]
    grad = jnp.where(numbers[base + 2] != 0, other_ref[...], grad_ref[...])
    raw = total_ref[:, :head_dim]
    d_raw = norm_back(raw, rms_factor(raw), gain_ref[...], grad[:, :head_dim].astype(jnp.float32))
    out_ref[:, :head_dim] = d_raw.astype(jnp.bfloat16)
    out_ref[:, head_dim:] = grad[:, head_dim:]


def turn(base, numbers, total, grad, other, gain):
    return pl.pallas_call(
        functools.partial(turn_kernel, base),
        in_specs=[SMEM] + [VMEM] * 4,
        out_specs=VMEM,
        out_shape=jax.ShapeDtypeStruct(grad.shape, jnp.bfloat16),
        compiler_params=PARAMS,
        cost_estimate=pl.CostEstimate(
            flops=6 * grad.size, bytes_accessed=8 * grad.size, transcendentals=grad.shape[0]
        ),
    )(numbers, total, grad, other, gain[None, :])


def first_part_kernel(*refs):
    sources, (grads_ref, out_ref) = refs[:-2], refs[-2:]
    depth = sources[0].shape[1]
    for k, source in enumerate(sources):
        out_ref[k * depth : (k + 1) * depth] = matmul(source[...], grads_ref[...], ((0,), (0,)))


def first_part(feats, grads):
    rows, depth = feats[0].shape
    both = grads.shape[1]
    return pl.pallas_call(
        first_part_kernel,
        in_specs=[VMEM] * (len(feats) + 1),
        out_specs=VMEM,
        out_shape=jax.ShapeDtypeStruct((len(feats) * depth, both), jnp.float32),
        compiler_params=PARAMS,
        cost_estimate=pl.CostEstimate(
            flops=2 * len(feats) * rows * depth * both,
            bytes_accessed=2 * len(feats) * rows * depth,
            transcendentals=0,
        ),
    )(*feats, grads)


def product_kernel(chip, *refs):
    sources, (grads_ref, part_ref), refs = refs[: 2 * RING], refs[2 * RING : 2 * RING + 2], refs[2 * RING + 2 :]
    outs, (held, sems) = refs[: 2 * RING + 2], refs[2 * RING + 2 :]
    sems_of = [sems.at[i] for i in range(len(outs))]
    depth = sources[0].shape[1]
    count = depth // 2
    z, y, x, core = (chip[CHIP + i] for i in range(4))
    for k, source in enumerate(sources):
        total = matmul(source[...], grads_ref[...], ((0,), (0,)))
        total = (total + part_ref[k * depth : (k + 1) * depth]).astype(held.dtype)
        by_z = (x - k // 2 - z + 2 * RING) % RING
        for h in range(2):
            by_y = (2 * (k % 2 ^ core) + h - y + RING) % RING
            outer_by = jnp.where(core == 0, by_y, by_z)
            inner_by = jnp.where(core == 0, by_z, by_y)
            start = pl.multiple_of(inner_by * count, count)
            held[outer_by, pl.ds(start, count)] = total[h * count : (h + 1) * count]
    half, head_dim = held.shape[1] // 2, held.shape[2] // 2
    parts = []
    for i in range(2):
        columns = pl.ds(i * head_dim, head_dim)
        parts += [held.at[2, pl.ds(0, half), columns], held.at[2, pl.ds(half, half), columns]]
        parts += [held.at[k, :, columns] for k in (1, 3, 0)]
    copies = [pltpu.make_async_copy(part, out, sem) for part, out, sem in zip(parts, outs, sems_of)]
    for copy in copies:
        copy.start()
    for copy in copies:
        copy.wait()


def product(chip, feats, grads, part):
    rows, depth = feats[0].shape
    both = grads.shape[1]
    shape = (RING * depth // 2, both)
    whole = jax.ShapeDtypeStruct((shape[0], both // 2), jnp.bfloat16)
    half = jax.ShapeDtypeStruct((shape[0] // 2, both // 2), jnp.bfloat16)
    return pl.pallas_call(
        product_kernel,
        in_specs=[SMEM] + [VMEM] * (len(feats) + 2),
        out_specs=[ANY] * (2 * RING + 2),
        out_shape=[half, half, whole, whole, whole] * 2,
        scratch_shapes=[
            pltpu.VMEM((RING, *shape), jnp.bfloat16),
            pltpu.SemaphoreType.DMA((2 * RING + 2,)),
        ],
        compiler_params=PARAMS,
        cost_estimate=pl.CostEstimate(
            flops=2 * len(feats) * rows * depth * both,
            bytes_accessed=2 * len(feats) * rows * depth,
            transcendentals=0,
        ),
    )(chip, *feats, grads, part)


def passed_kernel(after_ref, before_ref, upper_ref, lower_ref, to_after_ref, to_before_ref):
    half = upper_ref.shape[0]

    def added(block, piece):
        return (block.astype(jnp.float32) + piece.astype(jnp.float32)).astype(jnp.bfloat16)

    to_after_ref[:half] = added(after_ref[:half], upper_ref[...])
    to_after_ref[half:] = after_ref[half:]
    to_before_ref[:half] = before_ref[:half]
    to_before_ref[half:] = added(before_ref[half:], lower_ref[...])


def passed(after, before, upper, lower):
    return pl.pallas_call(
        passed_kernel,
        in_specs=[VMEM] * 4,
        out_specs=[VMEM] * 2,
        out_shape=[jax.ShapeDtypeStruct(after.shape, after.dtype)] * 2,
        compiler_params=PARAMS,
        cost_estimate=pl.CostEstimate(
            flops=after.size, bytes_accessed=10 * after.size, transcendentals=0
        ),
    )(after, before, upper, lower)


def attend_kernel(heads, base, index, ratio_ref, q_ref, cot_ref, kv_ref, away_ref, gain_ref, *refs):
    context_ref, d_query_ref, d_kv_ref, d_key_sum, d_value_sum = refs[-5:]
    step = pl.program_id(0)
    head_dim = gain_ref.shape[1]
    scale = head_dim ** (-0.5)
    count = index[base + 1]
    ratio = ratio_ref[0]
    gain = gain_ref[...]
    key_value = jnp.where(index[base + 2] != 0, away_ref[...], kv_ref[...])
    keys = key_value[:, :head_dim]
    vals = key_value[:, head_dim:]

    def stacked(ref):
        parts = [ref[0, :, h * head_dim : (h + 1) * head_dim] for h in range(heads)]
        return jnp.concatenate(parts, axis=0).astype(jnp.float32)

    def unstacked(ref, rows):
        text = rows.shape[0] // heads
        for h in range(heads):
            part = rows[h * text : (h + 1) * text]
            ref[0, :, h * head_dim : (h + 1) * head_dim] = part.astype(ref.dtype)

    @pl.when(step == 0)
    def _():
        d_key_sum[...] = jnp.zeros_like(d_key_sum)
        d_value_sum[...] = jnp.zeros_like(d_value_sum)

    q_raw = stacked(q_ref)
    q_factor = rms_factor(q_raw)
    q_norm = (q_raw * q_factor * gain).astype(jnp.bfloat16)
    raw = matmul(q_norm, keys, ((1,), (1,))) * scale
    place = lax.broadcasted_iota(jnp.int32, raw.shape, 1)
    expo = jnp.where(place < count * TILE, jnp.exp(raw), 0.0)
    total = jnp.sum(expo, axis=1, keepdims=True) + (count == 0).astype(jnp.float32)
    inverse = 1.0 / total
    weights_b = expo.astype(jnp.bfloat16)
    attended = matmul(weights_b, vals, ((1,), (0,))) * inverse
    unstacked(context_ref, ratio * attended)
    d_att = ratio * stacked(cot_ref)
    d_att_b = d_att.astype(jnp.bfloat16)
    scaled_b = (d_att * inverse).astype(jnp.bfloat16)
    delta = jnp.sum(d_att * attended, axis=1, keepdims=True)
    d_prob = matmul(d_att_b, vals, ((1,), (1,)))
    d_score = (expo * inverse * (d_prob - delta)).astype(jnp.bfloat16)
    d_qn = scale * matmul(d_score, keys, ((1,), (0,)))
    unstacked(d_query_ref, norm_back(q_raw, q_factor, gain, d_qn))
    d_key_sum[...] += matmul(d_score, q_norm, ((0,), (0,)))
    d_value_sum[...] += matmul(weights_b, scaled_b, ((0,), (0,)))

    @pl.when(step == pl.num_programs(0) - 1)
    def _():
        d_kv_ref[:, :head_dim] = (scale * d_key_sum[...]).astype(d_kv_ref.dtype)
        d_kv_ref[:, head_dim:] = d_value_sum[...].astype(d_kv_ref.dtype)


def attend(base, index, ratio, query, cot, key_value, away, gain, earlier, heads=2):
    rows, both = key_value.shape
    head_dim = both // 2
    text = query.shape[1]
    width = heads * head_dim
    block = pl.BlockSpec((1, text, width), lambda h, index: (index[base], 0, h))
    whole = lambda shape: pl.BlockSpec(shape, lambda h, index: (0, 0))
    in_specs = [
        pl.BlockSpec(memory_space=pltpu.SMEM),
        block,
        block,
        whole((rows, both)),
        whole((rows, both)),
        whole((1, head_dim)),
    ]
    aliases = {}
    if earlier:
        in_specs += [pl.BlockSpec(memory_space=pl.ANY)] * 2
        aliases = {7: 0, 8: 1}
    steps = query.shape[2] // width
    return pl.pallas_call(
        functools.partial(attend_kernel, heads, base),
        grid_spec=pltpu.PrefetchScalarGridSpec(
            num_scalar_prefetch=1,
            grid=(steps,),
            in_specs=in_specs,
            out_specs=[block, block, whole((rows, both))],
            scratch_shapes=[pltpu.VMEM((rows, head_dim), jnp.float32)] * 2,
        ),
        out_shape=[
            jax.ShapeDtypeStruct(query.shape, jnp.bfloat16),
            jax.ShapeDtypeStruct(query.shape, jnp.bfloat16),
            jax.ShapeDtypeStruct((rows, both), jnp.bfloat16),
        ],
        input_output_aliases=aliases,
        compiler_params=pltpu.CompilerParams(
            vmem_limit_bytes=24 * 1024 * 1024
        ),
        cost_estimate=pl.CostEstimate(
            flops=14 * steps * heads * text * rows * head_dim,
            bytes_accessed=8 * text * steps * width + 6 * rows * head_dim,
            transcendentals=steps * heads * text * rows,
        ),
    )(
        index,
        ratio,
        query,
        cot,
        key_value,
        away,
        gain[None, :],
        *earlier,
    )


def per_device(
    query,
    image,
    tiles,
    image_slot,
    key_weight_matrix,
    value_weight_matrix,
    query_gain,
    key_gain,
    gate,
    cotangent,
):
    ratio = jnp.tanh(gate)
    numbers, far_own, near_own = route(tiles, image_slot, image)

    def opposite(after, before):
        half = after.shape[0] // 2
        return along_x(after[:half], 1), along_x(before[half:], 3)

    far_x = [along_x(far_own, 1), along_x(far_own, 3)]
    shard = lay(numbers, key_weight_matrix, value_weight_matrix)
    pieces = gathered(jnp.concatenate(gathered(shard, inner), axis=0), outer)
    far_halves = opposite(*far_x)
    near_own, *far_halves = lax.optimization_barrier((near_own, *far_halves))
    near_x = [along_x(near_own, 1), along_x(near_own, 3)]
    weights = assemble(numbers, pieces)
    weights, *far_blocks = lax.optimization_barrier((weights, *far_x, *far_halves))

    def other_cores(*blocks):
        return [other_core(block) for block in blocks]

    def paired(own, other, after, before, opposite, after_other, before_other, opposite_other):
        return [own, other, after, after_other, opposite, opposite_other, before, before_other]

    def project(feats):
        depth = feats[0].shape[1]
        total = None
        for o in (0, 1, 3, 2):
            for k in (2 * o, 2 * o + 1):
                part = matmul(feats[k], weights[k * depth : (k + 1) * depth], ((1,), (0,)))
                total = part if total is None else total + part
        return total

    shared = (numbers, ratio, query, cotangent)
    after, before, *halves = far_blocks
    blocks = [after, before, jnp.concatenate(halves, axis=0)]
    far_feats = paired(far_own, other_core(far_own), *blocks, *other_cores(*blocks))
    far_total = project(far_feats)
    far_key_value = finish(far_total, key_gain)
    away = along_z(far_key_value, RING // 2)
    _, *near_late = lax.optimization_barrier((away, *near_x))
    near_halves = opposite(*near_late)
    near_others = other_cores(*near_late)
    away, _ = lax.optimization_barrier((away, near_others[0]))
    *earlier, far_grad = attend(FAR, *shared, far_key_value, away, query_gain, ())
    back = along_z(far_grad, RING // 2)
    far_rows = turn(FAR, numbers, far_total, far_grad, back, key_gain)
    part = first_part(far_feats, far_rows)

    blocks = [*near_x, jnp.concatenate(near_halves, axis=0)]
    near_others.append(other_core(blocks[2]))
    near_feats = paired(near_own, other_core(near_own), *blocks, *near_others)
    near_total = project(near_feats)
    near_key_value = finish(near_total, key_gain)
    context, d_query, near_grad = attend(
        NEAR, *shared, near_key_value, near_key_value, query_gain, earlier
    )
    near_rows = turn(NEAR, numbers, near_total, near_grad, near_grad, key_gain)

    blocks = product(numbers, near_feats, near_rows, part)
    chains = [blocks[: RING + 1], blocks[RING + 1 :]]
    chains = [(chain, outer(chain[0], 1), outer(chain[1], 3)) for chain in chains]
    halves = lax.optimization_barrier(tuple(half for chain in chains for half in chain[1:]))
    chains = [
        (chain[0], *passed(chain[0][2], chain[0][3], *halves[2 * i : 2 * i + 2]))
        for i, chain in enumerate(chains)
    ]
    totals = [
        summed([chain[4], outer(after, 1), outer(before, 3)]) for chain, after, before in chains
    ]
    shares = []
    for total in totals:
        count = total.shape[0] // RING
        parts = [total[d * count : (d + 1) * count] for d in range(RING)]
        sent = [None] + [part.astype(jnp.bfloat16) for part in parts[1:]]
        shares.append(summed([parts[0], *scattered(sent, inner)]))
    return (context, d_query, *shares)


def solution(mesh):
    placed = (
        P("dp", None, "tensor"),
        P("dp", None, "tensor"),
        P(),
        P(),
        P("dp", "tensor"),
        P("dp", "tensor"),
        P(),
        P(),
        P(),
        P("dp", None, "tensor"),
    )
    return jax.shard_map(
        per_device,
        mesh=mesh,
        in_specs=placed,
        out_specs=(
            P("dp", None, "tensor"),
            P("dp", None, "tensor"),
            P("dp", "tensor"),
            P("dp", "tensor"),
        ),
        check_vma=False,
    )
```

```python
import functools

import jax
import jax.numpy as jnp
from jax import lax
from jax.experimental import pallas as pl
from jax.experimental.pallas import tpu as pltpu
from jax.sharding import PartitionSpec as P

TILE = 128
RING = 4
EPS = 1e-06


def along_z(x, step):
    pairs = [(z * RING + y, (z + step) % RING * RING + y) for z in range(RING) for y in range(RING)]
    return lax.ppermute(x, "dp", pairs)


def by_core(x, step, z_core):
    pairs = []
    for z in range(RING):
        for y in range(RING):
            for i in range(RING):
                for c in range(2):
                    to_z, to_y = (z + step, y) if c == z_core else (z, y + step)
                    source = (z * RING + y) * 2 * RING + i * 2 + c
                    target = (to_z % RING * RING + to_y % RING) * 2 * RING + i * 2 + c
                    pairs.append((source, target))
    return lax.ppermute(x, ("dp", "tensor"), pairs)


def inner(x, step):
    return by_core(x, step, 0)


def outer(x, step):
    return by_core(x, step, 1)


def along_x(x, step):
    pairs = [(i * 2 + c, (i + step) % RING * 2 + c) for i in range(RING) for c in range(2)]
    return lax.ppermute(x, "tensor", pairs)


def other_core(x):
    return lax.ppermute(x, "tensor", [(i, i ^ 1) for i in range(2 * RING)])


def axis_groups(z_core):
    groups = []
    for i in range(2 * RING):
        for fixed in range(RING):
            along = [(k, fixed) if i % 2 == z_core else (fixed, k) for k in range(RING)]
            groups.append([(z * RING + y) * 2 * RING + i for z, y in along])
    return groups


def exchanged(blocks, z_core):
    return lax.all_to_all(
        blocks, ("dp", "tensor"), 0, 0, tiled=True, axis_index_groups=axis_groups(z_core)
    )


def gathered(block, move):
    far, after, before = (move(block, step) for step in (2, 1, 3))
    return [block, after, far, before]


def summed(blocks):
    total = blocks[0].astype(jnp.float32)
    for block in blocks[1:]:
        total = total + block.astype(jnp.float32)
    return total


def rms_factor(values):
    return lax.rsqrt(jnp.mean(values * values, axis=-1, keepdims=True) + EPS)


def norm_back(values, norm_multiplier, gain, grad):
    weighted = grad * gain
    inner = jnp.sum(weighted * values, axis=-1, keepdims=True)
    return (
        norm_multiplier * weighted
        - values * (norm_multiplier * norm_multiplier * norm_multiplier) * inner / values.shape[-1]
    )


def matmul(a, b, contract):
    return lax.dot_general(a, b, (contract, ((), ())), preferred_element_type=jnp.float32)


VMEM = pl.BlockSpec(memory_space=pltpu.VMEM)
SMEM = pl.BlockSpec(memory_space=pltpu.SMEM)
ANY = pl.BlockSpec(memory_space=pl.ANY)
HBM = pl.BlockSpec(memory_space=pltpu.HBM)
PARAMS = pltpu.CompilerParams(vmem_limit_bytes=16 * 1024 * 1024)


NEAR, FAR, CHIP = 0, 3, 6


def route_kernel(tiles, slots, image_ref, numbers, far_ref, near_ref, sems):
    rank, place = lax.axis_index("dp"), lax.axis_index("tensor")
    first = 2 * rank
    homes = (slots[first], slots[first + 1])
    away = [
        jnp.logical_and(homes[0] != first + i, homes[1] != first + i) for i in range(2)
    ]
    swaps = jnp.logical_or(away[0], away[1])
    far_slot = jnp.where(away[1], 1, 0)
    copies = []
    for i, (slot, target) in enumerate(((far_slot, far_ref), (1 - far_slot, near_ref))):
        copies.append(pltpu.make_async_copy(image_ref.at[slot], target, sems.at[i]))
        copies[i].start()
    of_slot = jnp.where(homes[1] == first + far_slot, 1, 0)
    far_own = jnp.where(swaps, jnp.where(homes[1] >> 1 != rank, 1, 0), of_slot)
    numbers[NEAR] = 1 - far_own
    numbers[NEAR + 1] = tiles[first + 1 - far_own]
    numbers[NEAR + 2] = 0
    numbers[FAR] = far_own
    numbers[FAR + 1] = tiles[first + far_own]
    numbers[FAR + 2] = jnp.where(swaps, 1, 0)
    numbers[CHIP] = rank // RING
    numbers[CHIP + 1] = rank % RING
    numbers[CHIP + 2] = place // 2
    numbers[CHIP + 3] = place % 2
    for copy in copies:
        copy.wait()


def route(tiles, image_slot, image):
    rows = jax.ShapeDtypeStruct(image.shape[1:], image.dtype)
    return pl.pallas_call(
        route_kernel,
        in_specs=[SMEM, SMEM, HBM],
        out_specs=[SMEM, VMEM, VMEM],
        out_shape=[jax.ShapeDtypeStruct((CHIP + 4,), jnp.int32), rows, rows],
        scratch_shapes=[pltpu.SemaphoreType.DMA((2,))],
        compiler_params=pltpu.CompilerParams(vmem_limit_bytes=60 * 1024 * 1024),
        cost_estimate=pl.CostEstimate(flops=0, bytes_accessed=4 * image.size, transcendentals=0),
    )(tiles, image_slot, image)


def lay_kernel(numbers, key_ref, value_ref, out_ref, sems):
    head_dim = key_ref.shape[1]
    copies = []
    for i, source in enumerate((key_ref, value_ref)):
        target = out_ref.at[:, pl.ds(i * head_dim, head_dim)]
        copies.append(pltpu.make_async_copy(source, target, sems.at[i]))
        copies[i].start()
    for copy in copies:
        copy.wait()


def lay(numbers, key_weights, value_weights):
    count, head_dim = key_weights.shape
    return pl.pallas_call(
        lay_kernel,
        in_specs=[SMEM, ANY, ANY],
        out_specs=VMEM,
        out_shape=jax.ShapeDtypeStruct((count, 2 * head_dim), key_weights.dtype),
        scratch_shapes=[pltpu.SemaphoreType.DMA((2,))],
        compiler_params=PARAMS,
        cost_estimate=pl.CostEstimate(
            flops=0, bytes_accessed=8 * count * head_dim, transcendentals=0
        ),
    )(numbers, key_weights, value_weights)


def assemble_kernel(chip, *refs):
    pieces, out_ref, sems = refs[: RING + 1], refs[RING + 1], refs[RING + 2]
    rows, both = pieces[0].shape
    count = rows // RING
    z, y, x, core = (chip[CHIP + i] for i in range(4))
    copies = []
    for b in range(RING):
        for a in range(RING):
            from_z = (z - jnp.where(core == 0, a, b) + RING) % RING
            from_y = (y - jnp.where(core == 0, b, a) + RING) % RING
            o = (x - from_z + RING) % RING
            start = ((o * 2 + ((from_y >> 1) ^ core)) * 2 + from_y % 2) * count
            target = out_ref.at[pl.ds(pl.multiple_of(start, count), count)]
            if b == 2:
                source = pieces[3 + a // 2].at[pl.ds(a % 2 * count, count)]
            else:
                source = pieces[min(b, 2)].at[pl.ds(a * count, count)]
            copies.append(pltpu.make_async_copy(source, target, sems.at[b, a]))
    for copy in copies:
        copy.start()
    for copy in copies:
        copy.wait()


def assemble(chip, pieces):
    rows, both = pieces[0].shape
    return pl.pallas_call(
        assemble_kernel,
        in_specs=[SMEM] + [ANY] * (RING + 1),
        out_specs=VMEM,
        out_shape=jax.ShapeDtypeStruct((RING * rows, both), pieces[0].dtype),
        scratch_shapes=[pltpu.SemaphoreType.DMA((RING, RING))],
        compiler_params=PARAMS,
        cost_estimate=pl.CostEstimate(
            flops=0, bytes_accessed=4 * RING * rows * both, transcendentals=0
        ),
    )(chip, *pieces)


def finish_kernel(total_ref, gain_ref, key_value_ref):
    head_dim = gain_ref.shape[1]
    raw = total_ref[:, :head_dim]
    keys = (raw * rms_factor(raw) * gain_ref[...]).astype(jnp.bfloat16)
    key_value_ref[:, :head_dim] = keys
    key_value_ref[:, head_dim:] = total_ref[:, head_dim:].astype(jnp.bfloat16)


def finish(total, gain):
    return pl.pallas_call(
        finish_kernel,
        in_specs=[VMEM] * 2,
        out_specs=VMEM,
        out_shape=jax.ShapeDtypeStruct(total.shape, jnp.bfloat16),
        compiler_params=PARAMS,
        cost_estimate=pl.CostEstimate(
            flops=3 * total.size, bytes_accessed=6 * total.size, transcendentals=total.shape[0]
        ),
    )(total, gain[None, :])


def turn_kernel(base, numbers, total_ref, grad_ref, other_ref, gain_ref, out_ref):
    head_dim = gain_ref.shape[1]
    grad = jnp.where(numbers[base + 2] != 0, other_ref[...], grad_ref[...])
    raw = total_ref[:, :head_dim]
    d_raw = norm_back(raw, rms_factor(raw), gain_ref[...], grad[:, :head_dim].astype(jnp.float32))
    out_ref[:, :head_dim] = d_raw.astype(jnp.bfloat16)
    out_ref[:, head_dim:] = grad[:, head_dim:]


def turn(base, numbers, total, grad, other, gain):
    return pl.pallas_call(
        functools.partial(turn_kernel, base),
        in_specs=[SMEM] + [VMEM] * 4,
        out_specs=VMEM,
        out_shape=jax.ShapeDtypeStruct(grad.shape, jnp.bfloat16),
        compiler_params=PARAMS,
        cost_estimate=pl.CostEstimate(
            flops=6 * grad.size, bytes_accessed=8 * grad.size, transcendentals=grad.shape[0]
        ),
    )(numbers, total, grad, other, gain[None, :])


def first_part_kernel(*refs):
    sources, (grads_ref, out_ref) = refs[:-2], refs[-2:]
    depth = sources[0].shape[1]
    for k, source in enumerate(sources):
        out_ref[k * depth : (k + 1) * depth] = matmul(source[...], grads_ref[...], ((0,), (0,)))


def first_part(feats, grads):
    rows, depth = feats[0].shape
    both = grads.shape[1]
    return pl.pallas_call(
        first_part_kernel,
        in_specs=[VMEM] * (len(feats) + 1),
        out_specs=VMEM,
        out_shape=jax.ShapeDtypeStruct((len(feats) * depth, both), jnp.float32),
        compiler_params=PARAMS,
        cost_estimate=pl.CostEstimate(
            flops=2 * len(feats) * rows * depth * both,
            bytes_accessed=2 * len(feats) * rows * depth,
            transcendentals=0,
        ),
    )(*feats, grads)


def product_kernel(chip, *refs):
    sources, (grads_ref, part_ref, out_ref) = refs[:-3], refs[-3:]
    depth = sources[0].shape[1]
    count = depth // 2
    x, core = chip[CHIP + 2], chip[CHIP + 3]
    for k, source in enumerate(sources):
        total = matmul(source[...], grads_ref[...], ((0,), (0,)))
        total = (total + part_ref[k * depth : (k + 1) * depth]).astype(out_ref.dtype)
        to_z = (x - k // 2 + RING) % RING
        for h in range(2):
            to_y = 2 * (k % 2 ^ core) + h
            block = jnp.where(core == 0, to_y * RING + to_z, to_z * RING + to_y)
            start = pl.multiple_of(block * count, count)
            out_ref[pl.ds(start, count)] = total[h * count : (h + 1) * count]


def product(chip, feats, grads, part):
    rows, depth = feats[0].shape
    both = grads.shape[1]
    return pl.pallas_call(
        product_kernel,
        in_specs=[SMEM] + [VMEM] * (len(feats) + 2),
        out_specs=VMEM,
        out_shape=jax.ShapeDtypeStruct((len(feats) * depth, both), jnp.bfloat16),
        compiler_params=PARAMS,
        cost_estimate=pl.CostEstimate(
            flops=2 * len(feats) * rows * depth * both,
            bytes_accessed=2 * len(feats) * rows * depth,
            transcendentals=0,
        ),
    )(chip, *feats, grads, part)


def attend_kernel(heads, base, index, ratio_ref, q_ref, cot_ref, kv_ref, away_ref, gain_ref, *refs):
    context_ref, d_query_ref, d_kv_ref, d_key_sum, d_value_sum = refs[-5:]
    step = pl.program_id(0)
    head_dim = gain_ref.shape[1]
    scale = head_dim ** (-0.5)
    count = index[base + 1]
    ratio = ratio_ref[0]
    gain = gain_ref[...]
    key_value = jnp.where(index[base + 2] != 0, away_ref[...], kv_ref[...])
    keys = key_value[:, :head_dim]
    vals = key_value[:, head_dim:]

    def stacked(ref):
        parts = [ref[0, :, h * head_dim : (h + 1) * head_dim] for h in range(heads)]
        return jnp.concatenate(parts, axis=0).astype(jnp.float32)

    def unstacked(ref, rows):
        text = rows.shape[0] // heads
        for h in range(heads):
            part = rows[h * text : (h + 1) * text]
            ref[0, :, h * head_dim : (h + 1) * head_dim] = part.astype(ref.dtype)

    @pl.when(step == 0)
    def _():
        d_key_sum[...] = jnp.zeros_like(d_key_sum)
        d_value_sum[...] = jnp.zeros_like(d_value_sum)

    q_raw = stacked(q_ref)
    q_factor = rms_factor(q_raw)
    q_norm = (q_raw * q_factor * gain).astype(jnp.bfloat16)
    raw = matmul(q_norm, keys, ((1,), (1,))) * scale
    place = lax.broadcasted_iota(jnp.int32, raw.shape, 1)
    expo = jnp.where(place < count * TILE, jnp.exp(raw), 0.0)
    total = jnp.sum(expo, axis=1, keepdims=True) + (count == 0).astype(jnp.float32)
    inverse = 1.0 / total
    weights_b = expo.astype(jnp.bfloat16)
    attended = matmul(weights_b, vals, ((1,), (0,))) * inverse
    unstacked(context_ref, ratio * attended)
    d_att = ratio * stacked(cot_ref)
    d_att_b = d_att.astype(jnp.bfloat16)
    scaled_b = (d_att * inverse).astype(jnp.bfloat16)
    delta = jnp.sum(d_att * attended, axis=1, keepdims=True)
    d_prob = matmul(d_att_b, vals, ((1,), (1,)))
    d_score = (expo * inverse * (d_prob - delta)).astype(jnp.bfloat16)
    d_qn = scale * matmul(d_score, keys, ((1,), (0,)))
    unstacked(d_query_ref, norm_back(q_raw, q_factor, gain, d_qn))
    d_key_sum[...] += matmul(d_score, q_norm, ((0,), (0,)))
    d_value_sum[...] += matmul(weights_b, scaled_b, ((0,), (0,)))

    @pl.when(step == pl.num_programs(0) - 1)
    def _():
        d_kv_ref[:, :head_dim] = (scale * d_key_sum[...]).astype(d_kv_ref.dtype)
        d_kv_ref[:, head_dim:] = d_value_sum[...].astype(d_kv_ref.dtype)


def attend(base, index, ratio, query, cot, key_value, away, gain, earlier, heads=2):
    rows, both = key_value.shape
    head_dim = both // 2
    text = query.shape[1]
    width = heads * head_dim
    block = pl.BlockSpec((1, text, width), lambda h, index: (index[base], 0, h))
    whole = lambda shape: pl.BlockSpec(shape, lambda h, index: (0, 0))
    in_specs = [
        pl.BlockSpec(memory_space=pltpu.SMEM),
        block,
        block,
        whole((rows, both)),
        whole((rows, both)),
        whole((1, head_dim)),
    ]
    aliases = {}
    if earlier:
        in_specs += [pl.BlockSpec(memory_space=pl.ANY)] * 2
        aliases = {7: 0, 8: 1}
    steps = query.shape[2] // width
    return pl.pallas_call(
        functools.partial(attend_kernel, heads, base),
        grid_spec=pltpu.PrefetchScalarGridSpec(
            num_scalar_prefetch=1,
            grid=(steps,),
            in_specs=in_specs,
            out_specs=[block, block, whole((rows, both))],
            scratch_shapes=[pltpu.VMEM((rows, head_dim), jnp.float32)] * 2,
        ),
        out_shape=[
            jax.ShapeDtypeStruct(query.shape, jnp.bfloat16),
            jax.ShapeDtypeStruct(query.shape, jnp.bfloat16),
            jax.ShapeDtypeStruct((rows, both), jnp.bfloat16),
        ],
        input_output_aliases=aliases,
        compiler_params=pltpu.CompilerParams(
            vmem_limit_bytes=24 * 1024 * 1024
        ),
        cost_estimate=pl.CostEstimate(
            flops=14 * steps * heads * text * rows * head_dim,
            bytes_accessed=8 * text * steps * width + 6 * rows * head_dim,
            transcendentals=steps * heads * text * rows,
        ),
    )(
        index,
        ratio,
        query,
        cot,
        key_value,
        away,
        gain[None, :],
        *earlier,
    )


def per_device(
    query,
    image,
    tiles,
    image_slot,
    key_weight_matrix,
    value_weight_matrix,
    query_gain,
    key_gain,
    gate,
    cotangent,
):
    ratio = jnp.tanh(gate)
    numbers, far_own, near_own = route(tiles, image_slot, image)

    def opposite(after, before, move):
        half = after.shape[0] // 2
        return [move(after[:half], 1), move(before[half:], 3)]

    shard = lay(numbers, key_weight_matrix, value_weight_matrix)
    far_x = [along_x(far_own, 1), along_x(far_own, 3)]
    shard = jnp.concatenate(gathered(shard, inner), axis=0)
    shard, *far_x = lax.optimization_barrier((shard, *far_x))
    far_halves = opposite(*far_x, along_x)
    pieces = [outer(shard, 1), outer(shard, 3)]
    near_own, *far_halves = lax.optimization_barrier((near_own, *far_halves))
    near_x = [along_x(near_own, 1), along_x(near_own, 3)]
    weights = assemble(numbers, [shard, *pieces, *opposite(*pieces, outer)])
    weights, *far_blocks = lax.optimization_barrier((weights, *far_x, *far_halves))

    def other_cores(*blocks):
        return [other_core(block) for block in blocks]

    def paired(own, other, after, before, opposite, after_other, before_other, opposite_other):
        return [own, other, after, after_other, opposite, opposite_other, before, before_other]

    def project(feats):
        depth = feats[0].shape[1]
        total = None
        for o in (0, 1, 3, 2):
            for k in (2 * o, 2 * o + 1):
                part = matmul(feats[k], weights[k * depth : (k + 1) * depth], ((1,), (0,)))
                total = part if total is None else total + part
        return total

    shared = (numbers, ratio, query, cotangent)
    after, before, *halves = far_blocks
    blocks = [after, before, jnp.concatenate(halves, axis=0)]
    far_feats = paired(far_own, other_core(far_own), *blocks, *other_cores(*blocks))
    far_total = project(far_feats)
    far_key_value = finish(far_total, key_gain)
    away = along_z(far_key_value, RING // 2)
    _, *near_late = lax.optimization_barrier((far_key_value, *near_x))
    near_halves = opposite(*near_late, along_x)
    near_others = other_cores(*near_late)
    *earlier, far_grad = attend(FAR, *shared, far_key_value, away, query_gain, ())
    back = along_z(far_grad, RING // 2)

    _, *near_halves = lax.optimization_barrier((far_grad, *near_halves))
    blocks = [*near_x, jnp.concatenate(near_halves, axis=0)]
    near_others.append(other_core(blocks[2]))
    near_feats = paired(near_own, other_core(near_own), *blocks, *near_others)
    near_total = project(near_feats)
    near_key_value = finish(near_total, key_gain)
    context, d_query, near_grad = attend(
        NEAR, *shared, near_key_value, near_key_value, query_gain, earlier
    )
    near_rows = turn(NEAR, numbers, near_total, near_grad, near_grad, key_gain)
    back, near_rows = lax.optimization_barrier((back, near_rows))
    far_rows = turn(FAR, numbers, far_total, far_grad, back, key_gain)
    part = first_part(far_feats, far_rows)

    blocks = product(numbers, near_feats, near_rows, part)
    for z_core in (1, 0):
        blocks = exchanged(blocks, z_core)
        blocks = summed(jnp.split(blocks, RING, axis=0))
        share, blocks = blocks, blocks.astype(jnp.bfloat16)
    head_dim = query_gain.shape[0]
    return (context, d_query, share[:, :head_dim], share[:, head_dim:])


def solution(mesh):
    placed = (
        P("dp", None, "tensor"),
        P("dp", None, "tensor"),
        P(),
        P(),
        P("dp", "tensor"),
        P("dp", "tensor"),
        P(),
        P(),
        P(),
        P("dp", None, "tensor"),
    )
    return jax.shard_map(
        per_device,
        mesh=mesh,
        in_specs=placed,
        out_specs=(
            P("dp", None, "tensor"),
            P("dp", None, "tensor"),
            P("dp", "tensor"),
            P("dp", "tensor"),
        ),
        check_vma=False,
    )
```

```python
import functools

import jax
import jax.numpy as jnp
from jax import lax
from jax.experimental import pallas as pl
from jax.experimental.pallas import tpu as pltpu
from jax.sharding import PartitionSpec as P

TILE = 128
RING = 4
EPS = 1e-06


def along_z(x, step):
    pairs = [(z * RING + y, (z + step) % RING * RING + y) for z in range(RING) for y in range(RING)]
    return lax.ppermute(x, "dp", pairs)


def along_x(x, step):
    pairs = [(i * 2 + c, (i + step) % RING * 2 + c) for i in range(RING) for c in range(2)]
    return lax.ppermute(x, "tensor", pairs)


def other_core(x):
    return lax.ppermute(x, "tensor", [(i, i ^ 1) for i in range(2 * RING)])


def axis_groups(z_core):
    groups = []
    for i in range(2 * RING):
        for fixed in range(RING):
            along = [(k, fixed) if i % 2 == z_core else (fixed, k) for k in range(RING)]
            groups.append([(z * RING + y) * 2 * RING + i for z, y in along])
    return groups


def exchanged(blocks, z_core):
    return lax.all_to_all(
        blocks, ("dp", "tensor"), 0, 0, tiled=True, axis_index_groups=axis_groups(z_core)
    )


def summed(blocks):
    total = blocks[0].astype(jnp.float32)
    for block in blocks[1:]:
        total = total + block.astype(jnp.float32)
    return total


def rms_factor(values):
    return lax.rsqrt(jnp.mean(values * values, axis=-1, keepdims=True) + EPS)


def norm_back(values, norm_multiplier, gain, grad):
    weighted = grad * gain
    inner = jnp.sum(weighted * values, axis=-1, keepdims=True)
    return (
        norm_multiplier * weighted
        - values * (norm_multiplier * norm_multiplier * norm_multiplier) * inner / values.shape[-1]
    )


def matmul(a, b, contract):
    return lax.dot_general(a, b, (contract, ((), ())), preferred_element_type=jnp.float32)


VMEM = pl.BlockSpec(memory_space=pltpu.VMEM)
SMEM = pl.BlockSpec(memory_space=pltpu.SMEM)
ANY = pl.BlockSpec(memory_space=pl.ANY)
HBM = pl.BlockSpec(memory_space=pltpu.HBM)
PARAMS = pltpu.CompilerParams(vmem_limit_bytes=16 * 1024 * 1024)


NEAR, FAR, CHIP = 0, 3, 6


def route_kernel(tiles, slots, image_ref, numbers, far_ref, near_ref, sems):
    rank, place = lax.axis_index("dp"), lax.axis_index("tensor")
    first = 2 * rank
    homes = (slots[first], slots[first + 1])
    away = [
        jnp.logical_and(homes[0] != first + i, homes[1] != first + i) for i in range(2)
    ]
    swaps = jnp.logical_or(away[0], away[1])
    far_slot = jnp.where(away[1], 1, 0)
    copies = []
    for i, (slot, target) in enumerate(((far_slot, far_ref), (1 - far_slot, near_ref))):
        copies.append(pltpu.make_async_copy(image_ref.at[slot], target, sems.at[i]))
        copies[i].start()
    of_slot = jnp.where(homes[1] == first + far_slot, 1, 0)
    far_own = jnp.where(swaps, jnp.where(homes[1] >> 1 != rank, 1, 0), of_slot)
    numbers[NEAR] = 1 - far_own
    numbers[NEAR + 1] = tiles[first + 1 - far_own]
    numbers[NEAR + 2] = 0
    numbers[FAR] = far_own
    numbers[FAR + 1] = tiles[first + far_own]
    numbers[FAR + 2] = jnp.where(swaps, 1, 0)
    numbers[CHIP] = rank // RING
    numbers[CHIP + 1] = rank % RING
    numbers[CHIP + 2] = place // 2
    numbers[CHIP + 3] = place % 2
    for copy in copies:
        copy.wait()


def route(tiles, image_slot, image):
    rows = jax.ShapeDtypeStruct(image.shape[1:], image.dtype)
    return pl.pallas_call(
        route_kernel,
        in_specs=[SMEM, SMEM, HBM],
        out_specs=[SMEM, VMEM, VMEM],
        out_shape=[jax.ShapeDtypeStruct((CHIP + 4,), jnp.int32), rows, rows],
        scratch_shapes=[pltpu.SemaphoreType.DMA((2,))],
        compiler_params=pltpu.CompilerParams(vmem_limit_bytes=60 * 1024 * 1024),
        cost_estimate=pl.CostEstimate(flops=0, bytes_accessed=4 * image.size, transcendentals=0),
    )(tiles, image_slot, image)


def lay_kernel(key_ref, value_ref, out_ref, sems):
    head_dim = key_ref.shape[1]
    copies = []
    for i, source in enumerate((key_ref, value_ref)):
        target = out_ref.at[:, pl.ds(i * head_dim, head_dim)]
        copies.append(pltpu.make_async_copy(source, target, sems.at[i]))
        copies[i].start()
    for copy in copies:
        copy.wait()


def lay(key_weights, value_weights):
    count, head_dim = key_weights.shape
    return pl.pallas_call(
        lay_kernel,
        in_specs=[ANY, ANY],
        out_specs=VMEM,
        out_shape=jax.ShapeDtypeStruct((count, 2 * head_dim), key_weights.dtype),
        scratch_shapes=[pltpu.SemaphoreType.DMA((2,))],
        compiler_params=pltpu.CompilerParams(vmem_limit_bytes=60 * 1024 * 1024),
        cost_estimate=pl.CostEstimate(
            flops=0, bytes_accessed=8 * count * head_dim, transcendentals=0
        ),
    )(key_weights, value_weights)


def finish_kernel(total_ref, gain_ref, key_value_ref):
    head_dim = gain_ref.shape[1]
    raw = total_ref[:, :head_dim]
    keys = (raw * rms_factor(raw) * gain_ref[...]).astype(jnp.bfloat16)
    key_value_ref[:, :head_dim] = keys
    key_value_ref[:, head_dim:] = total_ref[:, head_dim:].astype(jnp.bfloat16)


def finish(total, gain):
    return pl.pallas_call(
        finish_kernel,
        in_specs=[VMEM] * 2,
        out_specs=VMEM,
        out_shape=jax.ShapeDtypeStruct(total.shape, jnp.bfloat16),
        compiler_params=PARAMS,
        cost_estimate=pl.CostEstimate(
            flops=3 * total.size, bytes_accessed=6 * total.size, transcendentals=total.shape[0]
        ),
    )(total, gain[None, :])


def turn_kernel(base, numbers, total_ref, grad_ref, other_ref, gain_ref, out_ref):
    head_dim = gain_ref.shape[1]
    grad = jnp.where(numbers[base + 2] != 0, other_ref[...], grad_ref[...])
    raw = total_ref[:, :head_dim]
    d_raw = norm_back(raw, rms_factor(raw), gain_ref[...], grad[:, :head_dim].astype(jnp.float32))
    out_ref[:, :head_dim] = d_raw.astype(jnp.bfloat16)
    out_ref[:, head_dim:] = grad[:, head_dim:]


def turn(base, numbers, total, grad, other, gain):
    return pl.pallas_call(
        functools.partial(turn_kernel, base),
        in_specs=[SMEM] + [VMEM] * 4,
        out_specs=VMEM,
        out_shape=jax.ShapeDtypeStruct(grad.shape, jnp.bfloat16),
        compiler_params=PARAMS,
        cost_estimate=pl.CostEstimate(
            flops=6 * grad.size, bytes_accessed=8 * grad.size, transcendentals=grad.shape[0]
        ),
    )(numbers, total, grad, other, gain[None, :])


def first_part_kernel(*refs):
    sources, (grads_ref, out_ref) = refs[:-2], refs[-2:]
    depth = sources[0].shape[1]
    for k, source in enumerate(sources):
        out_ref[k * depth : (k + 1) * depth] = matmul(source[...], grads_ref[...], ((0,), (0,)))


def first_part(feats, grads):
    rows, depth = feats[0].shape
    both = grads.shape[1]
    return pl.pallas_call(
        first_part_kernel,
        in_specs=[VMEM] * (len(feats) + 1),
        out_specs=VMEM,
        out_shape=jax.ShapeDtypeStruct((len(feats) * depth, both), jnp.float32),
        compiler_params=PARAMS,
        cost_estimate=pl.CostEstimate(
            flops=2 * len(feats) * rows * depth * both,
            bytes_accessed=2 * len(feats) * rows * depth,
            transcendentals=0,
        ),
    )(*feats, grads)


def product_kernel(chip, *refs):
    sources, (grads_ref, part_ref, out_ref) = refs[:-3], refs[-3:]
    depth = sources[0].shape[1]
    count = depth // 2
    x, core = chip[CHIP + 2], chip[CHIP + 3]
    for k, source in enumerate(sources):
        total = matmul(source[...], grads_ref[...], ((0,), (0,)))
        total = (total + part_ref[k * depth : (k + 1) * depth]).astype(out_ref.dtype)
        to_z = (x - k // 2 + RING) % RING
        for h in range(2):
            to_y = 2 * (k % 2 ^ core) + h
            block = jnp.where(core == 0, to_y * RING + to_z, to_z * RING + to_y)
            start = pl.multiple_of(block * count, count)
            out_ref[pl.ds(start, count)] = total[h * count : (h + 1) * count]


def product(chip, feats, grads, part):
    rows, depth = feats[0].shape
    both = grads.shape[1]
    return pl.pallas_call(
        product_kernel,
        in_specs=[SMEM] + [VMEM] * (len(feats) + 2),
        out_specs=VMEM,
        out_shape=jax.ShapeDtypeStruct((len(feats) * depth, both), jnp.bfloat16),
        compiler_params=PARAMS,
        cost_estimate=pl.CostEstimate(
            flops=2 * len(feats) * rows * depth * both,
            bytes_accessed=2 * len(feats) * rows * depth,
            transcendentals=0,
        ),
    )(chip, *feats, grads, part)


def attend_kernel(heads, base, index, ratio_ref, q_ref, cot_ref, kv_ref, away_ref, gain_ref, *refs):
    context_ref, d_query_ref, d_kv_ref, d_key_sum, d_value_sum = refs[-5:]
    step = pl.program_id(0)
    head_dim = gain_ref.shape[1]
    scale = head_dim ** (-0.5)
    count = index[base + 1]
    ratio = ratio_ref[0]
    gain = gain_ref[...]
    key_value = jnp.where(index[base + 2] != 0, away_ref[...], kv_ref[...])
    keys = key_value[:, :head_dim]
    vals = key_value[:, head_dim:]

    def stacked(ref):
        parts = [ref[0, :, h * head_dim : (h + 1) * head_dim] for h in range(heads)]
        return jnp.concatenate(parts, axis=0).astype(jnp.float32)

    def unstacked(ref, rows):
        text = rows.shape[0] // heads
        for h in range(heads):
            part = rows[h * text : (h + 1) * text]
            ref[0, :, h * head_dim : (h + 1) * head_dim] = part.astype(ref.dtype)

    @pl.when(step == 0)
    def _():
        d_key_sum[...] = jnp.zeros_like(d_key_sum)
        d_value_sum[...] = jnp.zeros_like(d_value_sum)

    q_raw = stacked(q_ref)
    q_factor = rms_factor(q_raw)
    q_norm = (q_raw * q_factor * gain).astype(jnp.bfloat16)
    raw = matmul(q_norm, keys, ((1,), (1,))) * scale
    place = lax.broadcasted_iota(jnp.int32, raw.shape, 1)
    expo = jnp.where(place < count * TILE, jnp.exp(raw), 0.0)
    total = jnp.sum(expo, axis=1, keepdims=True) + (count == 0).astype(jnp.float32)
    inverse = 1.0 / total
    weights_b = expo.astype(jnp.bfloat16)
    attended = matmul(weights_b, vals, ((1,), (0,))) * inverse
    unstacked(context_ref, ratio * attended)
    d_att = ratio * stacked(cot_ref)
    d_att_b = d_att.astype(jnp.bfloat16)
    scaled_b = (d_att * inverse).astype(jnp.bfloat16)
    delta = jnp.sum(d_att * attended, axis=1, keepdims=True)
    d_prob = matmul(d_att_b, vals, ((1,), (1,)))
    d_score = (expo * inverse * (d_prob - delta)).astype(jnp.bfloat16)
    d_qn = scale * matmul(d_score, keys, ((1,), (0,)))
    unstacked(d_query_ref, norm_back(q_raw, q_factor, gain, d_qn))
    d_key_sum[...] += matmul(d_score, q_norm, ((0,), (0,)))
    d_value_sum[...] += matmul(weights_b, scaled_b, ((0,), (0,)))

    @pl.when(step == pl.num_programs(0) - 1)
    def _():
        d_kv_ref[:, :head_dim] = (scale * d_key_sum[...]).astype(d_kv_ref.dtype)
        d_kv_ref[:, head_dim:] = d_value_sum[...].astype(d_kv_ref.dtype)


def attend(base, index, ratio, query, cot, key_value, away, gain, earlier, heads=2):
    rows, both = key_value.shape
    head_dim = both // 2
    text = query.shape[1]
    width = heads * head_dim
    block = pl.BlockSpec((1, text, width), lambda h, index: (index[base], 0, h))
    whole = lambda shape: pl.BlockSpec(shape, lambda h, index: (0, 0))
    in_specs = [
        pl.BlockSpec(memory_space=pltpu.SMEM),
        block,
        block,
        whole((rows, both)),
        whole((rows, both)),
        whole((1, head_dim)),
    ]
    aliases = {}
    if earlier:
        in_specs += [pl.BlockSpec(memory_space=pl.ANY)] * 2
        aliases = {7: 0, 8: 1}
    steps = query.shape[2] // width
    return pl.pallas_call(
        functools.partial(attend_kernel, heads, base),
        grid_spec=pltpu.PrefetchScalarGridSpec(
            num_scalar_prefetch=1,
            grid=(steps,),
            in_specs=in_specs,
            out_specs=[block, block, whole((rows, both))],
            scratch_shapes=[pltpu.VMEM((rows, head_dim), jnp.float32)] * 2,
        ),
        out_shape=[
            jax.ShapeDtypeStruct(query.shape, jnp.bfloat16),
            jax.ShapeDtypeStruct(query.shape, jnp.bfloat16),
            jax.ShapeDtypeStruct((rows, both), jnp.bfloat16),
        ],
        input_output_aliases=aliases,
        compiler_params=pltpu.CompilerParams(
            vmem_limit_bytes=24 * 1024 * 1024
        ),
        cost_estimate=pl.CostEstimate(
            flops=14 * steps * heads * text * rows * head_dim,
            bytes_accessed=8 * text * steps * width + 6 * rows * head_dim,
            transcendentals=steps * heads * text * rows,
        ),
    )(
        index,
        ratio,
        query,
        cot,
        key_value,
        away,
        gain[None, :],
        *earlier,
    )


def per_device(
    query,
    image,
    tiles,
    image_slot,
    key_weight_matrix,
    value_weight_matrix,
    query_gain,
    key_gain,
    gate,
    cotangent,
):
    ratio = jnp.tanh(gate)
    numbers, far_own, near_own = route(tiles, image_slot, image)

    def halves_of(after, before):
        half = after.shape[0] // 2
        return after[:half], before[half:]

    def opposite(halves, move):
        return [move(halves[0], 1), move(halves[1], 3)]

    shard = lay(key_weight_matrix, value_weight_matrix)
    weights = lax.all_gather(shard, "dp", axis=0, tiled=True)
    far_x = [along_x(far_own, 1), along_x(far_own, 3)]
    near_own, *halves = lax.optimization_barrier((near_own, *halves_of(*far_x)))
    far_halves = opposite(halves, along_x)
    near_x = [along_x(near_own, 1), along_x(near_own, 3)]
    place = lax.axis_index("tensor")
    depth = image.shape[2]
    columns = []
    for o in range(RING):
        for e in range(2):
            start = ((place // 2 - o) % RING * 2 + (place % 2 ^ e)) * depth
            columns.append(lax.dynamic_slice_in_dim(weights, start, depth, 0))
    columns = lax.optimization_barrier(tuple(columns))

    def other_cores(*blocks):
        return [other_core(block) for block in blocks]

    def paired(own, other, after, before, opposite, after_other, before_other, opposite_other):
        return [own, other, after, after_other, opposite, opposite_other, before, before_other]

    def project(feats):
        total = None
        for o in (0, 1, 3, 2):
            for k in (2 * o, 2 * o + 1):
                part = matmul(feats[k], columns[k], ((1,), (0,)))
                total = part if total is None else total + part
        return total

    shared = (numbers, ratio, query, cotangent)
    blocks = [*far_x, jnp.concatenate(far_halves, axis=0)]
    far_feats = paired(far_own, other_core(far_own), *blocks, *other_cores(*blocks))
    far_total = project(far_feats)
    far_key_value = finish(far_total, key_gain)
    away = along_z(far_key_value, RING // 2)
    _, near_own, *near_x = lax.optimization_barrier((far_key_value, near_own, *near_x))
    near_halves = opposite(halves_of(*near_x), along_x)
    near_others = other_cores(*near_x)
    *earlier, far_grad = attend(FAR, *shared, far_key_value, away, query_gain, ())
    back = along_z(far_grad, RING // 2)

    _, *near_halves = lax.optimization_barrier((far_grad, *near_halves))
    blocks = [*near_x, jnp.concatenate(near_halves, axis=0)]
    near_others.append(other_core(blocks[2]))
    near_feats = paired(near_own, other_core(near_own), *blocks, *near_others)
    near_total = project(near_feats)
    near_key_value = finish(near_total, key_gain)
    context, d_query, near_grad = attend(
        NEAR, *shared, near_key_value, near_key_value, query_gain, earlier
    )
    near_rows = turn(NEAR, numbers, near_total, near_grad, near_grad, key_gain)
    back, near_rows = lax.optimization_barrier((back, near_rows))
    far_rows = turn(FAR, numbers, far_total, far_grad, back, key_gain)
    part = first_part(far_feats, far_rows)

    blocks = product(numbers, near_feats, near_rows, part)
    for z_core in (1, 0):
        blocks = exchanged(blocks, z_core)
        blocks = summed(jnp.split(blocks, RING, axis=0))
        share, blocks = blocks, blocks.astype(jnp.bfloat16)
    head_dim = query_gain.shape[0]
    return (context, d_query, share[:, :head_dim], share[:, head_dim:])


def solution(mesh):
    placed = (
        P("dp", None, "tensor"),
        P("dp", None, "tensor"),
        P(),
        P(),
        P("dp", "tensor"),
        P("dp", "tensor"),
        P(),
        P(),
        P(),
        P("dp", None, "tensor"),
    )
    return jax.shard_map(
        per_device,
        mesh=mesh,
        in_specs=placed,
        out_specs=(
            P("dp", None, "tensor"),
            P("dp", None, "tensor"),
            P("dp", "tensor"),
            P("dp", "tensor"),
        ),
        check_vma=False,
    )
```

```python
import functools

import jax
import jax.numpy as jnp
from jax import lax
from jax.experimental import pallas as pl
from jax.experimental.pallas import tpu as pltpu
from jax.sharding import PartitionSpec as P

TILE = 128
RING = 4
EPS = 1e-06


def along_z(x, step):
    pairs = [(z * RING + y, (z + step) % RING * RING + y) for z in range(RING) for y in range(RING)]
    return lax.ppermute(x, "dp", pairs)


def by_core(x, step, z_core):
    pairs = []
    for z in range(RING):
        for y in range(RING):
            for i in range(RING):
                for c in range(2):
                    to_z, to_y = (z + step, y) if c == z_core else (z, y + step)
                    source = (z * RING + y) * 2 * RING + i * 2 + c
                    target = (to_z % RING * RING + to_y % RING) * 2 * RING + i * 2 + c
                    pairs.append((source, target))
    return lax.ppermute(x, ("dp", "tensor"), pairs)


def inner(x, step):
    return by_core(x, step, 0)


def outer(x, step):
    return by_core(x, step, 1)


def along_x(x, step):
    pairs = [(i * 2 + c, (i + step) % RING * 2 + c) for i in range(RING) for c in range(2)]
    return lax.ppermute(x, "tensor", pairs)


def other_core(x):
    return lax.ppermute(x, "tensor", [(i, i ^ 1) for i in range(2 * RING)])


def gathered(block, move):
    far, after, before = (move(block, step) for step in (2, 1, 3))
    return [block, after, far, before]


def scattered(parts, move):
    return [move(parts[step], step) for step in (2, 1, 3)]


def summed(blocks):
    total = blocks[0].astype(jnp.float32)
    for block in blocks[1:]:
        total = total + block.astype(jnp.float32)
    return total


def rms_factor(values):
    return lax.rsqrt(jnp.mean(values * values, axis=-1, keepdims=True) + EPS)


def norm_back(values, norm_multiplier, gain, grad):
    weighted = grad * gain
    inner = jnp.sum(weighted * values, axis=-1, keepdims=True)
    return (
        norm_multiplier * weighted
        - values * (norm_multiplier * norm_multiplier * norm_multiplier) * inner / values.shape[-1]
    )


def matmul(a, b, contract):
    return lax.dot_general(a, b, (contract, ((), ())), preferred_element_type=jnp.float32)


VMEM = pl.BlockSpec(memory_space=pltpu.VMEM)
SMEM = pl.BlockSpec(memory_space=pltpu.SMEM)
ANY = pl.BlockSpec(memory_space=pl.ANY)
HBM = pl.BlockSpec(memory_space=pltpu.HBM)
PARAMS = pltpu.CompilerParams(vmem_limit_bytes=16 * 1024 * 1024)


NEAR, FAR, CHIP = 0, 3, 6


def route_kernel(tiles, slots, image_ref, numbers, far_ref, near_ref, sems):
    rank, place = lax.axis_index("dp"), lax.axis_index("tensor")
    first = 2 * rank
    homes = (slots[first], slots[first + 1])
    away = [
        jnp.logical_and(homes[0] != first + i, homes[1] != first + i) for i in range(2)
    ]
    swaps = jnp.logical_or(away[0], away[1])
    far_slot = jnp.where(away[1], 1, 0)
    copies = []
    for i, (slot, target) in enumerate(((far_slot, far_ref), (1 - far_slot, near_ref))):
        copies.append(pltpu.make_async_copy(image_ref.at[slot], target, sems.at[i]))
        copies[i].start()
    of_slot = jnp.where(homes[1] == first + far_slot, 1, 0)
    far_own = jnp.where(swaps, jnp.where(homes[1] >> 1 != rank, 1, 0), of_slot)
    numbers[NEAR] = 1 - far_own
    numbers[NEAR + 1] = tiles[first + 1 - far_own]
    numbers[NEAR + 2] = 0
    numbers[FAR] = far_own
    numbers[FAR + 1] = tiles[first + far_own]
    numbers[FAR + 2] = jnp.where(swaps, 1, 0)
    numbers[CHIP] = rank // RING
    numbers[CHIP + 1] = rank % RING
    numbers[CHIP + 2] = place // 2
    numbers[CHIP + 3] = place % 2
    for copy in copies:
        copy.wait()


def route(tiles, image_slot, image):
    rows = jax.ShapeDtypeStruct(image.shape[1:], image.dtype)
    return pl.pallas_call(
        route_kernel,
        in_specs=[SMEM, SMEM, HBM],
        out_specs=[SMEM, VMEM, VMEM],
        out_shape=[jax.ShapeDtypeStruct((CHIP + 4,), jnp.int32), rows, rows],
        scratch_shapes=[pltpu.SemaphoreType.DMA((2,))],
        compiler_params=pltpu.CompilerParams(vmem_limit_bytes=60 * 1024 * 1024),
        cost_estimate=pl.CostEstimate(flops=0, bytes_accessed=4 * image.size, transcendentals=0),
    )(tiles, image_slot, image)


def lay_kernel(numbers, key_ref, value_ref, out_ref, sems):
    head_dim = key_ref.shape[1]
    copies = []
    for i, source in enumerate((key_ref, value_ref)):
        target = out_ref.at[:, pl.ds(i * head_dim, head_dim)]
        copies.append(pltpu.make_async_copy(source, target, sems.at[i]))
        copies[i].start()
    for copy in copies:
        copy.wait()


def lay(numbers, key_weights, value_weights):
    count, head_dim = key_weights.shape
    return pl.pallas_call(
        lay_kernel,
        in_specs=[SMEM, ANY, ANY],
        out_specs=VMEM,
        out_shape=jax.ShapeDtypeStruct((count, 2 * head_dim), key_weights.dtype),
        scratch_shapes=[pltpu.SemaphoreType.DMA((2,))],
        compiler_params=PARAMS,
        cost_estimate=pl.CostEstimate(
            flops=0, bytes_accessed=8 * count * head_dim, transcendentals=0
        ),
    )(numbers, key_weights, value_weights)


def assemble_kernel(chip, *refs):
    pieces, out_ref, sems = refs[: RING + 1], refs[RING + 1], refs[RING + 2]
    rows, both = pieces[0].shape
    count = rows // RING
    z, y, x, core = (chip[CHIP + i] for i in range(4))
    copies = []
    for b in range(RING):
        for a in range(RING):
            from_z = (z - jnp.where(core == 0, a, b) + RING) % RING
            from_y = (y - jnp.where(core == 0, b, a) + RING) % RING
            o = (x - from_z + RING) % RING
            start = ((o * 2 + ((from_y >> 1) ^ core)) * 2 + from_y % 2) * count
            target = out_ref.at[pl.ds(pl.multiple_of(start, count), count)]
            if b == 2:
                source = pieces[3 + a // 2].at[pl.ds(a % 2 * count, count)]
            else:
                source = pieces[min(b, 2)].at[pl.ds(a * count, count)]
            copies.append(pltpu.make_async_copy(source, target, sems.at[b, a]))
    for copy in copies:
        copy.start()
    for copy in copies:
        copy.wait()


def assemble(chip, pieces):
    rows, both = pieces[0].shape
    return pl.pallas_call(
        assemble_kernel,
        in_specs=[SMEM] + [ANY] * (RING + 1),
        out_specs=VMEM,
        out_shape=jax.ShapeDtypeStruct((RING * rows, both), pieces[0].dtype),
        scratch_shapes=[pltpu.SemaphoreType.DMA((RING, RING))],
        compiler_params=PARAMS,
        cost_estimate=pl.CostEstimate(
            flops=0, bytes_accessed=4 * RING * rows * both, transcendentals=0
        ),
    )(chip, *pieces)


def finish_kernel(total_ref, gain_ref, key_value_ref):
    head_dim = gain_ref.shape[1]
    raw = total_ref[:, :head_dim]
    keys = (raw * rms_factor(raw) * gain_ref[...]).astype(jnp.bfloat16)
    key_value_ref[:, :head_dim] = keys
    key_value_ref[:, head_dim:] = total_ref[:, head_dim:].astype(jnp.bfloat16)


def finish(total, gain):
    return pl.pallas_call(
        finish_kernel,
        in_specs=[VMEM] * 2,
        out_specs=VMEM,
        out_shape=jax.ShapeDtypeStruct(total.shape, jnp.bfloat16),
        compiler_params=PARAMS,
        cost_estimate=pl.CostEstimate(
            flops=3 * total.size, bytes_accessed=6 * total.size, transcendentals=total.shape[0]
        ),
    )(total, gain[None, :])


def turn_kernel(base, numbers, total_ref, grad_ref, other_ref, gain_ref, out_ref):
    head_dim = gain_ref.shape[1]
    grad = jnp.where(numbers[base + 2] != 0, other_ref[...], grad_ref[...])
    raw = total_ref[:, :head_dim]
    d_raw = norm_back(raw, rms_factor(raw), gain_ref[...], grad[:, :head_dim].astype(jnp.float32))
    out_ref[:, :head_dim] = d_raw.astype(jnp.bfloat16)
    out_ref[:, head_dim:] = grad[:, head_dim:]


def turn(base, numbers, total, grad, other, gain):
    return pl.pallas_call(
        functools.partial(turn_kernel, base),
        in_specs=[SMEM] + [VMEM] * 4,
        out_specs=VMEM,
        out_shape=jax.ShapeDtypeStruct(grad.shape, jnp.bfloat16),
        compiler_params=PARAMS,
        cost_estimate=pl.CostEstimate(
            flops=6 * grad.size, bytes_accessed=8 * grad.size, transcendentals=grad.shape[0]
        ),
    )(numbers, total, grad, other, gain[None, :])


def first_part_kernel(*refs):
    sources, (grads_ref, out_ref) = refs[:-2], refs[-2:]
    depth = sources[0].shape[1]
    for k, source in enumerate(sources):
        out_ref[k * depth : (k + 1) * depth] = matmul(source[...], grads_ref[...], ((0,), (0,)))


def first_part(feats, grads):
    rows, depth = feats[0].shape
    both = grads.shape[1]
    return pl.pallas_call(
        first_part_kernel,
        in_specs=[VMEM] * (len(feats) + 1),
        out_specs=VMEM,
        out_shape=jax.ShapeDtypeStruct((len(feats) * depth, both), jnp.float32),
        compiler_params=PARAMS,
        cost_estimate=pl.CostEstimate(
            flops=2 * len(feats) * rows * depth * both,
            bytes_accessed=2 * len(feats) * rows * depth,
            transcendentals=0,
        ),
    )(*feats, grads)


def product_kernel(chip, *refs):
    sources, (grads_ref, part_ref), refs = refs[: 2 * RING], refs[2 * RING : 2 * RING + 2], refs[2 * RING + 2 :]
    outs, (held, sems) = refs[:RING], refs[RING:]
    depth = sources[0].shape[1]
    count = depth // 2
    z, y, x, core = (chip[CHIP + i] for i in range(4))
    for k, source in enumerate(sources):
        total = matmul(source[...], grads_ref[...], ((0,), (0,)))
        total = (total + part_ref[k * depth : (k + 1) * depth]).astype(held.dtype)
        by_z = (x - k // 2 - z + 2 * RING) % RING
        for h in range(2):
            by_y = (2 * (k % 2 ^ core) + h - y + RING) % RING
            outer_by = jnp.where(core == 0, by_y, by_z)
            inner_by = jnp.where(core == 0, by_z, by_y)
            start = pl.multiple_of(inner_by * count, count)
            held[outer_by, pl.ds(start, count)] = total[h * count : (h + 1) * count]
    copies = [pltpu.make_async_copy(held.at[k], outs[k], sems.at[k]) for k in range(RING)]
    for copy in copies:
        copy.start()
    for copy in copies:
        copy.wait()


def product(chip, feats, grads, part):
    rows, depth = feats[0].shape
    both = grads.shape[1]
    shape = (RING * depth // 2, both)
    return pl.pallas_call(
        product_kernel,
        in_specs=[SMEM] + [VMEM] * (len(feats) + 2),
        out_specs=[ANY] * RING,
        out_shape=[jax.ShapeDtypeStruct(shape, jnp.bfloat16)] * RING,
        scratch_shapes=[
            pltpu.VMEM((RING, *shape), jnp.bfloat16),
            pltpu.SemaphoreType.DMA((RING,)),
        ],
        compiler_params=PARAMS,
        cost_estimate=pl.CostEstimate(
            flops=2 * len(feats) * rows * depth * both,
            bytes_accessed=2 * len(feats) * rows * depth,
            transcendentals=0,
        ),
    )(chip, *feats, grads, part)


def attend_kernel(heads, base, index, ratio_ref, q_ref, cot_ref, kv_ref, away_ref, gain_ref, *refs):
    context_ref, d_query_ref, d_kv_ref, d_key_sum, d_value_sum = refs[-5:]
    step = pl.program_id(0)
    head_dim = gain_ref.shape[1]
    scale = head_dim ** (-0.5)
    count = index[base + 1]
    ratio = ratio_ref[0]
    gain = gain_ref[...]
    key_value = jnp.where(index[base + 2] != 0, away_ref[...], kv_ref[...])
    keys = key_value[:, :head_dim]
    vals = key_value[:, head_dim:]

    def stacked(ref):
        parts = [ref[0, :, h * head_dim : (h + 1) * head_dim] for h in range(heads)]
        return jnp.concatenate(parts, axis=0).astype(jnp.float32)

    def unstacked(ref, rows):
        text = rows.shape[0] // heads
        for h in range(heads):
            part = rows[h * text : (h + 1) * text]
            ref[0, :, h * head_dim : (h + 1) * head_dim] = part.astype(ref.dtype)

    @pl.when(step == 0)
    def _():
        d_key_sum[...] = jnp.zeros_like(d_key_sum)
        d_value_sum[...] = jnp.zeros_like(d_value_sum)

    q_raw = stacked(q_ref)
    q_factor = rms_factor(q_raw)
    q_norm = (q_raw * q_factor * gain).astype(jnp.bfloat16)
    raw = matmul(q_norm, keys, ((1,), (1,))) * scale
    place = lax.broadcasted_iota(jnp.int32, raw.shape, 1)
    expo = jnp.where(place < count * TILE, jnp.exp(raw), 0.0)
    total = jnp.sum(expo, axis=1, keepdims=True) + (count == 0).astype(jnp.float32)
    inverse = 1.0 / total
    weights_b = expo.astype(jnp.bfloat16)
    attended = matmul(weights_b, vals, ((1,), (0,))) * inverse
    unstacked(context_ref, ratio * attended)
    d_att = ratio * stacked(cot_ref)
    d_att_b = d_att.astype(jnp.bfloat16)
    scaled_b = (d_att * inverse).astype(jnp.bfloat16)
    delta = jnp.sum(d_att * attended, axis=1, keepdims=True)
    d_prob = matmul(d_att_b, vals, ((1,), (1,)))
    d_score = (expo * inverse * (d_prob - delta)).astype(jnp.bfloat16)
    d_qn = scale * matmul(d_score, keys, ((1,), (0,)))
    unstacked(d_query_ref, norm_back(q_raw, q_factor, gain, d_qn))
    d_key_sum[...] += matmul(d_score, q_norm, ((0,), (0,)))
    d_value_sum[...] += matmul(weights_b, scaled_b, ((0,), (0,)))

    @pl.when(step == pl.num_programs(0) - 1)
    def _():
        d_kv_ref[:, :head_dim] = (scale * d_key_sum[...]).astype(d_kv_ref.dtype)
        d_kv_ref[:, head_dim:] = d_value_sum[...].astype(d_kv_ref.dtype)


def attend(base, index, ratio, query, cot, key_value, away, gain, earlier, heads=2):
    rows, both = key_value.shape
    head_dim = both // 2
    text = query.shape[1]
    width = heads * head_dim
    block = pl.BlockSpec((1, text, width), lambda h, index: (index[base], 0, h))
    whole = lambda shape: pl.BlockSpec(shape, lambda h, index: (0, 0))
    in_specs = [
        pl.BlockSpec(memory_space=pltpu.SMEM),
        block,
        block,
        whole((rows, both)),
        whole((rows, both)),
        whole((1, head_dim)),
    ]
    aliases = {}
    if earlier:
        in_specs += [pl.BlockSpec(memory_space=pl.ANY)] * 2
        aliases = {7: 0, 8: 1}
    steps = query.shape[2] // width
    return pl.pallas_call(
        functools.partial(attend_kernel, heads, base),
        grid_spec=pltpu.PrefetchScalarGridSpec(
            num_scalar_prefetch=1,
            grid=(steps,),
            in_specs=in_specs,
            out_specs=[block, block, whole((rows, both))],
            scratch_shapes=[pltpu.VMEM((rows, head_dim), jnp.float32)] * 2,
        ),
        out_shape=[
            jax.ShapeDtypeStruct(query.shape, jnp.bfloat16),
            jax.ShapeDtypeStruct(query.shape, jnp.bfloat16),
            jax.ShapeDtypeStruct((rows, both), jnp.bfloat16),
        ],
        input_output_aliases=aliases,
        compiler_params=pltpu.CompilerParams(
            vmem_limit_bytes=24 * 1024 * 1024
        ),
        cost_estimate=pl.CostEstimate(
            flops=14 * steps * heads * text * rows * head_dim,
            bytes_accessed=8 * text * steps * width + 6 * rows * head_dim,
            transcendentals=steps * heads * text * rows,
        ),
    )(
        index,
        ratio,
        query,
        cot,
        key_value,
        away,
        gain[None, :],
        *earlier,
    )


def per_device(
    query,
    image,
    tiles,
    image_slot,
    key_weight_matrix,
    value_weight_matrix,
    query_gain,
    key_gain,
    gate,
    cotangent,
):
    ratio = jnp.tanh(gate)
    numbers, far_own, near_own = route(tiles, image_slot, image)

    half = image.shape[1] // 2

    def opposite(after, before, move):
        middle = after.shape[0] // 2
        return [move(after[:middle], 1), move(before[middle:], 3)]

    shard = lay(numbers, key_weight_matrix, value_weight_matrix)
    far_x = [along_x(far_own, 1), along_x(far_own, 3)]
    shard = jnp.concatenate(gathered(shard, inner), axis=0)
    ahead = [
        jnp.concatenate([near_own[:half], near_own], axis=0),
        jnp.concatenate([near_own[half:], near_own], axis=0),
    ]
    shard, *ahead = lax.optimization_barrier((shard, *ahead))
    far_other, near_other = other_core(far_own), other_core(near_own)
    shard, far_other, near_other, *far_x = lax.optimization_barrier(
        (shard, far_other, near_other, *far_x)
    )
    ahead = [
        lax.dynamic_update_slice_in_dim(ahead[0], far_x[0][:half], 0, 0),
        lax.dynamic_update_slice_in_dim(ahead[1], far_x[1][half:], 0, 0),
    ]
    ahead = [along_x(ahead[0], 1), along_x(ahead[1], 3)]
    pieces = [outer(shard, 1), outer(shard, 3)]
    weights = assemble(numbers, [shard, *pieces, *opposite(*pieces, outer)])
    weights, *far_x = lax.optimization_barrier((weights, *far_x))
    far_halves = [block[:half] for block in ahead]
    near_x = [block[half:] for block in ahead]
    near_halves = opposite(*near_x, along_x)

    def other_cores(*blocks):
        return [other_core(block) for block in blocks]

    def paired(own, other, after, before, opposite, after_other, before_other, opposite_other):
        return [own, other, after, after_other, opposite, opposite_other, before, before_other]

    def project(feats):
        depth = feats[0].shape[1]
        total = None
        for o in (0, 1, 3, 2):
            for k in (2 * o, 2 * o + 1):
                part = matmul(feats[k], weights[k * depth : (k + 1) * depth], ((1,), (0,)))
                total = part if total is None else total + part
        return total

    shared = (numbers, ratio, query, cotangent)
    blocks = [*far_x, jnp.concatenate(far_halves, axis=0)]
    far_feats = paired(far_own, far_other, *blocks, *other_cores(*blocks))
    far_total = project(far_feats)
    far_key_value = finish(far_total, key_gain)
    away = along_z(far_key_value, RING // 2)
    _, *blocks = lax.optimization_barrier((far_key_value, *near_x, *near_halves))
    near_x, near_halves = blocks[:2], blocks[2:]
    *earlier, far_grad = attend(FAR, *shared, far_key_value, away, query_gain, ())
    back = along_z(far_grad, RING // 2)

    blocks = [*near_x, jnp.concatenate(near_halves, axis=0)]
    near_feats = paired(near_own, near_other, *blocks, *other_cores(*blocks))
    near_total = project(near_feats)
    near_key_value = finish(near_total, key_gain)
    context, d_query, near_grad = attend(
        NEAR, *shared, near_key_value, near_key_value, query_gain, earlier
    )
    near_rows = turn(NEAR, numbers, near_total, near_grad, near_grad, key_gain)
    back, near_rows = lax.optimization_barrier((back, near_rows))
    far_rows = turn(FAR, numbers, far_total, far_grad, back, key_gain)
    part = first_part(far_feats, far_rows)

    blocks = product(numbers, near_feats, near_rows, part)
    total = summed([blocks[0], *scattered(blocks, outer)])
    count = total.shape[0] // RING
    parts = [total[d * count : (d + 1) * count] for d in range(RING)]
    sent = [None] + [part.astype(jnp.bfloat16) for part in parts[1:]]
    share = summed([parts[0], *scattered(sent, inner)])
    head_dim = query_gain.shape[0]
    return (context, d_query, share[:, :head_dim], share[:, head_dim:])


def solution(mesh):
    placed = (
        P("dp", None, "tensor"),
        P("dp", None, "tensor"),
        P(),
        P(),
        P("dp", "tensor"),
        P("dp", "tensor"),
        P(),
        P(),
        P(),
        P("dp", None, "tensor"),
    )
    return jax.shard_map(
        per_device,
        mesh=mesh,
        in_specs=placed,
        out_specs=(
            P("dp", None, "tensor"),
            P("dp", None, "tensor"),
            P("dp", "tensor"),
            P("dp", "tensor"),
        ),
        check_vma=False,
    )
```

```python
import functools

import jax
import jax.numpy as jnp
from jax import lax
from jax.experimental import pallas as pl
from jax.experimental.pallas import tpu as pltpu
from jax.sharding import PartitionSpec as P

TILE = 128
RING = 4
EPS = 1e-06


def along_z(x, step):
    pairs = [(z * RING + y, (z + step) % RING * RING + y) for z in range(RING) for y in range(RING)]
    return lax.ppermute(x, "dp", pairs)


def by_core(x, step, z_core):
    pairs = []
    for z in range(RING):
        for y in range(RING):
            for i in range(RING):
                for c in range(2):
                    to_z, to_y = (z + step, y) if c == z_core else (z, y + step)
                    source = (z * RING + y) * 2 * RING + i * 2 + c
                    target = (to_z % RING * RING + to_y % RING) * 2 * RING + i * 2 + c
                    pairs.append((source, target))
    return lax.ppermute(x, ("dp", "tensor"), pairs)


def inner(x, step):
    return by_core(x, step, 0)


def outer(x, step):
    return by_core(x, step, 1)


def along_x(x, step):
    pairs = [(i * 2 + c, (i + step) % RING * 2 + c) for i in range(RING) for c in range(2)]
    return lax.ppermute(x, "tensor", pairs)


def other_core(x):
    return lax.ppermute(x, "tensor", [(i, i ^ 1) for i in range(2 * RING)])


def gathered(block, move):
    far, after, before = (move(block, step) for step in (2, 1, 3))
    return [block, after, far, before]


def scattered(parts, move):
    return [move(parts[step], step) for step in (2, 1, 3)]


def summed(blocks):
    total = blocks[0].astype(jnp.float32)
    for block in blocks[1:]:
        total = total + block.astype(jnp.float32)
    return total


def rms_factor(values):
    return lax.rsqrt(jnp.mean(values * values, axis=-1, keepdims=True) + EPS)


def norm_back(values, norm_multiplier, gain, grad):
    weighted = grad * gain
    inner = jnp.sum(weighted * values, axis=-1, keepdims=True)
    return (
        norm_multiplier * weighted
        - values * (norm_multiplier * norm_multiplier * norm_multiplier) * inner / values.shape[-1]
    )


def matmul(a, b, contract):
    return lax.dot_general(a, b, (contract, ((), ())), preferred_element_type=jnp.float32)


VMEM = pl.BlockSpec(memory_space=pltpu.VMEM)
SMEM = pl.BlockSpec(memory_space=pltpu.SMEM)
ANY = pl.BlockSpec(memory_space=pl.ANY)
HBM = pl.BlockSpec(memory_space=pltpu.HBM)
PARAMS = pltpu.CompilerParams(vmem_limit_bytes=16 * 1024 * 1024)


NEAR, FAR, CHIP = 0, 3, 6


def route_kernel(tiles, slots, image_ref, numbers, far_ref, near_ref, sems):
    rank, place = lax.axis_index("dp"), lax.axis_index("tensor")
    first = 2 * rank
    homes = (slots[first], slots[first + 1])
    away = [
        jnp.logical_and(homes[0] != first + i, homes[1] != first + i) for i in range(2)
    ]
    swaps = jnp.logical_or(away[0], away[1])
    far_slot = jnp.where(away[1], 1, 0)
    copies = []
    for i, (slot, target) in enumerate(((far_slot, far_ref), (1 - far_slot, near_ref))):
        copies.append(pltpu.make_async_copy(image_ref.at[slot], target, sems.at[i]))
        copies[i].start()
    of_slot = jnp.where(homes[1] == first + far_slot, 1, 0)
    far_own = jnp.where(swaps, jnp.where(homes[1] >> 1 != rank, 1, 0), of_slot)
    numbers[NEAR] = 1 - far_own
    numbers[NEAR + 1] = tiles[first + 1 - far_own]
    numbers[NEAR + 2] = 0
    numbers[FAR] = far_own
    numbers[FAR + 1] = tiles[first + far_own]
    numbers[FAR + 2] = jnp.where(swaps, 1, 0)
    numbers[CHIP] = rank // RING
    numbers[CHIP + 1] = rank % RING
    numbers[CHIP + 2] = place // 2
    numbers[CHIP + 3] = place % 2
    for copy in copies:
        copy.wait()


def route(tiles, image_slot, image):
    rows = jax.ShapeDtypeStruct(image.shape[1:], image.dtype)
    return pl.pallas_call(
        route_kernel,
        in_specs=[SMEM, SMEM, HBM],
        out_specs=[SMEM, VMEM, VMEM],
        out_shape=[jax.ShapeDtypeStruct((CHIP + 4,), jnp.int32), rows, rows],
        scratch_shapes=[pltpu.SemaphoreType.DMA((2,))],
        compiler_params=pltpu.CompilerParams(vmem_limit_bytes=60 * 1024 * 1024),
        cost_estimate=pl.CostEstimate(flops=0, bytes_accessed=4 * image.size, transcendentals=0),
    )(tiles, image_slot, image)


def lay_kernel(numbers, key_ref, value_ref, out_ref, sems):
    head_dim = key_ref.shape[1]
    copies = []
    for i, source in enumerate((key_ref, value_ref)):
        target = out_ref.at[:, pl.ds(i * head_dim, head_dim)]
        copies.append(pltpu.make_async_copy(source, target, sems.at[i]))
        copies[i].start()
    for copy in copies:
        copy.wait()


def lay(numbers, key_weights, value_weights):
    count, head_dim = key_weights.shape
    return pl.pallas_call(
        lay_kernel,
        in_specs=[SMEM, ANY, ANY],
        out_specs=VMEM,
        out_shape=jax.ShapeDtypeStruct((count, 2 * head_dim), key_weights.dtype),
        scratch_shapes=[pltpu.SemaphoreType.DMA((2,))],
        compiler_params=PARAMS,
        cost_estimate=pl.CostEstimate(
            flops=0, bytes_accessed=8 * count * head_dim, transcendentals=0
        ),
    )(numbers, key_weights, value_weights)


def assemble_kernel(chip, *refs):
    pieces, out_ref, sems = refs[: RING + 1], refs[RING + 1], refs[RING + 2]
    rows, both = pieces[0].shape
    count = rows // RING
    z, y, x, core = (chip[CHIP + i] for i in range(4))
    copies = []
    for b in range(RING):
        for a in range(RING):
            from_z = (z - jnp.where(core == 0, a, b) + RING) % RING
            from_y = (y - jnp.where(core == 0, b, a) + RING) % RING
            o = (x - from_z + RING) % RING
            start = ((o * 2 + ((from_y >> 1) ^ core)) * 2 + from_y % 2) * count
            target = out_ref.at[pl.ds(pl.multiple_of(start, count), count)]
            if b == 2:
                source = pieces[3 + a // 2].at[pl.ds(a % 2 * count, count)]
            else:
                source = pieces[min(b, 2)].at[pl.ds(a * count, count)]
            copies.append(pltpu.make_async_copy(source, target, sems.at[b, a]))
    for copy in copies:
        copy.start()
    for copy in copies:
        copy.wait()


def assemble(chip, pieces):
    rows, both = pieces[0].shape
    return pl.pallas_call(
        assemble_kernel,
        in_specs=[SMEM] + [ANY] * (RING + 1),
        out_specs=VMEM,
        out_shape=jax.ShapeDtypeStruct((RING * rows, both), pieces[0].dtype),
        scratch_shapes=[pltpu.SemaphoreType.DMA((RING, RING))],
        compiler_params=PARAMS,
        cost_estimate=pl.CostEstimate(
            flops=0, bytes_accessed=4 * RING * rows * both, transcendentals=0
        ),
    )(chip, *pieces)


def finish_kernel(total_ref, gain_ref, key_value_ref):
    head_dim = gain_ref.shape[1]
    raw = total_ref[:, :head_dim]
    keys = (raw * rms_factor(raw) * gain_ref[...]).astype(jnp.bfloat16)
    key_value_ref[:, :head_dim] = keys
    key_value_ref[:, head_dim:] = total_ref[:, head_dim:].astype(jnp.bfloat16)


def finish(total, gain):
    return pl.pallas_call(
        finish_kernel,
        in_specs=[VMEM] * 2,
        out_specs=VMEM,
        out_shape=jax.ShapeDtypeStruct(total.shape, jnp.bfloat16),
        compiler_params=PARAMS,
        cost_estimate=pl.CostEstimate(
            flops=3 * total.size, bytes_accessed=6 * total.size, transcendentals=total.shape[0]
        ),
    )(total, gain[None, :])


def turn_kernel(base, numbers, total_ref, grad_ref, other_ref, gain_ref, out_ref):
    head_dim = gain_ref.shape[1]
    grad = jnp.where(numbers[base + 2] != 0, other_ref[...], grad_ref[...])
    raw = total_ref[:, :head_dim]
    d_raw = norm_back(raw, rms_factor(raw), gain_ref[...], grad[:, :head_dim].astype(jnp.float32))
    out_ref[:, :head_dim] = d_raw.astype(jnp.bfloat16)
    out_ref[:, head_dim:] = grad[:, head_dim:]


def turn(base, numbers, total, grad, other, gain):
    return pl.pallas_call(
        functools.partial(turn_kernel, base),
        in_specs=[SMEM] + [VMEM] * 4,
        out_specs=VMEM,
        out_shape=jax.ShapeDtypeStruct(grad.shape, jnp.bfloat16),
        compiler_params=PARAMS,
        cost_estimate=pl.CostEstimate(
            flops=6 * grad.size, bytes_accessed=8 * grad.size, transcendentals=grad.shape[0]
        ),
    )(numbers, total, grad, other, gain[None, :])


def first_part_kernel(*refs):
    sources, (grads_ref, out_ref) = refs[:-2], refs[-2:]
    depth = sources[0].shape[1]
    for k, source in enumerate(sources):
        out_ref[k * depth : (k + 1) * depth] = matmul(source[...], grads_ref[...], ((0,), (0,)))


def first_part(feats, grads):
    rows, depth = feats[0].shape
    both = grads.shape[1]
    return pl.pallas_call(
        first_part_kernel,
        in_specs=[VMEM] * (len(feats) + 1),
        out_specs=VMEM,
        out_shape=jax.ShapeDtypeStruct((len(feats) * depth, both), jnp.float32),
        compiler_params=PARAMS,
        cost_estimate=pl.CostEstimate(
            flops=2 * len(feats) * rows * depth * both,
            bytes_accessed=2 * len(feats) * rows * depth,
            transcendentals=0,
        ),
    )(*feats, grads)


def product_kernel(chip, *refs):
    sources, (grads_ref, part_ref), refs = refs[: 2 * RING], refs[2 * RING : 2 * RING + 2], refs[2 * RING + 2 :]
    outs, (held, sems) = refs[:RING], refs[RING:]
    depth = sources[0].shape[1]
    count = depth // 2
    z, y, x, core = (chip[CHIP + i] for i in range(4))
    for k, source in enumerate(sources):
        total = matmul(source[...], grads_ref[...], ((0,), (0,)))
        total = (total + part_ref[k * depth : (k + 1) * depth]).astype(held.dtype)
        by_z = (x - k // 2 - z + 2 * RING) % RING
        for h in range(2):
            by_y = (2 * (k % 2 ^ core) + h - y + RING) % RING
            outer_by = jnp.where(core == 0, by_y, by_z)
            inner_by = jnp.where(core == 0, by_z, by_y)
            start = pl.multiple_of(inner_by * count, count)
            held[outer_by, pl.ds(start, count)] = total[h * count : (h + 1) * count]
    copies = [pltpu.make_async_copy(held.at[k], outs[k], sems.at[k]) for k in range(RING)]
    for copy in copies:
        copy.start()
    for copy in copies:
        copy.wait()


def product(chip, feats, grads, part):
    rows, depth = feats[0].shape
    both = grads.shape[1]
    shape = (RING * depth // 2, both)
    return pl.pallas_call(
        product_kernel,
        in_specs=[SMEM] + [VMEM] * (len(feats) + 2),
        out_specs=[ANY] * RING,
        out_shape=[jax.ShapeDtypeStruct(shape, jnp.bfloat16)] * RING,
        scratch_shapes=[
            pltpu.VMEM((RING, *shape), jnp.bfloat16),
            pltpu.SemaphoreType.DMA((RING,)),
        ],
        compiler_params=PARAMS,
        cost_estimate=pl.CostEstimate(
            flops=2 * len(feats) * rows * depth * both,
            bytes_accessed=2 * len(feats) * rows * depth,
            transcendentals=0,
        ),
    )(chip, *feats, grads, part)


def attend_kernel(heads, base, index, ratio_ref, q_ref, cot_ref, kv_ref, away_ref, gain_ref, *refs):
    context_ref, d_query_ref, d_kv_ref, d_key_sum, d_value_sum = refs[-5:]
    step = pl.program_id(0)
    head_dim = gain_ref.shape[1]
    scale = head_dim ** (-0.5)
    count = index[base + 1]
    ratio = ratio_ref[0]
    gain = gain_ref[...]
    key_value = jnp.where(index[base + 2] != 0, away_ref[...], kv_ref[...])
    keys = key_value[:, :head_dim]
    vals = key_value[:, head_dim:]

    def stacked(ref):
        parts = [ref[0, :, h * head_dim : (h + 1) * head_dim] for h in range(heads)]
        return jnp.concatenate(parts, axis=0).astype(jnp.float32)

    def unstacked(ref, rows):
        text = rows.shape[0] // heads
        for h in range(heads):
            part = rows[h * text : (h + 1) * text]
            ref[0, :, h * head_dim : (h + 1) * head_dim] = part.astype(ref.dtype)

    @pl.when(step == 0)
    def _():
        d_key_sum[...] = jnp.zeros_like(d_key_sum)
        d_value_sum[...] = jnp.zeros_like(d_value_sum)

    q_raw = stacked(q_ref)
    q_factor = rms_factor(q_raw)
    q_norm = (q_raw * q_factor * gain).astype(jnp.bfloat16)
    raw = matmul(q_norm, keys, ((1,), (1,))) * scale
    place = lax.broadcasted_iota(jnp.int32, raw.shape, 1)
    expo = jnp.where(place < count * TILE, jnp.exp(raw), 0.0)
    total = jnp.sum(expo, axis=1, keepdims=True) + (count == 0).astype(jnp.float32)
    inverse = 1.0 / total
    weights_b = expo.astype(jnp.bfloat16)
    attended = matmul(weights_b, vals, ((1,), (0,))) * inverse
    unstacked(context_ref, ratio * attended)
    d_att = ratio * stacked(cot_ref)
    d_att_b = d_att.astype(jnp.bfloat16)
    scaled_b = (d_att * inverse).astype(jnp.bfloat16)
    delta = jnp.sum(d_att * attended, axis=1, keepdims=True)
    d_prob = matmul(d_att_b, vals, ((1,), (1,)))
    d_score = (expo * inverse * (d_prob - delta)).astype(jnp.bfloat16)
    d_qn = scale * matmul(d_score, keys, ((1,), (0,)))
    unstacked(d_query_ref, norm_back(q_raw, q_factor, gain, d_qn))
    d_key_sum[...] += matmul(d_score, q_norm, ((0,), (0,)))
    d_value_sum[...] += matmul(weights_b, scaled_b, ((0,), (0,)))

    @pl.when(step == pl.num_programs(0) - 1)
    def _():
        d_kv_ref[:, :head_dim] = (scale * d_key_sum[...]).astype(d_kv_ref.dtype)
        d_kv_ref[:, head_dim:] = d_value_sum[...].astype(d_kv_ref.dtype)


def attend(base, index, ratio, query, cot, key_value, away, gain, earlier, heads=2):
    rows, both = key_value.shape
    head_dim = both // 2
    text = query.shape[1]
    width = heads * head_dim
    block = pl.BlockSpec((1, text, width), lambda h, index: (index[base], 0, h))
    whole = lambda shape: pl.BlockSpec(shape, lambda h, index: (0, 0))
    in_specs = [
        pl.BlockSpec(memory_space=pltpu.SMEM),
        block,
        block,
        whole((rows, both)),
        whole((rows, both)),
        whole((1, head_dim)),
    ]
    aliases = {}
    if earlier:
        in_specs += [pl.BlockSpec(memory_space=pl.ANY)] * 2
        aliases = {7: 0, 8: 1}
    steps = query.shape[2] // width
    return pl.pallas_call(
        functools.partial(attend_kernel, heads, base),
        grid_spec=pltpu.PrefetchScalarGridSpec(
            num_scalar_prefetch=1,
            grid=(steps,),
            in_specs=in_specs,
            out_specs=[block, block, whole((rows, both))],
            scratch_shapes=[pltpu.VMEM((rows, head_dim), jnp.float32)] * 2,
        ),
        out_shape=[
            jax.ShapeDtypeStruct(query.shape, jnp.bfloat16),
            jax.ShapeDtypeStruct(query.shape, jnp.bfloat16),
            jax.ShapeDtypeStruct((rows, both), jnp.bfloat16),
        ],
        input_output_aliases=aliases,
        compiler_params=pltpu.CompilerParams(
            vmem_limit_bytes=24 * 1024 * 1024
        ),
        cost_estimate=pl.CostEstimate(
            flops=14 * steps * heads * text * rows * head_dim,
            bytes_accessed=8 * text * steps * width + 6 * rows * head_dim,
            transcendentals=steps * heads * text * rows,
        ),
    )(
        index,
        ratio,
        query,
        cot,
        key_value,
        away,
        gain[None, :],
        *earlier,
    )


def per_device(
    query,
    image,
    tiles,
    image_slot,
    key_weight_matrix,
    value_weight_matrix,
    query_gain,
    key_gain,
    gate,
    cotangent,
):
    ratio = jnp.tanh(gate)
    numbers, far_own, near_own = route(tiles, image_slot, image)

    def opposite(after, before, move):
        half = after.shape[0] // 2
        return [move(after[:half], 1), move(before[half:], 3)]

    shard = lay(numbers, key_weight_matrix, value_weight_matrix)
    far_x = [along_x(far_own, 1), along_x(far_own, 3)]
    shard = jnp.concatenate(gathered(shard, inner), axis=0)
    shard, *far_x = lax.optimization_barrier((shard, *far_x))
    far_halves = opposite(*far_x, along_x)
    pieces = [outer(shard, 1), outer(shard, 3)]
    near_own, *blocks = lax.optimization_barrier((near_own, *far_halves, *pieces))
    far_halves, pieces = blocks[:2], blocks[2:]
    near_x = [along_x(near_own, 1), along_x(near_own, 3)]
    weights = assemble(numbers, [shard, *pieces, *opposite(*pieces, outer)])
    weights, *far_blocks = lax.optimization_barrier((weights, *far_x, *far_halves))

    def other_cores(*blocks):
        return [other_core(block) for block in blocks]

    def paired(own, other, after, before, opposite, after_other, before_other, opposite_other):
        return [own, other, after, after_other, opposite, opposite_other, before, before_other]

    def project(feats):
        depth = feats[0].shape[1]
        total = None
        for o in (0, 1, 3, 2):
            for k in (2 * o, 2 * o + 1):
                part = matmul(feats[k], weights[k * depth : (k + 1) * depth], ((1,), (0,)))
                total = part if total is None else total + part
        return total

    shared = (numbers, ratio, query, cotangent)
    after, before, *halves = far_blocks
    blocks = [after, before, jnp.concatenate(halves, axis=0)]
    far_feats = paired(far_own, other_core(far_own), *blocks, *other_cores(*blocks))
    far_total = project(far_feats)
    far_key_value = finish(far_total, key_gain)
    away = along_z(far_key_value, RING // 2)
    _, near_own, *near_x = lax.optimization_barrier((far_key_value, near_own, *near_x))
    near_halves = opposite(*near_x, along_x)
    near_others = other_cores(*near_x)
    *earlier, far_grad = attend(FAR, *shared, far_key_value, away, query_gain, ())
    back = along_z(far_grad, RING // 2)

    _, *near_halves = lax.optimization_barrier((far_grad, *near_halves))
    blocks = [*near_x, jnp.concatenate(near_halves, axis=0)]
    near_others.append(other_core(blocks[2]))
    near_feats = paired(near_own, other_core(near_own), *blocks, *near_others)
    near_total = project(near_feats)
    near_key_value = finish(near_total, key_gain)
    context, d_query, near_grad = attend(
        NEAR, *shared, near_key_value, near_key_value, query_gain, earlier
    )
    near_rows = turn(NEAR, numbers, near_total, near_grad, near_grad, key_gain)
    back, near_rows = lax.optimization_barrier((back, near_rows))
    far_rows = turn(FAR, numbers, far_total, far_grad, back, key_gain)
    part = first_part(far_feats, far_rows)

    blocks = product(numbers, near_feats, near_rows, part)
    total = summed([blocks[0], *scattered(blocks, outer)])
    count = total.shape[0] // RING
    parts = [total[d * count : (d + 1) * count] for d in range(RING)]
    sent = [None] + [part.astype(jnp.bfloat16) for part in parts[1:]]
    share = summed([parts[0], *scattered(sent, inner)])
    head_dim = query_gain.shape[0]
    return (context, d_query, share[:, :head_dim], share[:, head_dim:])


def solution(mesh):
    placed = (
        P("dp", None, "tensor"),
        P("dp", None, "tensor"),
        P(),
        P(),
        P("dp", "tensor"),
        P("dp", "tensor"),
        P(),
        P(),
        P(),
        P("dp", None, "tensor"),
    )
    return jax.shard_map(
        per_device,
        mesh=mesh,
        in_specs=placed,
        out_specs=(
            P("dp", None, "tensor"),
            P("dp", None, "tensor"),
            P("dp", "tensor"),
            P("dp", "tensor"),
        ),
        check_vma=False,
    )
```

```python
import functools

import jax
import jax.numpy as jnp
from jax import lax
from jax.experimental import pallas as pl
from jax.experimental.pallas import tpu as pltpu
from jax.sharding import PartitionSpec as P

TILE = 128
RING = 4
EPS = 1e-06


def along_z(x, step):
    pairs = [(z * RING + y, (z + step) % RING * RING + y) for z in range(RING) for y in range(RING)]
    return lax.ppermute(x, "dp", pairs)


def by_core(x, step, z_core):
    pairs = []
    for z in range(RING):
        for y in range(RING):
            for i in range(RING):
                for c in range(2):
                    to_z, to_y = (z + step, y) if c == z_core else (z, y + step)
                    source = (z * RING + y) * 2 * RING + i * 2 + c
                    target = (to_z % RING * RING + to_y % RING) * 2 * RING + i * 2 + c
                    pairs.append((source, target))
    return lax.ppermute(x, ("dp", "tensor"), pairs)


def inner(x, step):
    return by_core(x, step, 0)


def outer(x, step):
    return by_core(x, step, 1)


def along_x(x, step):
    pairs = [(i * 2 + c, (i + step) % RING * 2 + c) for i in range(RING) for c in range(2)]
    return lax.ppermute(x, "tensor", pairs)


def other_core(x):
    return lax.ppermute(x, "tensor", [(i, i ^ 1) for i in range(2 * RING)])


def gathered(block, move):
    far, after, before = (move(block, step) for step in (2, 1, 3))
    return [block, after, far, before]


def scattered(parts, move):
    return [move(parts[step], step) for step in (2, 1, 3)]


def summed(blocks):
    total = blocks[0].astype(jnp.float32)
    for block in blocks[1:]:
        total = total + block.astype(jnp.float32)
    return total


def rms_factor(values):
    return lax.rsqrt(jnp.mean(values * values, axis=-1, keepdims=True) + EPS)


def norm_back(values, norm_multiplier, gain, grad):
    weighted = grad * gain
    inner = jnp.sum(weighted * values, axis=-1, keepdims=True)
    return (
        norm_multiplier * weighted
        - values * (norm_multiplier * norm_multiplier * norm_multiplier) * inner / values.shape[-1]
    )


def matmul(a, b, contract):
    return lax.dot_general(a, b, (contract, ((), ())), preferred_element_type=jnp.float32)


VMEM = pl.BlockSpec(memory_space=pltpu.VMEM)
SMEM = pl.BlockSpec(memory_space=pltpu.SMEM)
ANY = pl.BlockSpec(memory_space=pl.ANY)
HBM = pl.BlockSpec(memory_space=pltpu.HBM)
PARAMS = pltpu.CompilerParams(vmem_limit_bytes=16 * 1024 * 1024)


NEAR, FAR, CHIP = 0, 3, 6


def route_kernel(tiles, slots, image_ref, numbers, far_ref, near_ref, sems):
    rank, place = lax.axis_index("dp"), lax.axis_index("tensor")
    first = 2 * rank
    homes = (slots[first], slots[first + 1])
    away = [
        jnp.logical_and(homes[0] != first + i, homes[1] != first + i) for i in range(2)
    ]
    swaps = jnp.logical_or(away[0], away[1])
    far_slot = jnp.where(away[1], 1, 0)
    copies = []
    for i, (slot, target) in enumerate(((far_slot, far_ref), (1 - far_slot, near_ref))):
        copies.append(pltpu.make_async_copy(image_ref.at[slot], target, sems.at[i]))
        copies[i].start()
    of_slot = jnp.where(homes[1] == first + far_slot, 1, 0)
    far_own = jnp.where(swaps, jnp.where(homes[1] >> 1 != rank, 1, 0), of_slot)
    numbers[NEAR] = 1 - far_own
    numbers[NEAR + 1] = tiles[first + 1 - far_own]
    numbers[NEAR + 2] = 0
    numbers[FAR] = far_own
    numbers[FAR + 1] = tiles[first + far_own]
    numbers[FAR + 2] = jnp.where(swaps, 1, 0)
    numbers[CHIP] = rank // RING
    numbers[CHIP + 1] = rank % RING
    numbers[CHIP + 2] = place // 2
    numbers[CHIP + 3] = place % 2
    for copy in copies:
        copy.wait()


def route(tiles, image_slot, image):
    rows = jax.ShapeDtypeStruct(image.shape[1:], image.dtype)
    return pl.pallas_call(
        route_kernel,
        in_specs=[SMEM, SMEM, HBM],
        out_specs=[SMEM, VMEM, VMEM],
        out_shape=[jax.ShapeDtypeStruct((CHIP + 4,), jnp.int32), rows, rows],
        scratch_shapes=[pltpu.SemaphoreType.DMA((2,))],
        compiler_params=pltpu.CompilerParams(vmem_limit_bytes=60 * 1024 * 1024),
        cost_estimate=pl.CostEstimate(flops=0, bytes_accessed=4 * image.size, transcendentals=0),
    )(tiles, image_slot, image)


def lay_kernel(numbers, key_ref, value_ref, out_ref, sems):
    head_dim = key_ref.shape[1]
    copies = []
    for i, source in enumerate((key_ref, value_ref)):
        target = out_ref.at[:, pl.ds(i * head_dim, head_dim)]
        copies.append(pltpu.make_async_copy(source, target, sems.at[i]))
        copies[i].start()
    for copy in copies:
        copy.wait()


def lay(numbers, key_weights, value_weights):
    count, head_dim = key_weights.shape
    return pl.pallas_call(
        lay_kernel,
        in_specs=[SMEM, ANY, ANY],
        out_specs=VMEM,
        out_shape=jax.ShapeDtypeStruct((count, 2 * head_dim), key_weights.dtype),
        scratch_shapes=[pltpu.SemaphoreType.DMA((2,))],
        compiler_params=PARAMS,
        cost_estimate=pl.CostEstimate(
            flops=0, bytes_accessed=8 * count * head_dim, transcendentals=0
        ),
    )(numbers, key_weights, value_weights)


def assemble_kernel(chip, *refs):
    pieces, out_ref, sems = refs[:RING], refs[RING], refs[RING + 1]
    rows, both = pieces[0].shape
    count = rows // RING
    z, y, x, core = (chip[CHIP + i] for i in range(4))
    copies = []
    for b in range(RING):
        for a in range(RING):
            from_z = (z - jnp.where(core == 0, a, b) + RING) % RING
            from_y = (y - jnp.where(core == 0, b, a) + RING) % RING
            o = (x - from_z + RING) % RING
            start = ((o * 2 + ((from_y >> 1) ^ core)) * 2 + from_y % 2) * count
            target = out_ref.at[pl.ds(pl.multiple_of(start, count), count)]
            source = pieces[b].at[pl.ds(a * count, count)]
            copies.append(pltpu.make_async_copy(source, target, sems.at[b, a]))
    for copy in copies:
        copy.start()
    for copy in copies:
        copy.wait()


def assemble(chip, pieces):
    rows, both = pieces[0].shape
    return pl.pallas_call(
        assemble_kernel,
        in_specs=[SMEM] + [ANY] * RING,
        out_specs=VMEM,
        out_shape=jax.ShapeDtypeStruct((RING * rows, both), pieces[0].dtype),
        scratch_shapes=[pltpu.SemaphoreType.DMA((RING, RING))],
        compiler_params=PARAMS,
        cost_estimate=pl.CostEstimate(
            flops=0, bytes_accessed=4 * RING * rows * both, transcendentals=0
        ),
    )(chip, *pieces)


def finish_kernel(total_ref, gain_ref, key_value_ref):
    head_dim = gain_ref.shape[1]
    raw = total_ref[:, :head_dim]
    keys = (raw * rms_factor(raw) * gain_ref[...]).astype(jnp.bfloat16)
    key_value_ref[:, :head_dim] = keys
    key_value_ref[:, head_dim:] = total_ref[:, head_dim:].astype(jnp.bfloat16)


def finish(total, gain):
    return pl.pallas_call(
        finish_kernel,
        in_specs=[VMEM] * 2,
        out_specs=VMEM,
        out_shape=jax.ShapeDtypeStruct(total.shape, jnp.bfloat16),
        compiler_params=PARAMS,
        cost_estimate=pl.CostEstimate(
            flops=3 * total.size, bytes_accessed=6 * total.size, transcendentals=total.shape[0]
        ),
    )(total, gain[None, :])


def turn_kernel(base, numbers, total_ref, grad_ref, other_ref, gain_ref, out_ref):
    head_dim = gain_ref.shape[1]
    grad = jnp.where(numbers[base + 2] != 0, other_ref[...], grad_ref[...])
    raw = total_ref[:, :head_dim]
    d_raw = norm_back(raw, rms_factor(raw), gain_ref[...], grad[:, :head_dim].astype(jnp.float32))
    out_ref[:, :head_dim] = d_raw.astype(jnp.bfloat16)
    out_ref[:, head_dim:] = grad[:, head_dim:]


def turn(base, numbers, total, grad, other, gain):
    return pl.pallas_call(
        functools.partial(turn_kernel, base),
        in_specs=[SMEM] + [VMEM] * 4,
        out_specs=VMEM,
        out_shape=jax.ShapeDtypeStruct(grad.shape, jnp.bfloat16),
        compiler_params=PARAMS,
        cost_estimate=pl.CostEstimate(
            flops=6 * grad.size, bytes_accessed=8 * grad.size, transcendentals=grad.shape[0]
        ),
    )(numbers, total, grad, other, gain[None, :])


def first_part_kernel(*refs):
    sources, (grads_ref, out_ref) = refs[:-2], refs[-2:]
    depth = sources[0].shape[1]
    for k, source in enumerate(sources):
        out_ref[k * depth : (k + 1) * depth] = matmul(source[...], grads_ref[...], ((0,), (0,)))


def first_part(feats, grads):
    rows, depth = feats[0].shape
    both = grads.shape[1]
    return pl.pallas_call(
        first_part_kernel,
        in_specs=[VMEM] * (len(feats) + 1),
        out_specs=VMEM,
        out_shape=jax.ShapeDtypeStruct((len(feats) * depth, both), jnp.float32),
        compiler_params=PARAMS,
        cost_estimate=pl.CostEstimate(
            flops=2 * len(feats) * rows * depth * both,
            bytes_accessed=2 * len(feats) * rows * depth,
            transcendentals=0,
        ),
    )(*feats, grads)


def product_kernel(chip, *refs):
    sources, (grads_ref, part_ref), refs = refs[: 2 * RING], refs[2 * RING : 2 * RING + 2], refs[2 * RING + 2 :]
    outs, (held, sems) = refs[:RING], refs[RING:]
    depth = sources[0].shape[1]
    count = depth // 2
    z, y, x, core = (chip[CHIP + i] for i in range(4))
    for k, source in enumerate(sources):
        total = matmul(source[...], grads_ref[...], ((0,), (0,)))
        total = (total + part_ref[k * depth : (k + 1) * depth]).astype(held.dtype)
        by_z = (x - k // 2 - z + 2 * RING) % RING
        for h in range(2):
            by_y = (2 * (k % 2 ^ core) + h - y + RING) % RING
            outer_by = jnp.where(core == 0, by_y, by_z)
            inner_by = jnp.where(core == 0, by_z, by_y)
            start = pl.multiple_of(inner_by * count, count)
            held[outer_by, pl.ds(start, count)] = total[h * count : (h + 1) * count]
    copies = [pltpu.make_async_copy(held.at[k], outs[k], sems.at[k]) for k in range(RING)]
    for copy in copies:
        copy.start()
    for copy in copies:
        copy.wait()


def product(chip, feats, grads, part):
    rows, depth = feats[0].shape
    both = grads.shape[1]
    shape = (RING * depth // 2, both)
    return pl.pallas_call(
        product_kernel,
        in_specs=[SMEM] + [VMEM] * (len(feats) + 2),
        out_specs=[ANY] * RING,
        out_shape=[jax.ShapeDtypeStruct(shape, jnp.bfloat16)] * RING,
        scratch_shapes=[
            pltpu.VMEM((RING, *shape), jnp.bfloat16),
            pltpu.SemaphoreType.DMA((RING,)),
        ],
        compiler_params=PARAMS,
        cost_estimate=pl.CostEstimate(
            flops=2 * len(feats) * rows * depth * both,
            bytes_accessed=2 * len(feats) * rows * depth,
            transcendentals=0,
        ),
    )(chip, *feats, grads, part)


def attend_kernel(heads, base, index, ratio_ref, q_ref, cot_ref, kv_ref, away_ref, gain_ref, *refs):
    context_ref, d_query_ref, d_kv_ref, d_key_sum, d_value_sum = refs[-5:]
    step = pl.program_id(0)
    head_dim = gain_ref.shape[1]
    scale = head_dim ** (-0.5)
    count = index[base + 1]
    ratio = ratio_ref[0]
    gain = gain_ref[...]
    key_value = jnp.where(index[base + 2] != 0, away_ref[...], kv_ref[...])
    keys = key_value[:, :head_dim]
    vals = key_value[:, head_dim:]

    def stacked(ref):
        parts = [ref[0, :, h * head_dim : (h + 1) * head_dim] for h in range(heads)]
        return jnp.concatenate(parts, axis=0).astype(jnp.float32)

    def unstacked(ref, rows):
        text = rows.shape[0] // heads
        for h in range(heads):
            part = rows[h * text : (h + 1) * text]
            ref[0, :, h * head_dim : (h + 1) * head_dim] = part.astype(ref.dtype)

    @pl.when(step == 0)
    def _():
        d_key_sum[...] = jnp.zeros_like(d_key_sum)
        d_value_sum[...] = jnp.zeros_like(d_value_sum)

    q_raw = stacked(q_ref)
    q_factor = rms_factor(q_raw)
    q_norm = (q_raw * q_factor * gain).astype(jnp.bfloat16)
    raw = matmul(q_norm, keys, ((1,), (1,))) * scale
    place = lax.broadcasted_iota(jnp.int32, raw.shape, 1)
    expo = jnp.where(place < count * TILE, jnp.exp(raw), 0.0)
    total = jnp.sum(expo, axis=1, keepdims=True) + (count == 0).astype(jnp.float32)
    inverse = 1.0 / total
    weights_b = expo.astype(jnp.bfloat16)
    attended = matmul(weights_b, vals, ((1,), (0,))) * inverse
    unstacked(context_ref, ratio * attended)
    d_att = ratio * stacked(cot_ref)
    d_att_b = d_att.astype(jnp.bfloat16)
    scaled_b = (d_att * inverse).astype(jnp.bfloat16)
    delta = jnp.sum(d_att * attended, axis=1, keepdims=True)
    d_prob = matmul(d_att_b, vals, ((1,), (1,)))
    d_score = (expo * inverse * (d_prob - delta)).astype(jnp.bfloat16)
    d_qn = scale * matmul(d_score, keys, ((1,), (0,)))
    unstacked(d_query_ref, norm_back(q_raw, q_factor, gain, d_qn))
    d_key_sum[...] += matmul(d_score, q_norm, ((0,), (0,)))
    d_value_sum[...] += matmul(weights_b, scaled_b, ((0,), (0,)))

    @pl.when(step == pl.num_programs(0) - 1)
    def _():
        d_kv_ref[:, :head_dim] = (scale * d_key_sum[...]).astype(d_kv_ref.dtype)
        d_kv_ref[:, head_dim:] = d_value_sum[...].astype(d_kv_ref.dtype)


def attend(base, index, ratio, query, cot, key_value, away, gain, earlier, heads=2):
    rows, both = key_value.shape
    head_dim = both // 2
    text = query.shape[1]
    width = heads * head_dim
    block = pl.BlockSpec((1, text, width), lambda h, index: (index[base], 0, h))
    whole = lambda shape: pl.BlockSpec(shape, lambda h, index: (0, 0))
    in_specs = [
        pl.BlockSpec(memory_space=pltpu.SMEM),
        block,
        block,
        whole((rows, both)),
        whole((rows, both)),
        whole((1, head_dim)),
    ]
    aliases = {}
    if earlier:
        in_specs += [pl.BlockSpec(memory_space=pl.ANY)] * 2
        aliases = {7: 0, 8: 1}
    steps = query.shape[2] // width
    return pl.pallas_call(
        functools.partial(attend_kernel, heads, base),
        grid_spec=pltpu.PrefetchScalarGridSpec(
            num_scalar_prefetch=1,
            grid=(steps,),
            in_specs=in_specs,
            out_specs=[block, block, whole((rows, both))],
            scratch_shapes=[pltpu.VMEM((rows, head_dim), jnp.float32)] * 2,
        ),
        out_shape=[
            jax.ShapeDtypeStruct(query.shape, jnp.bfloat16),
            jax.ShapeDtypeStruct(query.shape, jnp.bfloat16),
            jax.ShapeDtypeStruct((rows, both), jnp.bfloat16),
        ],
        input_output_aliases=aliases,
        compiler_params=pltpu.CompilerParams(
            vmem_limit_bytes=24 * 1024 * 1024
        ),
        cost_estimate=pl.CostEstimate(
            flops=14 * steps * heads * text * rows * head_dim,
            bytes_accessed=8 * text * steps * width + 6 * rows * head_dim,
            transcendentals=steps * heads * text * rows,
        ),
    )(
        index,
        ratio,
        query,
        cot,
        key_value,
        away,
        gain[None, :],
        *earlier,
    )


def per_device(
    query,
    image,
    tiles,
    image_slot,
    key_weight_matrix,
    value_weight_matrix,
    query_gain,
    key_gain,
    gate,
    cotangent,
):
    ratio = jnp.tanh(gate)
    numbers, far_own, near_own = route(tiles, image_slot, image)

    def opposite(after, before, move):
        half = after.shape[0] // 2
        return [move(after[:half], 1), move(before[half:], 3)]

    shard = lay(numbers, key_weight_matrix, value_weight_matrix)
    far_x = [along_x(far_own, 1), along_x(far_own, 3)]
    shard = jnp.concatenate(gathered(shard, inner), axis=0)
    shard, *far_x = lax.optimization_barrier((shard, *far_x))
    far_halves = opposite(*far_x, along_x)
    pieces = gathered(shard, outer)
    near_own, far_own, *far_halves = lax.optimization_barrier((near_own, far_own, *far_halves))
    near_x = [along_x(near_own, 1), along_x(near_own, 3)]
    weights = assemble(numbers, pieces)
    weights, *far_blocks = lax.optimization_barrier((weights, *far_x, *far_halves))

    def other_cores(*blocks):
        return [other_core(block) for block in blocks]

    def paired(own, other, after, before, opposite, after_other, before_other, opposite_other):
        return [own, other, after, after_other, opposite, opposite_other, before, before_other]

    def project(feats):
        depth = feats[0].shape[1]
        total = None
        for o in (0, 1, 3, 2):
            for k in (2 * o, 2 * o + 1):
                part = matmul(feats[k], weights[k * depth : (k + 1) * depth], ((1,), (0,)))
                total = part if total is None else total + part
        return total

    shared = (numbers, ratio, query, cotangent)
    after, before, *halves = far_blocks
    blocks = [after, before, jnp.concatenate(halves, axis=0)]
    far_feats = paired(far_own, other_core(far_own), *blocks, *other_cores(*blocks))
    far_total = project(far_feats)
    far_key_value = finish(far_total, key_gain)
    away = along_z(far_key_value, RING // 2)
    _, near_own, *near_x = lax.optimization_barrier((far_key_value, near_own, *near_x))
    near_halves = opposite(*near_x, along_x)
    near_others = other_cores(*near_x)
    *earlier, far_grad = attend(FAR, *shared, far_key_value, away, query_gain, ())
    back = along_z(far_grad, RING // 2)

    back, *near_halves = lax.optimization_barrier((back, *near_halves))
    blocks = [*near_x, jnp.concatenate(near_halves, axis=0)]
    near_others.append(other_core(blocks[2]))
    near_feats = paired(near_own, other_core(near_own), *blocks, *near_others)
    near_total = project(near_feats)
    near_key_value = finish(near_total, key_gain)
    context, d_query, near_grad = attend(
        NEAR, *shared, near_key_value, near_key_value, query_gain, earlier
    )
    near_rows = turn(NEAR, numbers, near_total, near_grad, near_grad, key_gain)
    far_rows = turn(FAR, numbers, far_total, far_grad, back, key_gain)
    part = first_part(far_feats, far_rows)

    blocks = product(numbers, near_feats, near_rows, part)
    total = summed([blocks[0], *scattered(blocks, outer)])
    count = total.shape[0] // RING
    parts = [total[d * count : (d + 1) * count] for d in range(RING)]
    sent = [None] + [part.astype(jnp.bfloat16) for part in parts[1:]]
    share = summed([parts[0], *scattered(sent, inner)])
    head_dim = query_gain.shape[0]
    return (context, d_query, share[:, :head_dim], share[:, head_dim:])


def solution(mesh):
    placed = (
        P("dp", None, "tensor"),
        P("dp", None, "tensor"),
        P(),
        P(),
        P("dp", "tensor"),
        P("dp", "tensor"),
        P(),
        P(),
        P(),
        P("dp", None, "tensor"),
    )
    return jax.shard_map(
        per_device,
        mesh=mesh,
        in_specs=placed,
        out_specs=(
            P("dp", None, "tensor"),
            P("dp", None, "tensor"),
            P("dp", "tensor"),
            P("dp", "tensor"),
        ),
        check_vma=False,
    )
```

```python
import functools

import jax
import jax.numpy as jnp
from jax import lax
from jax.experimental import pallas as pl
from jax.experimental.pallas import tpu as pltpu
from jax.sharding import PartitionSpec as P

TILE = 128
RING = 4
EPS = 1e-06


def along_z(x, step):
    pairs = [(z * RING + y, (z + step) % RING * RING + y) for z in range(RING) for y in range(RING)]
    return lax.ppermute(x, "dp", pairs)


def by_core(x, step, z_core):
    pairs = []
    for z in range(RING):
        for y in range(RING):
            for i in range(RING):
                for c in range(2):
                    to_z, to_y = (z + step, y) if c == z_core else (z, y + step)
                    source = (z * RING + y) * 2 * RING + i * 2 + c
                    target = (to_z % RING * RING + to_y % RING) * 2 * RING + i * 2 + c
                    pairs.append((source, target))
    return lax.ppermute(x, ("dp", "tensor"), pairs)


def inner(x, step):
    return by_core(x, step, 0)


def outer(x, step):
    return by_core(x, step, 1)


def along_x(x, step):
    pairs = [(i * 2 + c, (i + step) % RING * 2 + c) for i in range(RING) for c in range(2)]
    return lax.ppermute(x, "tensor", pairs)


def other_core(x):
    return lax.ppermute(x, "tensor", [(i, i ^ 1) for i in range(2 * RING)])


def gathered(block, move):
    far, after, before = (move(block, step) for step in (2, 1, 3))
    return [block, after, far, before]


def scattered(parts, move):
    return [move(parts[step], step) for step in (2, 1, 3)]


def summed(blocks):
    total = blocks[0].astype(jnp.float32)
    for block in blocks[1:]:
        total = total + block.astype(jnp.float32)
    return total


def rms_factor(values):
    return lax.rsqrt(jnp.mean(values * values, axis=-1, keepdims=True) + EPS)


def norm_back(values, norm_multiplier, gain, grad):
    weighted = grad * gain
    inner = jnp.sum(weighted * values, axis=-1, keepdims=True)
    return (
        norm_multiplier * weighted
        - values * (norm_multiplier * norm_multiplier * norm_multiplier) * inner / values.shape[-1]
    )


def matmul(a, b, contract):
    return lax.dot_general(a, b, (contract, ((), ())), preferred_element_type=jnp.float32)


VMEM = pl.BlockSpec(memory_space=pltpu.VMEM)
SMEM = pl.BlockSpec(memory_space=pltpu.SMEM)
ANY = pl.BlockSpec(memory_space=pl.ANY)
HBM = pl.BlockSpec(memory_space=pltpu.HBM)
PARAMS = pltpu.CompilerParams(vmem_limit_bytes=16 * 1024 * 1024)


NEAR, FAR, CHIP = 0, 3, 6


def route_kernel(tiles, slots, image_ref, numbers, far_ref, near_ref, sems):
    rank, place = lax.axis_index("dp"), lax.axis_index("tensor")
    first = 2 * rank
    homes = (slots[first], slots[first + 1])
    away = [
        jnp.logical_and(homes[0] != first + i, homes[1] != first + i) for i in range(2)
    ]
    swaps = jnp.logical_or(away[0], away[1])
    far_slot = jnp.where(away[1], 1, 0)
    copies = []
    for i, (slot, target) in enumerate(((far_slot, far_ref), (1 - far_slot, near_ref))):
        copies.append(pltpu.make_async_copy(image_ref.at[slot], target, sems.at[i]))
        copies[i].start()
    of_slot = jnp.where(homes[1] == first + far_slot, 1, 0)
    far_own = jnp.where(swaps, jnp.where(homes[1] >> 1 != rank, 1, 0), of_slot)
    numbers[NEAR] = 1 - far_own
    numbers[NEAR + 1] = tiles[first + 1 - far_own]
    numbers[NEAR + 2] = 0
    numbers[FAR] = far_own
    numbers[FAR + 1] = tiles[first + far_own]
    numbers[FAR + 2] = jnp.where(swaps, 1, 0)
    numbers[CHIP] = rank // RING
    numbers[CHIP + 1] = rank % RING
    numbers[CHIP + 2] = place // 2
    numbers[CHIP + 3] = place % 2
    for copy in copies:
        copy.wait()


def route(tiles, image_slot, image):
    rows = jax.ShapeDtypeStruct(image.shape[1:], image.dtype)
    return pl.pallas_call(
        route_kernel,
        in_specs=[SMEM, SMEM, HBM],
        out_specs=[SMEM, VMEM, VMEM],
        out_shape=[jax.ShapeDtypeStruct((CHIP + 4,), jnp.int32), rows, rows],
        scratch_shapes=[pltpu.SemaphoreType.DMA((2,))],
        compiler_params=pltpu.CompilerParams(vmem_limit_bytes=60 * 1024 * 1024),
        cost_estimate=pl.CostEstimate(flops=0, bytes_accessed=4 * image.size, transcendentals=0),
    )(tiles, image_slot, image)


def lay_kernel(numbers, key_ref, value_ref, out_ref, sems):
    head_dim = key_ref.shape[1]
    copies = []
    for i, source in enumerate((key_ref, value_ref)):
        target = out_ref.at[:, pl.ds(i * head_dim, head_dim)]
        copies.append(pltpu.make_async_copy(source, target, sems.at[i]))
        copies[i].start()
    for copy in copies:
        copy.wait()


def lay(numbers, key_weights, value_weights):
    count, head_dim = key_weights.shape
    return pl.pallas_call(
        lay_kernel,
        in_specs=[SMEM, ANY, ANY],
        out_specs=VMEM,
        out_shape=jax.ShapeDtypeStruct((count, 2 * head_dim), key_weights.dtype),
        scratch_shapes=[pltpu.SemaphoreType.DMA((2,))],
        compiler_params=PARAMS,
        cost_estimate=pl.CostEstimate(
            flops=0, bytes_accessed=8 * count * head_dim, transcendentals=0
        ),
    )(numbers, key_weights, value_weights)


def assemble_kernel(chip, *refs):
    pieces, out_ref, sems = refs[:RING], refs[RING], refs[RING + 1]
    rows, both = pieces[0].shape
    count = rows // RING
    z, y, x, core = (chip[CHIP + i] for i in range(4))
    copies = []
    for b in range(RING):
        for a in range(RING):
            from_z = (z - jnp.where(core == 0, a, b) + RING) % RING
            from_y = (y - jnp.where(core == 0, b, a) + RING) % RING
            o = (x - from_z + RING) % RING
            start = ((o * 2 + ((from_y >> 1) ^ core)) * 2 + from_y % 2) * count
            target = out_ref.at[pl.ds(pl.multiple_of(start, count), count)]
            source = pieces[b].at[pl.ds(a * count, count)]
            copies.append(pltpu.make_async_copy(source, target, sems.at[b, a]))
    for copy in copies:
        copy.start()
    for copy in copies:
        copy.wait()


def assemble(chip, pieces):
    rows, both = pieces[0].shape
    return pl.pallas_call(
        assemble_kernel,
        in_specs=[SMEM] + [ANY] * RING,
        out_specs=VMEM,
        out_shape=jax.ShapeDtypeStruct((RING * rows, both), pieces[0].dtype),
        scratch_shapes=[pltpu.SemaphoreType.DMA((RING, RING))],
        compiler_params=PARAMS,
        cost_estimate=pl.CostEstimate(
            flops=0, bytes_accessed=4 * RING * rows * both, transcendentals=0
        ),
    )(chip, *pieces)


def finish_kernel(total_ref, gain_ref, key_value_ref):
    head_dim = gain_ref.shape[1]
    raw = total_ref[:, :head_dim]
    keys = (raw * rms_factor(raw) * gain_ref[...]).astype(jnp.bfloat16)
    key_value_ref[:, :head_dim] = keys
    key_value_ref[:, head_dim:] = total_ref[:, head_dim:].astype(jnp.bfloat16)


def finish(total, gain):
    return pl.pallas_call(
        finish_kernel,
        in_specs=[VMEM] * 2,
        out_specs=VMEM,
        out_shape=jax.ShapeDtypeStruct(total.shape, jnp.bfloat16),
        compiler_params=PARAMS,
        cost_estimate=pl.CostEstimate(
            flops=3 * total.size, bytes_accessed=6 * total.size, transcendentals=total.shape[0]
        ),
    )(total, gain[None, :])


def turn_kernel(base, numbers, total_ref, grad_ref, other_ref, gain_ref, out_ref):
    head_dim = gain_ref.shape[1]
    grad = jnp.where(numbers[base + 2] != 0, other_ref[...], grad_ref[...])
    raw = total_ref[:, :head_dim]
    d_raw = norm_back(raw, rms_factor(raw), gain_ref[...], grad[:, :head_dim].astype(jnp.float32))
    out_ref[:, :head_dim] = d_raw.astype(jnp.bfloat16)
    out_ref[:, head_dim:] = grad[:, head_dim:]


def turn(base, numbers, total, grad, other, gain):
    return pl.pallas_call(
        functools.partial(turn_kernel, base),
        in_specs=[SMEM] + [VMEM] * 4,
        out_specs=VMEM,
        out_shape=jax.ShapeDtypeStruct(grad.shape, jnp.bfloat16),
        compiler_params=PARAMS,
        cost_estimate=pl.CostEstimate(
            flops=6 * grad.size, bytes_accessed=8 * grad.size, transcendentals=grad.shape[0]
        ),
    )(numbers, total, grad, other, gain[None, :])


def product_kernel(chip, *refs):
    count = 2 * RING
    first, second, (first_ref, second_ref) = refs[:count], refs[count : 2 * count], refs[2 * count : 2 * count + 2]
    refs = refs[2 * count + 2 :]
    outs, (held, sems) = refs[:RING], refs[RING:]
    depth = first[0].shape[1]
    count = depth // 2
    z, y, x, core = (chip[CHIP + i] for i in range(4))
    for k in range(len(first)):
        total = matmul(first[k][...], first_ref[...], ((0,), (0,)))
        total = total + matmul(second[k][...], second_ref[...], ((0,), (0,)))
        total = total.astype(held.dtype)
        by_z = (x - k // 2 - z + 2 * RING) % RING
        for h in range(2):
            by_y = (2 * (k % 2 ^ core) + h - y + RING) % RING
            outer_by = jnp.where(core == 0, by_y, by_z)
            inner_by = jnp.where(core == 0, by_z, by_y)
            start = pl.multiple_of(inner_by * count, count)
            held[outer_by, pl.ds(start, count)] = total[h * count : (h + 1) * count]
    copies = [pltpu.make_async_copy(held.at[k], outs[k], sems.at[k]) for k in range(RING)]
    for copy in copies:
        copy.start()
    for copy in copies:
        copy.wait()


def product(chip, feats, others, grads, other_grads):
    rows, depth = feats[0].shape
    both = grads.shape[1]
    shape = (RING * depth // 2, both)
    return pl.pallas_call(
        product_kernel,
        in_specs=[SMEM] + [VMEM] * (2 * len(feats) + 2),
        out_specs=[ANY] * RING,
        out_shape=[jax.ShapeDtypeStruct(shape, jnp.bfloat16)] * RING,
        scratch_shapes=[
            pltpu.VMEM((RING, *shape), jnp.bfloat16),
            pltpu.SemaphoreType.DMA((RING,)),
        ],
        compiler_params=PARAMS,
        cost_estimate=pl.CostEstimate(
            flops=4 * len(feats) * rows * depth * both,
            bytes_accessed=4 * len(feats) * rows * depth,
            transcendentals=0,
        ),
    )(chip, *feats, *others, grads, other_grads)


def attend_kernel(heads, base, index, ratio_ref, q_ref, cot_ref, kv_ref, away_ref, gain_ref, *refs):
    context_ref, d_query_ref, d_kv_ref, d_key_sum, d_value_sum = refs[-5:]
    step = pl.program_id(0)
    head_dim = gain_ref.shape[1]
    scale = head_dim ** (-0.5)
    count = index[base + 1]
    ratio = ratio_ref[0]
    gain = gain_ref[...]
    key_value = jnp.where(index[base + 2] != 0, away_ref[...], kv_ref[...])
    keys = key_value[:, :head_dim]
    vals = key_value[:, head_dim:]

    def stacked(ref):
        parts = [ref[0, :, h * head_dim : (h + 1) * head_dim] for h in range(heads)]
        return jnp.concatenate(parts, axis=0).astype(jnp.float32)

    def unstacked(ref, rows):
        text = rows.shape[0] // heads
        for h in range(heads):
            part = rows[h * text : (h + 1) * text]
            ref[0, :, h * head_dim : (h + 1) * head_dim] = part.astype(ref.dtype)

    @pl.when(step == 0)
    def _():
        d_key_sum[...] = jnp.zeros_like(d_key_sum)
        d_value_sum[...] = jnp.zeros_like(d_value_sum)

    q_raw = stacked(q_ref)
    q_factor = rms_factor(q_raw)
    q_norm = (q_raw * q_factor * gain).astype(jnp.bfloat16)
    raw = matmul(q_norm, keys, ((1,), (1,))) * scale
    place = lax.broadcasted_iota(jnp.int32, raw.shape, 1)
    expo = jnp.where(place < count * TILE, jnp.exp(raw), 0.0)
    total = jnp.sum(expo, axis=1, keepdims=True) + (count == 0).astype(jnp.float32)
    inverse = 1.0 / total
    weights_b = expo.astype(jnp.bfloat16)
    attended = matmul(weights_b, vals, ((1,), (0,))) * inverse
    unstacked(context_ref, ratio * attended)
    d_att = ratio * stacked(cot_ref)
    d_att_b = d_att.astype(jnp.bfloat16)
    scaled_b = (d_att * inverse).astype(jnp.bfloat16)
    delta = jnp.sum(d_att * attended, axis=1, keepdims=True)
    d_prob = matmul(d_att_b, vals, ((1,), (1,)))
    d_score = (expo * inverse * (d_prob - delta)).astype(jnp.bfloat16)
    d_qn = scale * matmul(d_score, keys, ((1,), (0,)))
    unstacked(d_query_ref, norm_back(q_raw, q_factor, gain, d_qn))
    d_key_sum[...] += matmul(d_score, q_norm, ((0,), (0,)))
    d_value_sum[...] += matmul(weights_b, scaled_b, ((0,), (0,)))

    @pl.when(step == pl.num_programs(0) - 1)
    def _():
        d_kv_ref[:, :head_dim] = (scale * d_key_sum[...]).astype(d_kv_ref.dtype)
        d_kv_ref[:, head_dim:] = d_value_sum[...].astype(d_kv_ref.dtype)


def attend(base, index, ratio, query, cot, key_value, away, gain, earlier, heads=8):
    rows, both = key_value.shape
    head_dim = both // 2
    text = query.shape[1]
    width = heads * head_dim
    block = pl.BlockSpec((1, text, width), lambda h, index: (index[base], 0, h))
    whole = lambda shape: pl.BlockSpec(shape, lambda h, index: (0, 0))
    in_specs = [
        pl.BlockSpec(memory_space=pltpu.SMEM),
        block,
        block,
        whole((rows, both)),
        whole((rows, both)),
        whole((1, head_dim)),
    ]
    aliases = {}
    if earlier:
        in_specs += [pl.BlockSpec(memory_space=pl.ANY)] * 2
        aliases = {7: 0, 8: 1}
    steps = query.shape[2] // width
    return pl.pallas_call(
        functools.partial(attend_kernel, heads, base),
        grid_spec=pltpu.PrefetchScalarGridSpec(
            num_scalar_prefetch=1,
            grid=(steps,),
            in_specs=in_specs,
            out_specs=[block, block, whole((rows, both))],
            scratch_shapes=[pltpu.VMEM((rows, head_dim), jnp.float32)] * 2,
        ),
        out_shape=[
            jax.ShapeDtypeStruct(query.shape, jnp.bfloat16),
            jax.ShapeDtypeStruct(query.shape, jnp.bfloat16),
            jax.ShapeDtypeStruct((rows, both), jnp.bfloat16),
        ],
        input_output_aliases=aliases,
        compiler_params=pltpu.CompilerParams(
            vmem_limit_bytes=24 * 1024 * 1024
        ),
        cost_estimate=pl.CostEstimate(
            flops=14 * steps * heads * text * rows * head_dim,
            bytes_accessed=8 * text * steps * width + 6 * rows * head_dim,
            transcendentals=steps * heads * text * rows,
        ),
    )(
        index,
        ratio,
        query,
        cot,
        key_value,
        away,
        gain[None, :],
        *earlier,
    )


def per_device(
    query,
    image,
    tiles,
    image_slot,
    key_weight_matrix,
    value_weight_matrix,
    query_gain,
    key_gain,
    gate,
    cotangent,
):
    ratio = jnp.tanh(gate)
    numbers, far_own, near_own = route(tiles, image_slot, image)

    def opposite(after, before, move):
        half = after.shape[0] // 2
        return [move(after[:half], 1), move(before[half:], 3)]

    shard = lay(numbers, key_weight_matrix, value_weight_matrix)
    far_x = [along_x(far_own, 1), along_x(far_own, 3)]
    shard = jnp.concatenate(gathered(shard, inner), axis=0)
    shard, *far_x = lax.optimization_barrier((shard, *far_x))
    far_halves = opposite(*far_x, along_x)
    pieces = gathered(shard, outer)
    near_own, far_own, *far_halves = lax.optimization_barrier((near_own, far_own, *far_halves))
    near_x = [along_x(near_own, 1), along_x(near_own, 3)]
    weights = assemble(numbers, pieces)
    weights, *far_blocks = lax.optimization_barrier((weights, *far_x, *far_halves))

    def other_cores(*blocks):
        return [other_core(block) for block in blocks]

    def paired(own, other, after, before, opposite, after_other, before_other, opposite_other):
        return [own, other, after, after_other, opposite, opposite_other, before, before_other]

    def project(feats):
        depth = feats[0].shape[1]
        total = None
        for o in (0, 1, 3, 2):
            for k in (2 * o, 2 * o + 1):
                part = matmul(feats[k], weights[k * depth : (k + 1) * depth], ((1,), (0,)))
                total = part if total is None else total + part
        return total

    shared = (numbers, ratio, query, cotangent)
    after, before, *halves = far_blocks
    blocks = [after, before, jnp.concatenate(halves, axis=0)]
    far_feats = paired(far_own, other_core(far_own), *blocks, *other_cores(*blocks))
    far_total = project(far_feats)
    far_key_value = finish(far_total, key_gain)
    away = along_z(far_key_value, RING // 2)
    _, near_own, *near_x = lax.optimization_barrier((far_key_value, near_own, *near_x))
    near_halves = opposite(*near_x, along_x)
    near_others = other_cores(*near_x)
    *earlier, far_grad = attend(FAR, *shared, far_key_value, away, query_gain, ())
    back = along_z(far_grad, RING // 2)

    _, *near_halves = lax.optimization_barrier((far_grad, *near_halves))
    blocks = [*near_x, jnp.concatenate(near_halves, axis=0)]
    near_others.append(other_core(blocks[2]))
    near_feats = paired(near_own, other_core(near_own), *blocks, *near_others)
    near_total = project(near_feats)
    near_key_value = finish(near_total, key_gain)
    context, d_query, near_grad = attend(
        NEAR, *shared, near_key_value, near_key_value, query_gain, earlier
    )
    near_rows = turn(NEAR, numbers, near_total, near_grad, near_grad, key_gain)
    back, near_rows = lax.optimization_barrier((back, near_rows))
    far_rows = turn(FAR, numbers, far_total, far_grad, back, key_gain)

    blocks = product(numbers, far_feats, near_feats, far_rows, near_rows)
    total = summed([blocks[0], *scattered(blocks, outer)])
    count = total.shape[0] // RING
    parts = [total[d * count : (d + 1) * count] for d in range(RING)]
    sent = [None] + [part.astype(jnp.bfloat16) for part in parts[1:]]
    share = summed([parts[0], *scattered(sent, inner)])
    head_dim = query_gain.shape[0]
    return (context, d_query, share[:, :head_dim], share[:, head_dim:])


def solution(mesh):
    placed = (
        P("dp", None, "tensor"),
        P("dp", None, "tensor"),
        P(),
        P(),
        P("dp", "tensor"),
        P("dp", "tensor"),
        P(),
        P(),
        P(),
        P("dp", None, "tensor"),
    )
    return jax.shard_map(
        per_device,
        mesh=mesh,
        in_specs=placed,
        out_specs=(
            P("dp", None, "tensor"),
            P("dp", None, "tensor"),
            P("dp", "tensor"),
            P("dp", "tensor"),
        ),
        check_vma=False,
    )
```

```python
import functools

import jax
import jax.numpy as jnp
from jax import lax
from jax.experimental import pallas as pl
from jax.experimental.pallas import tpu as pltpu
from jax.sharding import PartitionSpec as P

TILE = 128
RING = 4
EPS = 1e-06


def along_z(x, step):
    pairs = [(z * RING + y, (z + step) % RING * RING + y) for z in range(RING) for y in range(RING)]
    return lax.ppermute(x, "dp", pairs)


def by_core(x, step, z_core):
    pairs = []
    for z in range(RING):
        for y in range(RING):
            for i in range(RING):
                for c in range(2):
                    to_z, to_y = (z + step, y) if c == z_core else (z, y + step)
                    source = (z * RING + y) * 2 * RING + i * 2 + c
                    target = (to_z % RING * RING + to_y % RING) * 2 * RING + i * 2 + c
                    pairs.append((source, target))
    return lax.ppermute(x, ("dp", "tensor"), pairs)


def inner(x, step):
    return by_core(x, step, 0)


def outer(x, step):
    return by_core(x, step, 1)


def along_x(x, step):
    pairs = [(i * 2 + c, (i + step) % RING * 2 + c) for i in range(RING) for c in range(2)]
    return lax.ppermute(x, "tensor", pairs)


def other_core(x):
    return lax.ppermute(x, "tensor", [(i, i ^ 1) for i in range(2 * RING)])


def gathered(block, move):
    far, after, before = (move(block, step) for step in (2, 1, 3))
    return [block, after, far, before]


def scattered(parts, move):
    return [move(parts[step], step) for step in (3, 1, 2)]


def summed(blocks):
    total = blocks[0].astype(jnp.float32)
    for block in blocks[1:]:
        total = total + block.astype(jnp.float32)
    return total


def rms_factor(values):
    return lax.rsqrt(jnp.mean(values * values, axis=-1, keepdims=True) + EPS)


def norm_back(values, norm_multiplier, gain, grad):
    weighted = grad * gain
    inner = jnp.sum(weighted * values, axis=-1, keepdims=True)
    return (
        norm_multiplier * weighted
        - values * (norm_multiplier * norm_multiplier * norm_multiplier) * inner / values.shape[-1]
    )


def matmul(a, b, contract):
    return lax.dot_general(a, b, (contract, ((), ())), preferred_element_type=jnp.float32)


VMEM = pl.BlockSpec(memory_space=pltpu.VMEM)
SMEM = pl.BlockSpec(memory_space=pltpu.SMEM)
ANY = pl.BlockSpec(memory_space=pl.ANY)
HBM = pl.BlockSpec(memory_space=pltpu.HBM)
PARAMS = pltpu.CompilerParams(vmem_limit_bytes=16 * 1024 * 1024)


NEAR, FAR, CHIP, NEAR_SLOT = 0, 3, 6, 10


def route_kernel(tiles, slots, image_ref, numbers, far_ref, sem):
    rank, place = lax.axis_index("dp"), lax.axis_index("tensor")
    first = 2 * rank
    homes = (slots[first], slots[first + 1])
    away = [
        jnp.logical_and(homes[0] != first + i, homes[1] != first + i) for i in range(2)
    ]
    swaps = jnp.logical_or(away[0], away[1])
    far_slot = jnp.where(away[1], 1, 0)
    copy = pltpu.make_async_copy(image_ref.at[far_slot], far_ref, sem)
    copy.start()
    of_slot = jnp.where(homes[1] == first + far_slot, 1, 0)
    far_own = jnp.where(swaps, jnp.where(homes[1] >> 1 != rank, 1, 0), of_slot)
    numbers[NEAR] = 1 - far_own
    numbers[NEAR + 1] = tiles[first + 1 - far_own]
    numbers[NEAR + 2] = 0
    numbers[FAR] = far_own
    numbers[FAR + 1] = tiles[first + far_own]
    numbers[FAR + 2] = jnp.where(swaps, 1, 0)
    numbers[CHIP] = rank // RING
    numbers[CHIP + 1] = rank % RING
    numbers[CHIP + 2] = place // 2
    numbers[CHIP + 3] = place % 2
    numbers[NEAR_SLOT] = 1 - far_slot
    copy.wait()


def route(tiles, image_slot, image):
    rows = jax.ShapeDtypeStruct(image.shape[1:], image.dtype)
    return pl.pallas_call(
        route_kernel,
        in_specs=[SMEM, SMEM, HBM],
        out_specs=[SMEM, VMEM],
        out_shape=[jax.ShapeDtypeStruct((NEAR_SLOT + 1,), jnp.int32), rows],
        scratch_shapes=[pltpu.SemaphoreType.DMA],
        compiler_params=pltpu.CompilerParams(vmem_limit_bytes=60 * 1024 * 1024),
        cost_estimate=pl.CostEstimate(flops=0, bytes_accessed=4 * image.size, transcendentals=0),
    )(tiles, image_slot, image)


def lay_kernel(numbers, image_ref, key_ref, value_ref, near_ref, out_ref, sems):
    head_dim = key_ref.shape[1]
    copies = [pltpu.make_async_copy(image_ref.at[numbers[NEAR_SLOT]], near_ref, sems.at[2])]
    copies[0].start()
    for i, source in enumerate((key_ref, value_ref)):
        target = out_ref.at[:, pl.ds(i * head_dim, head_dim)]
        copies.append(pltpu.make_async_copy(source, target, sems.at[i]))
        copies[1 + i].start()
    for copy in copies:
        copy.wait()


def lay(numbers, image, key_weights, value_weights):
    count, head_dim = key_weights.shape
    return pl.pallas_call(
        lay_kernel,
        in_specs=[SMEM, HBM, HBM, HBM],
        out_specs=[VMEM, VMEM],
        out_shape=[
            jax.ShapeDtypeStruct(image.shape[1:], image.dtype),
            jax.ShapeDtypeStruct((count, 2 * head_dim), key_weights.dtype),
        ],
        scratch_shapes=[pltpu.SemaphoreType.DMA((3,))],
        compiler_params=PARAMS,
        cost_estimate=pl.CostEstimate(
            flops=0, bytes_accessed=8 * count * head_dim, transcendentals=0
        ),
    )(numbers, image, key_weights, value_weights)


def assemble_kernel(chip, *refs):
    pieces, out_ref, sems = refs[:RING], refs[RING], refs[RING + 1]
    rows, both = pieces[0].shape
    count = rows // RING
    z, y, x, core = (chip[CHIP + i] for i in range(4))
    copies = []
    for b in range(RING):
        for a in range(RING):
            from_z = (z - jnp.where(core == 0, a, b) + RING) % RING
            from_y = (y - jnp.where(core == 0, b, a) + RING) % RING
            o = (x - from_z + RING) % RING
            start = ((o * 2 + ((from_y >> 1) ^ core)) * 2 + from_y % 2) * count
            target = out_ref.at[pl.ds(pl.multiple_of(start, count), count)]
            source = pieces[b].at[pl.ds(a * count, count)]
            copies.append(pltpu.make_async_copy(source, target, sems.at[b, a]))
    for copy in copies:
        copy.start()
    for copy in copies:
        copy.wait()


def assemble(chip, pieces):
    rows, both = pieces[0].shape
    return pl.pallas_call(
        assemble_kernel,
        in_specs=[SMEM] + [ANY] * RING,
        out_specs=VMEM,
        out_shape=jax.ShapeDtypeStruct((RING * rows, both), pieces[0].dtype),
        scratch_shapes=[pltpu.SemaphoreType.DMA((RING, RING))],
        compiler_params=PARAMS,
        cost_estimate=pl.CostEstimate(
            flops=0, bytes_accessed=4 * RING * rows * both, transcendentals=0
        ),
    )(chip, *pieces)


def finish_kernel(total_ref, gain_ref, key_value_ref):
    head_dim = gain_ref.shape[1]
    raw = total_ref[:, :head_dim]
    keys = (raw * rms_factor(raw) * gain_ref[...]).astype(jnp.bfloat16)
    key_value_ref[:, :head_dim] = keys
    key_value_ref[:, head_dim:] = total_ref[:, head_dim:].astype(jnp.bfloat16)


def finish(total, gain):
    return pl.pallas_call(
        finish_kernel,
        in_specs=[VMEM] * 2,
        out_specs=VMEM,
        out_shape=jax.ShapeDtypeStruct(total.shape, jnp.bfloat16),
        compiler_params=PARAMS,
        cost_estimate=pl.CostEstimate(
            flops=3 * total.size, bytes_accessed=6 * total.size, transcendentals=total.shape[0]
        ),
    )(total, gain[None, :])


def turn_kernel(base, numbers, total_ref, grad_ref, other_ref, gain_ref, out_ref):
    head_dim = gain_ref.shape[1]
    grad = jnp.where(numbers[base + 2] != 0, other_ref[...], grad_ref[...])
    raw = total_ref[:, :head_dim]
    d_raw = norm_back(raw, rms_factor(raw), gain_ref[...], grad[:, :head_dim].astype(jnp.float32))
    out_ref[:, :head_dim] = d_raw.astype(jnp.bfloat16)
    out_ref[:, head_dim:] = grad[:, head_dim:]


def turn(base, numbers, total, grad, other, gain):
    return pl.pallas_call(
        functools.partial(turn_kernel, base),
        in_specs=[SMEM] + [VMEM] * 4,
        out_specs=VMEM,
        out_shape=jax.ShapeDtypeStruct(grad.shape, jnp.bfloat16),
        compiler_params=PARAMS,
        cost_estimate=pl.CostEstimate(
            flops=6 * grad.size, bytes_accessed=8 * grad.size, transcendentals=grad.shape[0]
        ),
    )(numbers, total, grad, other, gain[None, :])


def product_kernel(chip, *refs):
    count = 2 * RING
    first, second, (first_ref, second_ref) = refs[:count], refs[count : 2 * count], refs[2 * count : 2 * count + 2]
    refs = refs[2 * count + 2 :]
    outs, (held, sems) = refs[:RING], refs[RING:]
    depth = first[0].shape[1]
    count = depth // 2
    z, y, x, core = (chip[CHIP + i] for i in range(4))
    for k in range(len(first)):
        total = matmul(first[k][...], first_ref[...], ((0,), (0,)))
        total = total + matmul(second[k][...], second_ref[...], ((0,), (0,)))
        total = total.astype(held.dtype)
        by_z = (x - k // 2 - z + 2 * RING) % RING
        for h in range(2):
            by_y = (2 * (k % 2 ^ core) + h - y + RING) % RING
            outer_by = jnp.where(core == 0, by_y, by_z)
            inner_by = jnp.where(core == 0, by_z, by_y)
            start = pl.multiple_of(inner_by * count, count)
            held[outer_by, pl.ds(start, count)] = total[h * count : (h + 1) * count]
    copies = [pltpu.make_async_copy(held.at[k], outs[k], sems.at[k]) for k in range(RING)]
    for copy in copies:
        copy.start()
    for copy in copies:
        copy.wait()


def product(chip, feats, others, grads, other_grads):
    rows, depth = feats[0].shape
    both = grads.shape[1]
    shape = (RING * depth // 2, both)
    return pl.pallas_call(
        product_kernel,
        in_specs=[SMEM] + [VMEM] * (2 * len(feats) + 2),
        out_specs=[ANY] * RING,
        out_shape=[jax.ShapeDtypeStruct(shape, jnp.bfloat16)] * RING,
        scratch_shapes=[
            pltpu.VMEM((RING, *shape), jnp.bfloat16),
            pltpu.SemaphoreType.DMA((RING,)),
        ],
        compiler_params=PARAMS,
        cost_estimate=pl.CostEstimate(
            flops=4 * len(feats) * rows * depth * both,
            bytes_accessed=4 * len(feats) * rows * depth,
            transcendentals=0,
        ),
    )(chip, *feats, *others, grads, other_grads)


def attend_kernel(heads, base, index, ratio_ref, q_ref, cot_ref, kv_ref, away_ref, gain_ref, *refs):
    context_ref, d_query_ref, d_kv_ref, d_key_sum, d_value_sum = refs[-5:]
    step = pl.program_id(0)
    head_dim = gain_ref.shape[1]
    scale = head_dim ** (-0.5)
    count = index[base + 1]
    ratio = ratio_ref[0]
    gain = gain_ref[...]
    key_value = jnp.where(index[base + 2] != 0, away_ref[...], kv_ref[...])
    keys = key_value[:, :head_dim]
    vals = key_value[:, head_dim:]

    def stacked(ref):
        parts = [ref[0, :, h * head_dim : (h + 1) * head_dim] for h in range(heads)]
        return jnp.concatenate(parts, axis=0).astype(jnp.float32)

    def unstacked(ref, rows):
        text = rows.shape[0] // heads
        for h in range(heads):
            part = rows[h * text : (h + 1) * text]
            ref[0, :, h * head_dim : (h + 1) * head_dim] = part.astype(ref.dtype)

    @pl.when(step == 0)
    def _():
        d_key_sum[...] = jnp.zeros_like(d_key_sum)
        d_value_sum[...] = jnp.zeros_like(d_value_sum)

    q_raw = stacked(q_ref)
    q_factor = rms_factor(q_raw)
    q_norm = (q_raw * q_factor * gain).astype(jnp.bfloat16)
    raw = matmul(q_norm, keys, ((1,), (1,))) * scale
    place = lax.broadcasted_iota(jnp.int32, raw.shape, 1)
    expo = jnp.where(place < count * TILE, jnp.exp(raw), 0.0)
    total = jnp.sum(expo, axis=1, keepdims=True) + (count == 0).astype(jnp.float32)
    inverse = 1.0 / total
    weights_b = expo.astype(jnp.bfloat16)
    attended = matmul(weights_b, vals, ((1,), (0,))) * inverse
    unstacked(context_ref, ratio * attended)
    d_att = ratio * stacked(cot_ref)
    d_att_b = d_att.astype(jnp.bfloat16)
    scaled_b = (d_att * inverse).astype(jnp.bfloat16)
    delta = jnp.sum(d_att * attended, axis=1, keepdims=True)
    d_prob = matmul(d_att_b, vals, ((1,), (1,)))
    d_score = (expo * inverse * (d_prob - delta)).astype(jnp.bfloat16)
    d_qn = scale * matmul(d_score, keys, ((1,), (0,)))
    unstacked(d_query_ref, norm_back(q_raw, q_factor, gain, d_qn))
    d_key_sum[...] += matmul(d_score, q_norm, ((0,), (0,)))
    d_value_sum[...] += matmul(weights_b, scaled_b, ((0,), (0,)))

    @pl.when(step == pl.num_programs(0) - 1)
    def _():
        d_kv_ref[:, :head_dim] = (scale * d_key_sum[...]).astype(d_kv_ref.dtype)
        d_kv_ref[:, head_dim:] = d_value_sum[...].astype(d_kv_ref.dtype)


def attend(base, index, ratio, query, cot, key_value, away, gain, earlier, heads=8):
    rows, both = key_value.shape
    head_dim = both // 2
    text = query.shape[1]
    width = heads * head_dim
    block = pl.BlockSpec((1, text, width), lambda h, index: (index[base], 0, h))
    whole = lambda shape: pl.BlockSpec(shape, lambda h, index: (0, 0))
    in_specs = [
        pl.BlockSpec(memory_space=pltpu.SMEM),
        block,
        block,
        whole((rows, both)),
        whole((rows, both)),
        whole((1, head_dim)),
    ]
    aliases = {}
    if earlier:
        in_specs += [pl.BlockSpec(memory_space=pl.ANY)] * 2
        aliases = {7: 0, 8: 1}
    steps = query.shape[2] // width
    return pl.pallas_call(
        functools.partial(attend_kernel, heads, base),
        grid_spec=pltpu.PrefetchScalarGridSpec(
            num_scalar_prefetch=1,
            grid=(steps,),
            in_specs=in_specs,
            out_specs=[block, block, whole((rows, both))],
            scratch_shapes=[pltpu.VMEM((rows, head_dim), jnp.float32)] * 2,
        ),
        out_shape=[
            jax.ShapeDtypeStruct(query.shape, jnp.bfloat16),
            jax.ShapeDtypeStruct(query.shape, jnp.bfloat16),
            jax.ShapeDtypeStruct((rows, both), jnp.bfloat16),
        ],
        input_output_aliases=aliases,
        compiler_params=pltpu.CompilerParams(
            vmem_limit_bytes=24 * 1024 * 1024
        ),
        cost_estimate=pl.CostEstimate(
            flops=14 * steps * heads * text * rows * head_dim,
            bytes_accessed=8 * text * steps * width + 6 * rows * head_dim,
            transcendentals=steps * heads * text * rows,
        ),
    )(
        index,
        ratio,
        query,
        cot,
        key_value,
        away,
        gain[None, :],
        *earlier,
    )


def per_device(
    query,
    image,
    tiles,
    image_slot,
    key_weight_matrix,
    value_weight_matrix,
    query_gain,
    key_gain,
    gate,
    cotangent,
):
    ratio = jnp.tanh(gate)
    numbers, far_own = route(tiles, image_slot, image)

    def opposite(after, before, move):
        half = after.shape[0] // 2
        return [move(after[:half], 1), move(before[half:], 3)]

    near_own, shard = lay(numbers, image, key_weight_matrix, value_weight_matrix)
    far_x = [along_x(far_own, 1), along_x(far_own, 3)]
    shard = jnp.concatenate(gathered(shard, inner), axis=0)
    shard, *far_x = lax.optimization_barrier((shard, *far_x))
    far_halves = opposite(*far_x, along_x)
    pieces = gathered(shard, outer)
    near_own, far_own, *far_halves = lax.optimization_barrier((near_own, far_own, *far_halves))
    near_x = [along_x(near_own, 1), along_x(near_own, 3)]
    weights = assemble(numbers, pieces)
    weights, *far_blocks = lax.optimization_barrier((weights, *far_x, *far_halves))

    def other_cores(*blocks):
        return [other_core(block) for block in blocks]

    def paired(own, other, after, before, opposite, after_other, before_other, opposite_other):
        return [own, other, after, after_other, opposite, opposite_other, before, before_other]

    def project(feats):
        depth = feats[0].shape[1]
        total = None
        for o in (0, 1, 3, 2):
            for k in (2 * o, 2 * o + 1):
                part = matmul(feats[k], weights[k * depth : (k + 1) * depth], ((1,), (0,)))
                total = part if total is None else total + part
        return total

    shared = (numbers, ratio, query, cotangent)
    after, before, *halves = far_blocks
    blocks = [after, before, jnp.concatenate(halves, axis=0)]
    far_feats = paired(far_own, other_core(far_own), *blocks, *other_cores(*blocks))
    far_total = project(far_feats)
    far_key_value = finish(far_total, key_gain)
    away = along_z(far_key_value, RING // 2)
    _, near_own, *near_x = lax.optimization_barrier((far_key_value, near_own, *near_x))
    near_halves = opposite(*near_x, along_x)
    near_others = other_cores(*near_x)
    *earlier, far_grad = attend(FAR, *shared, far_key_value, away, query_gain, ())
    back = along_z(far_grad, RING // 2)

    back, *near_halves = lax.optimization_barrier((back, *near_halves))
    blocks = [*near_x, jnp.concatenate(near_halves, axis=0)]
    near_others.append(other_core(blocks[2]))
    near_feats = paired(near_own, other_core(near_own), *blocks, *near_others)
    near_total = project(near_feats)
    near_key_value = finish(near_total, key_gain)
    context, d_query, near_grad = attend(
        NEAR, *shared, near_key_value, near_key_value, query_gain, earlier
    )
    near_rows = turn(NEAR, numbers, near_total, near_grad, near_grad, key_gain)
    far_rows = turn(FAR, numbers, far_total, far_grad, back, key_gain)

    blocks = product(numbers, far_feats, near_feats, far_rows, near_rows)
    total = summed([blocks[0], *scattered(blocks, outer)])
    count = total.shape[0] // RING
    parts = [total[d * count : (d + 1) * count] for d in range(RING)]
    sent = [None] + [part.astype(jnp.bfloat16) for part in parts[1:]]
    share = summed([parts[0], *scattered(sent, inner)])
    head_dim = query_gain.shape[0]
    return (context, d_query, share[:, :head_dim], share[:, head_dim:])


def solution(mesh):
    placed = (
        P("dp", None, "tensor"),
        P("dp", None, "tensor"),
        P(),
        P(),
        P("dp", "tensor"),
        P("dp", "tensor"),
        P(),
        P(),
        P(),
        P("dp", None, "tensor"),
    )
    return jax.shard_map(
        per_device,
        mesh=mesh,
        in_specs=placed,
        out_specs=(
            P("dp", None, "tensor"),
            P("dp", None, "tensor"),
            P("dp", "tensor"),
            P("dp", "tensor"),
        ),
        check_vma=False,
    )
```

```python
import functools

import jax
import jax.numpy as jnp
from jax import lax
from jax.experimental import pallas as pl
from jax.experimental.pallas import tpu as pltpu
from jax.sharding import PartitionSpec as P

TILE = 128
RING = 4
EPS = 1e-06


def along_z(x, step):
    pairs = [(z * RING + y, (z + step) % RING * RING + y) for z in range(RING) for y in range(RING)]
    return lax.ppermute(x, "dp", pairs)


def by_core(x, step, z_core):
    pairs = []
    for z in range(RING):
        for y in range(RING):
            for i in range(RING):
                for c in range(2):
                    to_z, to_y = (z + step, y) if c == z_core else (z, y + step)
                    source = (z * RING + y) * 2 * RING + i * 2 + c
                    target = (to_z % RING * RING + to_y % RING) * 2 * RING + i * 2 + c
                    pairs.append((source, target))
    return lax.ppermute(x, ("dp", "tensor"), pairs)


def inner(x, step):
    return by_core(x, step, 0)


def outer(x, step):
    return by_core(x, step, 1)


def along_x(x, step):
    pairs = [(i * 2 + c, (i + step) % RING * 2 + c) for i in range(RING) for c in range(2)]
    return lax.ppermute(x, "tensor", pairs)


def other_core(x):
    return lax.ppermute(x, "tensor", [(i, i ^ 1) for i in range(2 * RING)])


def gathered(block, move):
    far, after, before = (move(block, step) for step in (2, 1, 3))
    return [block, after, far, before]


def scattered(parts, move):
    return [move(parts[step], step) for step in (3, 1, 2)]


def summed(blocks):
    total = blocks[0].astype(jnp.float32)
    for block in blocks[1:]:
        total = total + block.astype(jnp.float32)
    return total


def rms_factor(values):
    return lax.rsqrt(jnp.mean(values * values, axis=-1, keepdims=True) + EPS)


def norm_back(values, norm_multiplier, gain, grad):
    weighted = grad * gain
    inner = jnp.sum(weighted * values, axis=-1, keepdims=True)
    return (
        norm_multiplier * weighted
        - values * (norm_multiplier * norm_multiplier * norm_multiplier) * inner / values.shape[-1]
    )


def matmul(a, b, contract):
    return lax.dot_general(a, b, (contract, ((), ())), preferred_element_type=jnp.float32)


VMEM = pl.BlockSpec(memory_space=pltpu.VMEM)
SMEM = pl.BlockSpec(memory_space=pltpu.SMEM)
ANY = pl.BlockSpec(memory_space=pl.ANY)
HBM = pl.BlockSpec(memory_space=pltpu.HBM)
PARAMS = pltpu.CompilerParams(vmem_limit_bytes=16 * 1024 * 1024)


NEAR, FAR, CHIP, NEAR_SLOT = 0, 3, 6, 10


def route_kernel(tiles, slots, image_ref, numbers, far_ref, sem):
    rank, place = lax.axis_index("dp"), lax.axis_index("tensor")
    first = 2 * rank
    homes = (slots[first], slots[first + 1])
    away = [
        jnp.logical_and(homes[0] != first + i, homes[1] != first + i) for i in range(2)
    ]
    swaps = jnp.logical_or(away[0], away[1])
    far_slot = jnp.where(away[1], 1, 0)
    copy = pltpu.make_async_copy(image_ref.at[far_slot], far_ref, sem)
    copy.start()
    of_slot = jnp.where(homes[1] == first + far_slot, 1, 0)
    far_own = jnp.where(swaps, jnp.where(homes[1] >> 1 != rank, 1, 0), of_slot)
    numbers[NEAR] = 1 - far_own
    numbers[NEAR + 1] = tiles[first + 1 - far_own]
    numbers[NEAR + 2] = 0
    numbers[FAR] = far_own
    numbers[FAR + 1] = tiles[first + far_own]
    numbers[FAR + 2] = jnp.where(swaps, 1, 0)
    numbers[CHIP] = rank // RING
    numbers[CHIP + 1] = rank % RING
    numbers[CHIP + 2] = place // 2
    numbers[CHIP + 3] = place % 2
    numbers[NEAR_SLOT] = 1 - far_slot
    copy.wait()


def route(tiles, image_slot, image):
    rows = jax.ShapeDtypeStruct(image.shape[1:], image.dtype)
    return pl.pallas_call(
        route_kernel,
        in_specs=[SMEM, SMEM, HBM],
        out_specs=[SMEM, VMEM],
        out_shape=[jax.ShapeDtypeStruct((NEAR_SLOT + 1,), jnp.int32), rows],
        scratch_shapes=[pltpu.SemaphoreType.DMA],
        compiler_params=pltpu.CompilerParams(vmem_limit_bytes=60 * 1024 * 1024),
        cost_estimate=pl.CostEstimate(flops=0, bytes_accessed=4 * image.size, transcendentals=0),
    )(tiles, image_slot, image)


def lay_kernel(numbers, image_ref, key_ref, value_ref, near_ref, out_ref, sems):
    head_dim = key_ref.shape[1]
    copies = [pltpu.make_async_copy(image_ref.at[numbers[NEAR_SLOT]], near_ref, sems.at[2])]
    copies[0].start()
    for i, source in enumerate((key_ref, value_ref)):
        target = out_ref.at[:, pl.ds(i * head_dim, head_dim)]
        copies.append(pltpu.make_async_copy(source, target, sems.at[i]))
        copies[1 + i].start()
    for copy in copies:
        copy.wait()


def lay(numbers, image, key_weights, value_weights):
    count, head_dim = key_weights.shape
    return pl.pallas_call(
        lay_kernel,
        in_specs=[SMEM, HBM, HBM, HBM],
        out_specs=[VMEM, VMEM],
        out_shape=[
            jax.ShapeDtypeStruct(image.shape[1:], image.dtype),
            jax.ShapeDtypeStruct((count, 2 * head_dim), key_weights.dtype),
        ],
        scratch_shapes=[pltpu.SemaphoreType.DMA((3,))],
        compiler_params=PARAMS,
        cost_estimate=pl.CostEstimate(
            flops=0, bytes_accessed=8 * count * head_dim, transcendentals=0
        ),
    )(numbers, image, key_weights, value_weights)


def assemble_kernel(chip, *refs):
    pieces, out_ref, sems = refs[:RING], refs[RING], refs[RING + 1]
    rows, both = pieces[0].shape
    count = rows // RING
    z, y, x, core = (chip[CHIP + i] for i in range(4))
    copies = []
    for b in range(RING):
        for a in range(RING):
            from_z = (z - jnp.where(core == 0, a, b) + RING) % RING
            from_y = (y - jnp.where(core == 0, b, a) + RING) % RING
            o = (x - from_z + RING) % RING
            start = ((o * 2 + ((from_y >> 1) ^ core)) * 2 + from_y % 2) * count
            target = out_ref.at[pl.ds(pl.multiple_of(start, count), count)]
            source = pieces[b].at[pl.ds(a * count, count)]
            copies.append(pltpu.make_async_copy(source, target, sems.at[b, a]))
    for copy in copies:
        copy.start()
    for copy in copies:
        copy.wait()


def assemble(chip, pieces):
    rows, both = pieces[0].shape
    return pl.pallas_call(
        assemble_kernel,
        in_specs=[SMEM] + [ANY] * RING,
        out_specs=VMEM,
        out_shape=jax.ShapeDtypeStruct((RING * rows, both), pieces[0].dtype),
        scratch_shapes=[pltpu.SemaphoreType.DMA((RING, RING))],
        compiler_params=PARAMS,
        cost_estimate=pl.CostEstimate(
            flops=0, bytes_accessed=4 * RING * rows * both, transcendentals=0
        ),
    )(chip, *pieces)


def finish_kernel(total_ref, gain_ref, key_value_ref):
    head_dim = gain_ref.shape[1]
    raw = total_ref[:, :head_dim]
    keys = (raw * rms_factor(raw) * gain_ref[...]).astype(jnp.bfloat16)
    key_value_ref[:, :head_dim] = keys
    key_value_ref[:, head_dim:] = total_ref[:, head_dim:].astype(jnp.bfloat16)


def finish(total, gain):
    return pl.pallas_call(
        finish_kernel,
        in_specs=[VMEM] * 2,
        out_specs=VMEM,
        out_shape=jax.ShapeDtypeStruct(total.shape, jnp.bfloat16),
        compiler_params=PARAMS,
        cost_estimate=pl.CostEstimate(
            flops=3 * total.size, bytes_accessed=6 * total.size, transcendentals=total.shape[0]
        ),
    )(total, gain[None, :])


def turned(total, grad, gain):
    head_dim = gain.shape[1]
    raw = total[:, :head_dim]
    d_raw = norm_back(raw, rms_factor(raw), gain, grad[:, :head_dim].astype(jnp.float32))
    return jnp.concatenate([d_raw.astype(jnp.bfloat16), grad[:, head_dim:]], axis=1)


def product_kernel(chip, *refs):
    count = 2 * RING
    first, second, refs = refs[:count], refs[count : 2 * count], refs[2 * count :]
    first_total, first_grad, first_back, second_total, second_grad, gain_ref, *refs = refs
    first_grads = jnp.where(chip[FAR + 2] != 0, first_back[...], first_grad[...])
    first_grads = turned(first_total[...], first_grads, gain_ref[...])
    second_grads = turned(second_total[...], second_grad[...], gain_ref[...])
    outs, (held, sems) = refs[:RING], refs[RING:]
    depth = first[0].shape[1]
    count = depth // 2
    z, y, x, core = (chip[CHIP + i] for i in range(4))
    for k in range(len(first)):
        total = matmul(first[k][...], first_grads, ((0,), (0,)))
        total = total + matmul(second[k][...], second_grads, ((0,), (0,)))
        total = total.astype(held.dtype)
        by_z = (x - k // 2 - z + 2 * RING) % RING
        for h in range(2):
            by_y = (2 * (k % 2 ^ core) + h - y + RING) % RING
            outer_by = jnp.where(core == 0, by_y, by_z)
            inner_by = jnp.where(core == 0, by_z, by_y)
            start = pl.multiple_of(inner_by * count, count)
            held[outer_by, pl.ds(start, count)] = total[h * count : (h + 1) * count]
    copies = [pltpu.make_async_copy(held.at[k], outs[k], sems.at[k]) for k in range(RING)]
    for copy in copies:
        copy.start()
    for copy in copies:
        copy.wait()


def product(chip, feats, others, first, second, gain):
    rows, depth = feats[0].shape
    both = first[0].shape[1]
    shape = (RING * depth // 2, both)
    return pl.pallas_call(
        product_kernel,
        in_specs=[SMEM] + [VMEM] * (2 * len(feats) + 6),
        out_specs=[ANY] * RING,
        out_shape=[jax.ShapeDtypeStruct(shape, jnp.bfloat16)] * RING,
        scratch_shapes=[
            pltpu.VMEM((RING, *shape), jnp.bfloat16),
            pltpu.SemaphoreType.DMA((RING,)),
        ],
        compiler_params=PARAMS,
        cost_estimate=pl.CostEstimate(
            flops=4 * len(feats) * rows * depth * both,
            bytes_accessed=4 * len(feats) * rows * depth,
            transcendentals=0,
        ),
    )(chip, *feats, *others, *first, *second, gain[None, :])


def attend_kernel(heads, base, index, ratio_ref, q_ref, cot_ref, kv_ref, away_ref, gain_ref, *refs):
    context_ref, d_query_ref, d_kv_ref, d_key_sum, d_value_sum = refs[-5:]
    step = pl.program_id(0)
    head_dim = gain_ref.shape[1]
    scale = head_dim ** (-0.5)
    count = index[base + 1]
    ratio = ratio_ref[0]
    gain = gain_ref[...]
    key_value = jnp.where(index[base + 2] != 0, away_ref[...], kv_ref[...])
    keys = key_value[:, :head_dim]
    vals = key_value[:, head_dim:]

    def stacked(ref):
        parts = [ref[0, :, h * head_dim : (h + 1) * head_dim] for h in range(heads)]
        return jnp.concatenate(parts, axis=0).astype(jnp.float32)

    def unstacked(ref, rows):
        text = rows.shape[0] // heads
        for h in range(heads):
            part = rows[h * text : (h + 1) * text]
            ref[0, :, h * head_dim : (h + 1) * head_dim] = part.astype(ref.dtype)

    @pl.when(step == 0)
    def _():
        d_key_sum[...] = jnp.zeros_like(d_key_sum)
        d_value_sum[...] = jnp.zeros_like(d_value_sum)

    q_raw = stacked(q_ref)
    q_factor = rms_factor(q_raw)
    q_norm = (q_raw * q_factor * gain).astype(jnp.bfloat16)
    raw = matmul(q_norm, keys, ((1,), (1,))) * scale
    place = lax.broadcasted_iota(jnp.int32, raw.shape, 1)
    expo = jnp.where(place < count * TILE, jnp.exp(raw), 0.0)
    total = jnp.sum(expo, axis=1, keepdims=True) + (count == 0).astype(jnp.float32)
    inverse = 1.0 / total
    weights_b = expo.astype(jnp.bfloat16)
    attended = matmul(weights_b, vals, ((1,), (0,))) * inverse
    unstacked(context_ref, ratio * attended)
    d_att = ratio * stacked(cot_ref)
    d_att_b = d_att.astype(jnp.bfloat16)
    scaled_b = (d_att * inverse).astype(jnp.bfloat16)
    delta = jnp.sum(d_att * attended, axis=1, keepdims=True)
    d_prob = matmul(d_att_b, vals, ((1,), (1,)))
    d_score = (expo * inverse * (d_prob - delta)).astype(jnp.bfloat16)
    d_qn = scale * matmul(d_score, keys, ((1,), (0,)))
    unstacked(d_query_ref, norm_back(q_raw, q_factor, gain, d_qn))
    d_key_sum[...] += matmul(d_score, q_norm, ((0,), (0,)))
    d_value_sum[...] += matmul(weights_b, scaled_b, ((0,), (0,)))

    @pl.when(step == pl.num_programs(0) - 1)
    def _():
        d_kv_ref[:, :head_dim] = (scale * d_key_sum[...]).astype(d_kv_ref.dtype)
        d_kv_ref[:, head_dim:] = d_value_sum[...].astype(d_kv_ref.dtype)


def attend(base, index, ratio, query, cot, key_value, away, gain, earlier, heads=8):
    rows, both = key_value.shape
    head_dim = both // 2
    text = query.shape[1]
    width = heads * head_dim
    block = pl.BlockSpec((1, text, width), lambda h, index: (index[base], 0, h))
    whole = lambda shape: pl.BlockSpec(shape, lambda h, index: (0, 0))
    in_specs = [
        pl.BlockSpec(memory_space=pltpu.SMEM),
        block,
        block,
        whole((rows, both)),
        whole((rows, both)),
        whole((1, head_dim)),
    ]
    aliases = {}
    if earlier:
        in_specs += [pl.BlockSpec(memory_space=pl.ANY)] * 2
        aliases = {7: 0, 8: 1}
    steps = query.shape[2] // width
    return pl.pallas_call(
        functools.partial(attend_kernel, heads, base),
        grid_spec=pltpu.PrefetchScalarGridSpec(
            num_scalar_prefetch=1,
            grid=(steps,),
            in_specs=in_specs,
            out_specs=[block, block, whole((rows, both))],
            scratch_shapes=[pltpu.VMEM((rows, head_dim), jnp.float32)] * 2,
        ),
        out_shape=[
            jax.ShapeDtypeStruct(query.shape, jnp.bfloat16),
            jax.ShapeDtypeStruct(query.shape, jnp.bfloat16),
            jax.ShapeDtypeStruct((rows, both), jnp.bfloat16),
        ],
        input_output_aliases=aliases,
        compiler_params=pltpu.CompilerParams(
            vmem_limit_bytes=24 * 1024 * 1024
        ),
        cost_estimate=pl.CostEstimate(
            flops=14 * steps * heads * text * rows * head_dim,
            bytes_accessed=8 * text * steps * width + 6 * rows * head_dim,
            transcendentals=steps * heads * text * rows,
        ),
    )(
        index,
        ratio,
        query,
        cot,
        key_value,
        away,
        gain[None, :],
        *earlier,
    )


def per_device(
    query,
    image,
    tiles,
    image_slot,
    key_weight_matrix,
    value_weight_matrix,
    query_gain,
    key_gain,
    gate,
    cotangent,
):
    ratio = jnp.tanh(gate)
    numbers, far_own = route(tiles, image_slot, image)

    def opposite(after, before, move):
        half = after.shape[0] // 2
        return [move(after[:half], 1), move(before[half:], 3)]

    near_own, shard = lay(numbers, image, key_weight_matrix, value_weight_matrix)
    far_x = [along_x(far_own, 1), along_x(far_own, 3)]
    shard = jnp.concatenate(gathered(shard, inner), axis=0)
    shard, *far_x = lax.optimization_barrier((shard, *far_x))
    far_halves = opposite(*far_x, along_x)
    pieces = gathered(shard, outer)
    near_own, far_own, *far_halves = lax.optimization_barrier((near_own, far_own, *far_halves))
    near_x = [along_x(near_own, 1), along_x(near_own, 3)]
    weights = assemble(numbers, pieces)
    weights, *far_blocks = lax.optimization_barrier((weights, *far_x, *far_halves))

    def other_cores(*blocks):
        return [other_core(block) for block in blocks]

    def paired(own, other, after, before, opposite, after_other, before_other, opposite_other):
        return [own, other, after, after_other, opposite, opposite_other, before, before_other]

    def project(feats):
        depth = feats[0].shape[1]
        total = None
        for o in (0, 1, 3, 2):
            for k in (2 * o, 2 * o + 1):
                part = matmul(feats[k], weights[k * depth : (k + 1) * depth], ((1,), (0,)))
                total = part if total is None else total + part
        return total

    shared = (numbers, ratio, query, cotangent)
    after, before, *halves = far_blocks
    blocks = [after, before, jnp.concatenate(halves, axis=0)]
    far_feats = paired(far_own, other_core(far_own), *blocks, *other_cores(*blocks))
    far_total = project(far_feats)
    far_key_value = finish(far_total, key_gain)
    away = along_z(far_key_value, RING // 2)
    _, near_own, *near_x = lax.optimization_barrier((far_key_value, near_own, *near_x))
    near_halves = opposite(*near_x, along_x)
    away, *near_x = lax.optimization_barrier((away, *near_x))
    near_others = other_cores(*near_x)
    *earlier, far_grad = attend(FAR, *shared, far_key_value, away, query_gain, ())
    back = along_z(far_grad, RING // 2)

    back, *near_halves = lax.optimization_barrier((back, *near_halves))
    blocks = [*near_x, jnp.concatenate(near_halves, axis=0)]
    near_others.append(other_core(blocks[2]))
    near_feats = paired(near_own, other_core(near_own), *blocks, *near_others)
    near_total = project(near_feats)
    near_key_value = finish(near_total, key_gain)
    context, d_query, near_grad = attend(
        NEAR, *shared, near_key_value, near_key_value, query_gain, earlier
    )

    far, near = (far_total, far_grad, back), (near_total, near_grad)
    blocks = product(numbers, far_feats, near_feats, far, near, key_gain)
    total = summed([blocks[0], *scattered(blocks, outer)])
    count = total.shape[0] // RING
    parts = [total[d * count : (d + 1) * count] for d in range(RING)]
    sent = [None] + [part.astype(jnp.bfloat16) for part in parts[1:]]
    share = summed([parts[0], *scattered(sent, inner)])
    head_dim = query_gain.shape[0]
    return (context, d_query, share[:, :head_dim], share[:, head_dim:])


def solution(mesh):
    placed = (
        P("dp", None, "tensor"),
        P("dp", None, "tensor"),
        P(),
        P(),
        P("dp", "tensor"),
        P("dp", "tensor"),
        P(),
        P(),
        P(),
        P("dp", None, "tensor"),
    )
    return jax.shard_map(
        per_device,
        mesh=mesh,
        in_specs=placed,
        out_specs=(
            P("dp", None, "tensor"),
            P("dp", None, "tensor"),
            P("dp", "tensor"),
            P("dp", "tensor"),
        ),
        check_vma=False,
    )
```

```python
import functools

import jax
import jax.numpy as jnp
from jax import lax
from jax.experimental import pallas as pl
from jax.experimental.pallas import tpu as pltpu
from jax.sharding import PartitionSpec as P

TILE = 128
RING = 4
EPS = 1e-06


def along_z(x, step):
    pairs = [(z * RING + y, (z + step) % RING * RING + y) for z in range(RING) for y in range(RING)]
    return lax.ppermute(x, "dp", pairs)


def by_core(x, step, z_core):
    pairs = []
    for z in range(RING):
        for y in range(RING):
            for i in range(RING):
                for c in range(2):
                    to_z, to_y = (z + step, y) if c == z_core else (z, y + step)
                    source = (z * RING + y) * 2 * RING + i * 2 + c
                    target = (to_z % RING * RING + to_y % RING) * 2 * RING + i * 2 + c
                    pairs.append((source, target))
    return lax.ppermute(x, ("dp", "tensor"), pairs)


def inner(x, step):
    return by_core(x, step, 0)


def outer(x, step):
    return by_core(x, step, 1)


def along_x(x, step):
    pairs = [(i * 2 + c, (i + step) % RING * 2 + c) for i in range(RING) for c in range(2)]
    return lax.ppermute(x, "tensor", pairs)


def other_core(x):
    return lax.ppermute(x, "tensor", [(i, i ^ 1) for i in range(2 * RING)])


def gathered(block, move):
    far, after, before = (move(block, step) for step in (2, 1, 3))
    return [block, after, far, before]


def scattered(parts, move):
    return [move(parts[step], step) for step in (3, 1, 2)]


def summed(blocks):
    total = blocks[0].astype(jnp.float32)
    for block in blocks[1:]:
        total = total + block.astype(jnp.float32)
    return total


def rms_factor(values):
    return lax.rsqrt(jnp.mean(values * values, axis=-1, keepdims=True) + EPS)


def norm_back(values, norm_multiplier, gain, grad):
    weighted = grad * gain
    inner = jnp.sum(weighted * values, axis=-1, keepdims=True)
    return (
        norm_multiplier * weighted
        - values * (norm_multiplier * norm_multiplier * norm_multiplier) * inner / values.shape[-1]
    )


def matmul(a, b, contract):
    return lax.dot_general(a, b, (contract, ((), ())), preferred_element_type=jnp.float32)


VMEM = pl.BlockSpec(memory_space=pltpu.VMEM)
SMEM = pl.BlockSpec(memory_space=pltpu.SMEM)
ANY = pl.BlockSpec(memory_space=pl.ANY)
HBM = pl.BlockSpec(memory_space=pltpu.HBM)
PARAMS = pltpu.CompilerParams(vmem_limit_bytes=16 * 1024 * 1024)


NEAR, FAR, CHIP, NEAR_SLOT = 0, 3, 6, 10


def route_kernel(tiles, slots, image_ref, numbers, far_ref, sem):
    rank, place = lax.axis_index("dp"), lax.axis_index("tensor")
    first = 2 * rank
    homes = (slots[first], slots[first + 1])
    away = [
        jnp.logical_and(homes[0] != first + i, homes[1] != first + i) for i in range(2)
    ]
    swaps = jnp.logical_or(away[0], away[1])
    far_slot = jnp.where(away[1], 1, 0)
    copy = pltpu.make_async_copy(image_ref.at[far_slot], far_ref, sem)
    copy.start()
    of_slot = jnp.where(homes[1] == first + far_slot, 1, 0)
    far_own = jnp.where(swaps, jnp.where(homes[1] >> 1 != rank, 1, 0), of_slot)
    numbers[NEAR] = 1 - far_own
    numbers[NEAR + 1] = tiles[first + 1 - far_own]
    numbers[NEAR + 2] = 0
    numbers[FAR] = far_own
    numbers[FAR + 1] = tiles[first + far_own]
    numbers[FAR + 2] = jnp.where(swaps, 1, 0)
    numbers[CHIP] = rank // RING
    numbers[CHIP + 1] = rank % RING
    numbers[CHIP + 2] = place // 2
    numbers[CHIP + 3] = place % 2
    numbers[NEAR_SLOT] = 1 - far_slot
    copy.wait()


def route(tiles, image_slot, image):
    rows = jax.ShapeDtypeStruct(image.shape[1:], image.dtype)
    return pl.pallas_call(
        route_kernel,
        in_specs=[SMEM, SMEM, HBM],
        out_specs=[SMEM, VMEM],
        out_shape=[jax.ShapeDtypeStruct((NEAR_SLOT + 1,), jnp.int32), rows],
        scratch_shapes=[pltpu.SemaphoreType.DMA],
        compiler_params=pltpu.CompilerParams(vmem_limit_bytes=60 * 1024 * 1024),
        cost_estimate=pl.CostEstimate(flops=0, bytes_accessed=4 * image.size, transcendentals=0),
    )(tiles, image_slot, image)


def lay_kernel(numbers, image_ref, key_ref, value_ref, near_ref, out_ref, sems):
    head_dim = key_ref.shape[1]
    copies = [pltpu.make_async_copy(image_ref.at[numbers[NEAR_SLOT]], near_ref, sems.at[2])]
    copies[0].start()
    for i, source in enumerate((key_ref, value_ref)):
        target = out_ref.at[:, pl.ds(i * head_dim, head_dim)]
        copies.append(pltpu.make_async_copy(source, target, sems.at[i]))
        copies[1 + i].start()
    for copy in copies:
        copy.wait()


def lay(numbers, image, key_weights, value_weights):
    count, head_dim = key_weights.shape
    return pl.pallas_call(
        lay_kernel,
        in_specs=[SMEM, HBM, HBM, HBM],
        out_specs=[VMEM, VMEM],
        out_shape=[
            jax.ShapeDtypeStruct(image.shape[1:], image.dtype),
            jax.ShapeDtypeStruct((count, 2 * head_dim), key_weights.dtype),
        ],
        scratch_shapes=[pltpu.SemaphoreType.DMA((3,))],
        compiler_params=PARAMS,
        cost_estimate=pl.CostEstimate(
            flops=0, bytes_accessed=8 * count * head_dim, transcendentals=0
        ),
    )(numbers, image, key_weights, value_weights)


def assemble_kernel(chip, *refs):
    pieces, out_ref, sems = refs[:RING], refs[RING], refs[RING + 1]
    rows, both = pieces[0].shape
    count = rows // RING
    z, y, x, core = (chip[CHIP + i] for i in range(4))
    copies = []
    for b in range(RING):
        for a in range(RING):
            from_z = (z - jnp.where(core == 0, a, b) + RING) % RING
            from_y = (y - jnp.where(core == 0, b, a) + RING) % RING
            o = (x - from_z + RING) % RING
            start = ((o * 2 + ((from_y >> 1) ^ core)) * 2 + from_y % 2) * count
            target = out_ref.at[pl.ds(pl.multiple_of(start, count), count)]
            source = pieces[b].at[pl.ds(a * count, count)]
            copies.append(pltpu.make_async_copy(source, target, sems.at[b, a]))
    for copy in copies:
        copy.start()
    for copy in copies:
        copy.wait()


def assemble(chip, pieces):
    rows, both = pieces[0].shape
    return pl.pallas_call(
        assemble_kernel,
        in_specs=[SMEM] + [ANY] * RING,
        out_specs=VMEM,
        out_shape=jax.ShapeDtypeStruct((RING * rows, both), pieces[0].dtype),
        scratch_shapes=[pltpu.SemaphoreType.DMA((RING, RING))],
        compiler_params=PARAMS,
        cost_estimate=pl.CostEstimate(
            flops=0, bytes_accessed=4 * RING * rows * both, transcendentals=0
        ),
    )(chip, *pieces)


def finish_kernel(total_ref, gain_ref, key_value_ref):
    head_dim = gain_ref.shape[1]
    raw = total_ref[:, :head_dim]
    keys = (raw * rms_factor(raw) * gain_ref[...]).astype(jnp.bfloat16)
    key_value_ref[:, :head_dim] = keys
    key_value_ref[:, head_dim:] = total_ref[:, head_dim:].astype(jnp.bfloat16)


def finish(total, gain):
    return pl.pallas_call(
        finish_kernel,
        in_specs=[VMEM] * 2,
        out_specs=VMEM,
        out_shape=jax.ShapeDtypeStruct(total.shape, jnp.bfloat16),
        compiler_params=PARAMS,
        cost_estimate=pl.CostEstimate(
            flops=3 * total.size, bytes_accessed=6 * total.size, transcendentals=total.shape[0]
        ),
    )(total, gain[None, :])


def turned(total, grad, gain):
    head_dim = gain.shape[1]
    raw = total[:, :head_dim]
    d_raw = norm_back(raw, rms_factor(raw), gain, grad[:, :head_dim].astype(jnp.float32))
    return jnp.concatenate([d_raw.astype(jnp.bfloat16), grad[:, head_dim:]], axis=1)


def product_kernel(chip, *refs):
    count = 2 * RING
    first, second, refs = refs[:count], refs[count : 2 * count], refs[2 * count :]
    first_total, first_grad, first_back, second_total, second_grad, gain_ref, *refs = refs
    first_grads = jnp.where(chip[FAR + 2] != 0, first_back[...], first_grad[...])
    first_grads = turned(first_total[...], first_grads, gain_ref[...])
    second_grads = turned(second_total[...], second_grad[...], gain_ref[...])
    outs, (held, sems) = refs[:RING], refs[RING:]
    depth = first[0].shape[1]
    count = depth // 2
    z, y, x, core = (chip[CHIP + i] for i in range(4))
    waits = []
    for k in range(len(first)):
        total = matmul(first[k][...], first_grads, ((0,), (0,)))
        total = total + matmul(second[k][...], second_grads, ((0,), (0,)))
        total = total.astype(held.dtype)
        by_z = (x - k // 2 - z + 2 * RING) % RING
        for h in range(2):
            by_y = (2 * (k % 2 ^ core) + h - y + RING) % RING
            outer_by = jnp.where(core == 0, by_y, by_z)
            inner_by = jnp.where(core == 0, by_z, by_y)
            start = pl.multiple_of(inner_by * count, count)
            held[outer_by, pl.ds(start, count)] = total[h * count : (h + 1) * count]
            for place, out in enumerate(outs):
                target = out.at[pl.ds(start, count)]
                copy = pltpu.make_async_copy(
                    held.at[place, pl.ds(start, count)], target, sems.at[k, h]
                )
                pl.when(outer_by == place)(copy.start)
            waits.append(copy)
    for copy in waits:
        copy.wait()


def product(chip, feats, others, first, second, gain):
    rows, depth = feats[0].shape
    both = first[0].shape[1]
    shape = (RING * depth // 2, both)
    return pl.pallas_call(
        product_kernel,
        in_specs=[SMEM] + [VMEM] * (2 * len(feats) + 6),
        out_specs=[ANY] * RING,
        out_shape=[jax.ShapeDtypeStruct(shape, jnp.bfloat16)] * RING,
        scratch_shapes=[
            pltpu.VMEM((RING, *shape), jnp.bfloat16),
            pltpu.SemaphoreType.DMA((len(feats), 2)),
        ],
        compiler_params=PARAMS,
        cost_estimate=pl.CostEstimate(
            flops=4 * len(feats) * rows * depth * both,
            bytes_accessed=4 * len(feats) * rows * depth,
            transcendentals=0,
        ),
    )(chip, *feats, *others, *first, *second, gain[None, :])


def attend_kernel(heads, base, index, ratio_ref, q_ref, cot_ref, kv_ref, away_ref, gain_ref, *refs):
    context_ref, d_query_ref, d_kv_ref, d_key_sum, d_value_sum = refs[-5:]
    step = pl.program_id(0)
    head_dim = gain_ref.shape[1]
    scale = head_dim ** (-0.5)
    count = index[base + 1]
    ratio = ratio_ref[0]
    gain = gain_ref[...]
    key_value = jnp.where(index[base + 2] != 0, away_ref[...], kv_ref[...])
    keys = key_value[:, :head_dim]
    vals = key_value[:, head_dim:]

    def stacked(ref):
        parts = [ref[0, :, h * head_dim : (h + 1) * head_dim] for h in range(heads)]
        return jnp.concatenate(parts, axis=0).astype(jnp.float32)

    def unstacked(ref, rows):
        text = rows.shape[0] // heads
        for h in range(heads):
            part = rows[h * text : (h + 1) * text]
            ref[0, :, h * head_dim : (h + 1) * head_dim] = part.astype(ref.dtype)

    @pl.when(step == 0)
    def _():
        d_key_sum[...] = jnp.zeros_like(d_key_sum)
        d_value_sum[...] = jnp.zeros_like(d_value_sum)

    q_raw = stacked(q_ref)
    q_factor = rms_factor(q_raw)
    q_norm = (q_raw * q_factor * gain).astype(jnp.bfloat16)
    raw = matmul(q_norm, keys, ((1,), (1,))) * scale
    place = lax.broadcasted_iota(jnp.int32, raw.shape, 1)
    expo = jnp.where(place < count * TILE, jnp.exp(raw), 0.0)
    total = jnp.sum(expo, axis=1, keepdims=True) + (count == 0).astype(jnp.float32)
    inverse = 1.0 / total
    weights_b = expo.astype(jnp.bfloat16)
    attended = matmul(weights_b, vals, ((1,), (0,))) * inverse
    unstacked(context_ref, ratio * attended)
    d_att = ratio * stacked(cot_ref)
    d_att_b = d_att.astype(jnp.bfloat16)
    scaled_b = (d_att * inverse).astype(jnp.bfloat16)
    delta = jnp.sum(d_att * attended, axis=1, keepdims=True)
    d_prob = matmul(d_att_b, vals, ((1,), (1,)))
    d_score = (expo * inverse * (d_prob - delta)).astype(jnp.bfloat16)
    d_qn = scale * matmul(d_score, keys, ((1,), (0,)))
    unstacked(d_query_ref, norm_back(q_raw, q_factor, gain, d_qn))
    d_key_sum[...] += matmul(d_score, q_norm, ((0,), (0,)))
    d_value_sum[...] += matmul(weights_b, scaled_b, ((0,), (0,)))

    @pl.when(step == pl.num_programs(0) - 1)
    def _():
        d_kv_ref[:, :head_dim] = (scale * d_key_sum[...]).astype(d_kv_ref.dtype)
        d_kv_ref[:, head_dim:] = d_value_sum[...].astype(d_kv_ref.dtype)


def attend(base, index, ratio, query, cot, key_value, away, gain, earlier, heads=8):
    rows, both = key_value.shape
    head_dim = both // 2
    text = query.shape[1]
    width = heads * head_dim
    block = pl.BlockSpec((1, text, width), lambda h, index: (index[base], 0, h))
    whole = lambda shape: pl.BlockSpec(shape, lambda h, index: (0, 0))
    in_specs = [
        pl.BlockSpec(memory_space=pltpu.SMEM),
        block,
        block,
        whole((rows, both)),
        whole((rows, both)),
        whole((1, head_dim)),
    ]
    aliases = {}
    if earlier:
        in_specs += [pl.BlockSpec(memory_space=pl.ANY)] * 2
        aliases = {7: 0, 8: 1}
    steps = query.shape[2] // width
    return pl.pallas_call(
        functools.partial(attend_kernel, heads, base),
        grid_spec=pltpu.PrefetchScalarGridSpec(
            num_scalar_prefetch=1,
            grid=(steps,),
            in_specs=in_specs,
            out_specs=[block, block, whole((rows, both))],
            scratch_shapes=[pltpu.VMEM((rows, head_dim), jnp.float32)] * 2,
        ),
        out_shape=[
            jax.ShapeDtypeStruct(query.shape, jnp.bfloat16),
            jax.ShapeDtypeStruct(query.shape, jnp.bfloat16),
            jax.ShapeDtypeStruct((rows, both), jnp.bfloat16),
        ],
        input_output_aliases=aliases,
        compiler_params=pltpu.CompilerParams(
            vmem_limit_bytes=24 * 1024 * 1024
        ),
        cost_estimate=pl.CostEstimate(
            flops=14 * steps * heads * text * rows * head_dim,
            bytes_accessed=8 * text * steps * width + 6 * rows * head_dim,
            transcendentals=steps * heads * text * rows,
        ),
    )(
        index,
        ratio,
        query,
        cot,
        key_value,
        away,
        gain[None, :],
        *earlier,
    )


def per_device(
    query,
    image,
    tiles,
    image_slot,
    key_weight_matrix,
    value_weight_matrix,
    query_gain,
    key_gain,
    gate,
    cotangent,
):
    ratio = jnp.tanh(gate)
    numbers, far_own = route(tiles, image_slot, image)

    def opposite(after, before, move):
        half = after.shape[0] // 2
        return [move(after[:half], 1), move(before[half:], 3)]

    near_own, shard = lay(numbers, image, key_weight_matrix, value_weight_matrix)
    far_x = [along_x(far_own, 1), along_x(far_own, 3)]
    shard = jnp.concatenate(gathered(shard, inner), axis=0)
    shard, *far_x = lax.optimization_barrier((shard, *far_x))
    far_halves = opposite(*far_x, along_x)
    pieces = gathered(shard, outer)
    near_own, far_own, *far_halves = lax.optimization_barrier((near_own, far_own, *far_halves))
    near_x = [along_x(near_own, 1), along_x(near_own, 3)]
    weights = assemble(numbers, pieces)
    weights, *far_blocks = lax.optimization_barrier((weights, *far_x, *far_halves))

    def other_cores(*blocks):
        return [other_core(block) for block in blocks]

    def paired(own, other, after, before, opposite, after_other, before_other, opposite_other):
        return [own, other, after, after_other, opposite, opposite_other, before, before_other]

    def project(feats):
        depth = feats[0].shape[1]
        total = None
        for o in (0, 1, 3, 2):
            for k in (2 * o, 2 * o + 1):
                part = matmul(feats[k], weights[k * depth : (k + 1) * depth], ((1,), (0,)))
                total = part if total is None else total + part
        return total

    shared = (numbers, ratio, query, cotangent)
    after, before, *halves = far_blocks
    blocks = [after, before, jnp.concatenate(halves, axis=0)]
    far_feats = paired(far_own, other_core(far_own), *blocks, *other_cores(*blocks))
    far_total = project(far_feats)
    far_key_value = finish(far_total, key_gain)
    away = along_z(far_key_value, RING // 2)
    _, near_own, *near_x = lax.optimization_barrier((far_key_value, near_own, *near_x))
    near_halves = opposite(*near_x, along_x)
    away, *near_x = lax.optimization_barrier((away, *near_x))
    near_others = other_cores(*near_x)
    *earlier, far_grad = attend(FAR, *shared, far_key_value, away, query_gain, ())
    back = along_z(far_grad, RING // 2)

    back, *near_halves = lax.optimization_barrier((back, *near_halves))
    blocks = [*near_x, jnp.concatenate(near_halves, axis=0)]
    near_others.append(other_core(blocks[2]))
    near_feats = paired(near_own, other_core(near_own), *blocks, *near_others)
    near_total = project(near_feats)
    near_key_value = finish(near_total, key_gain)
    context, d_query, near_grad = attend(
        NEAR, *shared, near_key_value, near_key_value, query_gain, earlier
    )

    far, near = (far_total, far_grad, back), (near_total, near_grad)
    blocks = product(numbers, far_feats, near_feats, far, near, key_gain)
    total = summed([blocks[0], *scattered(blocks, outer)])
    count = total.shape[0] // RING
    parts = [total[d * count : (d + 1) * count] for d in range(RING)]
    sent = [None] + [part.astype(jnp.bfloat16) for part in parts[1:]]
    share = summed([parts[0], *scattered(sent, inner)])
    head_dim = query_gain.shape[0]
    return (context, d_query, share[:, :head_dim], share[:, head_dim:])


def solution(mesh):
    placed = (
        P("dp", None, "tensor"),
        P("dp", None, "tensor"),
        P(),
        P(),
        P("dp", "tensor"),
        P("dp", "tensor"),
        P(),
        P(),
        P(),
        P("dp", None, "tensor"),
    )
    return jax.shard_map(
        per_device,
        mesh=mesh,
        in_specs=placed,
        out_specs=(
            P("dp", None, "tensor"),
            P("dp", None, "tensor"),
            P("dp", "tensor"),
            P("dp", "tensor"),
        ),
        check_vma=False,
    )
```

```python
import functools

import jax
import jax.numpy as jnp
from jax import lax
from jax.experimental import pallas as pl
from jax.experimental.pallas import tpu as pltpu
from jax.sharding import PartitionSpec as P

TILE = 128
RING = 4
EPS = 1e-06


def along_z(x, step):
    pairs = [(z * RING + y, (z + step) % RING * RING + y) for z in range(RING) for y in range(RING)]
    return lax.ppermute(x, "dp", pairs)


def by_core(x, step, z_core):
    pairs = []
    for z in range(RING):
        for y in range(RING):
            for i in range(RING):
                for c in range(2):
                    to_z, to_y = (z + step, y) if c == z_core else (z, y + step)
                    source = (z * RING + y) * 2 * RING + i * 2 + c
                    target = (to_z % RING * RING + to_y % RING) * 2 * RING + i * 2 + c
                    pairs.append((source, target))
    return lax.ppermute(x, ("dp", "tensor"), pairs)


def inner(x, step):
    return by_core(x, step, 0)


def outer(x, step):
    return by_core(x, step, 1)


def along_x(x, step):
    pairs = [(i * 2 + c, (i + step) % RING * 2 + c) for i in range(RING) for c in range(2)]
    return lax.ppermute(x, "tensor", pairs)


def other_core(x):
    return lax.ppermute(x, "tensor", [(i, i ^ 1) for i in range(2 * RING)])


def gathered(block, move):
    far, after, before = (move(block, step) for step in (2, 1, 3))
    return [block, after, far, before]


def scattered(parts, move):
    return [move(parts[step], step) for step in (3, 1, 2)]


def summed(blocks):
    total = blocks[0].astype(jnp.float32)
    for block in blocks[1:]:
        total = total + block.astype(jnp.float32)
    return total


def rms_factor(values):
    return lax.rsqrt(jnp.mean(values * values, axis=-1, keepdims=True) + EPS)


def norm_back(values, norm_multiplier, gain, grad):
    weighted = grad * gain
    inner = jnp.sum(weighted * values, axis=-1, keepdims=True)
    return (
        norm_multiplier * weighted
        - values * (norm_multiplier * norm_multiplier * norm_multiplier) * inner / values.shape[-1]
    )


def matmul(a, b, contract):
    return lax.dot_general(a, b, (contract, ((), ())), preferred_element_type=jnp.float32)


VMEM = pl.BlockSpec(memory_space=pltpu.VMEM)
SMEM = pl.BlockSpec(memory_space=pltpu.SMEM)
ANY = pl.BlockSpec(memory_space=pl.ANY)
HBM = pl.BlockSpec(memory_space=pltpu.HBM)
PARAMS = pltpu.CompilerParams(vmem_limit_bytes=16 * 1024 * 1024)


NEAR, FAR, CHIP, NEAR_SLOT = 0, 3, 6, 10


def route_kernel(tiles, slots, image_ref, numbers, far_ref, sem):
    rank, place = lax.axis_index("dp"), lax.axis_index("tensor")
    first = 2 * rank
    homes = (slots[first], slots[first + 1])
    away = [
        jnp.logical_and(homes[0] != first + i, homes[1] != first + i) for i in range(2)
    ]
    swaps = jnp.logical_or(away[0], away[1])
    far_slot = jnp.where(away[1], 1, 0)
    copy = pltpu.make_async_copy(image_ref.at[far_slot], far_ref, sem)
    copy.start()
    of_slot = jnp.where(homes[1] == first + far_slot, 1, 0)
    far_own = jnp.where(swaps, jnp.where(homes[1] >> 1 != rank, 1, 0), of_slot)
    numbers[NEAR] = 1 - far_own
    numbers[NEAR + 1] = tiles[first + 1 - far_own]
    numbers[NEAR + 2] = 0
    numbers[FAR] = far_own
    numbers[FAR + 1] = tiles[first + far_own]
    numbers[FAR + 2] = jnp.where(swaps, 1, 0)
    numbers[CHIP] = rank // RING
    numbers[CHIP + 1] = rank % RING
    numbers[CHIP + 2] = place // 2
    numbers[CHIP + 3] = place % 2
    numbers[NEAR_SLOT] = 1 - far_slot
    copy.wait()


def route(tiles, image_slot, image):
    rows = jax.ShapeDtypeStruct(image.shape[1:], image.dtype)
    return pl.pallas_call(
        route_kernel,
        in_specs=[SMEM, SMEM, HBM],
        out_specs=[SMEM, VMEM],
        out_shape=[jax.ShapeDtypeStruct((NEAR_SLOT + 1,), jnp.int32), rows],
        scratch_shapes=[pltpu.SemaphoreType.DMA],
        compiler_params=pltpu.CompilerParams(vmem_limit_bytes=60 * 1024 * 1024),
        cost_estimate=pl.CostEstimate(flops=0, bytes_accessed=4 * image.size, transcendentals=0),
    )(tiles, image_slot, image)


def lay_kernel(numbers, image_ref, key_ref, value_ref, near_ref, out_ref, sems):
    head_dim = key_ref.shape[1]
    copies = [pltpu.make_async_copy(image_ref.at[numbers[NEAR_SLOT]], near_ref, sems.at[2])]
    copies[0].start()
    for i, source in enumerate((key_ref, value_ref)):
        target = out_ref.at[:, pl.ds(i * head_dim, head_dim)]
        copies.append(pltpu.make_async_copy(source, target, sems.at[i]))
        copies[1 + i].start()
    for copy in copies:
        copy.wait()


def lay(numbers, image, key_weights, value_weights):
    count, head_dim = key_weights.shape
    return pl.pallas_call(
        lay_kernel,
        in_specs=[SMEM, HBM, HBM, HBM],
        out_specs=[VMEM, VMEM],
        out_shape=[
            jax.ShapeDtypeStruct(image.shape[1:], image.dtype),
            jax.ShapeDtypeStruct((count, 2 * head_dim), key_weights.dtype),
        ],
        scratch_shapes=[pltpu.SemaphoreType.DMA((3,))],
        compiler_params=PARAMS,
        cost_estimate=pl.CostEstimate(
            flops=0, bytes_accessed=8 * count * head_dim, transcendentals=0
        ),
    )(numbers, image, key_weights, value_weights)


def assemble_kernel(chip, *refs):
    pieces, out_ref, sems = refs[:RING], refs[RING], refs[RING + 1]
    rows, both = pieces[0].shape
    count = rows // RING
    z, y, x, core = (chip[CHIP + i] for i in range(4))
    copies = []
    for b in range(RING):
        for a in range(RING):
            from_z = (z - jnp.where(core == 0, a, b) + RING) % RING
            from_y = (y - jnp.where(core == 0, b, a) + RING) % RING
            o = (x - from_z + RING) % RING
            start = ((o * 2 + ((from_y >> 1) ^ core)) * 2 + from_y % 2) * count
            target = out_ref.at[pl.ds(pl.multiple_of(start, count), count)]
            source = pieces[b].at[pl.ds(a * count, count)]
            copies.append(pltpu.make_async_copy(source, target, sems.at[b, a]))
    for copy in copies:
        copy.start()
    for copy in copies:
        copy.wait()


def assemble(chip, pieces):
    rows, both = pieces[0].shape
    return pl.pallas_call(
        assemble_kernel,
        in_specs=[SMEM] + [ANY] * RING,
        out_specs=VMEM,
        out_shape=jax.ShapeDtypeStruct((RING * rows, both), pieces[0].dtype),
        scratch_shapes=[pltpu.SemaphoreType.DMA((RING, RING))],
        compiler_params=PARAMS,
        cost_estimate=pl.CostEstimate(
            flops=0, bytes_accessed=4 * RING * rows * both, transcendentals=0
        ),
    )(chip, *pieces)


def finish_kernel(total_ref, gain_ref, key_value_ref):
    head_dim = gain_ref.shape[1]
    raw = total_ref[:, :head_dim]
    keys = (raw * rms_factor(raw) * gain_ref[...]).astype(jnp.bfloat16)
    key_value_ref[:, :head_dim] = keys
    key_value_ref[:, head_dim:] = total_ref[:, head_dim:].astype(jnp.bfloat16)


def finish(total, gain):
    return pl.pallas_call(
        finish_kernel,
        in_specs=[VMEM] * 2,
        out_specs=VMEM,
        out_shape=jax.ShapeDtypeStruct(total.shape, jnp.bfloat16),
        compiler_params=PARAMS,
        cost_estimate=pl.CostEstimate(
            flops=3 * total.size, bytes_accessed=6 * total.size, transcendentals=total.shape[0]
        ),
    )(total, gain[None, :])


def turned(total, grad, gain):
    head_dim = gain.shape[1]
    raw = total[:, :head_dim]
    d_raw = norm_back(raw, rms_factor(raw), gain, grad[:, :head_dim].astype(jnp.float32))
    return jnp.concatenate([d_raw.astype(jnp.bfloat16), grad[:, head_dim:]], axis=1)


def product_kernel(chip, *refs):
    count = 2 * RING
    first, second, refs = refs[:count], refs[count : 2 * count], refs[2 * count :]
    first_total, first_grad, first_back, second_total, second_grad, gain_ref, *refs = refs
    first_grads = jnp.where(chip[FAR + 2] != 0, first_back[...], first_grad[...])
    first_grads = turned(first_total[...], first_grads, gain_ref[...])
    second_grads = turned(second_total[...], second_grad[...], gain_ref[...])
    (out_ref,) = refs
    depth = first[0].shape[1]
    count = depth // 2
    z, y, x, core = (chip[CHIP + i] for i in range(4))
    for k in range(len(first)):
        total = matmul(first[k][...], first_grads, ((0,), (0,)))
        total = total + matmul(second[k][...], second_grads, ((0,), (0,)))
        total = total.astype(out_ref.dtype)
        by_z = (x - k // 2 - z + 2 * RING) % RING
        for h in range(2):
            by_y = (2 * (k % 2 ^ core) + h - y + RING) % RING
            outer_by = jnp.where(core == 0, by_y, by_z)
            inner_by = jnp.where(core == 0, by_z, by_y)
            start = pl.multiple_of((outer_by * RING + inner_by) * count, count)
            out_ref[pl.ds(start, count)] = total[h * count : (h + 1) * count]


def product(chip, feats, others, first, second, gain):
    rows, depth = feats[0].shape
    both = first[0].shape[1]
    shape = (RING * depth // 2, both)
    return pl.pallas_call(
        product_kernel,
        in_specs=[SMEM] + [VMEM] * (2 * len(feats) + 6),
        out_specs=VMEM,
        out_shape=jax.ShapeDtypeStruct((RING * shape[0], both), jnp.bfloat16),
        compiler_params=PARAMS,
        cost_estimate=pl.CostEstimate(
            flops=4 * len(feats) * rows * depth * both,
            bytes_accessed=4 * len(feats) * rows * depth,
            transcendentals=0,
        ),
    )(chip, *feats, *others, *first, *second, gain[None, :])


def attend_kernel(heads, base, index, ratio_ref, q_ref, cot_ref, kv_ref, away_ref, gain_ref, *refs):
    context_ref, d_query_ref, d_kv_ref, d_key_sum, d_value_sum = refs[-5:]
    step = pl.program_id(0)
    head_dim = gain_ref.shape[1]
    scale = head_dim ** (-0.5)
    count = index[base + 1]
    ratio = ratio_ref[0]
    gain = gain_ref[...]
    key_value = jnp.where(index[base + 2] != 0, away_ref[...], kv_ref[...])
    keys = key_value[:, :head_dim]
    vals = key_value[:, head_dim:]

    def stacked(ref):
        parts = [ref[0, :, h * head_dim : (h + 1) * head_dim] for h in range(heads)]
        return jnp.concatenate(parts, axis=0).astype(jnp.float32)

    def unstacked(ref, rows):
        text = rows.shape[0] // heads
        for h in range(heads):
            part = rows[h * text : (h + 1) * text]
            ref[0, :, h * head_dim : (h + 1) * head_dim] = part.astype(ref.dtype)

    @pl.when(step == 0)
    def _():
        d_key_sum[...] = jnp.zeros_like(d_key_sum)
        d_value_sum[...] = jnp.zeros_like(d_value_sum)

    q_raw = stacked(q_ref)
    q_factor = rms_factor(q_raw)
    q_norm = (q_raw * q_factor * gain).astype(jnp.bfloat16)
    raw = matmul(q_norm, keys, ((1,), (1,))) * scale
    place = lax.broadcasted_iota(jnp.int32, raw.shape, 1)
    expo = jnp.where(place < count * TILE, jnp.exp(raw), 0.0)
    total = jnp.sum(expo, axis=1, keepdims=True) + (count == 0).astype(jnp.float32)
    inverse = 1.0 / total
    weights_b = expo.astype(jnp.bfloat16)
    attended = matmul(weights_b, vals, ((1,), (0,))) * inverse
    unstacked(context_ref, ratio * attended)
    d_att = ratio * stacked(cot_ref)
    d_att_b = d_att.astype(jnp.bfloat16)
    scaled_b = (d_att * inverse).astype(jnp.bfloat16)
    delta = jnp.sum(d_att * attended, axis=1, keepdims=True)
    d_prob = matmul(d_att_b, vals, ((1,), (1,)))
    d_score = (expo * inverse * (d_prob - delta)).astype(jnp.bfloat16)
    d_qn = scale * matmul(d_score, keys, ((1,), (0,)))
    unstacked(d_query_ref, norm_back(q_raw, q_factor, gain, d_qn))
    d_key_sum[...] += matmul(d_score, q_norm, ((0,), (0,)))
    d_value_sum[...] += matmul(weights_b, scaled_b, ((0,), (0,)))

    @pl.when(step == pl.num_programs(0) - 1)
    def _():
        d_kv_ref[:, :head_dim] = (scale * d_key_sum[...]).astype(d_kv_ref.dtype)
        d_kv_ref[:, head_dim:] = d_value_sum[...].astype(d_kv_ref.dtype)


def attend(base, index, ratio, query, cot, key_value, away, gain, earlier, heads=8):
    rows, both = key_value.shape
    head_dim = both // 2
    text = query.shape[1]
    width = heads * head_dim
    block = pl.BlockSpec((1, text, width), lambda h, index: (index[base], 0, h))
    whole = lambda shape: pl.BlockSpec(shape, lambda h, index: (0, 0))
    in_specs = [
        pl.BlockSpec(memory_space=pltpu.SMEM),
        block,
        block,
        whole((rows, both)),
        whole((rows, both)),
        whole((1, head_dim)),
    ]
    aliases = {}
    if earlier:
        in_specs += [pl.BlockSpec(memory_space=pl.ANY)] * 2
        aliases = {7: 0, 8: 1}
    steps = query.shape[2] // width
    return pl.pallas_call(
        functools.partial(attend_kernel, heads, base),
        grid_spec=pltpu.PrefetchScalarGridSpec(
            num_scalar_prefetch=1,
            grid=(steps,),
            in_specs=in_specs,
            out_specs=[block, block, whole((rows, both))],
            scratch_shapes=[pltpu.VMEM((rows, head_dim), jnp.float32)] * 2,
        ),
        out_shape=[
            jax.ShapeDtypeStruct(query.shape, jnp.bfloat16),
            jax.ShapeDtypeStruct(query.shape, jnp.bfloat16),
            jax.ShapeDtypeStruct((rows, both), jnp.bfloat16),
        ],
        input_output_aliases=aliases,
        compiler_params=pltpu.CompilerParams(
            vmem_limit_bytes=24 * 1024 * 1024
        ),
        cost_estimate=pl.CostEstimate(
            flops=14 * steps * heads * text * rows * head_dim,
            bytes_accessed=8 * text * steps * width + 6 * rows * head_dim,
            transcendentals=steps * heads * text * rows,
        ),
    )(
        index,
        ratio,
        query,
        cot,
        key_value,
        away,
        gain[None, :],
        *earlier,
    )


def per_device(
    query,
    image,
    tiles,
    image_slot,
    key_weight_matrix,
    value_weight_matrix,
    query_gain,
    key_gain,
    gate,
    cotangent,
):
    ratio = jnp.tanh(gate)
    numbers, far_own = route(tiles, image_slot, image)

    def opposite(after, before, move):
        half = after.shape[0] // 2
        return [move(after[:half], 1), move(before[half:], 3)]

    near_own, shard = lay(numbers, image, key_weight_matrix, value_weight_matrix)
    far_x = [along_x(far_own, 1), along_x(far_own, 3)]
    shard = jnp.concatenate(gathered(shard, inner), axis=0)
    shard, *far_x = lax.optimization_barrier((shard, *far_x))
    far_halves = opposite(*far_x, along_x)
    pieces = gathered(shard, outer)
    near_own, far_own, *far_halves = lax.optimization_barrier((near_own, far_own, *far_halves))
    near_x = [along_x(near_own, 1), along_x(near_own, 3)]
    weights = assemble(numbers, pieces)
    weights, *far_blocks = lax.optimization_barrier((weights, *far_x, *far_halves))

    def other_cores(*blocks):
        return [other_core(block) for block in blocks]

    def paired(own, other, after, before, opposite, after_other, before_other, opposite_other):
        return [own, other, after, after_other, opposite, opposite_other, before, before_other]

    def project(feats):
        depth = feats[0].shape[1]
        total = None
        for o in (0, 1, 3, 2):
            for k in (2 * o, 2 * o + 1):
                part = matmul(feats[k], weights[k * depth : (k + 1) * depth], ((1,), (0,)))
                total = part if total is None else total + part
        return total

    shared = (numbers, ratio, query, cotangent)
    after, before, *halves = far_blocks
    blocks = [after, before, jnp.concatenate(halves, axis=0)]
    far_feats = paired(far_own, other_core(far_own), *blocks, *other_cores(*blocks))
    far_total = project(far_feats)
    far_key_value = finish(far_total, key_gain)
    away = along_z(far_key_value, RING // 2)
    _, near_own, *near_x = lax.optimization_barrier((far_key_value, near_own, *near_x))
    near_halves = opposite(*near_x, along_x)
    away, *near_x = lax.optimization_barrier((away, *near_x))
    near_others = other_cores(*near_x)
    *earlier, far_grad = attend(FAR, *shared, far_key_value, away, query_gain, ())
    back = along_z(far_grad, RING // 2)

    back, *near_halves = lax.optimization_barrier((back, *near_halves))
    blocks = [*near_x, jnp.concatenate(near_halves, axis=0)]
    near_others.append(other_core(blocks[2]))
    near_feats = paired(near_own, other_core(near_own), *blocks, *near_others)
    near_total = project(near_feats)
    near_key_value = finish(near_total, key_gain)
    context, d_query, near_grad = attend(
        NEAR, *shared, near_key_value, near_key_value, query_gain, earlier
    )

    far, near = (far_total, far_grad, back), (near_total, near_grad)
    blocks = product(numbers, far_feats, near_feats, far, near, key_gain)
    blocks = jnp.split(blocks, RING, axis=0)
    total = summed([blocks[0], *scattered(blocks, outer)])
    count = total.shape[0] // RING
    parts = [total[d * count : (d + 1) * count] for d in range(RING)]
    sent = [None] + [part.astype(jnp.bfloat16) for part in parts[1:]]
    share = summed([parts[0], *scattered(sent, inner)])
    head_dim = query_gain.shape[0]
    return (context, d_query, share[:, :head_dim], share[:, head_dim:])


def solution(mesh):
    placed = (
        P("dp", None, "tensor"),
        P("dp", None, "tensor"),
        P(),
        P(),
        P("dp", "tensor"),
        P("dp", "tensor"),
        P(),
        P(),
        P(),
        P("dp", None, "tensor"),
    )
    return jax.shard_map(
        per_device,
        mesh=mesh,
        in_specs=placed,
        out_specs=(
            P("dp", None, "tensor"),
            P("dp", None, "tensor"),
            P("dp", "tensor"),
            P("dp", "tensor"),
        ),
        check_vma=False,
    )
```
